32 devices in a mesh: blk: 4 (over z), wide: 8 (over y, x, core).
Axes of the slice: x: 2, y: 2, z: 4, core: 2. Of those that a mesh axis runs over, the one named last changes fastest.
Arguments:
- tokens: bfloat16 [8, 1280, 2048], P('wide', 'blk'), may hold values from -6 to 6
- lengths: int32 [8, 3], replicated, may hold values from 1 to 1278, as said below
- query_weight: bfloat16 [2048, 2048], P('blk', 'wide'), may hold values from -0.125 to 0.125
- key_weight: bfloat16 [2048, 2048], P('blk', 'wide'), may hold values from -0.125 to 0.125
- value_weight: bfloat16 [2048, 2048], P('blk', 'wide'), may hold values from -0.125 to 0.125
- output_weight: bfloat16 [2048, 2048], P('wide', 'blk'), may hold values from -0.125 to 0.125
- query_gain: bfloat16 [2048], P('wide'), may hold values from 0.796875 to 1.59375
- key_gain: bfloat16 [2048], P('wide'), may hold values from 0.796875 to 1.59375
- attention_gain: bfloat16 [2048], P('wide'), may hold values from 0.5 to 1.5
- gate_weight: bfloat16 [2048, 8192], P(None, 'wide'), may hold values from -0.125 to 0.125
- up_weight: bfloat16 [2048, 8192], P(None, 'wide'), may hold values from -0.125 to 0.125
- down_weight: bfloat16 [8192, 2048], P('wide'), may hold values from -0.0625 to 0.0625
- feedforward_gain: bfloat16 [2048], P('wide'), may hold values from 0.5 to 1.5
- cotangent: bfloat16 [8, 1280, 2048], P('wide', 'blk'), may hold values from -6 to 6
Outputs:
- block_output: bfloat16 [8, 1280, 2048], P('wide', 'blk')
- tokens_grad: float32 [8, 1280, 2048], P('wide', 'blk')
- query_grad: float32 [2048, 2048], P('blk', 'wide')
- key_grad: float32 [2048, 2048], P('blk', 'wide')
- value_grad: float32 [2048, 2048], P('blk', 'wide')
- output_grad: float32 [2048, 2048], P('wide', 'blk')
- query_gain_grad: float32 [2048], P(('blk', 'wide'))
- key_gain_grad: float32 [2048], P(('blk', 'wide'))
- attention_gain_grad: float32 [2048], P(('blk', 'wide'))
- gate_grad: float32 [2048, 8192], P('blk', 'wide')
- up_grad: float32 [2048, 8192], P('blk', 'wide')
- down_grad: float32 [8192, 2048], P('wide', 'blk')
- feedforward_gain_grad: float32 [2048], P(('blk', 'wide'))
The draws below stay inside these ranges and needn't reach their ends.
Inputs may be any that keep to these rules, and one draw needn't show every extreme that they name: Each group holds 3 packed sequences whose lengths sum to 1280; the first and the last hold at most a quarter of 320 tokens each.
All inputs are finite; a program needn't handle non-finite values.
Results may differ from the reference program's by a relative error of at most 0.033.
Values may be sent and summed in bfloat16 or wider, within the bound.
A program may use at most 384 MiB of HBM per device.

```python
import jax
import jax.numpy as jnp
from jax import lax

D = 2048
H = 16
HD = 128
FF = 8192
GROUPS = 8
GROUP_TOK = 1280
DEV_ROWS = 320


def draw_lengths(key, part):
    key = jax.random.fold_in(key, 11)
    lead_key, trail_key, pick_key = jax.random.split(key, 3)
    quarter = DEV_ROWS // 4
    leading = jax.random.randint(lead_key, (GROUPS, 1), 1, quarter + 1, dtype=jnp.int32)
    trailing = jax.random.randint(trail_key, (GROUPS, 1), 1, quarter + 1, dtype=jnp.int32)
    chosen = jax.random.randint(pick_key, (), 0, GROUPS, dtype=jnp.int32)
    marked = (jnp.arange(GROUPS, dtype=jnp.int32) == chosen)[:, None]
    leading = jnp.where(marked, 1, leading).astype(jnp.int32)
    trailing = jnp.where(marked, 1, trailing).astype(jnp.int32)
    central = GROUP_TOK - leading - trailing
    return jnp.concatenate([leading, central, trailing], axis=1).astype(jnp.int32)


def level_of(rng, dims, cuts, least, high):
    factor_of, own = 1.0, jax.random.fold_in(rng, 6)
    for dim, shards_of in cuts:
        heights = jnp.exp(jax.random.uniform(jax.random.fold_in(own, dim), (shards_of,), jnp.float32, least / len(cuts), high / len(cuts)))
        factor_of = factor_of * jnp.repeat(heights, dims[dim] // shards_of).reshape([-1 if axis == dim else 1 for axis in range(len(dims))])
    return factor_of


def noise(own_key, extent, width, reach, shards=(), kind=jnp.bfloat16):
    loudness = level_of(own_key, extent, shards, -0.22, 0.18) if shards else 1.0
    values = jax.random.normal(own_key, extent, jnp.float32) * width * loudness
    return jnp.minimum(jnp.maximum(values, -reach), reach).astype(kind)


def setup_inputs(seed: int = 0) -> dict:
    key_list = jax.random.split(jax.random.key(seed), 15)
    return {
        "tokens": noise(key_list[0], (GROUPS, GROUP_TOK, D), 1.0, 6.0, ((0, 8), (1, 4))),
        "lengths": draw_lengths(jax.random.fold_in(key_list[14], 71), 0),
        "query_weight": noise(key_list[2], (D, D), D ** -0.5, 0.125, ((0, 4), (1, 8))),
        "key_weight": noise(key_list[3], (D, D), D ** -0.5, 0.125, ((0, 4), (1, 8))),
        "value_weight": noise(key_list[4], (D, D), D ** -0.5, 0.125, ((0, 4), (1, 8))),
        "output_weight": noise(key_list[5], (D, D), D ** -0.5, 0.125, ((0, 8), (1, 4))),
        "query_gain": jnp.clip(0.796875 + 0.796875 * jax.random.uniform(key_list[6], (D,), jnp.float32) ** level_of(key_list[6], (D,), ((0, 8),), -0.2, 0.2), 0.796875, 1.59375).astype(jnp.bfloat16),
        "key_gain": jnp.clip(0.796875 + 0.796875 * jax.random.uniform(key_list[7], (D,), jnp.float32) ** level_of(key_list[7], (D,), ((0, 8),), -0.2, 0.2), 0.796875, 1.59375).astype(jnp.bfloat16),
        "attention_gain": jnp.clip(0.5 + 1.0 * jax.random.uniform(key_list[8], (D,), jnp.float32) ** level_of(key_list[8], (D,), ((0, 8),), -0.2, 0.2), 0.5, 1.5).astype(jnp.bfloat16),
        "gate_weight": noise(key_list[9], (D, FF), D ** -0.5, 0.125, ((1, 8),)),
        "up_weight": noise(key_list[10], (D, FF), D ** -0.5, 0.125, ((1, 8),)),
        "down_weight": noise(key_list[11], (FF, D), FF ** -0.5, 0.0625, ((0, 8),)),
        "feedforward_gain": jnp.clip(0.5 + 1.0 * jax.random.uniform(key_list[12], (D,), jnp.float32) ** level_of(key_list[12], (D,), ((0, 8),), -0.2, 0.2), 0.5, 1.5).astype(jnp.bfloat16),
        "cotangent": noise(key_list[13], (GROUPS, GROUP_TOK, D), 1.0, 6.0, ((0, 8), (1, 4))),
    }


EPS = 1e-06
ROPE_BASE = 500000.0
NEG_FILL = -1e+30

@jax.custom_vjp
def low(v):
    return lax.optimization_barrier(v.astype(jnp.bfloat16)).astype(jnp.float32)

@jax.custom_vjp
def low_back(v):
    return v

def low_keep(v):
    return (low(v), None)

def low_pass(kept, grad):
    return (grad,)

def back_keep(v):
    return (v, None)

def back_low(kept, grad):
    return (low(grad),)
low.defvjp(low_keep, low_pass)
low_back.defvjp(back_keep, back_low)

def normalize(values):
    return values * lax.rsqrt(lax.optimization_barrier(jnp.mean(values * values, axis=-1, keepdims=True)) + EPS)

def layout(seq_lengths, row_count):
    indices = jnp.arange(row_count, dtype=jnp.int32)
    first_end = seq_lengths[0].astype(jnp.int32)
    second_end = (seq_lengths[0] + seq_lengths[1]).astype(jnp.int32)
    segment = (indices >= first_end).astype(jnp.int32) + (indices >= second_end).astype(jnp.int32)
    offsets = jnp.where(segment == 0, 0, jnp.where(segment == 1, first_end, second_end)).astype(jnp.int32)
    return (segment, (indices - offsets).astype(jnp.int32))

def rotary(values, position, direction):
    row_count = values.shape[0]
    heads_split = values.reshape(row_count, H, HD)
    frequency = ROPE_BASE ** (-jnp.arange(0, HD, 2, dtype=jnp.float32) / HD)
    angles = position.astype(jnp.float32)[:, None] * frequency[None, :]
    cosine_table = jnp.concatenate([jnp.cos(angles), jnp.cos(angles)], axis=-1)[:, None, :]
    sine_table = direction * jnp.concatenate([jnp.sin(angles), jnp.sin(angles)], axis=-1)[:, None, :]
    first_half = heads_split[..., :HD // 2]
    second_half = heads_split[..., HD // 2:]
    turned = jnp.concatenate([-second_half, first_half], axis=-1)
    return (heads_split * cosine_table + turned * sine_table).reshape(row_count, D)

def layer(inputs, seq_lengths, query_weight, key_weight, value_weight, output_weight, query_gain, key_gain, attention_gain, gate_weight, up_weight, down_weight, feedforward_gain):
    highest = lax.Precision.HIGHEST
    row_count = inputs.shape[0]
    segment, position = layout(seq_lengths, row_count)
    query_pre = low_back(jnp.dot(inputs, query_weight, precision=highest))
    key_pre = low_back(jnp.dot(inputs, key_weight, precision=highest))
    value_pre = low_back(jnp.dot(inputs, value_weight, precision=highest))
    queries = low(rotary(normalize(query_pre) * query_gain, position, 1.0))
    key_rows = low(rotary(normalize(key_pre) * key_gain, position, 1.0))
    values = low(value_pre)
    query_heads = queries.reshape(row_count, H, HD)
    key_heads = key_rows.reshape(row_count, H, HD)
    value_heads = values.reshape(row_count, H, HD)
    scores = low_back(jnp.einsum('qhd,khd->hqk', query_heads, key_heads, precision=highest) * HD ** (-0.5))
    indices = jnp.arange(row_count, dtype=jnp.int32)
    allowed = (segment[:, None] == segment[None, :]) & (indices[:, None] >= indices[None, :])
    scores = jnp.where(allowed[None], scores, NEG_FILL)
    weights = low(jax.nn.softmax(scores, axis=-1))
    mixed = jnp.einsum('hqk,khd->qhd', weights, value_heads, precision=highest).reshape(row_count, D)
    mixed = low(low_back(mixed))
    projected = low_back(jnp.dot(mixed, output_weight, precision=highest))
    hidden_state = inputs + normalize(projected) * attention_gain
    rounded = low(hidden_state)
    gate_rows = low_back(jnp.dot(rounded, gate_weight, precision=highest))
    upward = low_back(jnp.dot(rounded, up_weight, precision=highest))
    activated = low(jax.nn.silu(gate_rows) * upward)
    reduced = low_back(jnp.dot(activated, down_weight, precision=highest))
    return hidden_state + normalize(reduced) * feedforward_gain

def reference(tokens, lengths, query_weight, key_weight, value_weight, output_weight, query_gain, key_gain, attention_gain, gate_weight, up_weight, down_weight, feedforward_gain, cotangent):
    params = tuple((weight.astype(jnp.float32) for weight in (query_weight, key_weight, value_weight, output_weight, query_gain, key_gain, attention_gain, gate_weight, up_weight, down_weight, feedforward_gain)))

    def one_group(totals, slices):
        inputs, seq_lengths, grad_out = slices

        def forward(inputs, *weights):
            return layer(inputs, seq_lengths, *weights)
        result, pullback = jax.vjp(forward, inputs, *params)
        gradients = pullback(grad_out)
        totals = tuple((total + grad for total, grad in zip(totals, gradients[1:])))
        return (totals, (result.astype(jnp.bfloat16), gradients[0]))
    initial = tuple((jnp.zeros_like(weight) for weight in params))
    totals, (outputs, input_grads) = lax.scan(one_group, initial, (tokens.astype(jnp.float32), lengths, cotangent.astype(jnp.float32)))
    return (outputs, input_grads, totals[0], totals[1], totals[2], totals[3], totals[4], totals[5], totals[6], totals[7], totals[8], totals[9], totals[10])
```

```python
import functools

import jax
import jax.numpy as jnp
from jax import lax
from jax.experimental import pallas as pl
from jax.experimental.pallas import tpu as pltpu
from jax.sharding import PartitionSpec as P

MESH = pl.DeviceIdType.MESH

D = 2048
HD = 128
EPS = 1e-06
ROPE_BASE = 500000.0
NEG_FILL = -1e30
VMEM_LIMIT = 60 * 1024 * 1024
SCALE = HD ** (-0.5)


def busy(micros):
    return pl.CostEstimate(flops=0, bytes_accessed=int(micros * 3.5e6), transcendentals=0)


def layout(seq_lengths, row_count):
    indices = jnp.arange(row_count, dtype=jnp.int32)
    first_end = seq_lengths[0]
    second_end = seq_lengths[0] + seq_lengths[1]
    segment = (indices >= first_end).astype(jnp.int32) + (indices >= second_end).astype(jnp.int32)
    offsets = jnp.where(segment == 0, 0, jnp.where(segment == 1, first_end, second_end))
    return (segment, indices - offsets)


def rope_tables(position):
    frequency = ROPE_BASE ** (-jnp.arange(0, HD, 2, dtype=jnp.float32) / HD)
    angles = position.astype(jnp.float32)[:, None] * frequency[None, :]
    cosine, sine = jnp.cos(angles), jnp.sin(angles)
    return (jnp.concatenate([cosine, cosine], -1), jnp.concatenate([-sine, sine], -1))


def rms_pair(values):
    inverse = lax.rsqrt(jnp.mean(values * values, axis=-1, keepdims=True) + EPS)
    return (values * inverse, inverse)


def norm_back(normed, inverse, grad_normed):
    return inverse * (grad_normed - normed * jnp.mean(grad_normed * normed, axis=-1, keepdims=True))


def dot(left, right):
    return jnp.dot(left, right, preferred_element_type=jnp.float32)


def contract_rows(left, right):
    return lax.dot_general(
        left, right, (((0,), (0,)), ((), ())), preferred_element_type=jnp.float32
    )


def contract_cols(left, right):
    return lax.dot_general(
        left, right, (((1,), (1,)), ((), ())), preferred_element_type=jnp.float32
    )


def flip(me, k):
    out, bit = me, 1
    while bit <= k:
        if k & bit:
            out = out + bit * (1 - 2 * ((me // bit) % 2))
        bit *= 2
    return out


def greet(axis, me, others):
    barrier = pltpu.get_barrier_semaphore()
    for k in others:
        pl.semaphore_signal(barrier, inc=1, device_id={axis: flip(me, k)}, device_id_type=MESH)
    pl.semaphore_wait(barrier, len(others))


def gather_body(width, slots, side, *refs):
    if side is None:
        x_ref, out_ref, here, send, recv = refs
    else:
        x_ref, side_ref, out_ref, side_out, here, send, recv, side_send, side_recv = refs
    me = lax.axis_index("wide")
    rows = x_ref.shape[0]
    half = rows // 2
    evens = list(range(2, width, 2))
    peers = [{"wide": flip(me, k)} for k in [1] + evens]
    if side is not None:
        hops = Hops(width // slots, slots, rows)
        peers = peers + [{"blk": (hops.plane + k) % hops.planes} for k in range(1, hops.planes)]
    hello(peers)
    if side is not None:
        job = hops.join if side == "join" else hops.spread
        job(side_ref, side_out, side_send, side_recv, True, True)

    def spot(who, first, count):
        base = ((who % slots) * (width // slots) + who // slots) * rows
        return out_ref.at[pl.ds(pl.multiple_of(base + first, half), count)]

    def move(origin, target, k, part):
        if origin is None:
            source = x_ref.at[pl.ds(part * half, half)]
        else:
            source = spot(flip(me, origin), part * half, half)
        return pltpu.make_async_remote_copy(
            src_ref=source,
            dst_ref=spot(flip(flip(me, target), k), part * half, half),
            send_sem=send.at[k, part],
            recv_sem=recv.at[k, part],
            device_id={"wide": flip(me, target)},
            device_id_type=MESH,
        )

    def arrived(k, part):
        block = spot(flip(me, k), part * half, half)
        pltpu.make_async_copy(block, block, recv.at[k, part]).wait()

    moves = []

    def go(origin, target, k, part):
        copy = move(origin, target, k, part)
        copy.start()
        moves.append(copy)

    mine = pltpu.make_async_copy(x_ref, spot(me, 0, rows), here)
    mine.start()
    if width == 8:
        go(None, 2, 2, 0)
        go(None, 4, 4, 1)
        go(None, 2, 2, 1)
        go(None, 4, 4, 0)
        go(None, 1, 1, 0)
        go(None, 1, 1, 1)
        arrived(2, 0)
        go(2, 4, 6, 0)
        go(2, 1, 3, 0)
        arrived(4, 1)
        go(4, 2, 6, 1)
        go(4, 1, 5, 1)
        order = [(2, 1), (4, 0), (6, 0), (6, 1)]
    else:
        for k in evens:
            go(None, k, k, 0)
            go(None, k, k, 1)
        go(None, 1, 1, 0)
        go(None, 1, 1, 1)
        order = [(k, part) for k in evens for part in (0, 1)]
    for k, part in order:
        arrived(k, part)
        go(k, 1, k + 1, part)
    for k in range(1, width, 2):
        for part in (0, 1):
            arrived(k, part)
    for copy in moves:
        copy.wait_send()
    mine.wait()
    if side is not None:
        job(side_ref, side_out, side_send, side_recv, True, False)


def gather(x, width, slots, ident, name, side=None, side_x=None):
    rows, cols = x.shape
    planes = width // slots
    dma = pltpu.SemaphoreType.DMA
    shapes = [jax.ShapeDtypeStruct((rows * width, cols), x.dtype)]
    scratch = [dma, dma((width, 2)), dma((width, 2))]
    inputs = [x]
    if side is not None:
        inputs.append(side_x)
        extent = rows if side == "join" else many_rows(planes, rows)
        shapes.append(jax.ShapeDtypeStruct((extent, cols), side_x.dtype))
        scratch += [dma((planes,)), dma((planes,))]
    outs = pl.pallas_call(
        functools.partial(gather_body, width, slots, side),
        out_shape=shapes,
        in_specs=[pl.BlockSpec(memory_space=pl.ANY)] * len(inputs),
        out_specs=[pl.BlockSpec(memory_space=pl.ANY)] * len(shapes),
        scratch_shapes=scratch,
        cost_estimate=busy(50),
        compiler_params=pltpu.CompilerParams(collective_id=ident, has_side_effects=True, vmem_limit_bytes=VMEM_LIMIT),
        name=name,
    )(*inputs)
    return outs[0] if side is None else outs


def scatter_body(width, slots, flat, count, step, *refs):
    lefts, rights = refs[:count], refs[count : 2 * count]
    out_ref, odd, even, from_twin, from_far, passing, sends, recvs, pass_send, pass_recv, twin_send, twin_recv = refs[2 * count :]
    me = lax.axis_index("wide")
    rows, cols = out_ref.shape
    half = rows // 2
    evens = list(range(2, width, 2))
    greet("wide", me, [1] + evens)
    dims = (((1,), (1 if flat else 0,)), ((), ()))

    def produce(k, put, adds=()):
        who = flip(me, k)
        start = pl.multiple_of(((who % slots) * (width // slots) + who // slots) * rows, rows)

        def tile(n, carry):
            at = pl.ds(pl.multiple_of(n * step, step), step)
            total = None
            for left, right in zip(lefts, rights):
                other = right[at, :] if flat else right[:, at]
                term = lax.dot_general(
                    left[pl.ds(start, rows), :], other, dims, preferred_element_type=jnp.float32
                )
                total = term if total is None else total + term
            for ref in adds:
                total = total + ref[:, at].astype(jnp.float32)
            put[:, at] = total.astype(put.dtype)
            return carry

        lax.fori_loop(0, cols // step, tile, 0)

    def twin(k):
        return pltpu.make_async_remote_copy(
            src_ref=odd.at[k // 2],
            dst_ref=from_twin.at[k // 2],
            send_sem=twin_send.at[k // 2],
            recv_sem=twin_recv.at[k // 2],
            device_id={"wide": flip(me, 1)},
            device_id_type=MESH,
        )

    def far(k, part):
        at = pl.ds(part * half, half)
        return pltpu.make_async_remote_copy(
            src_ref=even.at[k // 2 - 1, at],
            dst_ref=from_far.at[k // 2 - 1, at],
            send_sem=sends.at[k // 2 - 1, part],
            recv_sem=recvs.at[k // 2 - 1, part],
            device_id={"wide": flip(me, k)},
            device_id_type=MESH,
        )

    def relay(part):
        at = pl.ds(part * half, half)
        return pltpu.make_async_remote_copy(
            src_ref=even.at[2, at],
            dst_ref=passing.at[part],
            send_sem=pass_send.at[part],
            recv_sem=pass_recv.at[part],
            device_id={"wide": flip(me, 2 if part == 0 else 4)},
            device_id_type=MESH,
        )

    def to_twin(k):
        produce(k + 1, odd.at[k // 2])
        twin(k).start()

    def merge(k):
        twin(k).wait_recv()
        produce(k, even.at[k // 2 - 1], (from_twin.at[k // 2],))

    def pass_on(k, part):
        relay(part).wait_recv()
        at = pl.ds(part * half, half)
        even[k // 2 - 1, at, :] = (
            even[k // 2 - 1, at, :].astype(jnp.float32) + passing[part].astype(jnp.float32)
        ).astype(jnp.bfloat16)
        far(k, part).start()

    if width == 8:
        to_twin(6)
        to_twin(2)
        to_twin(4)
        merge(6)
        relay(0).start()
        relay(1).start()
        merge(2)
        far(2, 0).start()
        merge(4)
        far(4, 1).start()
        to_twin(0)
        pass_on(2, 1)
        pass_on(4, 0)
        sources = [2, 4]
    else:
        for k in evens:
            to_twin(k)
        to_twin(0)
        for k in evens:
            merge(k)
            far(k, 0).start()
            far(k, 1).start()
        sources = evens
    twin(0).wait_recv()
    produce(0, out_ref, (from_twin.at[0],))
    for k in sources:
        far(k, 0).wait_recv()
        far(k, 1).wait_recv()
        out_ref[...] = out_ref[...] + from_far[k // 2 - 1].astype(jnp.float32)
    for k in sources:
        far(k, 0).wait_send()
        far(k, 1).wait_send()
    for k in range(0, width, 2):
        twin(k).wait_send()
    if width == 8:
        relay(0).wait_send()
        relay(1).wait_send()


def scatter(lefts, rights, width, slots, flat, ident, name, step=1024):
    rows = lefts[0].shape[0] // width
    cols = rights[0].shape[0 if flat else 1]
    chips = width // 2
    low = jnp.bfloat16
    block = lambda n: pltpu.VMEM((n, rows, cols), low)
    dma = pltpu.SemaphoreType.DMA
    return pl.pallas_call(
        functools.partial(scatter_body, width, slots, flat, len(lefts), step),
        out_shape=jax.ShapeDtypeStruct((rows, cols), jnp.float32),
        in_specs=[pl.BlockSpec(memory_space=pltpu.VMEM)] * (2 * len(lefts)),
        out_specs=pl.BlockSpec(memory_space=pltpu.VMEM),
        scratch_shapes=[
            block(chips), block(chips - 1), block(chips), block(chips - 1),
            pltpu.VMEM((2, rows // 2, cols), low),
            dma((chips - 1, 2)), dma((chips - 1, 2)), dma((2,)), dma((2,)), dma((chips,)), dma((chips,)),
        ],
        cost_estimate=busy(60),
        compiler_params=pltpu.CompilerParams(collective_id=ident, has_side_effects=True, vmem_limit_bytes=VMEM_LIMIT),
        name=name,
    )(*lefts, *rights)


def total_body(axis, width, x_ref, out_ref, slots, send, recv):
    me = lax.axis_index(axis)
    others = list(range(1, width))
    greet(axis, me, others)
    moves = []
    for k in others:
        copy = pltpu.make_async_remote_copy(
            src_ref=x_ref,
            dst_ref=slots.at[k - 1],
            send_sem=send.at[k - 1],
            recv_sem=recv.at[k - 1],
            device_id={axis: flip(me, k)},
            device_id_type=MESH,
        )
        copy.start()
        moves.append(copy)
    out_ref[...] = x_ref[...]
    for copy, k in zip(moves, others):
        copy.wait_recv()
        out_ref[...] = out_ref[...] + slots[k - 1]
    for copy in moves:
        copy.wait_send()


def total(x, axis, width, ident, name):
    return pl.pallas_call(
        functools.partial(total_body, axis, width),
        out_shape=jax.ShapeDtypeStruct(x.shape, x.dtype),
        in_specs=[pl.BlockSpec(memory_space=pltpu.VMEM)],
        out_specs=pl.BlockSpec(memory_space=pltpu.VMEM),
        scratch_shapes=[
            pltpu.VMEM((width - 1,) + x.shape, x.dtype),
            pltpu.SemaphoreType.DMA((width - 1,)),
            pltpu.SemaphoreType.DMA((width - 1,)),
        ],
        cost_estimate=busy(7),
        compiler_params=pltpu.CompilerParams(collective_id=ident, has_side_effects=True, vmem_limit_bytes=VMEM_LIMIT),
        name=name,
    )(x)


class Hops:
    def __init__(self, planes, slots, rows):
        self.planes, self.slots = planes, slots
        self.count = max(n for n in range(1, planes + 1) if planes % n == 0 and rows % (16 * n) == 0)
        self.per = planes // self.count
        self.piece = rows // self.count
        self.plane, self.place = lax.axis_index("blk"), lax.axis_index("wide")
        self.chip, self.slot = self.place // slots, self.place % slots
        self.active = self.chip // self.count == self.plane % self.per

    def peers(self):
        near = [{"wide": (self.chip + k) % self.planes * self.slots + self.slot} for k in range(1, self.planes)]
        return near + [{"blk": (self.plane + k) % self.planes} for k in range(1, self.planes)]

    def when(self, condition, action):
        if self.per == 1:
            action()
        else:
            pl.when(condition)(action)

    def split(self, condition, yes, no):
        if self.per == 1:
            yes()
        else:
            pl.when(condition)(yes)
            pl.when(jnp.logical_not(condition))(no)

    def cut(self, ref, index):
        return ref.at[pl.ds(pl.multiple_of(index * self.piece, self.piece), self.piece)]

    def remote(self, src, dst, send, recv, device):
        return pltpu.make_async_remote_copy(
            src_ref=src, dst_ref=dst, send_sem=send, recv_sem=recv, device_id=device, device_id_type=MESH
        )

    def spread(self, some, many, send, recv, across, start):
        if across:
            axis, here = "blk", self.plane
            targets = [
                ((self.plane // self.per + k) % self.count) for k in range(self.count)
            ]
            device = lambda piece: piece * self.per + self.chip // self.count
        else:
            axis, here = "wide", self.chip
            targets = [((self.chip + k) % self.count) for k in range(self.count)]
            device = lambda piece: (self.plane % self.per) * self.count + piece
        address = (lambda who: {"blk": who}) if across else (
            lambda who: {"wide": who * self.slots + self.slot}
        )
        for k, piece in enumerate(targets):
            who = device(piece)
            far = self.remote(
                self.cut(some, piece), self.cut(many, here), send.at[piece],
                recv.at[(here - who + self.planes) % self.planes], address(who),
            )
            own = pltpu.make_async_copy(self.cut(some, piece), self.cut(many, here), send.at[piece])
            if k:
                far.start() if start else far.wait_send()
            elif start:
                self.split(self.active, own.start, far.start)
            else:
                self.split(self.active, own.wait, far.wait_send)
        if not start:
            def receive():
                for k in range(1, self.planes):
                    block = self.cut(many, (here + k) % self.planes)
                    pltpu.make_async_copy(block, block, recv.at[k]).wait()

            self.when(self.active, receive)

    def join(self, many, some, send, recv, across, start):
        if across:
            here = self.plane
            index = self.plane // self.per
            address = lambda who: {"blk": who}
        else:
            here = self.chip
            index = self.chip % self.count
            address = lambda who: {"wide": who * self.slots + self.slot}

        def give():
            for k in range(1, self.planes):
                who = (here + k) % self.planes
                far = self.remote(
                    self.cut(many, who), self.cut(some, index), send.at[k], recv.at[index], address(who)
                )
                far.start() if start else far.wait_send()
            own = pltpu.make_async_copy(self.cut(many, here), self.cut(some, index), send.at[0])
            own.start() if start else own.wait()

        self.when(self.active, give)
        if not start:
            for k in range(self.count):
                piece = (index + k) % self.count
                block = self.cut(some, piece)
                arrival = pltpu.make_async_copy(block, block, recv.at[piece])
                if k:
                    arrival.wait()
                elif self.per > 1:
                    pl.when(jnp.logical_not(self.active))(arrival.wait)


def hello(peers):
    barrier = pltpu.get_barrier_semaphore()
    for peer in peers:
        pl.semaphore_signal(barrier, inc=1, device_id=peer, device_id_type=MESH)
    pl.semaphore_wait(barrier, len(peers))


def turn_in_body(planes, slots, x_ref, c_ref, near_x, near_c, out_ref, *sems):
    hops = Hops(planes, slots, x_ref.shape[0])
    hello(hops.peers())
    hops.spread(x_ref, near_x, sems[0], sems[1], False, True)
    hops.spread(x_ref, near_x, sems[0], sems[1], False, False)
    hops.join(near_x, out_ref, sems[2], sems[3], True, True)
    hops.spread(c_ref, near_c, sems[4], sems[5], False, True)
    hops.spread(c_ref, near_c, sems[4], sems[5], False, False)
    hops.join(near_x, out_ref, sems[2], sems[3], True, False)


def turn_out_body(planes, slots, x_ref, far_c, far_x, out_c, out_ref, *sems):
    hops = Hops(planes, slots, x_ref.shape[0])
    hello(hops.peers())
    hops.spread(x_ref, far_x, sems[0], sems[1], True, True)
    hops.join(far_c, out_c, sems[2], sems[3], False, True)
    hops.spread(x_ref, far_x, sems[0], sems[1], True, False)
    hops.join(far_x, out_ref, sems[4], sems[5], False, True)
    hops.join(far_c, out_c, sems[2], sems[3], False, False)
    hops.join(far_x, out_ref, sems[4], sems[5], False, False)


def many_rows(planes, rows):
    count = max(n for n in range(1, planes + 1) if planes % n == 0 and rows % (16 * n) == 0)
    return planes * (rows // count)


def turn(body, inputs, outputs, planes, slots, ident, name):
    rows, cols = inputs[0].shape
    low = inputs[0].dtype
    shape = lambda many: jax.ShapeDtypeStruct((many_rows(planes, rows) if many else rows, cols), low)
    return pl.pallas_call(
        functools.partial(body, planes, slots),
        out_shape=[shape(many) for many in outputs],
        in_specs=[pl.BlockSpec(memory_space=pl.ANY)] * len(inputs),
        out_specs=[pl.BlockSpec(memory_space=pl.ANY)] * len(outputs),
        scratch_shapes=[pltpu.SemaphoreType.DMA((planes,))] * 6,
        cost_estimate=busy(45),
        compiler_params=pltpu.CompilerParams(collective_id=ident, has_side_effects=True, vmem_limit_bytes=VMEM_LIMIT),
        name=name,
    )(*inputs)


def mask_scores(scores, first, begin, size):
    span = scores.shape[0]
    index = lax.broadcasted_iota(jnp.int32, scores.shape, 0)
    query = lax.broadcasted_iota(jnp.int32, scores.shape, 1) + first
    return jnp.where((index <= query) & (index >= begin), scores, NEG_FILL)


def nt(left, right):
    return lax.dot_general(left, right, (((1,), (1,)), ((), ())), preferred_element_type=jnp.float32)


def nn(left, right):
    return jnp.dot(left, right, preferred_element_type=jnp.float32)


def piece_map(span, size):
    planes = span // size
    count = max(n for n in range(1, planes + 1) if planes % n == 0 and size % (16 * n) == 0)
    per, piece = planes // count, size // count
    pairs = []
    for t in range(count):
        for high in range(per):
            for low in range(count):
                natural = ((t * per + high) * count + low) * piece
                pairs.append((natural, ((high * count + low) * count + t) * piece))
    return pairs, piece


def attend_body(size, q_ref, k_ref, v_ref, inv_ref, gain_ref, cos_ref, sin_ref, begin_ref,
                qo_ref, ko_ref, vo_ref, mix_ref, log_ref):
    low = jnp.bfloat16
    span = q_ref.shape[0]

    def prepare(ref, col):
        value = ref[...] * inv_ref[:, col : col + 1] * gain_ref[col : col + 1, :]
        return (value * cos_ref[...] + pltpu.roll(value, HD // 2, 1) * sin_ref[...]).astype(low)

    pairs, piece = piece_map(span, size)

    def arrange(ref, value):
        for natural, block in pairs:
            ref[natural : natural + piece, :] = value[block : block + piece, :]

    arrange(qo_ref, prepare(q_ref, 0))
    arrange(ko_ref, prepare(k_ref, 1))
    arrange(vo_ref, v_ref[...].astype(low))
    flipped = vo_ref[...].astype(jnp.float32).T.astype(low)
    for i in range(span // size):
        last = (i + 1) * size
        cols = slice(i * size, last)
        scores = nt(ko_ref[:last, :], qo_ref[cols, :]) * SCALE
        scores = mask_scores(scores, i * size, begin_ref[:, cols], size)
        top = jnp.max(scores, axis=0, keepdims=True)
        raw = jnp.exp(scores - top)
        weight = jnp.sum(raw, axis=0, keepdims=True)
        mixed = nn(flipped[:, :last], raw.astype(low)) * (1.0 / weight)
        mixed = mixed.T.astype(low)
        for natural, block in pairs:
            if i * size <= natural < last:
                at = natural - i * size
                mix_ref[block : block + piece, :] = mixed[at : at + piece, :]
        log_ref[:, cols] = top + jnp.log(weight)


def attend(pre, inverse, gains, cosine, sine, begin, heads, size):
    slots, span, _ = pre.shape
    low, f32 = jnp.bfloat16, jnp.float32
    head = lambda offset: pl.BlockSpec((None, span, HD), lambda g, h: (g, 0, offset + h))
    every = lambda cols: pl.BlockSpec((None, span, cols), lambda g, h: (g, 0, 0))
    line = pl.BlockSpec((None, 1, span), lambda g, h: (g, 0, 0))
    out = jax.ShapeDtypeStruct((slots, span, heads * HD), low)
    return pl.pallas_call(
        functools.partial(attend_body, size),
        grid=(slots, heads),
        out_shape=[out, out, out, out, jax.ShapeDtypeStruct((slots, heads, 1, span), f32)],
        in_specs=[
            head(0), head(heads), head(2 * heads), every(2),
            pl.BlockSpec((2, HD), lambda g, h: (0, h)), every(HD), every(HD), line,
        ],
        out_specs=[head(0)] * 4 + [pl.BlockSpec((None, None, 1, span), lambda g, h: (g, h, 0, 0))],
        compiler_params=pltpu.CompilerParams(vmem_limit_bytes=VMEM_LIMIT),
        cost_estimate=busy(17),
        name="attend",
    )(pre, pre, pre, inverse, gains, cosine, sine, begin)


def attend_back_body(size, q_ref, k_ref, v_ref, g_ref, log_ref, qp_ref, kp_ref, inv_ref, gain_ref,
                     cos_ref, sin_ref, begin_ref, sq_ref, sk_ref, gv_ref, sums_ref, part_ref,
                     keys_sum, values_sum, queries_sum, held, g_held):
    low = jnp.bfloat16
    span = q_ref.shape[0]
    pairs, piece = piece_map(span, size)
    for natural, block in pairs:
        g_held[natural : natural + piece, :] = g_ref[block : block + piece, :]
    flipped = k_ref[...].astype(jnp.float32).T.astype(low)
    keys_sum[...] = jnp.zeros_like(keys_sum)
    values_sum[...] = jnp.zeros_like(values_sum)
    for i in range(span // size):
        last = (i + 1) * size
        cols = slice(i * size, last)
        scores = nt(k_ref[:last, :], q_ref[cols, :]) * SCALE
        scores = mask_scores(scores, i * size, begin_ref[:, cols], size)
        probs = jnp.exp(scores - log_ref[:, cols])
        grad_probs = nt(v_ref[:last, :], g_held[cols, :])
        delta = jnp.sum(probs * grad_probs, axis=0, keepdims=True)
        grad_scores = (probs * (grad_probs - delta)).astype(low)
        values_sum[:last, :] += nn(probs.astype(low), g_held[cols, :])
        keys_sum[:last, :] += nn(grad_scores, q_ref[cols, :])
        queries_sum[cols, :] = nn(flipped[:, :last], grad_scores).T

    def finish(total_ref, pre_ref, out_ref, col):
        for natural, block in pairs:
            held[block : block + piece, :] = total_ref[natural : natural + piece, :]
        grad = held[...] * SCALE
        back = grad * cos_ref[...] - pltpu.roll(grad, HD // 2, 1) * sin_ref[...]
        normed = pre_ref[...] * inv_ref[:, col : col + 1]
        part_ref[col : col + 1, :] = jnp.sum(back * normed, axis=0, keepdims=True)
        scaled = back * gain_ref[col : col + 1, :]
        out_ref[...] = scaled
        sums_ref[:, col : col + 1] = jnp.sum(scaled * normed, axis=1, keepdims=True)

    finish(queries_sum, qp_ref, sq_ref, 0)
    finish(keys_sum, kp_ref, sk_ref, 1)
    for natural, block in pairs:
        gv_ref[block : block + piece, :] = values_sum[natural : natural + piece, :].astype(low)


def attend_back(queries, keys, values, grads, logs, pre, inverse, gains, cosine, sine, begin, heads, size):
    slots, span, _ = pre.shape
    low, f32 = jnp.bfloat16, jnp.float32
    head = lambda offset: pl.BlockSpec((None, span, HD), lambda g, h: (g, 0, offset + h))
    every = lambda cols: pl.BlockSpec((None, span, cols), lambda g, h: (g, 0, 0))
    line = pl.BlockSpec((None, 1, span), lambda g, h: (g, 0, 0))
    wide = jax.ShapeDtypeStruct((slots, span, heads * HD), f32)
    return pl.pallas_call(
        functools.partial(attend_back_body, size),
        grid=(slots, heads),
        out_shape=[
            wide, wide, jax.ShapeDtypeStruct((slots, span, heads * HD), low),
            jax.ShapeDtypeStruct((heads, slots, span, 2), f32),
            jax.ShapeDtypeStruct((slots, 2, heads * HD), f32),
        ],
        in_specs=[
            head(0), head(0), head(0), head(0),
            pl.BlockSpec((None, None, 1, span), lambda g, h: (g, h, 0, 0)),
            head(0), head(heads), every(2),
            pl.BlockSpec((2, HD), lambda g, h: (0, h)), every(HD), every(HD), line,
        ],
        out_specs=[
            head(0), head(0), head(0),
            pl.BlockSpec((None, None, span, 2), lambda g, h: (h, g, 0, 0)),
            pl.BlockSpec((None, 2, HD), lambda g, h: (g, 0, h)),
        ],
        scratch_shapes=[pltpu.VMEM((span, HD), f32)] * 4 + [pltpu.VMEM((span, HD), low)],
        compiler_params=pltpu.CompilerParams(vmem_limit_bytes=VMEM_LIMIT),
        cost_estimate=busy(28),
        name="attend_back",
    )(queries, keys, values, grads, logs, pre, pre, inverse, gains, cosine, sine, begin)


def local(
    tokens,
    lengths,
    query_weight,
    key_weight,
    value_weight,
    output_weight,
    query_gain,
    key_gain,
    attention_gain,
    gate_weight,
    up_weight,
    down_weight,
    feedforward_gain,
    cotangent,
):
    low, f32 = jnp.bfloat16, jnp.float32
    planes, width = lax.axis_size("blk"), lax.axis_size("wide")
    slots = width // planes
    rows = tokens.shape[1]
    span = rows * planes
    count = slots * span
    share = query_weight.shape[1]
    heads = share // HD
    plane, place = lax.axis_index("blk"), lax.axis_index("wide")
    after = lambda value, *others: lax.optimization_barrier((value,) + others)[0]

    def over_blk(value, axis):
        return lax.psum_scatter(
            value.astype(low), "blk", scatter_dimension=axis, tiled=True
        ).astype(f32)

    _, near_cotangent, mine = turn(
        turn_in_body, [tokens[0], cotangent[0]], [True, True, False], planes, slots, 1, "turn_in"
    )
    qkv_rows = after(jnp.concatenate([query_weight, key_weight, value_weight], 1), mine)
    w_qkv = lax.all_gather(qkv_rows, "blk", axis=0, tiled=True)
    w_o = lax.all_gather(after(output_weight, w_qkv), "blk", axis=1, tiled=True)
    gains = jnp.stack([query_gain, key_gain]).astype(f32)
    both = after(jnp.stack([attention_gain, feedforward_gain]), w_qkv)
    both = lax.all_gather(both, "wide", axis=1, tiled=True).astype(f32)
    gain_mix, gain_feed = both[0], both[1]

    plane_lengths = lax.dynamic_slice_in_dim(lengths, plane * slots, slots, 0)
    segment, position = jax.vmap(lambda one: layout(one, span))(plane_lengths)
    begin = (jnp.arange(span, dtype=jnp.int32)[None] - position)[:, None, :]
    pairs, piece = piece_map(span, rows)
    order = sorted(pairs, key=lambda pair: pair[1])
    position = jnp.concatenate([position[:, at : at + piece] for at, _ in order], 1)
    cosine, sine = rope_tables(position.reshape(-1))
    cosine, sine = cosine.reshape(slots, span, HD), sine.reshape(slots, span, HD)

    inputs = gather(mine, width, slots, 2, "gather_tokens")
    pre = dot(inputs, w_qkv)
    squares = jnp.stack([jnp.sum(pre[:, a * share : (a + 1) * share] ** 2, -1) for a in (0, 1)])
    squares = total(squares.reshape(-1, 128), "wide", width, 3, "total_squares")
    inverse = lax.rsqrt(squares.reshape(2, count) / D + EPS)
    inv_cols = inverse.T.reshape(slots, span, 2)
    pre_groups = pre.reshape(slots, span, 3 * share)
    queries, keys, values, mixed, logs = attend(
        pre_groups, inv_cols, gains, cosine, sine, begin, heads, rows
    )
    mixed = mixed.reshape(count, share)
    projected = scatter([mixed], [w_o], width, slots, False, 4, "scatter_mixed")
    proj_normed, proj_inv = rms_pair(projected)
    hidden = mine.astype(f32) + proj_normed * gain_mix
    gathered, grad_out = gather(
        hidden.astype(low), width, slots, 5, "gather_hidden", "join", near_cotangent
    )
    grad_out = grad_out.astype(f32)
    gate = dot(gathered, gate_weight)
    upward = dot(gathered, up_weight)
    sigmoid = jax.nn.sigmoid(gate)
    activated = (gate * sigmoid * upward).astype(low)
    reduced = scatter([activated], [down_weight], width, slots, False, 6, "scatter_down")
    red_normed, red_inv = rms_pair(reduced)
    block_output = (hidden + red_normed * gain_feed).astype(low)

    feed_gain_part = jnp.sum(grad_out * red_normed, axis=0)
    grad_reduced = norm_back(red_normed, red_inv, grad_out * gain_feed).astype(low)
    grad_rows, far_output = gather(
        grad_reduced, width, slots, 7, "gather_grad", "spread", block_output
    )
    down_part = contract_rows(activated, grad_rows).astype(low)
    grad_rows, down_part = lax.optimization_barrier((grad_rows, down_part))
    down_grad = over_blk(down_part, 1)
    grad_act = contract_cols(grad_rows, down_weight)
    grad_up = (grad_act * gate * sigmoid).astype(low)
    grad_gate = (grad_act * upward * sigmoid * (1.0 + gate * (1.0 - sigmoid))).astype(low)
    gate_part = contract_rows(gathered, grad_gate).astype(low)
    grad_up, gate_part = lax.optimization_barrier((grad_up, gate_part))
    gate_grad = over_blk(gate_part, 0)
    grad_hidden = grad_out + scatter(
        [grad_gate, grad_up], [gate_weight, up_weight], width, slots, True, 8, "scatter_hidden"
    )
    up_part = contract_rows(gathered, after(grad_up, grad_hidden)).astype(low)
    up_grad = over_blk(up_part, 0)
    mix_gain_part = jnp.sum(grad_hidden * proj_normed, axis=0)
    grad_proj = norm_back(proj_normed, proj_inv, grad_hidden * gain_mix).astype(low)
    grad_proj = gather(after(grad_proj, up_part, down_grad), width, slots, 9, "gather_proj")
    output_part = contract_rows(mixed, grad_proj).astype(low)
    grad_mixed = contract_cols(grad_proj, w_o).astype(low).reshape(slots, span, share)
    grad_mixed = after(grad_mixed, gate_grad)
    scaled_q, scaled_k, grad_v, sums, parts = attend_back(
        queries, keys, values, grad_mixed, logs, pre_groups, inv_cols, gains, cosine, sine, begin,
        heads, rows,
    )
    means = jnp.sum(sums, axis=0).reshape(count, 2).T.reshape(-1, 128)
    means = total(means, "wide", width, 10, "total_means").reshape(2, count) / D

    def finish(scaled, index):
        normed = pre[:, index * share : (index + 1) * share] * inverse[index][:, None]
        scaled = scaled.reshape(count, share)
        return (inverse[index][:, None] * (scaled - normed * means[index][:, None])).astype(low)

    grads = jnp.concatenate([finish(scaled_q, 0), finish(scaled_k, 1), grad_v.reshape(count, share)], 1)
    grads = after(grads, up_grad)
    tokens_part = scatter([grads], [w_qkv], width, slots, True, 11, "scatter_tokens")
    _, block_output, tokens_grad = turn(
        turn_out_body, [(grad_hidden + tokens_part).astype(low), far_output], [True, False, False],
        planes, slots, 14, "turn_out",
    )
    output_grad = over_blk(output_part, 1)
    qkv_part = contract_rows(inputs, grads)
    qkv_grad = over_blk(qkv_part, 0)

    gain_parts = jnp.sum(parts, axis=0)
    local_gains = lax.dynamic_update_slice(jnp.zeros((2, D), f32), gain_parts, (0, place * share))
    sums = jnp.concatenate([local_gains, jnp.stack([mix_gain_part, feed_gain_part])])
    sums = total(sums.reshape(-1, 128), "wide", width, 12, "total_gains")
    sums = total(sums, "blk", planes, 13, "total_gains_blk").reshape(4, D)
    portion = D // (planes * width)
    sums = lax.dynamic_slice_in_dim(sums, (plane * width + place) * portion, portion, 1)
    return (
        block_output[None],
        tokens_grad[None].astype(f32),
        qkv_grad[:, :share],
        qkv_grad[:, share : 2 * share],
        qkv_grad[:, 2 * share :],
        output_grad,
        sums[0],
        sums[1],
        sums[2],
        gate_grad,
        up_grad,
        down_grad,
        sums[3],
    )


def solution(mesh):
    placed = (
        P("wide", "blk", None),
        P(),
        P("blk", "wide"),
        P("blk", "wide"),
        P("blk", "wide"),
        P("wide", "blk"),
        P("wide"),
        P("wide"),
        P("wide"),
        P(None, "wide"),
        P(None, "wide"),
        P("wide", None),
        P("wide"),
        P("wide", "blk", None),
    )
    return jax.shard_map(
        local,
        mesh=mesh,
        in_specs=placed,
        out_specs=(
            P("wide", "blk", None),
            P("wide", "blk", None),
            P("blk", "wide"),
            P("blk", "wide"),
            P("blk", "wide"),
            P("wide", "blk"),
            P(("blk", "wide")),
            P(("blk", "wide")),
            P(("blk", "wide")),
            P("blk", "wide"),
            P("blk", "wide"),
            P("wide", "blk"),
            P(("blk", "wide")),
        ),
        check_vma=False,
    )
```

```python
import functools

import jax
import jax.numpy as jnp
from jax import lax
from jax.experimental import pallas as pl
from jax.experimental.pallas import tpu as pltpu
from jax.sharding import PartitionSpec as P

MESH = pl.DeviceIdType.MESH

D = 2048
HD = 128
EPS = 1e-06
ROPE_BASE = 500000.0
NEG_FILL = -1e30
VMEM_LIMIT = 60 * 1024 * 1024
SCALE = HD ** (-0.5)


def busy(micros):
    return pl.CostEstimate(flops=0, bytes_accessed=int(micros * 3.5e6), transcendentals=0)


def layout(seq_lengths, row_count):
    indices = jnp.arange(row_count, dtype=jnp.int32)
    first_end = seq_lengths[0]
    second_end = seq_lengths[0] + seq_lengths[1]
    segment = (indices >= first_end).astype(jnp.int32) + (indices >= second_end).astype(jnp.int32)
    offsets = jnp.where(segment == 0, 0, jnp.where(segment == 1, first_end, second_end))
    return (segment, indices - offsets)


def rope_tables(position):
    frequency = ROPE_BASE ** (-jnp.arange(0, HD, 2, dtype=jnp.float32) / HD)
    angles = position.astype(jnp.float32)[:, None] * frequency[None, :]
    cosine, sine = jnp.cos(angles), jnp.sin(angles)
    return (jnp.concatenate([cosine, cosine], -1), jnp.concatenate([-sine, sine], -1))


def rms_pair(values):
    inverse = lax.rsqrt(jnp.mean(values * values, axis=-1, keepdims=True) + EPS)
    return (values * inverse, inverse)


def norm_back(normed, inverse, grad_normed):
    return inverse * (grad_normed - normed * jnp.mean(grad_normed * normed, axis=-1, keepdims=True))


def dot(left, right):
    return jnp.dot(left, right, preferred_element_type=jnp.float32)


def contract_rows(left, right):
    return lax.dot_general(
        left, right, (((0,), (0,)), ((), ())), preferred_element_type=jnp.float32
    )


def contract_cols(left, right):
    return lax.dot_general(
        left, right, (((1,), (1,)), ((), ())), preferred_element_type=jnp.float32
    )


def flip(me, k):
    out, bit = me, 1
    while bit <= k:
        if k & bit:
            out = out + bit * (1 - 2 * ((me // bit) % 2))
        bit *= 2
    return out


def greet(axis, me, others):
    barrier = pltpu.get_barrier_semaphore()
    for k in others:
        pl.semaphore_signal(barrier, inc=1, device_id={axis: flip(me, k)}, device_id_type=MESH)
    pl.semaphore_wait(barrier, len(others))


class Flow:
    def __init__(self, me, source, spot, half, send, recv):
        self.me, self.source, self.spot, self.half = me, source, spot, half
        self.send, self.recv, self.moves = send, recv, []

    def go(self, origin, target, k, part):
        if origin is None:
            source = self.source.at[pl.ds(part * self.half, self.half)]
        else:
            source = self.spot(flip(self.me, origin), part)
        copy = pltpu.make_async_remote_copy(
            src_ref=source,
            dst_ref=self.spot(flip(flip(self.me, target), k), part),
            send_sem=self.send.at[k, part],
            recv_sem=self.recv.at[k, part],
            device_id={"wide": flip(self.me, target)},
            device_id_type=MESH,
        )
        copy.start()
        self.moves.append(copy)

    def arrived(self, k, part):
        block = self.spot(flip(self.me, k), part)
        pltpu.make_async_copy(block, block, self.recv.at[k, part]).wait()

    def finish(self):
        for copy in self.moves:
            copy.wait_send()


class Sums:
    def __init__(self, width, me, out_ref, refs):
        self.width, self.me, self.out = width, me, out_ref
        (self.odd, self.even, self.from_twin, self.from_far, self.passing, self.sends, self.recvs,
         self.pass_send, self.pass_recv, self.twin_send, self.twin_recv) = refs
        self.half = out_ref.shape[0] // 2

    def rows(self, part):
        return pl.ds(part * self.half, self.half)

    def copy(self, src, dst, send, recv, k):
        return pltpu.make_async_remote_copy(
            src_ref=src, dst_ref=dst, send_sem=send, recv_sem=recv,
            device_id={"wide": flip(self.me, k)}, device_id_type=MESH,
        )

    def twin(self, k, part):
        i, at = k // 2, self.rows(part)
        return self.copy(
            self.odd.at[i, at], self.from_twin.at[i, at], self.twin_send.at[i, part],
            self.twin_recv.at[i, part], 1,
        )

    def far(self, k, part):
        i, at = k // 2 - 1, self.rows(part)
        return self.copy(
            self.even.at[i, at], self.from_far.at[i, at], self.sends.at[i, part], self.recvs.at[i, part], k
        )

    def relay(self, part):
        return self.copy(
            self.even.at[2, self.rows(part)], self.passing.at[part], self.pass_send.at[part],
            self.pass_recv.at[part], 2 if part == 0 else 4,
        )

    def give(self, k):
        self.twin(k, 0).start()
        self.twin(k, 1).start()

    def got(self, k):
        self.twin(k, 0).wait_recv()
        self.twin(k, 1).wait_recv()

    def pass_on(self, k, part):
        self.relay(part).wait_recv()
        at = self.rows(part)
        self.even[k // 2 - 1, at, :] = (
            self.even[k // 2 - 1, at, :].astype(jnp.float32) + self.passing[part].astype(jnp.float32)
        ).astype(jnp.bfloat16)
        self.far(k, part).start()

    def finish(self):
        sources = [2, 4] if self.width == 8 else list(range(2, self.width, 2))
        for k in sources:
            for part in (0, 1):
                self.far(k, part).wait_recv()
        extra = self.from_far[sources[0] // 2 - 1].astype(jnp.float32)
        for k in sources[1:]:
            extra = extra + self.from_far[k // 2 - 1].astype(jnp.float32)
        self.out[...] = self.out[...] + extra
        for part in (0, 1):
            for k in sources:
                self.far(k, part).wait_send()
            for k in range(0, self.width, 2):
                self.twin(k, part).wait_send()
            if self.width == 8:
                self.relay(part).wait_send()


def sum_scratch(width, rows, cols):
    chips, dma = width // 2, pltpu.SemaphoreType.DMA
    block = lambda n: pltpu.VMEM((n, rows, cols), jnp.bfloat16)
    return [
        block(chips), block(chips - 1), block(chips), block(2 if width == 8 else chips - 1),
        pltpu.VMEM((2, rows // 2, cols), jnp.bfloat16),
        dma((chips - 1, 2)), dma((chips - 1, 2)), dma((2,)), dma((2,)), dma((chips, 2)), dma((chips, 2)),
    ]


def wide_peers(width, me):
    return [{"wide": flip(me, k)} for k in [1] + list(range(2, width, 2))]


def local_copies(pairs, sem):
    return [pltpu.make_async_copy(src, dst, sem.at[i]) for i, (src, dst) in enumerate(pairs)]


def gather_body(width, slots, side, *refs):
    if side is None:
        x_ref, out_ref, here, send, recv = refs
    else:
        x_ref, side_ref, out_ref, side_out, here, send, recv, side_send, side_recv = refs
    me = lax.axis_index("wide")
    rows = x_ref.shape[0]
    half = rows // 2
    evens = list(range(2, width, 2))
    peers = [{"wide": flip(me, k)} for k in [1] + evens]
    if side is not None:
        hops = Hops(width // slots, slots, rows)
        peers = peers + [{"blk": (hops.plane + k) % hops.planes} for k in range(1, hops.planes)]
    hello(peers)
    if side is not None:
        job = hops.join if side == "join" else hops.spread
        job(side_ref, side_out, side_send, side_recv, True, True)

    def spot(who, first, count):
        base = ((who % slots) * (width // slots) + who // slots) * rows
        return out_ref.at[pl.ds(pl.multiple_of(base + first, half), count)]

    def move(origin, target, k, part):
        if origin is None:
            source = x_ref.at[pl.ds(part * half, half)]
        else:
            source = spot(flip(me, origin), part * half, half)
        return pltpu.make_async_remote_copy(
            src_ref=source,
            dst_ref=spot(flip(flip(me, target), k), part * half, half),
            send_sem=send.at[k, part],
            recv_sem=recv.at[k, part],
            device_id={"wide": flip(me, target)},
            device_id_type=MESH,
        )

    def arrived(k, part):
        block = spot(flip(me, k), part * half, half)
        pltpu.make_async_copy(block, block, recv.at[k, part]).wait()

    moves = []

    def go(origin, target, k, part):
        copy = move(origin, target, k, part)
        copy.start()
        moves.append(copy)

    mine = pltpu.make_async_copy(x_ref, spot(me, 0, rows), here)
    mine.start()
    if width == 8:
        go(None, 2, 2, 0)
        go(None, 4, 4, 1)
        go(None, 2, 2, 1)
        go(None, 4, 4, 0)
        go(None, 1, 1, 0)
        go(None, 1, 1, 1)
        arrived(2, 0)
        go(2, 4, 6, 0)
        go(2, 1, 3, 0)
        arrived(4, 1)
        go(4, 2, 6, 1)
        go(4, 1, 5, 1)
        order = [(2, 1), (4, 0), (6, 0), (6, 1)]
    else:
        for k in evens:
            go(None, k, k, 0)
            go(None, k, k, 1)
        go(None, 1, 1, 0)
        go(None, 1, 1, 1)
        order = [(k, part) for k in evens for part in (0, 1)]
    for k, part in order:
        arrived(k, part)
        go(k, 1, k + 1, part)
    for k in range(1, width, 2):
        for part in (0, 1):
            arrived(k, part)
    for copy in moves:
        copy.wait_send()
    mine.wait()
    if side is not None:
        job(side_ref, side_out, side_send, side_recv, True, False)


def gather(x, width, slots, ident, name, side=None, side_x=None):
    rows, cols = x.shape
    planes = width // slots
    dma = pltpu.SemaphoreType.DMA
    shapes = [jax.ShapeDtypeStruct((rows * width, cols), x.dtype)]
    scratch = [dma, dma((width, 2)), dma((width, 2))]
    inputs = [x]
    if side is not None:
        inputs.append(side_x)
        extent = rows if side == "join" else many_rows(planes, rows)
        shapes.append(jax.ShapeDtypeStruct((extent, cols), side_x.dtype))
        scratch += [dma((planes,)), dma((planes,))]
    outs = pl.pallas_call(
        functools.partial(gather_body, width, slots, side),
        out_shape=shapes,
        in_specs=[pl.BlockSpec(memory_space=pl.ANY)] * len(inputs),
        out_specs=[pl.BlockSpec(memory_space=pl.ANY)] * len(shapes),
        scratch_shapes=scratch,
        cost_estimate=busy(10),
        compiler_params=pltpu.CompilerParams(collective_id=ident, has_side_effects=True, vmem_limit_bytes=VMEM_LIMIT),
        name=name,
    )(*inputs)
    return outs[0] if side is None else outs


def scatter_body(width, slots, flat, count, step, *refs):
    lefts, rights = refs[:count], refs[count : 2 * count]
    out_ref = refs[2 * count]
    me = lax.axis_index("wide")
    rows, cols = out_ref.shape
    hello(wide_peers(width, me))
    sums = Sums(width, me, out_ref, refs[2 * count + 1 :])
    dims = (((1,), (1 if flat else 0,)), ((), ()))

    def produce(k, put, adds=()):
        who = flip(me, k)
        start = pl.multiple_of(((who % slots) * (width // slots) + who // slots) * rows, rows)

        def tile(n, carry):
            at = pl.ds(pl.multiple_of(n * step, step), step)
            total = None
            for left, right in zip(lefts, rights):
                other = right[at, :] if flat else right[:, at]
                term = lax.dot_general(
                    left[pl.ds(start, rows), :], other, dims, preferred_element_type=jnp.float32
                )
                total = term if total is None else total + term
            for ref in adds:
                total = total + ref[:, at].astype(jnp.float32)
            put[:, at] = total.astype(put.dtype)
            return carry

        lax.fori_loop(0, cols // step, tile, 0)

    def give(k):
        produce(k + 1, sums.odd.at[k // 2])
        sums.give(k)

    def merge(k):
        sums.got(k)
        produce(k, sums.even.at[k // 2 - 1], (sums.from_twin.at[k // 2],))

    if width == 8:
        give(6)
        give(2)
        give(4)
        merge(6)
        sums.relay(0).start()
        sums.relay(1).start()
        merge(2)
        sums.far(2, 0).start()
        merge(4)
        sums.far(4, 1).start()
        give(0)
        sums.pass_on(2, 1)
        sums.pass_on(4, 0)
    else:
        for k in range(0, width, 2):
            give(k)
        for k in range(2, width, 2):
            merge(k)
            sums.far(k, 0).start()
            sums.far(k, 1).start()
    sums.got(0)
    produce(0, out_ref, (sums.from_twin.at[0],))
    sums.finish()


def scatter(lefts, rights, width, slots, flat, ident, name, step=1024):
    rows = lefts[0].shape[0] // width
    cols = rights[0].shape[0 if flat else 1]
    return pl.pallas_call(
        functools.partial(scatter_body, width, slots, flat, len(lefts), step),
        out_shape=jax.ShapeDtypeStruct((rows, cols), jnp.float32),
        in_specs=[pl.BlockSpec(memory_space=pltpu.VMEM)] * (2 * len(lefts)),
        out_specs=pl.BlockSpec(memory_space=pltpu.VMEM),
        scratch_shapes=sum_scratch(width, rows, cols),
        cost_estimate=busy(10),
        compiler_params=pltpu.CompilerParams(collective_id=ident, has_side_effects=True, vmem_limit_bytes=VMEM_LIMIT),
        name=name,
    )(*lefts, *rights)


def total_body(axis, width, x_ref, out_ref, slots, send, recv):
    me = lax.axis_index(axis)
    others = list(range(1, width))
    greet(axis, me, others)
    moves = []
    for k in others:
        copy = pltpu.make_async_remote_copy(
            src_ref=x_ref,
            dst_ref=slots.at[k - 1],
            send_sem=send.at[k - 1],
            recv_sem=recv.at[k - 1],
            device_id={axis: flip(me, k)},
            device_id_type=MESH,
        )
        copy.start()
        moves.append(copy)
    out_ref[...] = x_ref[...]
    for copy, k in zip(moves, others):
        copy.wait_recv()
        out_ref[...] = out_ref[...] + slots[k - 1]
    for copy in moves:
        copy.wait_send()


def total(x, axis, width, ident, name):
    return pl.pallas_call(
        functools.partial(total_body, axis, width),
        out_shape=jax.ShapeDtypeStruct(x.shape, x.dtype),
        in_specs=[pl.BlockSpec(memory_space=pltpu.VMEM)],
        out_specs=pl.BlockSpec(memory_space=pltpu.VMEM),
        scratch_shapes=[
            pltpu.VMEM((width - 1,) + x.shape, x.dtype),
            pltpu.SemaphoreType.DMA((width - 1,)),
            pltpu.SemaphoreType.DMA((width - 1,)),
        ],
        cost_estimate=busy(7),
        compiler_params=pltpu.CompilerParams(collective_id=ident, has_side_effects=True, vmem_limit_bytes=VMEM_LIMIT),
        name=name,
    )(x)


class Hops:
    def __init__(self, planes, slots, rows):
        self.planes, self.slots = planes, slots
        self.count = max(n for n in range(1, planes + 1) if planes % n == 0 and rows % (16 * n) == 0)
        self.per = planes // self.count
        self.piece = rows // self.count
        self.plane, self.place = lax.axis_index("blk"), lax.axis_index("wide")
        self.chip, self.slot = self.place // slots, self.place % slots
        self.active = self.chip // self.count == self.plane % self.per

    def peers(self):
        near = [{"wide": (self.chip + k) % self.planes * self.slots + self.slot} for k in range(1, self.planes)]
        return near + [{"blk": (self.plane + k) % self.planes} for k in range(1, self.planes)]

    def when(self, condition, action):
        if self.per == 1:
            action()
        else:
            pl.when(condition)(action)

    def split(self, condition, yes, no):
        if self.per == 1:
            yes()
        else:
            pl.when(condition)(yes)
            pl.when(jnp.logical_not(condition))(no)

    def cut(self, ref, index):
        return ref.at[pl.ds(pl.multiple_of(index * self.piece, self.piece), self.piece)]

    def remote(self, src, dst, send, recv, device):
        return pltpu.make_async_remote_copy(
            src_ref=src, dst_ref=dst, send_sem=send, recv_sem=recv, device_id=device, device_id_type=MESH
        )

    def spread(self, some, many, send, recv, across, start):
        if across:
            axis, here = "blk", self.plane
            targets = [
                ((self.plane // self.per + k) % self.count) for k in range(self.count)
            ]
            device = lambda piece: piece * self.per + self.chip // self.count
        else:
            axis, here = "wide", self.chip
            targets = [((self.chip + k) % self.count) for k in range(self.count)]
            device = lambda piece: (self.plane % self.per) * self.count + piece
        address = (lambda who: {"blk": who}) if across else (
            lambda who: {"wide": who * self.slots + self.slot}
        )
        for k, piece in enumerate(targets):
            who = device(piece)
            far = self.remote(
                self.cut(some, piece), self.cut(many, here), send.at[piece],
                recv.at[(here - who + self.planes) % self.planes], address(who),
            )
            own = pltpu.make_async_copy(self.cut(some, piece), self.cut(many, here), send.at[piece])
            if k:
                far.start() if start else far.wait_send()
            elif start:
                self.split(self.active, own.start, far.start)
            else:
                self.split(self.active, own.wait, far.wait_send)
        if not start:
            def receive():
                for k in range(1, self.planes):
                    block = self.cut(many, (here + k) % self.planes)
                    pltpu.make_async_copy(block, block, recv.at[k]).wait()

            self.when(self.active, receive)

    def join(self, many, some, send, recv, across, start):
        if across:
            here = self.plane
            index = self.plane // self.per
            address = lambda who: {"blk": who}
        else:
            here = self.chip
            index = self.chip % self.count
            address = lambda who: {"wide": who * self.slots + self.slot}

        def give():
            for k in range(1, self.planes):
                who = (here + k) % self.planes
                far = self.remote(
                    self.cut(many, who), self.cut(some, index), send.at[k], recv.at[index], address(who)
                )
                far.start() if start else far.wait_send()
            own = pltpu.make_async_copy(self.cut(many, here), self.cut(some, index), send.at[0])
            own.start() if start else own.wait()

        self.when(self.active, give)
        if not start:
            for k in range(self.count):
                piece = (index + k) % self.count
                block = self.cut(some, piece)
                arrival = pltpu.make_async_copy(block, block, recv.at[piece])
                if k:
                    arrival.wait()
                elif self.per > 1:
                    pl.when(jnp.logical_not(self.active))(arrival.wait)


def hello(peers):
    barrier = pltpu.get_barrier_semaphore()
    for peer in peers:
        pl.semaphore_signal(barrier, inc=1, device_id=peer, device_id_type=MESH)
    pl.semaphore_wait(barrier, len(peers))


def turn_in_body(planes, slots, x_ref, c_ref, near_x, near_c, out_ref, *sems):
    hops = Hops(planes, slots, x_ref.shape[0])
    hello(hops.peers())
    hops.spread(x_ref, near_x, sems[0], sems[1], False, True)
    hops.spread(x_ref, near_x, sems[0], sems[1], False, False)
    hops.join(near_x, out_ref, sems[2], sems[3], True, True)
    hops.spread(c_ref, near_c, sems[4], sems[5], False, True)
    hops.spread(c_ref, near_c, sems[4], sems[5], False, False)
    hops.join(near_x, out_ref, sems[2], sems[3], True, False)


def turn_out_body(planes, slots, x_ref, far_c, far_x, out_c, out_ref, *sems):
    hops = Hops(planes, slots, x_ref.shape[0])
    hello(hops.peers())
    hops.spread(x_ref, far_x, sems[0], sems[1], True, True)
    hops.join(far_c, out_c, sems[2], sems[3], False, True)
    hops.spread(x_ref, far_x, sems[0], sems[1], True, False)
    hops.join(far_x, out_ref, sems[4], sems[5], False, True)
    hops.join(far_c, out_c, sems[2], sems[3], False, False)
    hops.join(far_x, out_ref, sems[4], sems[5], False, False)


def many_rows(planes, rows):
    count = max(n for n in range(1, planes + 1) if planes % n == 0 and rows % (16 * n) == 0)
    return planes * (rows // count)


def turn(body, inputs, outputs, planes, slots, ident, name):
    rows, cols = inputs[0].shape
    low = inputs[0].dtype
    shape = lambda many: jax.ShapeDtypeStruct((many_rows(planes, rows) if many else rows, cols), low)
    return pl.pallas_call(
        functools.partial(body, planes, slots),
        out_shape=[shape(many) for many in outputs],
        in_specs=[pl.BlockSpec(memory_space=pl.ANY)] * len(inputs),
        out_specs=[pl.BlockSpec(memory_space=pl.ANY)] * len(outputs),
        scratch_shapes=[pltpu.SemaphoreType.DMA((planes,))] * 6,
        cost_estimate=busy(10),
        compiler_params=pltpu.CompilerParams(collective_id=ident, has_side_effects=True, vmem_limit_bytes=VMEM_LIMIT),
        name=name,
    )(*inputs)


def mask_scores(scores, first, begin, size):
    span = scores.shape[0]
    index = lax.broadcasted_iota(jnp.int32, scores.shape, 0)
    query = lax.broadcasted_iota(jnp.int32, scores.shape, 1) + first
    return jnp.where((index <= query) & (index >= begin), scores, NEG_FILL)


def nt(left, right):
    return lax.dot_general(left, right, (((1,), (1,)), ((), ())), preferred_element_type=jnp.float32)


def nn(left, right):
    return jnp.dot(left, right, preferred_element_type=jnp.float32)


def piece_map(span, size):
    planes = span // size
    count = max(n for n in range(1, planes + 1) if planes % n == 0 and size % (16 * n) == 0)
    per, piece = planes // count, size // count
    pairs = []
    for t in range(count):
        for high in range(per):
            for low in range(count):
                natural = ((t * per + high) * count + low) * piece
                pairs.append((natural, ((high * count + low) * count + t) * piece))
    return pairs, piece


def attend_body(size, q_ref, k_ref, v_ref, inv_ref, gain_ref, cos_ref, sin_ref, begin_ref,
                qo_ref, ko_ref, vo_ref, mix_ref, log_ref):
    low = jnp.bfloat16
    span = q_ref.shape[0]

    def prepare(ref, col):
        value = ref[...] * inv_ref[:, col : col + 1] * gain_ref[col : col + 1, :]
        return (value * cos_ref[...] + pltpu.roll(value, HD // 2, 1) * sin_ref[...]).astype(low)

    pairs, piece = piece_map(span, size)

    def arrange(ref, value):
        for natural, block in pairs:
            ref[natural : natural + piece, :] = value[block : block + piece, :]

    arrange(qo_ref, prepare(q_ref, 0))
    arrange(ko_ref, prepare(k_ref, 1))
    arrange(vo_ref, v_ref[...].astype(low))
    flipped = vo_ref[...].astype(jnp.float32).T.astype(low)
    for i in range(span // size):
        last = (i + 1) * size
        cols = slice(i * size, last)
        scores = nt(ko_ref[:last, :], qo_ref[cols, :]) * SCALE
        scores = mask_scores(scores, i * size, begin_ref[:, cols], size)
        top = jnp.max(scores, axis=0, keepdims=True)
        raw = jnp.exp(scores - top)
        weight = jnp.sum(raw, axis=0, keepdims=True)
        mixed = nn(flipped[:, :last], raw.astype(low)) * (1.0 / weight)
        mixed = mixed.T.astype(low)
        for natural, block in pairs:
            if i * size <= natural < last:
                at = natural - i * size
                mix_ref[block : block + piece, :] = mixed[at : at + piece, :]
        log_ref[:, cols] = top + jnp.log(weight)


def attend(pre, inverse, gains, cosine, sine, begin, heads, size):
    slots, span, _ = pre.shape
    low, f32 = jnp.bfloat16, jnp.float32
    head = lambda offset: pl.BlockSpec((None, span, HD), lambda g, h: (g, 0, offset + h))
    every = lambda cols: pl.BlockSpec((None, span, cols), lambda g, h: (g, 0, 0))
    line = pl.BlockSpec((None, 1, span), lambda g, h: (g, 0, 0))
    out = jax.ShapeDtypeStruct((slots, span, heads * HD), low)
    return pl.pallas_call(
        functools.partial(attend_body, size),
        grid=(slots, heads),
        out_shape=[out, out, out, out, jax.ShapeDtypeStruct((slots, heads, 1, span), f32)],
        in_specs=[
            head(0), head(heads), head(2 * heads), every(2),
            pl.BlockSpec((2, HD), lambda g, h: (0, h)), every(HD), every(HD), line,
        ],
        out_specs=[head(0)] * 4 + [pl.BlockSpec((None, None, 1, span), lambda g, h: (g, h, 0, 0))],
        compiler_params=pltpu.CompilerParams(vmem_limit_bytes=VMEM_LIMIT),
        cost_estimate=busy(5),
        name="attend",
    )(pre, pre, pre, inverse, gains, cosine, sine, begin)


def attend_back_body(size, q_ref, k_ref, v_ref, g_ref, log_ref, qp_ref, kp_ref, inv_ref, gain_ref,
                     cos_ref, sin_ref, begin_ref, sq_ref, sk_ref, gv_ref, sums_ref, part_ref,
                     keys_sum, values_sum, queries_sum, held, g_held):
    low = jnp.bfloat16
    span = q_ref.shape[0]
    pairs, piece = piece_map(span, size)
    for natural, block in pairs:
        g_held[natural : natural + piece, :] = g_ref[block : block + piece, :]
    flipped = k_ref[...].astype(jnp.float32).T.astype(low)
    keys_sum[...] = jnp.zeros_like(keys_sum)
    values_sum[...] = jnp.zeros_like(values_sum)
    for i in range(span // size):
        last = (i + 1) * size
        cols = slice(i * size, last)
        scores = nt(k_ref[:last, :], q_ref[cols, :]) * SCALE
        scores = mask_scores(scores, i * size, begin_ref[:, cols], size)
        probs = jnp.exp(scores - log_ref[:, cols])
        grad_probs = nt(v_ref[:last, :], g_held[cols, :])
        delta = jnp.sum(probs * grad_probs, axis=0, keepdims=True)
        grad_scores = (probs * (grad_probs - delta)).astype(low)
        values_sum[:last, :] += nn(probs.astype(low), g_held[cols, :])
        keys_sum[:last, :] += nn(grad_scores, q_ref[cols, :])
        queries_sum[cols, :] = nn(flipped[:, :last], grad_scores).T

    def finish(total_ref, pre_ref, out_ref, col):
        for natural, block in pairs:
            held[block : block + piece, :] = total_ref[natural : natural + piece, :]
        grad = held[...] * SCALE
        back = grad * cos_ref[...] - pltpu.roll(grad, HD // 2, 1) * sin_ref[...]
        normed = pre_ref[...] * inv_ref[:, col : col + 1]
        part_ref[col : col + 1, :] = jnp.sum(back * normed, axis=0, keepdims=True)
        scaled = back * gain_ref[col : col + 1, :]
        out_ref[...] = scaled
        sums_ref[:, col : col + 1] = jnp.sum(scaled * normed, axis=1, keepdims=True)

    finish(queries_sum, qp_ref, sq_ref, 0)
    finish(keys_sum, kp_ref, sk_ref, 1)
    for natural, block in pairs:
        gv_ref[block : block + piece, :] = values_sum[natural : natural + piece, :].astype(low)


def attend_back(queries, keys, values, grads, logs, pre, inverse, gains, cosine, sine, begin, heads, size):
    slots, span, _ = pre.shape
    low, f32 = jnp.bfloat16, jnp.float32
    head = lambda offset: pl.BlockSpec((None, span, HD), lambda g, h: (g, 0, offset + h))
    every = lambda cols: pl.BlockSpec((None, span, cols), lambda g, h: (g, 0, 0))
    line = pl.BlockSpec((None, 1, span), lambda g, h: (g, 0, 0))
    wide = jax.ShapeDtypeStruct((slots, span, heads * HD), f32)
    return pl.pallas_call(
        functools.partial(attend_back_body, size),
        grid=(slots, heads),
        out_shape=[
            wide, wide, jax.ShapeDtypeStruct((slots, span, heads * HD), low),
            jax.ShapeDtypeStruct((heads, slots, span, 2), f32),
            jax.ShapeDtypeStruct((slots, 2, heads * HD), f32),
        ],
        in_specs=[
            head(0), head(0), head(0), head(0),
            pl.BlockSpec((None, None, 1, span), lambda g, h: (g, h, 0, 0)),
            head(0), head(heads), every(2),
            pl.BlockSpec((2, HD), lambda g, h: (0, h)), every(HD), every(HD), line,
        ],
        out_specs=[
            head(0), head(0), head(0),
            pl.BlockSpec((None, None, span, 2), lambda g, h: (h, g, 0, 0)),
            pl.BlockSpec((None, 2, HD), lambda g, h: (g, 0, h)),
        ],
        scratch_shapes=[pltpu.VMEM((span, HD), f32)] * 4 + [pltpu.VMEM((span, HD), low)],
        compiler_params=pltpu.CompilerParams(vmem_limit_bytes=VMEM_LIMIT),
        cost_estimate=busy(5),
        name="attend_back",
    )(queries, keys, values, grads, logs, pre, pre, inverse, gains, cosine, sine, begin)


def feed_body(width, slots, step, h_ref, c_ref, wg_hbm, wu_hbm, wd_hbm, out_ref, all_ref, act_ref, one_ref,
              two_ref, c_out, buf, wg, wu, wd, stage, here, load, send, recv, side_send, side_recv, store,
              keep, *sum_refs):
    me = lax.axis_index("wide")
    planes = width // slots
    rows, cols = h_ref.shape
    hidden = wg.shape[1]
    half = rows // 2
    low = jnp.bfloat16
    loads = local_copies([(wg_hbm, wg), (wu_hbm, wu), (wd_hbm, wd)], load)
    mine = pltpu.make_async_copy(h_ref, buf.at[me], here)
    mine.start()
    for copy in loads:
        copy.start()
    hops = Hops(planes, slots, rows)
    hello(wide_peers(width, me) + [{"blk": (hops.plane + k) % planes} for k in range(1, planes)])
    flow = Flow(me, h_ref, lambda who, part: buf.at[who, pl.ds(part * half, half)], half, send, recv)
    sums = Sums(width, me, out_ref, sum_refs)
    outs = (act_ref, one_ref, two_ref)
    pending = [[], []]
    turn_count = [0]
    kept = []

    def where(k):
        who = flip(me, k)
        return pl.multiple_of(((who % slots) * planes + who // slots) * rows, rows)

    def keep_block(k):
        copy = pltpu.make_async_copy(buf.at[flip(me, k)], all_ref.at[pl.ds(where(k), rows)], keep.at[k])
        copy.start()
        kept.append(copy)

    def work(k, part, put, adds=()):
        first, count = (0, rows) if part is None else (part * half, half)
        slot = turn_count[0] % 2
        turn_count[0] += 1
        for copy in pending[slot]:
            copy.wait()
        block = buf.at[flip(me, k), pl.ds(first, count)]
        act, one, two = (stage.at[slot, i, pl.ds(0, count)] for i in range(3))

        def inner(n, carry):
            at = pl.ds(pl.multiple_of(n * step, step), step)
            gate = jnp.dot(block[...], wg[:, at], preferred_element_type=jnp.float32)
            upward = jnp.dot(block[...], wu[:, at], preferred_element_type=jnp.float32)
            sigmoid = jax.nn.sigmoid(gate)
            silu = gate * sigmoid
            act[:, at] = (silu * upward).astype(low)
            one[:, at] = silu.astype(low)
            two[:, at] = (upward * (sigmoid + silu * (1.0 - sigmoid))).astype(low)
            return carry

        lax.fori_loop(0, hidden // step, inner, 0)
        target = pl.ds(pl.multiple_of(where(k) + first, half), count)
        pending[slot] = []
        for i, ref in enumerate(outs):
            copy = pltpu.make_async_copy(stage.at[slot, i, pl.ds(0, count)], ref.at[target], store.at[slot, i])
            copy.start()
            pending[slot].append(copy)
        broad = 2 * step

        def outer(n, carry):
            at = pl.ds(pl.multiple_of(n * broad, broad), broad)
            total = jnp.dot(act[...], wd[:, at], preferred_element_type=jnp.float32)
            for ref in adds:
                total = total + ref[:, at].astype(jnp.float32)
            put[:, at] = total.astype(put.dtype)
            return carry

        lax.fori_loop(0, cols // broad, outer, 0)

    def odd_work(k, part):
        if part is None:
            work(k + 1, None, sums.odd.at[k // 2])
            sums.give(k)
        else:
            work(k + 1, part, sums.odd.at[k // 2, sums.rows(part)])
            sums.twin(k, part).start()

    def even_work(k, part):
        i = k // 2
        if part is None:
            sums.got(k)
            work(k, None, sums.even.at[i - 1], (sums.from_twin.at[i],))
        else:
            sums.twin(k, part).wait_recv()
            at = sums.rows(part)
            work(k, part, sums.even.at[i - 1, at], (sums.from_twin.at[i, at],))

    if width == 8:
        flow.go(None, 2, 2, 0)
        flow.go(None, 4, 4, 1)
        flow.go(None, 1, 1, 0)
        flow.go(None, 1, 1, 1)
        hops.join(c_ref, c_out, side_send, side_recv, True, True)
        mine.wait()
        for copy in loads:
            copy.wait()
        work(0, None, out_ref)
        keep_block(0)
        flow.arrived(1, 0)
        flow.arrived(1, 1)
        keep_block(1)
        odd_work(0, None)
        flow.arrived(2, 0)
        flow.go(2, 4, 6, 0)
        flow.arrived(4, 1)
        flow.go(4, 2, 6, 1)
        flow.go(2, 1, 3, 0)
        flow.go(4, 1, 5, 1)
        flow.go(None, 2, 2, 1)
        flow.go(None, 4, 4, 0)
        flow.arrived(3, 0)
        odd_work(2, 0)
        flow.arrived(5, 1)
        odd_work(4, 1)
        even_work(2, 0)
        even_work(4, 1)
        for part in (0, 1):
            flow.arrived(6, part)
            flow.go(6, 1, 7, part)
        for part in (0, 1):
            flow.arrived(7, part)
        keep_block(6)
        keep_block(7)
        odd_work(6, None)
        even_work(6, None)
        sums.relay(0).start()
        sums.relay(1).start()
        flow.arrived(2, 1)
        flow.go(2, 1, 3, 1)
        flow.arrived(4, 0)
        flow.go(4, 1, 5, 0)
        sums.far(2, 0).start()
        sums.far(4, 1).start()
        flow.arrived(3, 1)
        odd_work(2, 1)
        flow.arrived(5, 0)
        odd_work(4, 0)
        for k in (2, 3, 4, 5):
            keep_block(k)
        even_work(2, 1)
        sums.pass_on(2, 1)
        even_work(4, 0)
        sums.pass_on(4, 0)
    else:
        hops.join(c_ref, c_out, side_send, side_recv, True, True)
        for k in range(2, width, 2):
            flow.go(None, k, k, 0)
            flow.go(None, k, k, 1)
        flow.go(None, 1, 1, 0)
        flow.go(None, 1, 1, 1)
        mine.wait()
        for copy in loads:
            copy.wait()
        work(0, None, out_ref)
        keep_block(0)
        flow.arrived(1, 0)
        flow.arrived(1, 1)
        keep_block(1)
        odd_work(0, None)
        for k in range(2, width, 2):
            for part in (0, 1):
                flow.arrived(k, part)
                flow.go(k, 1, k + 1, part)
            for part in (0, 1):
                flow.arrived(k + 1, part)
            keep_block(k)
            keep_block(k + 1)
            odd_work(k, None)
            even_work(k, None)
            sums.far(k, 0).start()
            sums.far(k, 1).start()
    sums.got(0)
    out_ref[...] = out_ref[...] + sums.from_twin[0].astype(jnp.float32)
    sums.finish()
    flow.finish()
    for copy in kept + pending[0] + pending[1]:
        copy.wait()
    hops.join(c_ref, c_out, side_send, side_recv, True, False)


def feed(h, side_x, gate_weight, up_weight, down_weight, width, slots, ident, name):
    rows, cols = h.shape
    hidden = gate_weight.shape[1]
    low, dma = h.dtype, pltpu.SemaphoreType.DMA
    step = min(512, hidden)
    anywhere = pl.BlockSpec(memory_space=pl.ANY)
    saved = jax.ShapeDtypeStruct((rows * width, hidden), low)
    return pl.pallas_call(
        functools.partial(feed_body, width, slots, step),
        out_shape=[
            jax.ShapeDtypeStruct((rows, cols), jnp.float32), jax.ShapeDtypeStruct((rows * width, cols), low),
            saved, saved, saved, jax.ShapeDtypeStruct((rows, cols), low),
        ],
        in_specs=[anywhere] * 5,
        out_specs=[pl.BlockSpec(memory_space=pltpu.VMEM)] + [anywhere] * 5,
        scratch_shapes=[
            pltpu.VMEM((width, rows, cols), low), pltpu.VMEM((cols, hidden), low), pltpu.VMEM((cols, hidden), low),
            pltpu.VMEM((hidden, cols), low), pltpu.VMEM((2, 3, rows, hidden), low),
            dma, dma((3,)), dma((width, 2)), dma((width, 2)), dma((width // slots,)), dma((width // slots,)),
            dma((2, 3)), dma((width,)),
        ] + sum_scratch(width, rows, cols),
        cost_estimate=busy(90),
        compiler_params=pltpu.CompilerParams(collective_id=ident, has_side_effects=True, vmem_limit_bytes=VMEM_LIMIT),
        name=name,
    )(h, side_x, gate_weight, up_weight, down_weight)


def push_body(width, slots, step, g_ref, c_ref, wd_hbm, act_hbm, one_hbm, two_hbm, down_ref, gg_ref, gu_ref, c_out,
              buf, wd, held, ins, outs, here, load, send, recv, side_send, side_recv, fetch, store):
    me = lax.axis_index("wide")
    planes = width // slots
    rows, cols = g_ref.shape
    hidden = wd.shape[0]
    half = rows // 2
    low = jnp.bfloat16
    weights = pltpu.make_async_copy(wd_hbm, wd, load)
    mine = pltpu.make_async_copy(g_ref, buf.at[me // 2, me % 2], here)
    mine.start()
    weights.start()
    sources = (act_hbm, one_hbm, two_hbm)

    def where(pair, side):
        who = flip(me // 2, pair) * 2 + side
        return pl.ds(pl.multiple_of(((who % slots) * planes + who // slots) * rows, rows), rows)

    def fetches(pair):
        return [
            pltpu.make_async_copy(ref.at[where(pair, side)], ins.at[pair % 2, i, side], fetch.at[pair % 2, i, side])
            for i, ref in enumerate(sources)
            for side in (0, 1)
        ]

    def stores(pair):
        return [
            pltpu.make_async_copy(outs.at[pair % 2, i, side], ref.at[where(pair, side)], store.at[pair % 2, i, side])
            for i, ref in enumerate((gg_ref, gu_ref))
            for side in (0, 1)
        ]

    for copy in fetches(0):
        copy.start()
    hops = Hops(planes, slots, rows)
    hello(wide_peers(width, me) + [{"blk": (hops.plane + k) % planes} for k in range(1, planes)])
    flow = Flow(me, g_ref, lambda who, part: buf.at[who // 2, who % 2, pl.ds(part * half, half)], half, send, recv)
    pairs = width // 2

    def work(pair):
        for copy in fetches(pair):
            copy.wait()
        if pair + 1 < pairs:
            for copy in fetches(pair + 1):
                copy.start()
        if pair >= 2:
            for copy in stores(pair - 2):
                copy.wait()
        chip = flip(me // 2, pair)
        slot = pair % 2
        grads = buf[chip].reshape(2 * rows, cols)

        def inner(n, carry):
            at = pl.ds(pl.multiple_of(n * step, step), step)
            grad = lax.dot_general(
                grads, wd[at, :], (((1,), (1,)), ((), ())), preferred_element_type=jnp.float32
            ).reshape(2, rows, step)
            outs[slot, 0, :, :, at] = (grad * ins[slot, 2, :, :, at].astype(jnp.float32)).astype(low)
            outs[slot, 1, :, :, at] = (grad * ins[slot, 1, :, :, at].astype(jnp.float32)).astype(low)
            return carry

        lax.fori_loop(0, hidden // step, inner, 0)
        for copy in stores(pair):
            copy.start()
        tall = min(256, hidden)

        def outer(n, carry):
            at = pl.ds(pl.multiple_of(n * tall, tall), tall)
            act = ins[slot, 0, :, :, at].reshape(2 * rows, tall)
            term = lax.dot_general(act, grads, (((0,), (0,)), ((), ())), preferred_element_type=jnp.float32)
            if pair:
                term = term + held[at, :]
            if pair + 1 < pairs:
                held[at, :] = term
            else:
                down_ref[at, :] = term.astype(low)
            return carry

        lax.fori_loop(0, hidden // tall, outer, 0)

    def pair_ready(k):
        for part in (0, 1):
            flow.arrived(k + 1, part)

    if width == 8:
        flow.go(None, 2, 2, 0)
        flow.go(None, 4, 4, 1)
        flow.go(None, 2, 2, 1)
        flow.go(None, 4, 4, 0)
    else:
        for k in range(2, width, 2):
            flow.go(None, k, k, 0)
            flow.go(None, k, k, 1)
    flow.go(None, 1, 1, 0)
    flow.go(None, 1, 1, 1)
    hops.spread(c_ref, c_out, side_send, side_recv, True, True)
    mine.wait()
    weights.wait()
    pair_ready(0)
    work(0)
    if width == 8:
        flow.arrived(2, 0)
        flow.go(2, 4, 6, 0)
        flow.go(2, 1, 3, 0)
        flow.arrived(4, 1)
        flow.go(4, 2, 6, 1)
        flow.go(4, 1, 5, 1)
        flow.arrived(2, 1)
        flow.go(2, 1, 3, 1)
        flow.arrived(4, 0)
        flow.go(4, 1, 5, 0)
        pair_ready(2)
        work(1)
        pair_ready(4)
        work(2)
        for part in (0, 1):
            flow.arrived(6, part)
            flow.go(6, 1, 7, part)
        pair_ready(6)
        work(3)
    else:
        for k in range(2, width, 2):
            for part in (0, 1):
                flow.arrived(k, part)
                flow.go(k, 1, k + 1, part)
            pair_ready(k)
            work(k // 2)
    flow.finish()
    for pair in (pairs - 2, pairs - 1):
        for copy in stores(pair):
            copy.wait()
    hops.spread(c_ref, c_out, side_send, side_recv, True, False)


def push(g, side_x, down_weight, act, one, two, width, slots, ident, name):
    rows, cols = g.shape
    hidden = down_weight.shape[0]
    low, dma = g.dtype, pltpu.SemaphoreType.DMA
    step = min(512, hidden)
    planes = width // slots
    anywhere = pl.BlockSpec(memory_space=pl.ANY)
    saved = jax.ShapeDtypeStruct((rows * width, hidden), low)
    return pl.pallas_call(
        functools.partial(push_body, width, slots, step),
        out_shape=[
            jax.ShapeDtypeStruct((hidden, cols), low), saved, saved,
            jax.ShapeDtypeStruct((many_rows(planes, rows), cols), low),
        ],
        in_specs=[anywhere] * 6,
        out_specs=[pl.BlockSpec(memory_space=pltpu.VMEM)] + [anywhere] * 3,
        scratch_shapes=[
            pltpu.VMEM((width // 2, 2, rows, cols), low), pltpu.VMEM((hidden, cols), low),
            pltpu.VMEM((hidden, cols), jnp.float32), pltpu.VMEM((2, 3, 2, rows, hidden), low),
            pltpu.VMEM((2, 2, 2, rows, hidden), low),
            dma, dma, dma((width, 2)), dma((width, 2)), dma((planes,)), dma((planes,)),
            dma((2, 3, 2)), dma((2, 2, 2)),
        ],
        cost_estimate=busy(10),
        compiler_params=pltpu.CompilerParams(collective_id=ident, has_side_effects=True, vmem_limit_bytes=VMEM_LIMIT),
        name=name,
    )(g, side_x, down_weight, act, one, two)


def pull_body(width, slots, step, chunk, gg_hbm, gu_hbm, wg_hbm, wu_hbm, h_hbm, out_ref, dw_hbm, gg, gu, wg, wu,
              columns, tiles, load, fetch, store, *sum_refs):
    me = lax.axis_index("wide")
    planes = width // slots
    rows, cols = out_ref.shape
    hidden = wg.shape[1]
    loads = local_copies([(wg_hbm, wg), (wu_hbm, wu), (gg_hbm, gg), (gu_hbm, gu)], load)
    for copy in loads:
        copy.start()
    chunks = cols // chunk

    def fetched(n):
        at = pl.ds(pl.multiple_of(n * chunk, chunk), chunk)
        return pltpu.make_async_copy(h_hbm.at[:, at], columns.at[n % 2], fetch.at[n % 2])

    def stored(n):
        at = pl.ds(pl.multiple_of(n * chunk, chunk), chunk)
        return pltpu.make_async_copy(tiles.at[n % 2], dw_hbm.at[at], store.at[n % 2])

    fetched(0).start()
    hello(wide_peers(width, me))
    sums = Sums(width, me, out_ref, sum_refs)

    def produce(k, put, adds=()):
        who = flip(me, k)
        at_rows = pl.ds(pl.multiple_of(((who % slots) * planes + who // slots) * rows, rows), rows)

        def tile(n, carry):
            at = pl.ds(pl.multiple_of(n * step, step), step)
            total = nt(gg[at_rows, :], wg[at, :]) + nt(gu[at_rows, :], wu[at, :])
            for ref in adds:
                total = total + ref[:, at].astype(jnp.float32)
            put[:, at] = total.astype(put.dtype)
            return carry

        lax.fori_loop(0, cols // step, tile, 0)

    def grads(first, last):
        def one_chunk(n, carry):
            fetched(n).wait()

            @pl.when(n + 1 < chunks)
            def _():
                fetched(n + 1).start()

            @pl.when(n >= 2)
            def _():
                stored(n - 2).wait()

            for i, ref in enumerate((gg, gu)):
                tiles[n % 2, :, pl.ds(i * hidden, hidden)] = lax.dot_general(
                    columns[n % 2], ref[...], (((0,), (0,)), ((), ())), preferred_element_type=jnp.float32
                ).astype(jnp.bfloat16)
            stored(n).start()
            return carry

        lax.fori_loop(first, last, one_chunk, 0)

    def give(k):
        produce(k + 1, sums.odd.at[k // 2])
        sums.give(k)

    def merge(k):
        sums.got(k)
        produce(k, sums.even.at[k // 2 - 1], (sums.from_twin.at[k // 2],))

    for copy in loads:
        copy.wait()
    if width == 8:
        give(6)
        give(2)
        give(4)
        merge(6)
        sums.relay(0).start()
        sums.relay(1).start()
        merge(2)
        sums.far(2, 0).start()
        merge(4)
        sums.far(4, 1).start()
        give(0)
        middle = (3 * chunks) // 8
        grads(0, middle)
        sums.pass_on(2, 1)
        sums.pass_on(4, 0)
        grads(middle, chunks)
    else:
        for k in range(0, width, 2):
            give(k)
        for k in range(2, width, 2):
            merge(k)
            sums.far(k, 0).start()
            sums.far(k, 1).start()
        grads(0, chunks)
    sums.got(0)
    produce(0, out_ref, (sums.from_twin.at[0],))
    sums.finish()
    stored(chunks - 2).wait()
    stored(chunks - 1).wait()


def pull(grad_gate, grad_up, gate_weight, up_weight, gathered, width, slots, ident, name):
    count, cols = gathered.shape
    hidden = gate_weight.shape[1]
    rows = count // width
    low, dma = gathered.dtype, pltpu.SemaphoreType.DMA
    chunk = 256
    anywhere = pl.BlockSpec(memory_space=pl.ANY)
    return pl.pallas_call(
        functools.partial(pull_body, width, slots, 1024, chunk),
        out_shape=[
            jax.ShapeDtypeStruct((rows, cols), jnp.float32), jax.ShapeDtypeStruct((cols, 2 * hidden), low),
        ],
        in_specs=[anywhere] * 5,
        out_specs=[pl.BlockSpec(memory_space=pltpu.VMEM), anywhere],
        scratch_shapes=[
            pltpu.VMEM((count, hidden), low), pltpu.VMEM((count, hidden), low),
            pltpu.VMEM((cols, hidden), low), pltpu.VMEM((cols, hidden), low),
            pltpu.VMEM((2, count, chunk), low), pltpu.VMEM((2, chunk, 2 * hidden), low),
            dma((4,)), dma((2,)), dma((2,)),
        ] + sum_scratch(width, rows, cols),
        cost_estimate=busy(10),
        compiler_params=pltpu.CompilerParams(collective_id=ident, has_side_effects=True, vmem_limit_bytes=VMEM_LIMIT),
        name=name,
    )(grad_gate, grad_up, gate_weight, up_weight, gathered)


def local(
    tokens,
    lengths,
    query_weight,
    key_weight,
    value_weight,
    output_weight,
    query_gain,
    key_gain,
    attention_gain,
    gate_weight,
    up_weight,
    down_weight,
    feedforward_gain,
    cotangent,
):
    low, f32 = jnp.bfloat16, jnp.float32
    planes, width = lax.axis_size("blk"), lax.axis_size("wide")
    slots = width // planes
    rows = tokens.shape[1]
    span = rows * planes
    count = slots * span
    share = query_weight.shape[1]
    heads = share // HD
    plane, place = lax.axis_index("blk"), lax.axis_index("wide")
    after = lambda value, *others: lax.optimization_barrier((value,) + others)[0]

    def over_blk(value, axis):
        return lax.psum_scatter(
            value.astype(low), "blk", scatter_dimension=axis, tiled=True
        ).astype(f32)

    _, near_cotangent, mine = turn(
        turn_in_body, [tokens[0], cotangent[0]], [True, True, False], planes, slots, 1, "turn_in"
    )
    qkv_rows = after(jnp.concatenate([query_weight, key_weight, value_weight], 1), mine)
    w_qkv = lax.all_gather(qkv_rows, "blk", axis=0, tiled=True)
    w_o = lax.all_gather(after(output_weight, w_qkv), "blk", axis=1, tiled=True)
    gains = jnp.stack([query_gain, key_gain]).astype(f32)
    plane_lengths = lax.dynamic_slice_in_dim(lengths, plane * slots, slots, 0)
    segment, position = jax.vmap(lambda one: layout(one, span))(plane_lengths)
    begin = (jnp.arange(span, dtype=jnp.int32)[None] - position)[:, None, :]
    pairs, piece = piece_map(span, rows)
    order = sorted(pairs, key=lambda pair: pair[1])
    position = jnp.concatenate([position[:, at : at + piece] for at, _ in order], 1)
    cosine, sine = rope_tables(position.reshape(-1))
    cosine, sine = cosine.reshape(slots, span, HD), sine.reshape(slots, span, HD)

    inputs = gather(mine, width, slots, 2, "gather_tokens")
    pre = dot(inputs, w_qkv)
    squares = jnp.stack([jnp.sum(pre[:, a * share : (a + 1) * share] ** 2, -1) for a in (0, 1)])
    both = lax.dynamic_update_slice(
        jnp.zeros((2, D), f32), jnp.stack([attention_gain, feedforward_gain]).astype(f32), (0, place * share)
    )
    squares = jnp.concatenate([squares.reshape(-1, 128), both.reshape(-1, 128)])
    squares = total(squares, "wide", width, 3, "total_squares")
    both = squares[2 * count // 128 :].reshape(2, D)
    gain_mix, gain_feed = both[0], both[1]
    inverse = lax.rsqrt(squares[: 2 * count // 128].reshape(2, count) / D + EPS)
    inv_cols = inverse.T.reshape(slots, span, 2)
    pre_groups = pre.reshape(slots, span, 3 * share)
    queries, keys, values, mixed, logs = attend(
        pre_groups, inv_cols, gains, cosine, sine, begin, heads, rows
    )
    mixed = mixed.reshape(count, share)
    projected = scatter([mixed], [w_o], width, slots, False, 4, "scatter_mixed")
    proj_normed, proj_inv = rms_pair(projected)
    hidden = mine.astype(f32) + proj_normed * gain_mix
    reduced, gathered, activated, up_factor, gate_factor, grad_out = feed(
        hidden.astype(low), near_cotangent, gate_weight, up_weight, down_weight, width, slots, 5, "feed"
    )
    grad_out = grad_out.astype(f32)
    red_normed, red_inv = rms_pair(reduced)
    block_output = (hidden + red_normed * gain_feed).astype(low)

    feed_gain_part = jnp.sum(grad_out * red_normed, axis=0)
    grad_reduced = norm_back(red_normed, red_inv, grad_out * gain_feed).astype(low)
    down_part, grad_gate, grad_up, far_output = push(
        grad_reduced, block_output, down_weight, activated, up_factor, gate_factor, width, slots, 7, "push"
    )
    down_grad = over_blk(down_part, 1)
    hidden_part, inner_part = pull(
        grad_gate, grad_up, gate_weight, up_weight, gathered, width, slots, 8, "pull"
    )
    grad_hidden = grad_out + hidden_part
    inner_grad = over_blk(inner_part, 0)
    mix_gain_part = jnp.sum(grad_hidden * proj_normed, axis=0)
    grad_proj = norm_back(proj_normed, proj_inv, grad_hidden * gain_mix).astype(low)
    grad_proj = gather(grad_proj, width, slots, 9, "gather_proj")
    output_part = contract_rows(grad_proj, mixed).astype(low)
    grad_proj = after(grad_proj, down_grad)
    grad_mixed = contract_cols(grad_proj, w_o).astype(low).reshape(slots, span, share)
    scaled_q, scaled_k, grad_v, sums, parts = attend_back(
        queries, keys, values, grad_mixed, logs, pre_groups, inv_cols, gains, cosine, sine, begin,
        heads, rows,
    )
    means = jnp.sum(sums, axis=0).reshape(count, 2).T.reshape(-1, 128)
    means = total(means, "wide", width, 10, "total_means").reshape(2, count) / D

    def finish(scaled, index):
        normed = pre[:, index * share : (index + 1) * share] * inverse[index][:, None]
        scaled = scaled.reshape(count, share)
        return (inverse[index][:, None] * (scaled - normed * means[index][:, None])).astype(low)

    grads = jnp.concatenate([finish(scaled_q, 0), finish(scaled_k, 1), grad_v.reshape(count, share)], 1)
    tokens_part = scatter([grads], [w_qkv], width, slots, True, 11, "scatter_tokens")
    _, block_output, tokens_grad = turn(
        turn_out_body, [after((grad_hidden + tokens_part).astype(low), inner_grad), far_output], [True, False, False],
        planes, slots, 14, "turn_out",
    )
    qkv_part = contract_rows(inputs, grads).astype(low)
    side_grad = over_blk(jnp.concatenate([qkv_part, output_part], 1), 0)

    gain_parts = jnp.sum(parts, axis=0)
    local_gains = lax.dynamic_update_slice(jnp.zeros((2, D), f32), gain_parts, (0, place * share))
    sums = jnp.concatenate([local_gains, jnp.stack([mix_gain_part, feed_gain_part])])
    sums = total(sums.reshape(-1, 128), "wide", width, 12, "total_gains")
    sums = total(sums, "blk", planes, 13, "total_gains_blk").reshape(4, D)
    portion = D // (planes * width)
    sums = lax.dynamic_slice_in_dim(sums, (plane * width + place) * portion, portion, 1)
    return (
        block_output[None],
        tokens_grad[None].astype(f32),
        side_grad[:, :share],
        side_grad[:, share : 2 * share],
        side_grad[:, 2 * share : 3 * share],
        side_grad[:, 3 * share :].T,
        sums[0],
        sums[1],
        sums[2],
        inner_grad[:, : gate_weight.shape[1]],
        inner_grad[:, gate_weight.shape[1] :],
        down_grad,
        sums[3],
    )


def solution(mesh):
    placed = (
        P("wide", "blk", None),
        P(),
        P("blk", "wide"),
        P("blk", "wide"),
        P("blk", "wide"),
        P("wide", "blk"),
        P("wide"),
        P("wide"),
        P("wide"),
        P(None, "wide"),
        P(None, "wide"),
        P("wide", None),
        P("wide"),
        P("wide", "blk", None),
    )
    return jax.shard_map(
        local,
        mesh=mesh,
        in_specs=placed,
        out_specs=(
            P("wide", "blk", None),
            P("wide", "blk", None),
            P("blk", "wide"),
            P("blk", "wide"),
            P("blk", "wide"),
            P("wide", "blk"),
            P(("blk", "wide")),
            P(("blk", "wide")),
            P(("blk", "wide")),
            P("blk", "wide"),
            P("blk", "wide"),
            P("wide", "blk"),
            P(("blk", "wide")),
        ),
        check_vma=False,
    )
```

```python
import functools

import jax
import jax.numpy as jnp
import numpy as np
from jax import lax
from jax.experimental import pallas as pl
from jax.experimental.pallas import tpu as pltpu
from jax.sharding import PartitionSpec as P

MESH = pl.DeviceIdType.MESH

D = 2048
HD = 128
EPS = 1e-06
ROPE_BASE = 500000.0
NEG_FILL = -1e30
VMEM_LIMIT = 60 * 1024 * 1024
SCALE = HD ** (-0.5)


def busy(micros):
    return pl.CostEstimate(flops=0, bytes_accessed=int(micros * 3.5e6), transcendentals=0)


def layout(seq_lengths, row_count):
    indices = jnp.arange(row_count, dtype=jnp.int32)
    first_end = seq_lengths[0]
    second_end = seq_lengths[0] + seq_lengths[1]
    segment = (indices >= first_end).astype(jnp.int32) + (indices >= second_end).astype(jnp.int32)
    offsets = jnp.where(segment == 0, 0, jnp.where(segment == 1, first_end, second_end))
    return (segment, indices - offsets)


def rope_tables(index, begin):
    frequency = ROPE_BASE ** (-np.arange(0, HD, 2, dtype=np.float64) / HD)
    angles = np.asarray(index, np.float64)[:, None] * frequency
    sign = np.concatenate([-np.ones(HD // 2), np.ones(HD // 2)])
    twice = lambda value: np.concatenate([value, value], -1).astype(np.float32)
    cosine, sine = jnp.asarray(twice(np.cos(angles))), jnp.asarray(twice(np.sin(angles)))
    shift = begin.astype(jnp.float32)[..., None] * jnp.asarray(twice(frequency))
    return cosine, sine, jnp.cos(shift), jnp.sin(shift), jnp.asarray(sign.astype(np.float32))


def rms_pair(values):
    inverse = lax.rsqrt(jnp.mean(values * values, axis=-1, keepdims=True) + EPS)
    return (values * inverse, inverse)


def norm_back(normed, inverse, grad_normed):
    return inverse * (grad_normed - normed * jnp.mean(grad_normed * normed, axis=-1, keepdims=True))


def dot(left, right):
    return jnp.dot(left, right, preferred_element_type=jnp.float32)


def contract_rows(left, right):
    return lax.dot_general(
        left, right, (((0,), (0,)), ((), ())), preferred_element_type=jnp.float32
    )


def contract_cols(left, right):
    return lax.dot_general(
        left, right, (((1,), (1,)), ((), ())), preferred_element_type=jnp.float32
    )


def flip(me, k):
    out, bit = me, 1
    while bit <= k:
        if k & bit:
            out = out + bit * (1 - 2 * ((me // bit) % 2))
        bit *= 2
    return out


def greet(axis, me, others):
    barrier = pltpu.get_barrier_semaphore()
    for k in others:
        pl.semaphore_signal(barrier, inc=1, device_id={axis: flip(me, k)}, device_id_type=MESH)
    pl.semaphore_wait(barrier, len(others))


class Flow:
    def __init__(self, me, source, spot, half, send, recv):
        self.me, self.source, self.spot, self.half = me, source, spot, half
        self.send, self.recv, self.moves = send, recv, []

    def go(self, origin, target, k, part):
        if origin is None:
            source = self.source.at[pl.ds(part * self.half, self.half)]
        else:
            source = self.spot(flip(self.me, origin), part)
        copy = pltpu.make_async_remote_copy(
            src_ref=source,
            dst_ref=self.spot(flip(flip(self.me, target), k), part),
            send_sem=self.send.at[k, part],
            recv_sem=self.recv.at[k, part],
            device_id={"wide": flip(self.me, target)},
            device_id_type=MESH,
        )
        copy.start()
        self.moves.append(copy)

    def arrived(self, k, part):
        block = self.spot(flip(self.me, k), part)
        pltpu.make_async_copy(block, block, self.recv.at[k, part]).wait()

    def finish(self):
        for copy in self.moves:
            copy.wait_send()


class Sums:
    def __init__(self, width, me, out_ref, refs):
        self.width, self.me, self.out = width, me, out_ref
        (self.odd, self.even, self.from_twin, self.from_far, self.passing, self.sends, self.recvs,
         self.pass_send, self.pass_recv, self.twin_send, self.twin_recv) = refs
        self.half = out_ref.shape[0] // 2

    def rows(self, part):
        return pl.ds(part * self.half, self.half)

    def copy(self, src, dst, send, recv, k):
        return pltpu.make_async_remote_copy(
            src_ref=src, dst_ref=dst, send_sem=send, recv_sem=recv,
            device_id={"wide": flip(self.me, k)}, device_id_type=MESH,
        )

    def twin(self, k, part):
        i, at = k // 2, self.rows(part)
        return self.copy(
            self.odd.at[i, at], self.from_twin.at[i, at], self.twin_send.at[i, part],
            self.twin_recv.at[i, part], 1,
        )

    def far(self, k, part):
        i, at = k // 2 - 1, self.rows(part)
        return self.copy(
            self.even.at[i, at], self.from_far.at[i, at], self.sends.at[i, part], self.recvs.at[i, part], k
        )

    def relay(self, part):
        return self.copy(
            self.even.at[2, self.rows(part)], self.passing.at[part], self.pass_send.at[part],
            self.pass_recv.at[part], 2 if part == 0 else 4,
        )

    def give(self, k):
        self.twin(k, 0).start()
        self.twin(k, 1).start()

    def got(self, k):
        self.twin(k, 0).wait_recv()
        self.twin(k, 1).wait_recv()

    def pass_on(self, k, part):
        self.relay(part).wait_recv()
        at = self.rows(part)
        self.even[k // 2 - 1, at, :] = (
            self.even[k // 2 - 1, at, :].astype(jnp.float32) + self.passing[part].astype(jnp.float32)
        ).astype(jnp.bfloat16)
        self.far(k, part).start()

    def finish(self):
        sources = [2, 4] if self.width == 8 else list(range(2, self.width, 2))
        for k in sources:
            for part in (0, 1):
                self.far(k, part).wait_recv()
        extra = self.from_far[sources[0] // 2 - 1].astype(jnp.float32)
        for k in sources[1:]:
            extra = extra + self.from_far[k // 2 - 1].astype(jnp.float32)
        self.out[...] = self.out[...] + extra
        for part in (0, 1):
            for k in sources:
                self.far(k, part).wait_send()
            for k in range(0, self.width, 2):
                self.twin(k, part).wait_send()
            if self.width == 8:
                self.relay(part).wait_send()


def run_sums(width, sums, produce, beside=None, steps=0):
    half = sums.half
    rows = 2 * half

    def give(k, part=None):
        if part is None:
            produce(k + 1, 0, rows, sums.odd.at[k // 2])
            sums.give(k)
        else:
            produce(k + 1, part * half, half, sums.odd.at[k // 2, sums.rows(part)])
            sums.twin(k, part).start()

    def merge(k, part=None):
        if part is None:
            sums.got(k)
            produce(k, 0, rows, sums.even.at[k // 2 - 1], (sums.from_twin.at[k // 2],))
        else:
            sums.twin(k, part).wait_recv()
            at = sums.rows(part)
            produce(k, part * half, half, sums.even.at[k // 2 - 1, at], (sums.from_twin.at[k // 2, at],))

    if width == 8:
        give(6, 0)
        give(6, 1)
        merge(6, 0)
        sums.relay(0).start()
        merge(6, 1)
        sums.relay(1).start()
        give(2)
        give(4)
        merge(2)
        sums.far(2, 0).start()
        merge(4)
        sums.far(4, 1).start()
        sums.pass_on(2, 1)
        sums.pass_on(4, 0)
        give(0)
    else:
        for k in range(0, width, 2):
            give(k)
        for k in range(2, width, 2):
            merge(k)
            sums.far(k, 0).start()
            sums.far(k, 1).start()
    if beside is not None:
        beside(0, steps)
    sums.got(0)
    produce(0, 0, rows, sums.out, (sums.from_twin.at[0],))
    sums.finish()


def sum_scratch(width, rows, cols):
    chips, dma = width // 2, pltpu.SemaphoreType.DMA
    block = lambda n: pltpu.VMEM((n, rows, cols), jnp.bfloat16)
    return [
        block(chips), block(chips - 1), block(chips), block(2 if width == 8 else chips - 1),
        pltpu.VMEM((2, rows // 2, cols), jnp.bfloat16),
        dma((chips - 1, 2)), dma((chips - 1, 2)), dma((2,)), dma((2,)), dma((chips, 2)), dma((chips, 2)),
    ]


def wide_peers(width, me):
    return [{"wide": flip(me, k)} for k in [1] + list(range(2, width, 2))]


def local_copies(pairs, sem):
    return [pltpu.make_async_copy(src, dst, sem.at[i]) for i, (src, dst) in enumerate(pairs)]


def gather_body(width, slots, side, *refs):
    if side is None:
        x_ref, out_ref, here, send, recv = refs
    else:
        x_ref, side_ref, out_ref, side_out, here, send, recv, side_send, side_recv = refs
    me = lax.axis_index("wide")
    rows = x_ref.shape[0]
    half = rows // 2
    evens = list(range(2, width, 2))
    peers = [{"wide": flip(me, k)} for k in [1] + evens]
    if side is not None:
        hops = Hops(width // slots, slots, rows)
        peers = peers + [{"blk": (hops.plane + k) % hops.planes} for k in range(1, hops.planes)]
    hello(peers)
    if side is not None:
        job = hops.join if side == "join" else hops.spread
        job(side_ref, side_out, side_send, side_recv, True, True)

    def spot(who, first, count):
        base = ((who % slots) * (width // slots) + who // slots) * rows
        return out_ref.at[pl.ds(pl.multiple_of(base + first, half), count)]

    def move(origin, target, k, part):
        if origin is None:
            source = x_ref.at[pl.ds(part * half, half)]
        else:
            source = spot(flip(me, origin), part * half, half)
        return pltpu.make_async_remote_copy(
            src_ref=source,
            dst_ref=spot(flip(flip(me, target), k), part * half, half),
            send_sem=send.at[k, part],
            recv_sem=recv.at[k, part],
            device_id={"wide": flip(me, target)},
            device_id_type=MESH,
        )

    def arrived(k, part):
        block = spot(flip(me, k), part * half, half)
        pltpu.make_async_copy(block, block, recv.at[k, part]).wait()

    moves = []

    def go(origin, target, k, part):
        copy = move(origin, target, k, part)
        copy.start()
        moves.append(copy)

    mine = pltpu.make_async_copy(x_ref, spot(me, 0, rows), here)
    mine.start()
    if width == 8:
        go(None, 2, 2, 0)
        go(None, 4, 4, 1)
        go(None, 2, 2, 1)
        go(None, 4, 4, 0)
        go(None, 1, 1, 0)
        go(None, 1, 1, 1)
        arrived(2, 0)
        go(2, 4, 6, 0)
        go(2, 1, 3, 0)
        arrived(4, 1)
        go(4, 2, 6, 1)
        go(4, 1, 5, 1)
        order = [(2, 1), (4, 0), (6, 0), (6, 1)]
    else:
        for k in evens:
            go(None, k, k, 0)
            go(None, k, k, 1)
        go(None, 1, 1, 0)
        go(None, 1, 1, 1)
        order = [(k, part) for k in evens for part in (0, 1)]
    for k, part in order:
        arrived(k, part)
        go(k, 1, k + 1, part)
    for k in range(1, width, 2):
        for part in (0, 1):
            arrived(k, part)
    for copy in moves:
        copy.wait_send()
    mine.wait()
    if side is not None:
        job(side_ref, side_out, side_send, side_recv, True, False)


def gather(x, width, slots, ident, name, side=None, side_x=None):
    rows, cols = x.shape
    planes = width // slots
    dma = pltpu.SemaphoreType.DMA
    shapes = [jax.ShapeDtypeStruct((rows * width, cols), x.dtype)]
    scratch = [dma, dma((width, 2)), dma((width, 2))]
    inputs = [x]
    if side is not None:
        inputs.append(side_x)
        extent = rows if side == "join" else many_rows(planes, rows)
        shapes.append(jax.ShapeDtypeStruct((extent, cols), side_x.dtype))
        scratch += [dma((planes,)), dma((planes,))]
    outs = pl.pallas_call(
        functools.partial(gather_body, width, slots, side),
        out_shape=shapes,
        in_specs=[pl.BlockSpec(memory_space=pl.ANY)] * len(inputs),
        out_specs=[pl.BlockSpec(memory_space=pl.ANY)] * len(shapes),
        scratch_shapes=scratch,
        cost_estimate=busy(10),
        compiler_params=pltpu.CompilerParams(collective_id=ident, has_side_effects=True, vmem_limit_bytes=VMEM_LIMIT),
        name=name,
    )(*inputs)
    return outs[0] if side is None else outs


def scatter_body(width, slots, flat, count, step, finish, *refs):
    lefts, rights = refs[:count], refs[count : 2 * count]
    if finish == "norm":
        x_ref, gain_ref, hidden_ref, low_ref, out_ref, inv_ref = refs[2 * count : 2 * count + 6]
        rest = refs[2 * count + 6 :]
    else:
        more_ref, low_ref, out_ref = refs[2 * count : 2 * count + 3]
        rest = refs[2 * count + 3 :]
    me = lax.axis_index("wide")
    rows, cols = out_ref.shape
    hello(wide_peers(width, me))
    sums = Sums(width, me, out_ref, rest)
    dims = (((1,), (1 if flat else 0,)), ((), ()))

    def produce(k, first, some, put, adds=()):
        who = flip(me, k)
        start = ((who % slots) * (width // slots) + who // slots) * rows + first
        start = pl.multiple_of(start, rows // 2)

        def tile(n, carry):
            at = pl.ds(pl.multiple_of(n * step, step), step)
            total = None
            for left, right in zip(lefts, rights):
                other = right[at, :] if flat else right[:, at]
                term = lax.dot_general(
                    left[pl.ds(start, some), :], other, dims, preferred_element_type=jnp.float32
                )
                total = term if total is None else total + term
            for ref in adds:
                total = total + ref[:, at].astype(jnp.float32)
            put[:, at] = total.astype(put.dtype)
            return carry

        lax.fori_loop(0, cols // step, tile, 0)

    run_sums(width, sums, produce)
    if finish == "add":
        def close(n, carry):
            at = pl.ds(pl.multiple_of(n * 32, 32), 32)
            low_ref[at, :] = (out_ref[at, :] + more_ref[at, :]).astype(low_ref.dtype)
            return carry

        lax.fori_loop(0, rows // 32, close, 0)
    if finish != "norm":
        return
    few = 32

    def norm(n, carry):
        at = pl.ds(pl.multiple_of(n * few, few), few)
        value = out_ref[at, :]
        inverse = lax.rsqrt(jnp.sum(value * value, axis=-1, keepdims=True) * (1.0 / cols) + EPS)
        value = value * inverse
        out_ref[at, :] = value
        inv_ref[at, :] = inverse
        hidden = x_ref[at, :].astype(jnp.float32) + value * gain_ref[...]
        hidden_ref[at, :] = hidden
        low_ref[at, :] = hidden.astype(low_ref.dtype)
        return carry

    lax.fori_loop(0, rows // few, norm, 0)


def scatter(lefts, rights, width, slots, flat, ident, name, finish, more, step=1024):
    rows = lefts[0].shape[0] // width
    cols = rights[0].shape[0 if flat else 1]
    f32, vmem = jnp.float32, pl.BlockSpec(memory_space=pltpu.VMEM)
    whole, low = jax.ShapeDtypeStruct((rows, cols), f32), jax.ShapeDtypeStruct((rows, cols), lefts[0].dtype)
    shapes = [whole, low, whole, jax.ShapeDtypeStruct((rows, 1), f32)] if finish == "norm" else [low]
    scratch = sum_scratch(width, rows, cols)
    if finish == "add":
        scratch = [pltpu.VMEM((rows, cols), f32)] + scratch
    outs = pl.pallas_call(
        functools.partial(scatter_body, width, slots, flat, len(lefts), step, finish),
        out_shape=shapes,
        in_specs=[vmem] * (2 * len(lefts) + len(more)),
        out_specs=[vmem] * len(shapes),
        scratch_shapes=scratch,
        cost_estimate=busy(10),
        compiler_params=pltpu.CompilerParams(collective_id=ident, has_side_effects=True, vmem_limit_bytes=VMEM_LIMIT),
        name=name,
    )(*lefts, *rights, *more)
    return outs if finish == "norm" else outs[0]


def total_body(axis, width, x_ref, out_ref, slots, send, recv):
    me = lax.axis_index(axis)
    others = list(range(1, width))
    greet(axis, me, others)
    moves = []
    for k in others:
        copy = pltpu.make_async_remote_copy(
            src_ref=x_ref,
            dst_ref=slots.at[k - 1],
            send_sem=send.at[k - 1],
            recv_sem=recv.at[k - 1],
            device_id={axis: flip(me, k)},
            device_id_type=MESH,
        )
        copy.start()
        moves.append(copy)
    out_ref[...] = x_ref[...]
    for copy, k in zip(moves, others):
        copy.wait_recv()
        out_ref[...] = out_ref[...] + slots[k - 1]
    for copy in moves:
        copy.wait_send()


def total(x, axis, width, ident, name):
    return pl.pallas_call(
        functools.partial(total_body, axis, width),
        out_shape=jax.ShapeDtypeStruct(x.shape, x.dtype),
        in_specs=[pl.BlockSpec(memory_space=pltpu.VMEM)],
        out_specs=pl.BlockSpec(memory_space=pltpu.VMEM),
        scratch_shapes=[
            pltpu.VMEM((width - 1,) + x.shape, x.dtype),
            pltpu.SemaphoreType.DMA((width - 1,)),
            pltpu.SemaphoreType.DMA((width - 1,)),
        ],
        cost_estimate=busy(7),
        compiler_params=pltpu.CompilerParams(collective_id=ident, has_side_effects=True, vmem_limit_bytes=VMEM_LIMIT),
        name=name,
    )(x)


class Hops:
    def __init__(self, planes, slots, rows):
        self.planes, self.slots = planes, slots
        self.count = max(n for n in range(1, planes + 1) if planes % n == 0 and rows % (16 * n) == 0)
        self.per = planes // self.count
        self.piece = rows // self.count
        self.plane, self.place = lax.axis_index("blk"), lax.axis_index("wide")
        self.chip, self.slot = self.place // slots, self.place % slots
        self.active = self.chip // self.count == self.plane % self.per

    def peers(self):
        near = [{"wide": (self.chip + k) % self.planes * self.slots + self.slot} for k in range(1, self.planes)]
        return near + [{"blk": (self.plane + k) % self.planes} for k in range(1, self.planes)]

    def when(self, condition, action):
        if self.per == 1:
            action()
        else:
            pl.when(condition)(action)

    def split(self, condition, yes, no):
        if self.per == 1:
            yes()
        else:
            pl.when(condition)(yes)
            pl.when(jnp.logical_not(condition))(no)

    def cut(self, ref, index):
        return ref.at[pl.ds(pl.multiple_of(index * self.piece, self.piece), self.piece)]

    def remote(self, src, dst, send, recv, device):
        return pltpu.make_async_remote_copy(
            src_ref=src, dst_ref=dst, send_sem=send, recv_sem=recv, device_id=device, device_id_type=MESH
        )

    def spread(self, some, many, send, recv, across, start):
        if across:
            axis, here = "blk", self.plane
            targets = [
                ((self.plane // self.per + k) % self.count) for k in range(self.count)
            ]
            device = lambda piece: piece * self.per + self.chip // self.count
        else:
            axis, here = "wide", self.chip
            targets = [((self.chip + k) % self.count) for k in range(self.count)]
            device = lambda piece: (self.plane % self.per) * self.count + piece
        address = (lambda who: {"blk": who}) if across else (
            lambda who: {"wide": who * self.slots + self.slot}
        )
        for k, piece in enumerate(targets):
            who = device(piece)
            far = self.remote(
                self.cut(some, piece), self.cut(many, here), send.at[piece],
                recv.at[(here - who + self.planes) % self.planes], address(who),
            )
            own = pltpu.make_async_copy(self.cut(some, piece), self.cut(many, here), send.at[piece])
            if k:
                far.start() if start else far.wait_send()
            elif start:
                self.split(self.active, own.start, far.start)
            else:
                self.split(self.active, own.wait, far.wait_send)
        if not start:
            def receive():
                for k in range(1, self.planes):
                    block = self.cut(many, (here + k) % self.planes)
                    pltpu.make_async_copy(block, block, recv.at[k]).wait()

            self.when(self.active, receive)

    def join(self, many, some, send, recv, across, start, ready=None):
        if across:
            here = self.plane
            index = self.plane // self.per
            address = lambda who: {"blk": who}
        else:
            here = self.chip
            index = self.chip % self.count
            address = lambda who: {"wide": who * self.slots + self.slot}

        def give():
            for k in list(range(1, self.planes)) + [0]:
                who = (here + k) % self.planes
                if ready is not None:
                    ready(who)
                if k:
                    copy = self.remote(
                        self.cut(many, who), self.cut(some, index), send.at[k], recv.at[index], address(who)
                    )
                    copy.start() if start else copy.wait_send()
                else:
                    own = pltpu.make_async_copy(self.cut(many, here), self.cut(some, index), send.at[0])
                    own.start() if start else own.wait()

        self.when(self.active, give)
        if not start:
            for k in range(self.count):
                piece = (index + k) % self.count
                block = self.cut(some, piece)
                arrival = pltpu.make_async_copy(block, block, recv.at[piece])
                if k:
                    arrival.wait()
                elif self.per > 1:
                    pl.when(jnp.logical_not(self.active))(arrival.wait)

    def arrival(self, some, many, send, recv, across):
        here = self.plane if across else self.chip
        own_piece = self.plane // self.per if across else self.chip % self.count

        def ready(who):
            block = self.cut(many, who)

            @pl.when(who == here)
            def _():
                pltpu.make_async_copy(self.cut(some, own_piece), block, send.at[own_piece]).wait()

            @pl.when(who != here)
            def _():
                pltpu.make_async_copy(block, block, recv.at[(who - here + self.planes) % self.planes]).wait()

        return ready

    def sent(self, some, many, send, across):
        pieces = self.plane // self.per if across else self.chip
        for k in range(self.count):
            piece = (pieces + k) % self.count
            block = self.cut(some, piece)
            out = pltpu.make_async_copy(block, block, send.at[piece])
            if k:
                out.wait()
            elif self.per > 1:
                pl.when(jnp.logical_not(self.active))(out.wait)


def hello(peers):
    barrier = pltpu.get_barrier_semaphore()
    for peer in peers:
        pl.semaphore_signal(barrier, inc=1, device_id=peer, device_id_type=MESH)
    pl.semaphore_wait(barrier, len(peers))


def turn_in_body(planes, slots, x_ref, c_ref, near_x, near_c, out_ref, *sems):
    hops = Hops(planes, slots, x_ref.shape[0])
    hello(hops.peers())
    hops.spread(x_ref, near_x, sems[0], sems[1], False, True)
    ready = hops.arrival(x_ref, near_x, sems[0], sems[1], False)
    hops.join(near_x, out_ref, sems[2], sems[3], True, True, ready)
    hops.sent(x_ref, near_x, sems[0], False)
    hops.spread(c_ref, near_c, sems[4], sems[5], False, True)
    hops.spread(c_ref, near_c, sems[4], sems[5], False, False)
    hops.join(near_x, out_ref, sems[2], sems[3], True, False)


def turn_out_body(planes, slots, x_ref, far_c, v_ref, far_x, out_c, out_ref, v_out, *sems):
    hops = Hops(planes, slots, x_ref.shape[0])
    hello(hops.peers())
    parts, send, recv = sems[6:]
    moves = []
    for k in range(1, planes):
        copy = hops.remote(
            v_ref, parts.at[planes - k - 1], send.at[k - 1], recv.at[planes - k - 1],
            {"blk": (hops.plane + k) % planes},
        )
        copy.start()
        moves.append(copy)
    hops.spread(x_ref, far_x, sems[0], sems[1], True, True)
    hops.join(far_c, out_c, sems[2], sems[3], False, True)
    ready = hops.arrival(x_ref, far_x, sems[0], sems[1], True)
    hops.join(far_x, out_ref, sems[4], sems[5], False, True, ready)
    hops.sent(x_ref, far_x, sems[0], True)
    amount = v_ref[...]
    for k in range(1, planes):
        block = parts.at[k - 1]
        pltpu.make_async_copy(block, block, recv.at[k - 1]).wait()
        amount = amount + parts[k - 1]
    v_out[...] = amount
    for copy in moves:
        copy.wait_send()
    hops.join(far_c, out_c, sems[2], sems[3], False, False)
    hops.join(far_x, out_ref, sems[4], sems[5], False, False)


def many_rows(planes, rows):
    count = max(n for n in range(1, planes + 1) if planes % n == 0 and rows % (16 * n) == 0)
    return planes * (rows // count)


def turn(body, inputs, outputs, planes, slots, ident, name, extra=None):
    rows, cols = inputs[0].shape
    low = inputs[0].dtype
    dma = pltpu.SemaphoreType.DMA
    shape = lambda many: jax.ShapeDtypeStruct((many_rows(planes, rows) if many else rows, cols), low)
    anywhere, vmem = pl.BlockSpec(memory_space=pl.ANY), pl.BlockSpec(memory_space=pltpu.VMEM)
    more = [] if extra is None else [extra]
    scratch = [dma((planes,))] * 6
    for value in more:
        scratch += [pltpu.VMEM((planes - 1,) + value.shape, value.dtype), dma((planes - 1,)), dma((planes - 1,))]
    return pl.pallas_call(
        functools.partial(body, planes, slots),
        out_shape=[shape(many) for many in outputs] + [jax.ShapeDtypeStruct(v.shape, v.dtype) for v in more],
        in_specs=[anywhere] * len(inputs) + [vmem] * len(more),
        out_specs=[anywhere] * len(outputs) + [vmem] * len(more),
        scratch_shapes=scratch,
        cost_estimate=busy(10),
        compiler_params=pltpu.CompilerParams(collective_id=ident, has_side_effects=True, vmem_limit_bytes=VMEM_LIMIT),
        name=name,
    )(*inputs, *more)


def mask_scores(scores, first, begin, size):
    span = scores.shape[0]
    index = lax.broadcasted_iota(jnp.int32, scores.shape, 0)
    query = lax.broadcasted_iota(jnp.int32, scores.shape, 1) + first
    return jnp.where((index <= query) & (index >= begin), scores, NEG_FILL)


def nt(left, right):
    return lax.dot_general(left, right, (((1,), (1,)), ((), ())), preferred_element_type=jnp.float32)


def nn(left, right):
    return jnp.dot(left, right, preferred_element_type=jnp.float32)


def piece_map(span, size):
    planes = span // size
    count = max(n for n in range(1, planes + 1) if planes % n == 0 and size % (16 * n) == 0)
    per, piece = planes // count, size // count
    pairs = []
    for t in range(count):
        for high in range(per):
            for low in range(count):
                natural = ((t * per + high) * count + low) * piece
                pairs.append((natural, ((high * count + low) * count + t) * piece))
    return pairs, piece


def attend_body(size, q_ref, k_ref, v_ref, inv_ref, gain_ref, cos_ref, sin_ref, begin_ref,
                qo_ref, ko_ref, vo_ref, mix_ref, log_ref):
    low = jnp.bfloat16
    span = q_ref.shape[0]

    def prepare(ref, col):
        value = ref[...] * inv_ref[:, col : col + 1] * gain_ref[col : col + 1, :]
        return (value * cos_ref[...] + pltpu.roll(value, HD // 2, 1) * sin_ref[...]).astype(low)

    pairs, piece = piece_map(span, size)

    def arrange(ref, value):
        for natural, block in pairs:
            ref[natural : natural + piece, :] = value[block : block + piece, :]

    arrange(qo_ref, prepare(q_ref, 0))
    arrange(ko_ref, prepare(k_ref, 1))
    arrange(vo_ref, v_ref[...].astype(low))
    flipped = vo_ref[...].astype(jnp.float32).T.astype(low)
    for i in range(span // size):
        last = (i + 1) * size
        cols = slice(i * size, last)
        scores = nt(ko_ref[:last, :], qo_ref[cols, :]) * SCALE
        scores = mask_scores(scores, i * size, begin_ref[:, cols], size)
        top = jnp.max(scores, axis=0, keepdims=True)
        raw = jnp.exp(scores - top)
        weight = jnp.sum(raw, axis=0, keepdims=True)
        mixed = nn(flipped[:, :last], raw.astype(low)) * (1.0 / weight)
        mixed = mixed.T.astype(low)
        for natural, block in pairs:
            if i * size <= natural < last:
                at = natural - i * size
                mix_ref[block : block + piece, :] = mixed[at : at + piece, :]
        log_ref[:, cols] = top + jnp.log(weight)


def attend(pre, inverse, gains, cosine, sine, begin, heads, size):
    slots, span, _ = pre.shape
    low, f32 = jnp.bfloat16, jnp.float32
    head = lambda offset: pl.BlockSpec((None, span, HD), lambda g, h: (g, 0, offset + h))
    every = lambda cols: pl.BlockSpec((None, span, cols), lambda g, h: (g, 0, 0))
    line = pl.BlockSpec((None, 1, span), lambda g, h: (g, 0, 0))
    out = jax.ShapeDtypeStruct((slots, span, heads * HD), low)
    return pl.pallas_call(
        functools.partial(attend_body, size),
        grid=(slots, heads),
        out_shape=[out, out, out, out, jax.ShapeDtypeStruct((slots, heads, 1, span), f32)],
        in_specs=[
            head(0), head(heads), head(2 * heads), every(2),
            pl.BlockSpec((2, HD), lambda g, h: (0, h)), every(HD), every(HD), line,
        ],
        out_specs=[head(0)] * 4 + [pl.BlockSpec((None, None, 1, span), lambda g, h: (g, h, 0, 0))],
        compiler_params=pltpu.CompilerParams(vmem_limit_bytes=VMEM_LIMIT),
        cost_estimate=busy(5),
        name="attend",
    )(pre, pre, pre, inverse, gains, cosine, sine, begin)


def attend_back_body(size, q_ref, k_ref, v_ref, g_ref, log_ref, qp_ref, kp_ref, inv_ref, gain_ref,
                     cos_ref, sin_ref, begin_ref, sq_ref, sk_ref, gv_ref, sums_ref, part_ref,
                     keys_sum, values_sum, queries_sum, held, g_held):
    low = jnp.bfloat16
    span = q_ref.shape[0]
    pairs, piece = piece_map(span, size)
    for natural, block in pairs:
        g_held[natural : natural + piece, :] = g_ref[block : block + piece, :]
    flipped = k_ref[...].astype(jnp.float32).T.astype(low)
    keys_sum[...] = jnp.zeros_like(keys_sum)
    values_sum[...] = jnp.zeros_like(values_sum)
    for i in range(span // size):
        last = (i + 1) * size
        cols = slice(i * size, last)
        scores = nt(k_ref[:last, :], q_ref[cols, :]) * SCALE
        scores = mask_scores(scores, i * size, begin_ref[:, cols], size)
        probs = jnp.exp(scores - log_ref[:, cols])
        grad_probs = nt(v_ref[:last, :], g_held[cols, :])
        delta = jnp.sum(probs * grad_probs, axis=0, keepdims=True)
        grad_scores = (probs * (grad_probs - delta)).astype(low)
        values_sum[:last, :] += nn(probs.astype(low), g_held[cols, :])
        keys_sum[:last, :] += nn(grad_scores, q_ref[cols, :])
        queries_sum[cols, :] = nn(flipped[:, :last], grad_scores).T

    def finish(total_ref, pre_ref, out_ref, col):
        for natural, block in pairs:
            held[block : block + piece, :] = total_ref[natural : natural + piece, :]
        grad = held[...] * SCALE
        back = grad * cos_ref[...] - pltpu.roll(grad, HD // 2, 1) * sin_ref[...]
        normed = pre_ref[...] * inv_ref[:, col : col + 1]
        part_ref[col : col + 1, :] = jnp.sum(back * normed, axis=0, keepdims=True)
        scaled = back * gain_ref[col : col + 1, :]
        out_ref[...] = scaled
        sums_ref[:, col : col + 1] = jnp.sum(scaled * normed, axis=1, keepdims=True)

    finish(queries_sum, qp_ref, sq_ref, 0)
    finish(keys_sum, kp_ref, sk_ref, 1)
    for natural, block in pairs:
        gv_ref[block : block + piece, :] = values_sum[natural : natural + piece, :].astype(low)


def attend_back(queries, keys, values, grads, logs, pre, inverse, gains, cosine, sine, begin, heads, size):
    slots, span, _ = pre.shape
    low, f32 = jnp.bfloat16, jnp.float32
    head = lambda offset: pl.BlockSpec((None, span, HD), lambda g, h: (g, 0, offset + h))
    every = lambda cols: pl.BlockSpec((None, span, cols), lambda g, h: (g, 0, 0))
    line = pl.BlockSpec((None, 1, span), lambda g, h: (g, 0, 0))
    wide = jax.ShapeDtypeStruct((slots, span, heads * HD), f32)
    return pl.pallas_call(
        functools.partial(attend_back_body, size),
        grid=(slots, heads),
        out_shape=[
            wide, wide, jax.ShapeDtypeStruct((slots, span, heads * HD), low),
            jax.ShapeDtypeStruct((heads, slots, span, 2), f32),
            jax.ShapeDtypeStruct((slots, 2, heads * HD), f32),
        ],
        in_specs=[
            head(0), head(0), head(0), head(0),
            pl.BlockSpec((None, None, 1, span), lambda g, h: (g, h, 0, 0)),
            head(0), head(heads), every(2),
            pl.BlockSpec((2, HD), lambda g, h: (0, h)), every(HD), every(HD), line,
        ],
        out_specs=[
            head(0), head(0), head(0),
            pl.BlockSpec((None, None, span, 2), lambda g, h: (h, g, 0, 0)),
            pl.BlockSpec((None, 2, HD), lambda g, h: (g, 0, h)),
        ],
        scratch_shapes=[pltpu.VMEM((span, HD), f32)] * 4 + [pltpu.VMEM((span, HD), low)],
        compiler_params=pltpu.CompilerParams(vmem_limit_bytes=VMEM_LIMIT),
        cost_estimate=busy(5),
        name="attend_back",
    )(queries, keys, values, grads, logs, pre, pre, inverse, gains, cosine, sine, begin)


def row_sums(value):
    return jnp.sum(value.reshape(-1, 8, value.shape[-1]), axis=0)


def feed_body(width, slots, step, h_ref, c_ref, wg_hbm, wu_hbm, wd_hbm, hidden_ref, gain_ref, block_ref,
              first_ref, second_ref, gain_out, all_ref, act_ref, one_ref, two_ref, c_out, buf, wg, wu, wd, stage, out_ref,
              c_held, here, load, send, recv, side_send, side_recv, store, keep, *sum_refs):
    me = lax.axis_index("wide")
    planes = width // slots
    rows, cols = h_ref.shape
    hidden = wg.shape[1]
    half = rows // 2
    low = jnp.bfloat16
    loads = local_copies([(wg_hbm, wg), (wu_hbm, wu), (wd_hbm, wd)], load)
    mine = pltpu.make_async_copy(h_ref, buf.at[me], here)
    mine.start()
    for copy in loads:
        copy.start()
    hops = Hops(planes, slots, rows)
    hello(wide_peers(width, me) + [{"blk": (hops.plane + k) % planes} for k in range(1, planes)])
    flow = Flow(me, h_ref, lambda who, part: buf.at[who, pl.ds(part * half, half)], half, send, recv)
    sums = Sums(width, me, out_ref, sum_refs)
    outs = (act_ref, one_ref, two_ref)
    pending = [[], []]
    turn_count = [0]
    kept = []

    def where(k):
        who = flip(me, k)
        return pl.multiple_of(((who % slots) * planes + who // slots) * rows, rows)

    def keep_block(k):
        copy = pltpu.make_async_copy(buf.at[flip(me, k)], all_ref.at[pl.ds(where(k), rows)], keep.at[k])
        copy.start()
        kept.append(copy)

    def work(k, part, put, adds=()):
        first, count = (0, rows) if part is None else (part * half, half)
        slot = turn_count[0] % 2
        turn_count[0] += 1
        for copy in pending[slot]:
            copy.wait()
        block = buf.at[flip(me, k), pl.ds(first, count)]
        act, one, two = (stage.at[slot, i, pl.ds(0, count)] for i in range(3))

        def inner(n, carry):
            at = pl.ds(pl.multiple_of(n * step, step), step)
            gate = jnp.dot(block[...], wg[:, at], preferred_element_type=jnp.float32)
            upward = jnp.dot(block[...], wu[:, at], preferred_element_type=jnp.float32)
            sigmoid = jax.nn.sigmoid(gate)
            silu = gate * sigmoid
            act[:, at] = (silu * upward).astype(low)
            one[:, at] = silu.astype(low)
            two[:, at] = (upward * (sigmoid + silu * (1.0 - sigmoid))).astype(low)
            return carry

        lax.fori_loop(0, hidden // step, inner, 0)
        target = pl.ds(pl.multiple_of(where(k) + first, half), count)
        pending[slot] = []
        for i, ref in enumerate(outs):
            copy = pltpu.make_async_copy(stage.at[slot, i, pl.ds(0, count)], ref.at[target], store.at[slot, i])
            copy.start()
            pending[slot].append(copy)
        broad = 2 * step

        def outer(n, carry):
            at = pl.ds(pl.multiple_of(n * broad, broad), broad)
            total = jnp.dot(act[...], wd[:, at], preferred_element_type=jnp.float32)
            for ref in adds:
                total = total + ref[:, at].astype(jnp.float32)
            put[:, at] = total.astype(put.dtype)
            return carry

        lax.fori_loop(0, cols // broad, outer, 0)

    def odd_work(k, part):
        if part is None:
            work(k + 1, None, sums.odd.at[k // 2])
            sums.give(k)
        else:
            work(k + 1, part, sums.odd.at[k // 2, sums.rows(part)])
            sums.twin(k, part).start()

    def even_work(k, part):
        i = k // 2
        if part is None:
            sums.got(k)
            work(k, None, sums.even.at[i - 1], (sums.from_twin.at[i],))
        else:
            sums.twin(k, part).wait_recv()
            at = sums.rows(part)
            work(k, part, sums.even.at[i - 1, at], (sums.from_twin.at[i, at],))

    if width == 8:
        flow.go(None, 2, 2, 0)
        flow.go(None, 4, 4, 1)
        flow.go(None, 1, 1, 0)
        flow.go(None, 1, 1, 1)
        hops.join(c_ref, c_out, side_send, side_recv, True, True)
        mine.wait()
        for copy in loads:
            copy.wait()
        work(0, None, out_ref)
        keep_block(0)
        flow.arrived(1, 0)
        flow.arrived(1, 1)
        keep_block(1)
        odd_work(0, None)
        flow.arrived(2, 0)
        flow.go(2, 4, 6, 0)
        flow.arrived(4, 1)
        flow.go(4, 2, 6, 1)
        flow.go(2, 1, 3, 0)
        flow.go(4, 1, 5, 1)
        flow.go(None, 2, 2, 1)
        flow.go(None, 4, 4, 0)
        flow.arrived(3, 0)
        odd_work(2, 0)
        flow.arrived(5, 1)
        odd_work(4, 1)
        even_work(2, 0)
        even_work(4, 1)
        for part in (0, 1):
            flow.arrived(6, part)
            flow.go(6, 1, 7, part)
        for part in (0, 1):
            flow.arrived(7, part)
        keep_block(6)
        keep_block(7)
        odd_work(6, None)
        even_work(6, None)
        sums.relay(0).start()
        sums.relay(1).start()
        flow.arrived(2, 1)
        flow.go(2, 1, 3, 1)
        flow.arrived(4, 0)
        flow.go(4, 1, 5, 0)
        sums.far(2, 0).start()
        sums.far(4, 1).start()
        flow.arrived(3, 1)
        odd_work(2, 1)
        flow.arrived(5, 0)
        odd_work(4, 0)
        for k in (2, 3, 4, 5):
            keep_block(k)
        even_work(2, 1)
        sums.pass_on(2, 1)
        even_work(4, 0)
        sums.pass_on(4, 0)
    else:
        hops.join(c_ref, c_out, side_send, side_recv, True, True)
        for k in range(2, width, 2):
            flow.go(None, k, k, 0)
            flow.go(None, k, k, 1)
        flow.go(None, 1, 1, 0)
        flow.go(None, 1, 1, 1)
        mine.wait()
        for copy in loads:
            copy.wait()
        work(0, None, out_ref)
        keep_block(0)
        flow.arrived(1, 0)
        flow.arrived(1, 1)
        keep_block(1)
        odd_work(0, None)
        for k in range(2, width, 2):
            for part in (0, 1):
                flow.arrived(k, part)
                flow.go(k, 1, k + 1, part)
            for part in (0, 1):
                flow.arrived(k + 1, part)
            keep_block(k)
            keep_block(k + 1)
            odd_work(k, None)
            even_work(k, None)
            sums.far(k, 0).start()
            sums.far(k, 1).start()
    sums.got(0)
    out_ref[...] = out_ref[...] + sums.from_twin[0].astype(jnp.float32)
    sums.finish()
    flow.finish()
    hops.join(c_ref, c_out, side_send, side_recv, True, False)
    held = pltpu.make_async_copy(c_out, c_held, here)
    held.start()
    held.wait()
    gain_out[...] = jnp.zeros_like(gain_out)
    few = 32
    own = cols // planes
    half_own = own // 2

    def norm(n, carry):
        at = pl.ds(pl.multiple_of(n * few, few), few)
        value = out_ref[at, :]
        inverse = lax.rsqrt(jnp.sum(value * value, axis=-1, keepdims=True) * (1.0 / cols) + EPS)
        normed = value * inverse
        block_ref[at, :] = (hidden_ref[at, :] + normed * gain_ref[...]).astype(low)
        grad = c_held[at, :].astype(jnp.float32)
        gain_out[...] = gain_out[...] + row_sums(grad * normed)
        grad = grad * gain_ref[...]
        mean = jnp.sum(grad * normed, axis=-1, keepdims=True) * (1.0 / cols)
        grad = (inverse * (grad - normed * mean)).astype(low)
        for b in range(planes):
            for side in (0, 1):
                first = b * own + side * half_own
                (first_ref, second_ref)[side][at, b * half_own : (b + 1) * half_own] = grad[:, first : first + half_own]
        return carry

    lax.fori_loop(0, rows // few, norm, 0)
    for copy in kept + pending[0] + pending[1]:
        copy.wait()


def feed(h, side_x, gate_weight, up_weight, down_weight, hidden, gain, width, slots, ident, name):
    rows, cols = h.shape
    inner = gate_weight.shape[1]
    low, f32, dma = h.dtype, jnp.float32, pltpu.SemaphoreType.DMA
    step = min(512, inner)
    anywhere, vmem = pl.BlockSpec(memory_space=pl.ANY), pl.BlockSpec(memory_space=pltpu.VMEM)
    saved = jax.ShapeDtypeStruct((rows * width, inner), low)
    return pl.pallas_call(
        functools.partial(feed_body, width, slots, step),
        out_shape=[
            jax.ShapeDtypeStruct((rows, cols), low), jax.ShapeDtypeStruct((rows, cols // 2), low),
            jax.ShapeDtypeStruct((rows, cols // 2), low),
            jax.ShapeDtypeStruct((8, cols), f32), jax.ShapeDtypeStruct((rows * width, cols), low),
            saved, saved, saved, jax.ShapeDtypeStruct((rows, cols), low),
        ],
        in_specs=[anywhere] * 5 + [vmem] * 2,
        out_specs=[vmem] * 4 + [anywhere] * 5,
        scratch_shapes=[
            pltpu.VMEM((width, rows, cols), low), pltpu.VMEM((cols, inner), low), pltpu.VMEM((cols, inner), low),
            pltpu.VMEM((inner, cols), low), pltpu.VMEM((2, 3, rows, inner), low),
            pltpu.VMEM((rows, cols), f32), pltpu.VMEM((rows, cols), low),
            dma, dma((3,)), dma((width, 2)), dma((width, 2)), dma((width // slots,)), dma((width // slots,)),
            dma((2, 3)), dma((width,)),
        ] + sum_scratch(width, rows, cols),
        cost_estimate=busy(90),
        compiler_params=pltpu.CompilerParams(collective_id=ident, has_side_effects=True, vmem_limit_bytes=VMEM_LIMIT),
        name=name,
    )(h, side_x, gate_weight, up_weight, down_weight, hidden, gain)


def push_body(second, width, slots, *refs):
    if second:
        (g_ref, act_hbm, wd_hbm, one_hbm, two_hbm, first_hbm, down_ref, gg_ref, gu_ref,
         buf, held, acts, here, send, recv, fetch, wd, before, ins, outs, load, take, store) = refs
    else:
        (g_ref, act_hbm, c_ref, down_ref, all_ref, c_out,
         buf, held, acts, here, send, recv, fetch, keep, side_send, side_recv) = refs
    me = lax.axis_index("wide")
    planes = width // slots
    pairs = width // 2
    rows, cols = g_ref.shape
    inner = down_ref.shape[0]
    half = rows // 2
    low = jnp.bfloat16
    mine = pltpu.make_async_copy(g_ref, buf.at[me // 2, me % 2], here)
    mine.start()

    def where(pair, side):
        who = flip(me // 2, pair) * 2 + side
        return pl.ds(pl.multiple_of(((who % slots) * planes + who // slots) * rows, rows), rows)

    def fetches(pair):
        copies = [
            pltpu.make_async_copy(act_hbm.at[where(pair, side)], acts.at[pair % 2, side], fetch.at[pair % 2, side])
            for side in (0, 1)
        ]
        if second:
            copies += [
                pltpu.make_async_copy(ref.at[where(pair, side)], ins.at[pair % 2, i, side], take.at[pair % 2, i, side])
                for i, ref in enumerate((one_hbm, two_hbm))
                for side in (0, 1)
            ]
        return copies

    def stores(pair):
        return [
            pltpu.make_async_copy(outs.at[pair % 2, i, side], ref.at[where(pair, side)], store.at[pair % 2, i, side])
            for i, ref in enumerate((gg_ref, gu_ref))
            for side in (0, 1)
        ]

    def keeps(pair):
        chip = flip(me // 2, pair)
        return pltpu.make_async_copy(buf.at[chip], all_ref.at[chip], keep.at[pair])

    for copy in fetches(0):
        copy.start()
    peers = wide_peers(width, me)
    if second:
        own = cols // planes
        loads = [
            pltpu.make_async_copy(
                wd_hbm.at[:, pl.ds((2 * b + side) * own, own)], wd.at[:, pl.ds(side * cols + b * own, own)],
                load.at[b, side],
            )
            for b in range(planes)
            for side in (0, 1)
        ]
        loads.append(pltpu.make_async_copy(first_hbm, before, load.at[planes, 0]))
        for copy in loads:
            copy.start()
    else:
        hops = Hops(planes, slots, rows)
        peers = peers + [{"blk": (hops.plane + k) % planes} for k in range(1, planes)]
    hello(peers)
    flow = Flow(me, g_ref, lambda who, part: buf.at[who // 2, who % 2, pl.ds(part * half, half)], half, send, recv)

    def work(pair):
        for copy in fetches(pair):
            copy.wait()
        if pair + 1 < pairs:
            for copy in fetches(pair + 1):
                copy.start()
        chip = flip(me // 2, pair)
        slot = pair % 2
        grads = buf[chip].reshape(2 * rows, cols)
        if second:
            if pair >= 2:
                for copy in stores(pair - 2):
                    copy.wait()
            old = before[chip].reshape(2 * rows, cols)
            step = min(512, inner)

            def units(n, carry):
                at = pl.ds(pl.multiple_of(n * step, step), step)
                grad = (nt(old, wd[at, :cols]) + nt(grads, wd[at, cols:])).reshape(2, rows, step)
                outs[slot, 0, :, :, at] = (grad * ins[slot, 1, :, :, at].astype(jnp.float32)).astype(low)
                outs[slot, 1, :, :, at] = (grad * ins[slot, 0, :, :, at].astype(jnp.float32)).astype(low)
                return carry

            lax.fori_loop(0, inner // step, units, 0)
            for copy in stores(pair):
                copy.start()
        else:
            keeps(pair).start()
        tall = min(512, inner)

        def outer(n, carry):
            at = pl.ds(pl.multiple_of(n * tall, tall), tall)
            act = acts[slot, :, :, at].reshape(2 * rows, tall)
            term = lax.dot_general(act, grads, (((0,), (0,)), ((), ())), preferred_element_type=jnp.float32)
            if pair:
                term = term + held[at, :]
            if pair + 1 < pairs:
                held[at, :] = term
            else:
                down_ref[at, :] = term.astype(low)
            return carry

        lax.fori_loop(0, inner // tall, outer, 0)

    def pair_ready(k):
        for part in (0, 1):
            flow.arrived(k + 1, part)

    if width == 8:
        flow.go(None, 2, 2, 0)
        flow.go(None, 4, 4, 1)
        flow.go(None, 2, 2, 1)
        flow.go(None, 4, 4, 0)
    else:
        for k in range(2, width, 2):
            flow.go(None, k, k, 0)
            flow.go(None, k, k, 1)
    flow.go(None, 1, 1, 0)
    flow.go(None, 1, 1, 1)
    if second:
        for copy in loads:
            copy.wait()
    else:
        hops.spread(c_ref, c_out, side_send, side_recv, True, True)
    mine.wait()
    pair_ready(0)
    work(0)
    if width == 8:
        flow.arrived(2, 0)
        flow.go(2, 4, 6, 0)
        flow.go(2, 1, 3, 0)
        flow.arrived(4, 1)
        flow.go(4, 2, 6, 1)
        flow.go(4, 1, 5, 1)
        flow.arrived(2, 1)
        flow.go(2, 1, 3, 1)
        flow.arrived(4, 0)
        flow.go(4, 1, 5, 0)
        pair_ready(2)
        work(1)
        pair_ready(4)
        work(2)
        for part in (0, 1):
            flow.arrived(6, part)
            flow.go(6, 1, 7, part)
        pair_ready(6)
        work(3)
    else:
        for k in range(2, width, 2):
            for part in (0, 1):
                flow.arrived(k, part)
                flow.go(k, 1, k + 1, part)
            pair_ready(k)
            work(k // 2)
    flow.finish()
    if second:
        for pair in (pairs - 2, pairs - 1):
            for copy in stores(pair):
                copy.wait()
    else:
        for pair in range(pairs):
            keeps(pair).wait()
        hops.spread(c_ref, c_out, side_send, side_recv, True, False)


def push(second, g, act, width, slots, ident, name, others):
    rows, cols = g.shape
    inner = act.shape[1]
    low, dma = g.dtype, pltpu.SemaphoreType.DMA
    planes, pairs = width // slots, width // 2
    anywhere, vmem = pl.BlockSpec(memory_space=pl.ANY), pl.BlockSpec(memory_space=pltpu.VMEM)
    blocks = (pairs, 2, rows, cols)
    scratch = [
        pltpu.VMEM(blocks, low), pltpu.VMEM((inner, cols), jnp.float32), pltpu.VMEM((2, 2, rows, inner), low),
        dma, dma((width, 2)), dma((width, 2)), dma((2, 2)),
    ]
    shapes = [jax.ShapeDtypeStruct((inner, cols), low)]
    if second:
        saved = jax.ShapeDtypeStruct((rows * width, inner), low)
        shapes += [saved, saved]
        scratch += [
            pltpu.VMEM((inner, 2 * cols), low), pltpu.VMEM(blocks, low), pltpu.VMEM((2, 2, 2, rows, inner), low),
            pltpu.VMEM((2, 2, 2, rows, inner), low), dma((planes + 1, 2)), dma((2, 2, 2)), dma((2, 2, 2)),
        ]
    else:
        shapes += [
            jax.ShapeDtypeStruct(blocks, low),
            jax.ShapeDtypeStruct((many_rows(planes, rows), others[0].shape[1]), low),
        ]
        scratch += [dma((pairs,)), dma((planes,)), dma((planes,))]
    inputs = [g, act] + others
    return pl.pallas_call(
        functools.partial(push_body, second, width, slots),
        out_shape=shapes,
        in_specs=[anywhere] * len(inputs),
        out_specs=[vmem] + [anywhere] * (len(shapes) - 1),
        scratch_shapes=scratch,
        cost_estimate=busy(10),
        compiler_params=pltpu.CompilerParams(collective_id=ident, has_side_effects=True, vmem_limit_bytes=VMEM_LIMIT),
        name=name,
    )(*inputs)


def pull_body(width, slots, step, chunk, gg_hbm, gu_hbm, wg_hbm, wu_hbm, h_hbm, c_ref, normed_ref, inv_ref, gain_ref,
              out_ref, proj_ref, gain_out, du_hbm, gg, gu, wg, wu, columns, tiles, load, take, fetch, store, *sum_refs):
    me = lax.axis_index("wide")
    planes = width // slots
    rows, cols = out_ref.shape
    half = rows // 2
    chunks = cols // chunk
    loads = local_copies([(wg_hbm, wg), (wu_hbm, wu)], load)
    for copy in loads:
        copy.start()

    def where(k, first, count):
        who = flip(me, k)
        start = ((who % slots) * planes + who // slots) * rows + first
        return pl.ds(pl.multiple_of(start, half), count)

    def takes(k):
        at = where(k, 0, rows)
        return [
            pltpu.make_async_copy(src.at[at], dst.at[at], take.at[k, i])
            for i, (src, dst) in enumerate(((gg_hbm, gg), (gu_hbm, gu)))
        ]

    order = [7, 6, 3, 5, 2, 4, 1, 0] if width == 8 else [k ^ 1 for k in range(width)]
    for k in order:
        for copy in takes(k):
            copy.start()
    taken = []

    def need(k):
        if k not in taken:
            taken.append(k)
            for copy in takes(k):
                copy.wait()

    def fetched(n):
        at = pl.ds(pl.multiple_of(n * chunk, chunk), chunk)
        return pltpu.make_async_copy(h_hbm.at[:, at], columns.at[n % 2], fetch.at[n % 2])

    def stored(n):
        at = pl.ds(pl.multiple_of(n * chunk, chunk), chunk)
        return [
            pltpu.make_async_copy(tiles.at[n % 2, i], ref.at[at], store.at[n % 2, i])
            for i, ref in enumerate((du_hbm,))
        ]

    fetched(0).start()
    hello(wide_peers(width, me))
    sums = Sums(width, me, out_ref, sum_refs)

    def produce(k, first, count, put, adds=()):
        need(k)
        at_rows = where(k, first, count)

        def tile(n, carry):
            at = pl.ds(pl.multiple_of(n * step, step), step)
            total = nt(gg[at_rows, :], wg[at, :]) + nt(gu[at_rows, :], wu[at, :])
            for ref in adds:
                total = total + ref[:, at].astype(jnp.float32)
            put[:, at] = total.astype(put.dtype)
            return carry

        lax.fori_loop(0, cols // step, tile, 0)

    def grads(first, last):
        for k in order:
            need(k)

        def one_chunk(n, carry):
            fetched(n).wait()

            @pl.when(n + 1 < chunks)
            def _():
                fetched(n + 1).start()

            @pl.when(n >= 2)
            def _():
                for copy in stored(n - 2):
                    copy.wait()

            for i, ref in enumerate((gu,)):
                tiles[n % 2, i] = lax.dot_general(
                    columns[n % 2], ref[...], (((0,), (0,)), ((), ())), preferred_element_type=jnp.float32
                ).astype(jnp.bfloat16)
            for copy in stored(n):
                copy.start()
            return carry

        lax.fori_loop(first, last, one_chunk, 0)

    for copy in loads:
        copy.wait()
    run_sums(width, sums, produce, grads, chunks)
    gain_out[...] = jnp.zeros_like(gain_out)
    few = 32

    def norm(n, carry):
        at = pl.ds(pl.multiple_of(n * few, few), few)
        grad = out_ref[at, :] + c_ref[at, :].astype(jnp.float32)
        out_ref[at, :] = grad
        normed = normed_ref[at, :]
        gain_out[...] = gain_out[...] + row_sums(grad * normed)
        grad = grad * gain_ref[...]
        mean = jnp.sum(grad * normed, axis=-1, keepdims=True) * (1.0 / cols)
        proj_ref[at, :] = (inv_ref[at, :] * (grad - normed * mean)).astype(jnp.bfloat16)
        return carry

    lax.fori_loop(0, rows // few, norm, 0)
    for copy in stored(chunks - 2) + stored(chunks - 1):
        copy.wait()


def pull(grad_gate, grad_up, gate_weight, up_weight, gathered, grad_out, normed, inverse, gain, width, slots, ident, name):
    count, cols = gathered.shape
    inner = gate_weight.shape[1]
    rows = count // width
    low, f32, dma = gathered.dtype, jnp.float32, pltpu.SemaphoreType.DMA
    chunk = 256
    anywhere, vmem = pl.BlockSpec(memory_space=pl.ANY), pl.BlockSpec(memory_space=pltpu.VMEM)
    return pl.pallas_call(
        functools.partial(pull_body, width, slots, 1024, chunk),
        out_shape=[
            jax.ShapeDtypeStruct((rows, cols), f32), jax.ShapeDtypeStruct((rows, cols), low),
            jax.ShapeDtypeStruct((8, cols), f32), jax.ShapeDtypeStruct((cols, inner), low),
        ],
        in_specs=[anywhere] * 5 + [vmem] * 4,
        out_specs=[vmem] * 3 + [anywhere],
        scratch_shapes=[
            pltpu.VMEM((count, inner), low), pltpu.VMEM((count, inner), low),
            pltpu.VMEM((cols, inner), low), pltpu.VMEM((cols, inner), low),
            pltpu.VMEM((2, count, chunk), low), pltpu.VMEM((2, 1, chunk, inner), low),
            dma((2,)), dma((width, 2)), dma((2,)), dma((2, 1)),
        ] + sum_scratch(width, rows, cols),
        cost_estimate=busy(10),
        compiler_params=pltpu.CompilerParams(collective_id=ident, has_side_effects=True, vmem_limit_bytes=VMEM_LIMIT),
        name=name,
    )(grad_gate, grad_up, gate_weight, up_weight, gathered, grad_out, normed, inverse, gain)


def side_body(x_ref, p_ref, g_ref, m_ref, out_ref):
    dims = (((0,), (0,)), ((), ()))
    split = g_ref.shape[1]
    out_ref[:, :split] = lax.dot_general(
        x_ref[...], g_ref[...], dims, preferred_element_type=jnp.float32
    ).astype(out_ref.dtype)
    out_ref[:, split:] = lax.dot_general(
        p_ref[...], m_ref[...], dims, preferred_element_type=jnp.float32
    ).astype(out_ref.dtype)


def side_grads(inputs, grad_proj, grads, mixed):
    count, cols = inputs.shape
    extent = grads.shape[1] + mixed.shape[1]
    chunk = 256
    return pl.pallas_call(
        side_body,
        grid=(cols // chunk,),
        out_shape=jax.ShapeDtypeStruct((cols, extent), inputs.dtype),
        in_specs=[
            pl.BlockSpec((count, chunk), lambda n: (0, n)), pl.BlockSpec((count, chunk), lambda n: (0, n)),
            pl.BlockSpec(grads.shape, lambda n: (0, 0)), pl.BlockSpec(mixed.shape, lambda n: (0, 0)),
        ],
        out_specs=pl.BlockSpec((chunk, extent), lambda n: (n, 0)),
        compiler_params=pltpu.CompilerParams(vmem_limit_bytes=VMEM_LIMIT),
        cost_estimate=busy(10),
        name="side_grads",
    )(inputs, grad_proj, grads, mixed)


def local(
    tokens,
    lengths,
    query_weight,
    key_weight,
    value_weight,
    output_weight,
    query_gain,
    key_gain,
    attention_gain,
    gate_weight,
    up_weight,
    down_weight,
    feedforward_gain,
    cotangent,
):
    low, f32 = jnp.bfloat16, jnp.float32
    planes, width = lax.axis_size("blk"), lax.axis_size("wide")
    slots = width // planes
    rows = tokens.shape[1]
    span = rows * planes
    count = slots * span
    share = query_weight.shape[1]
    heads = share // HD
    plane, place = lax.axis_index("blk"), lax.axis_index("wide")
    after = lambda value, *others: lax.optimization_barrier((value,) + others)[0]

    def sum_blk(value, axis):
        return lax.psum_scatter(value, "blk", scatter_dimension=axis, tiled=True)

    _, near_cotangent, mine = turn(
        turn_in_body, [tokens[0], cotangent[0]], [True, True, False], planes, slots, 1, "turn_in"
    )
    w_qkv = after(jnp.concatenate([query_weight, key_weight, value_weight], 1), mine)
    w_qkv = lax.all_gather(w_qkv, "blk", axis=0, tiled=True)
    gains = jnp.stack([query_gain, key_gain]).astype(f32)
    plane_lengths = lax.dynamic_slice_in_dim(lengths, plane * slots, slots, 0)
    segment, position = jax.vmap(lambda one: layout(one, span))(plane_lengths)
    begin = (jnp.arange(span, dtype=jnp.int32)[None] - position)[:, None, :]
    pairs, piece = piece_map(span, rows)
    order = sorted(pairs, key=lambda pair: pair[1])
    index = np.concatenate([np.arange(at, at + piece) for at, _ in order])
    starts = jnp.stack([plane_lengths[:, 0] * 0, plane_lengths[:, 0], plane_lengths[:, 0] + plane_lengths[:, 1]], 1)
    cos_a, sin_a, cos_b, sin_b, sign = rope_tables(index, starts)
    group = jnp.concatenate([segment[:, at : at + piece] for at, _ in order], 1)[..., None]
    pick = lambda table: jnp.where(
        group == 0, table[:, 0:1], jnp.where(group == 1, table[:, 1:2], table[:, 2:3])
    )
    cos_b, sin_b = pick(cos_b), pick(sin_b)
    cosine = cos_a * cos_b + sin_a * sin_b
    sine = (sin_a * cos_b - cos_a * sin_b) * sign

    inputs = gather(mine, width, slots, 2, "gather_tokens")
    pre = dot(inputs, w_qkv)
    squares = jnp.stack([jnp.sum(pre[:, a * share : (a + 1) * share] ** 2, -1) for a in (0, 1)])
    both = lax.dynamic_update_slice(
        jnp.zeros((2, D), f32), jnp.stack([attention_gain, feedforward_gain]).astype(f32), (0, place * share)
    )
    squares = jnp.concatenate([squares.reshape(-1, 128), both.reshape(-1, 128)])
    squares = total(squares, "wide", width, 3, "total_squares")
    both = squares[2 * count // 128 :].reshape(2, D)
    gain_mix, gain_feed = both[0], both[1]
    inverse = lax.rsqrt(squares[: 2 * count // 128].reshape(2, count) / D + EPS)
    inv_cols = inverse.T.reshape(slots, span, 2)
    w_o = lax.all_gather(after(output_weight, w_qkv), "blk", axis=1, tiled=True)
    pre_groups = pre.reshape(slots, span, 3 * share)
    queries, keys, values, mixed, logs = attend(
        pre_groups, inv_cols, gains, cosine, sine, begin, heads, rows
    )
    mixed = mixed.reshape(count, share)
    hidden, hidden_low, proj_normed, proj_inv = scatter(
        [mixed], [w_o], width, slots, False, 4, "scatter_mixed", "norm", (mine, gain_mix[None])
    )
    block_output, first_half, second_half, feed_gain_part, gathered, activated, up_factor, gate_factor, grad_out = feed(
        hidden_low, near_cotangent, gate_weight, up_weight, down_weight, hidden, gain_feed[None], width, slots, 5,
        "feed",
    )
    down_first, first_rows, far_output = push(
        False, first_half, activated, width, slots, 6, "push_first", [block_output]
    )
    down_first = sum_blk(down_first, 1)
    down_second, grad_gate, grad_up = push(
        True, second_half, activated, width, slots, 7, "push_second",
        [down_weight, up_factor, gate_factor, first_rows],
    )
    down_second = sum_blk(down_second, 1)
    gate_part = contract_rows(gathered, grad_gate).astype(low)
    gate_grad = sum_blk(gate_part, 0)
    grad_hidden, grad_proj, mix_gain_part, up_part = pull(
        after(grad_gate, gate_part, down_first), grad_up, gate_weight, up_weight, gathered, grad_out, proj_normed,
        proj_inv, gain_mix[None], width, slots, 8, "pull",
    )
    up_grad = sum_blk(up_part, 0)
    grad_proj = gather(grad_proj, width, slots, 9, "gather_proj")
    grad_mixed = contract_cols(after(grad_proj, down_first, down_second), w_o).astype(low).reshape(slots, span, share)
    scaled_q, scaled_k, grad_v, sums, parts = attend_back(
        queries, keys, values, grad_mixed, logs, pre_groups, inv_cols, gains, cosine, sine, begin,
        heads, rows,
    )
    means = jnp.sum(sums, axis=0).reshape(count, 2).T.reshape(-1, 128)
    local_gains = lax.dynamic_update_slice(
        jnp.zeros((2, D), f32), jnp.sum(parts, axis=0), (0, place * share)
    )
    gain_parts = jnp.concatenate([local_gains, jnp.stack([mix_gain_part.sum(0), feed_gain_part.sum(0)])])
    means = jnp.concatenate([means, gain_parts.reshape(-1, 128)])
    means = total(after(means, gate_grad), "wide", width, 10, "total_means")
    gain_parts = means[2 * count // 128 :]
    means = means[: 2 * count // 128].reshape(2, count) / D

    def finish(scaled, index):
        normed = pre[:, index * share : (index + 1) * share] * inverse[index][:, None]
        scaled = scaled.reshape(count, share)
        return (inverse[index][:, None] * (scaled - normed * means[index][:, None])).astype(low)

    grads = jnp.concatenate([finish(scaled_q, 0), finish(scaled_k, 1), grad_v.reshape(count, share)], 1)
    side_part = side_grads(inputs, grad_proj, grads, mixed)
    tokens_low = scatter(
        [grads], [w_qkv], width, slots, True, 11, "scatter_tokens", "add", (grad_hidden,)
    )
    down_grad = jnp.concatenate([down_first, down_second], 1).astype(f32)
    gate_grad, up_grad = gate_grad.astype(f32), up_grad.astype(f32)
    tokens_low, down_grad, gate_grad, up_grad = lax.optimization_barrier((tokens_low, down_grad, gate_grad, up_grad))
    _, block_output, tokens_grad, gain_sums = turn(
        turn_out_body, [tokens_low, far_output], [True, False, False],
        planes, slots, 14, "turn_out", gain_parts,
    )
    side_grad = sum_blk(side_part, 0).astype(f32)

    sums = gain_sums.reshape(4, D)
    portion = D // (planes * width)
    sums = lax.dynamic_slice_in_dim(sums, (plane * width + place) * portion, portion, 1)
    return (
        block_output[None],
        tokens_grad[None].astype(f32),
        side_grad[:, :share],
        side_grad[:, share : 2 * share],
        side_grad[:, 2 * share : 3 * share],
        side_grad[:, 3 * share :].T,
        sums[0],
        sums[1],
        sums[2],
        gate_grad,
        up_grad,
        down_grad,
        sums[3],
    )


def solution(mesh):
    placed = (
        P("wide", "blk", None),
        P(),
        P("blk", "wide"),
        P("blk", "wide"),
        P("blk", "wide"),
        P("wide", "blk"),
        P("wide"),
        P("wide"),
        P("wide"),
        P(None, "wide"),
        P(None, "wide"),
        P("wide", None),
        P("wide"),
        P("wide", "blk", None),
    )
    return jax.shard_map(
        local,
        mesh=mesh,
        in_specs=placed,
        out_specs=(
            P("wide", "blk", None),
            P("wide", "blk", None),
            P("blk", "wide"),
            P("blk", "wide"),
            P("blk", "wide"),
            P("wide", "blk"),
            P(("blk", "wide")),
            P(("blk", "wide")),
            P(("blk", "wide")),
            P("blk", "wide"),
            P("blk", "wide"),
            P("wide", "blk"),
            P(("blk", "wide")),
        ),
        check_vma=False,
    )
```

```python
import functools

import jax
import jax.numpy as jnp
import numpy as np
from jax import lax
from jax.experimental import pallas as pl
from jax.experimental.pallas import tpu as pltpu
from jax.sharding import PartitionSpec as P

MESH = pl.DeviceIdType.MESH

D = 2048
HD = 128
EPS = 1e-06
ROPE_BASE = 500000.0
NEG_FILL = -1e30
VMEM_LIMIT = 60 * 1024 * 1024
SCALE = HD ** (-0.5)


def busy(micros):
    return pl.CostEstimate(flops=0, bytes_accessed=int(micros * 3.5e6), transcendentals=0)


def layout(seq_lengths, row_count):
    indices = jnp.arange(row_count, dtype=jnp.int32)
    first_end = seq_lengths[0]
    second_end = seq_lengths[0] + seq_lengths[1]
    segment = (indices >= first_end).astype(jnp.int32) + (indices >= second_end).astype(jnp.int32)
    offsets = jnp.where(segment == 0, 0, jnp.where(segment == 1, first_end, second_end))
    return (segment, indices - offsets)


def rope_tables(index, begin):
    frequency = ROPE_BASE ** (-np.arange(0, HD, 2, dtype=np.float64) / HD)
    angles = np.asarray(index, np.float64)[:, None] * frequency
    sign = np.concatenate([-np.ones(HD // 2), np.ones(HD // 2)])
    twice = lambda value: np.concatenate([value, value], -1).astype(np.float32)
    cosine, sine = jnp.asarray(twice(np.cos(angles))), jnp.asarray(twice(np.sin(angles)))
    shift = begin.astype(jnp.float32)[..., None] * jnp.asarray(twice(frequency))
    return cosine, sine, jnp.cos(shift), jnp.sin(shift), jnp.asarray(sign.astype(np.float32))


def rms_pair(values):
    inverse = lax.rsqrt(jnp.mean(values * values, axis=-1, keepdims=True) + EPS)
    return (values * inverse, inverse)


def norm_back(normed, inverse, grad_normed):
    return inverse * (grad_normed - normed * jnp.mean(grad_normed * normed, axis=-1, keepdims=True))


def dot(left, right):
    return jnp.dot(left, right, preferred_element_type=jnp.float32)


def contract_rows(left, right):
    return lax.dot_general(
        left, right, (((0,), (0,)), ((), ())), preferred_element_type=jnp.float32
    )


def contract_cols(left, right):
    return lax.dot_general(
        left, right, (((1,), (1,)), ((), ())), preferred_element_type=jnp.float32
    )


def flip(me, k):
    out, bit = me, 1
    while bit <= k:
        if k & bit:
            out = out + bit * (1 - 2 * ((me // bit) % 2))
        bit *= 2
    return out


def greet(axis, me, others):
    barrier = pltpu.get_barrier_semaphore()
    for k in others:
        pl.semaphore_signal(barrier, inc=1, device_id={axis: flip(me, k)}, device_id_type=MESH)
    pl.semaphore_wait(barrier, len(others))


class Flow:
    def __init__(self, me, source, spot, half, send, recv):
        self.me, self.source, self.spot, self.half = me, source, spot, half
        self.send, self.recv, self.moves = send, recv, []

    def go(self, origin, target, k, part):
        if origin is None:
            source = self.source.at[pl.ds(part * self.half, self.half)]
        else:
            source = self.spot(flip(self.me, origin), part)
        copy = pltpu.make_async_remote_copy(
            src_ref=source,
            dst_ref=self.spot(flip(flip(self.me, target), k), part),
            send_sem=self.send.at[k, part],
            recv_sem=self.recv.at[k, part],
            device_id={"wide": flip(self.me, target)},
            device_id_type=MESH,
        )
        copy.start()
        self.moves.append(copy)

    def arrived(self, k, part):
        block = self.spot(flip(self.me, k), part)
        pltpu.make_async_copy(block, block, self.recv.at[k, part]).wait()

    def finish(self):
        for copy in self.moves:
            copy.wait_send()


class Sums:
    def __init__(self, width, me, out_ref, refs):
        self.width, self.me, self.out = width, me, out_ref
        (self.odd, self.even, self.from_twin, self.from_far, self.passing, self.sends, self.recvs,
         self.pass_send, self.pass_recv, self.twin_send, self.twin_recv) = refs
        self.half = out_ref.shape[0] // 2

    def rows(self, part):
        return pl.ds(part * self.half, self.half)

    def copy(self, src, dst, send, recv, k):
        return pltpu.make_async_remote_copy(
            src_ref=src, dst_ref=dst, send_sem=send, recv_sem=recv,
            device_id={"wide": flip(self.me, k)}, device_id_type=MESH,
        )

    def twin(self, k, part):
        i, at = k // 2, self.rows(part)
        return self.copy(
            self.odd.at[i, at], self.from_twin.at[i, at], self.twin_send.at[i, part],
            self.twin_recv.at[i, part], 1,
        )

    def far(self, k, part):
        i, at = k // 2 - 1, self.rows(part)
        return self.copy(
            self.even.at[i, at], self.from_far.at[i, at], self.sends.at[i, part], self.recvs.at[i, part], k
        )

    def relay(self, part):
        return self.copy(
            self.even.at[2, self.rows(part)], self.passing.at[part], self.pass_send.at[part],
            self.pass_recv.at[part], 2 if part == 0 else 4,
        )

    def give(self, k):
        self.twin(k, 0).start()
        self.twin(k, 1).start()

    def got(self, k):
        self.twin(k, 0).wait_recv()
        self.twin(k, 1).wait_recv()

    def pass_on(self, k, part):
        self.relay(part).wait_recv()
        at = self.rows(part)
        self.even[k // 2 - 1, at, :] = (
            self.even[k // 2 - 1, at, :].astype(jnp.float32) + self.passing[part].astype(jnp.float32)
        ).astype(jnp.bfloat16)
        self.far(k, part).start()

    def finish(self):
        sources = [2, 4] if self.width == 8 else list(range(2, self.width, 2))
        for k in sources:
            for part in (0, 1):
                self.far(k, part).wait_recv()
        extra = self.from_far[sources[0] // 2 - 1].astype(jnp.float32)
        for k in sources[1:]:
            extra = extra + self.from_far[k // 2 - 1].astype(jnp.float32)
        self.out[...] = self.out[...] + extra
        for part in (0, 1):
            for k in sources:
                self.far(k, part).wait_send()
            for k in range(0, self.width, 2):
                self.twin(k, part).wait_send()
            if self.width == 8:
                self.relay(part).wait_send()


def run_sums(width, sums, produce, beside=None, steps=0):
    half = sums.half
    rows = 2 * half

    def give(k, part=None):
        if part is None:
            produce(k + 1, 0, rows, sums.odd.at[k // 2])
            sums.give(k)
        else:
            produce(k + 1, part * half, half, sums.odd.at[k // 2, sums.rows(part)])
            sums.twin(k, part).start()

    def merge(k, part=None):
        if part is None:
            sums.got(k)
            produce(k, 0, rows, sums.even.at[k // 2 - 1], (sums.from_twin.at[k // 2],))
        else:
            sums.twin(k, part).wait_recv()
            at = sums.rows(part)
            produce(k, part * half, half, sums.even.at[k // 2 - 1, at], (sums.from_twin.at[k // 2, at],))

    if width == 8:
        give(6, 0)
        give(6, 1)
        merge(6, 0)
        sums.relay(0).start()
        merge(6, 1)
        sums.relay(1).start()
        give(2)
        give(4)
        merge(2)
        sums.far(2, 0).start()
        merge(4)
        sums.far(4, 1).start()
        sums.pass_on(2, 1)
        sums.pass_on(4, 0)
        give(0)
    else:
        for k in range(0, width, 2):
            give(k)
        for k in range(2, width, 2):
            merge(k)
            sums.far(k, 0).start()
            sums.far(k, 1).start()
    if beside is not None:
        beside(0, steps)
    sums.got(0)
    produce(0, 0, rows, sums.out, (sums.from_twin.at[0],))
    sums.finish()


def sum_scratch(width, rows, cols):
    chips, dma = width // 2, pltpu.SemaphoreType.DMA
    block = lambda n: pltpu.VMEM((n, rows, cols), jnp.bfloat16)
    return [
        block(chips), block(chips - 1), block(chips), block(2 if width == 8 else chips - 1),
        pltpu.VMEM((2, rows // 2, cols), jnp.bfloat16),
        dma((chips - 1, 2)), dma((chips - 1, 2)), dma((2,)), dma((2,)), dma((chips, 2)), dma((chips, 2)),
    ]


def wide_peers(width, me):
    return [{"wide": flip(me, k)} for k in [1] + list(range(2, width, 2))]


def local_copies(pairs, sem):
    return [pltpu.make_async_copy(src, dst, sem.at[i]) for i, (src, dst) in enumerate(pairs)]


def gather_body(width, slots, weights, *refs):
    if weights:
        x_ref, w_ref, lower_ref, upper_ref, out_ref, w_out, here, send, recv, keep, w_send, w_recv = refs
    else:
        x_ref, out_ref, here, send, recv = refs
    me = lax.axis_index("wide")
    planes = width // slots
    rows = x_ref.shape[0]
    half = rows // 2
    peers = wide_peers(width, me)
    if weights:
        plane = lax.axis_index("blk")
        extent = w_ref.shape[0]
        peers = peers + [{"blk": (plane + k) % planes} for k in range(1, planes)]

        def shard(which):
            return w_out.at[pl.ds(pl.multiple_of(which * extent, extent), extent)]

        def pass_on(step, far):
            way = 0 if step > 0 else 1
            origin = plane - step * far
            source = shard(origin) if far > 1 else (lower_ref, upper_ref)[way]
            return pltpu.make_async_remote_copy(
                src_ref=source, dst_ref=shard(origin), send_sem=w_send.at[way, far], recv_sem=w_recv.at[way, far + 1],
                device_id={"blk": plane + step}, device_id_type=MESH,
            )

        def between(step, far, action):
            first, last = plane - step * far, plane + step
            fits = (first >= 0) & (first < planes) & (last >= 0) & (last < planes)
            pl.when(fits)(action)

        def landed(step, far):
            way = 0 if step > 0 else 1
            block = shard(plane - step * far)
            copy = pltpu.make_async_copy(block, block, w_recv.at[way, far])
            beyond(plane, planes, -step * far, copy.wait)

        keeps = [
            (0, pltpu.make_async_copy(w_ref, shard(plane), keep.at[0])),
            (-1, pltpu.make_async_copy(lower_ref, shard(plane - 1), keep.at[1])),
            (1, pltpu.make_async_copy(upper_ref, shard(plane + 1), keep.at[2])),
        ]
    hello(peers)
    if weights:
        for step in (1, -1):
            between(step, 1, lambda step=step: pass_on(step, 1).start())

    def spot(who, part):
        base = ((who % slots) * planes + who // slots) * rows + part * half
        return out_ref.at[pl.ds(pl.multiple_of(base, half), half)]

    flow = Flow(me, x_ref, spot, half, send, recv)
    mine = [
        pltpu.make_async_copy(x_ref.at[pl.ds(part * half, half)], spot(me, part), here.at[part]) for part in (0, 1)
    ]
    for copy in mine:
        copy.start()

    def relay_weights(far):
        if weights and far < planes:
            for step in (1, -1):
                landed(step, far)
                between(step, far, lambda step=step: pass_on(step, far).start())

    if width == 8:
        flow.go(None, 2, 2, 0)
        flow.go(None, 4, 4, 1)
        flow.go(None, 2, 2, 1)
        flow.go(None, 4, 4, 0)
        flow.go(None, 1, 1, 0)
        flow.go(None, 1, 1, 1)
        if weights:
            for step, copy in keeps:
                beyond(plane, planes, step, copy.start)
        flow.arrived(2, 0)
        flow.go(2, 4, 6, 0)
        flow.go(2, 1, 3, 0)
        flow.arrived(4, 1)
        flow.go(4, 2, 6, 1)
        flow.go(4, 1, 5, 1)
        relay_weights(2)
        order = [(2, 1), (4, 0), (6, 0), (6, 1)]
    else:
        for k in range(2, width, 2):
            flow.go(None, k, k, 0)
            flow.go(None, k, k, 1)
        flow.go(None, 1, 1, 0)
        flow.go(None, 1, 1, 1)
        if weights:
            for step, copy in keeps:
                beyond(plane, planes, step, copy.start)
        relay_weights(2)
        order = [(k, part) for k in range(2, width, 2) for part in (0, 1)]
    for k, part in order:
        flow.arrived(k, part)
        flow.go(k, 1, k + 1, part)
    for far in range(3, planes):
        relay_weights(far)
    for k in range(1, width, 2):
        for part in (0, 1):
            flow.arrived(k, part)
    flow.finish()
    for copy in mine:
        copy.wait()
    if weights:
        for step, copy in keeps:
            beyond(plane, planes, step, copy.wait)
        for far in range(1, planes - 1):
            for step in (1, -1):
                between(step, far, lambda step=step, far=far: pass_on(step, far).wait_send())


def gather(x, width, slots, ident, name, weights=()):
    rows, cols = x.shape
    planes = width // slots
    dma = pltpu.SemaphoreType.DMA
    shapes = [jax.ShapeDtypeStruct((rows * width, cols), x.dtype)]
    scratch = [dma((2,)), dma((width, 2)), dma((width, 2))]
    if weights:
        extent, share = weights[0].shape
        shapes.append(jax.ShapeDtypeStruct((planes * extent, share), x.dtype))
        scratch += [dma((3,)), dma((2, planes + 1)), dma((2, planes + 1))]
    anywhere = pl.BlockSpec(memory_space=pl.ANY)
    outs = pl.pallas_call(
        functools.partial(gather_body, width, slots, bool(weights)),
        out_shape=shapes,
        in_specs=[anywhere] * (1 + len(weights)),
        out_specs=[anywhere] * len(shapes),
        scratch_shapes=scratch,
        cost_estimate=busy(10),
        compiler_params=pltpu.CompilerParams(collective_id=ident, has_side_effects=True, vmem_limit_bytes=VMEM_LIMIT),
        name=name,
    )(x, *weights)
    return outs if weights else outs[0]


def scatter_body(width, slots, flat, count, step, finish, *refs):
    lefts, rights = refs[:count], refs[count : 2 * count]
    if finish == "norm":
        x_ref, gain_ref, hidden_ref, low_ref, out_ref, inv_ref = refs[2 * count : 2 * count + 6]
        rest = refs[2 * count + 6 :]
    else:
        more_ref, low_ref, out_ref = refs[2 * count : 2 * count + 3]
        rest = refs[2 * count + 3 :]
    me = lax.axis_index("wide")
    rows, cols = out_ref.shape
    hello(wide_peers(width, me))
    sums = Sums(width, me, out_ref, rest)
    dims = (((1,), (1 if flat else 0,)), ((), ()))

    def produce(k, first, some, put, adds=()):
        who = flip(me, k)
        start = ((who % slots) * (width // slots) + who // slots) * rows + first
        start = pl.multiple_of(start, rows // 2)

        def tile(n, carry):
            at = pl.ds(pl.multiple_of(n * step, step), step)
            total = None
            for left, right in zip(lefts, rights):
                other = right[at, :] if flat else right[:, at]
                term = lax.dot_general(
                    left[pl.ds(start, some), :], other, dims, preferred_element_type=jnp.float32
                )
                total = term if total is None else total + term
            for ref in adds:
                total = total + ref[:, at].astype(jnp.float32)
            put[:, at] = total.astype(put.dtype)
            return carry

        lax.fori_loop(0, cols // step, tile, 0)

    run_sums(width, sums, produce)
    if finish == "add":
        def close(n, carry):
            at = pl.ds(pl.multiple_of(n * 32, 32), 32)
            low_ref[at, :] = (out_ref[at, :] + more_ref[at, :]).astype(low_ref.dtype)
            return carry

        lax.fori_loop(0, rows // 32, close, 0)
    if finish != "norm":
        return
    few = 32

    def norm(n, carry):
        at = pl.ds(pl.multiple_of(n * few, few), few)
        value = out_ref[at, :]
        inverse = lax.rsqrt(jnp.sum(value * value, axis=-1, keepdims=True) * (1.0 / cols) + EPS)
        value = value * inverse
        out_ref[at, :] = value
        inv_ref[at, :] = inverse
        hidden = x_ref[at, :].astype(jnp.float32) + value * gain_ref[...]
        hidden_ref[at, :] = hidden
        low_ref[at, :] = hidden.astype(low_ref.dtype)
        return carry

    lax.fori_loop(0, rows // few, norm, 0)


def scatter(lefts, rights, width, slots, flat, ident, name, finish, more, step=1024):
    rows = lefts[0].shape[0] // width
    cols = rights[0].shape[0 if flat else 1]
    f32, vmem = jnp.float32, pl.BlockSpec(memory_space=pltpu.VMEM)
    whole, low = jax.ShapeDtypeStruct((rows, cols), f32), jax.ShapeDtypeStruct((rows, cols), lefts[0].dtype)
    shapes = [whole, low, whole, jax.ShapeDtypeStruct((rows, 1), f32)] if finish == "norm" else [low]
    scratch = sum_scratch(width, rows, cols)
    if finish == "add":
        scratch = [pltpu.VMEM((rows, cols), f32)] + scratch
    outs = pl.pallas_call(
        functools.partial(scatter_body, width, slots, flat, len(lefts), step, finish),
        out_shape=shapes,
        in_specs=[vmem] * (2 * len(lefts) + len(more)),
        out_specs=[vmem] * len(shapes),
        scratch_shapes=scratch,
        cost_estimate=busy(10),
        compiler_params=pltpu.CompilerParams(collective_id=ident, has_side_effects=True, vmem_limit_bytes=VMEM_LIMIT),
        name=name,
    )(*lefts, *rights, *more)
    return outs if finish == "norm" else outs[0]


def total_body(axis, width, x_ref, out_ref, slots, send, recv):
    me = lax.axis_index(axis)
    others = list(range(1, width))
    greet(axis, me, others)
    moves = []
    for k in others:
        copy = pltpu.make_async_remote_copy(
            src_ref=x_ref,
            dst_ref=slots.at[k - 1],
            send_sem=send.at[k - 1],
            recv_sem=recv.at[k - 1],
            device_id={axis: flip(me, k)},
            device_id_type=MESH,
        )
        copy.start()
        moves.append(copy)
    out_ref[...] = x_ref[...]
    for copy, k in zip(moves, others):
        copy.wait_recv()
        out_ref[...] = out_ref[...] + slots[k - 1]
    for copy in moves:
        copy.wait_send()


def total(x, axis, width, ident, name):
    return pl.pallas_call(
        functools.partial(total_body, axis, width),
        out_shape=jax.ShapeDtypeStruct(x.shape, x.dtype),
        in_specs=[pl.BlockSpec(memory_space=pltpu.VMEM)],
        out_specs=pl.BlockSpec(memory_space=pltpu.VMEM),
        scratch_shapes=[
            pltpu.VMEM((width - 1,) + x.shape, x.dtype),
            pltpu.SemaphoreType.DMA((width - 1,)),
            pltpu.SemaphoreType.DMA((width - 1,)),
        ],
        cost_estimate=busy(7),
        compiler_params=pltpu.CompilerParams(collective_id=ident, has_side_effects=True, vmem_limit_bytes=VMEM_LIMIT),
        name=name,
    )(x)


class Hops:
    def __init__(self, planes, slots, rows):
        self.planes, self.slots = planes, slots
        self.count = max(n for n in range(1, planes + 1) if planes % n == 0 and rows % (16 * n) == 0)
        self.per = planes // self.count
        self.piece = rows // self.count
        self.plane, self.place = lax.axis_index("blk"), lax.axis_index("wide")
        self.chip, self.slot = self.place // slots, self.place % slots
        self.active = self.chip // self.count == self.plane % self.per

    def peers(self):
        near = [{"wide": (self.chip + k) % self.planes * self.slots + self.slot} for k in range(1, self.planes)]
        return near + [{"blk": (self.plane + k) % self.planes} for k in range(1, self.planes)]

    def when(self, condition, action):
        if self.per == 1:
            action()
        else:
            pl.when(condition)(action)

    def split(self, condition, yes, no):
        if self.per == 1:
            yes()
        else:
            pl.when(condition)(yes)
            pl.when(jnp.logical_not(condition))(no)

    def cut(self, ref, index):
        return ref.at[pl.ds(pl.multiple_of(index * self.piece, self.piece), self.piece)]

    def remote(self, src, dst, send, recv, device):
        return pltpu.make_async_remote_copy(
            src_ref=src, dst_ref=dst, send_sem=send, recv_sem=recv, device_id=device, device_id_type=MESH
        )

    def spread(self, some, many, send, recv, across, start):
        if across:
            axis, here = "blk", self.plane
            targets = [
                ((self.plane // self.per + k) % self.count) for k in range(self.count)
            ]
            device = lambda piece: piece * self.per + self.chip // self.count
        else:
            axis, here = "wide", self.chip
            targets = [((self.chip + k) % self.count) for k in range(self.count)]
            device = lambda piece: (self.plane % self.per) * self.count + piece
        address = (lambda who: {"blk": who}) if across else (
            lambda who: {"wide": who * self.slots + self.slot}
        )
        for k, piece in enumerate(targets):
            who = device(piece)
            far = self.remote(
                self.cut(some, piece), self.cut(many, here), send.at[piece],
                recv.at[(here - who + self.planes) % self.planes], address(who),
            )
            own = pltpu.make_async_copy(self.cut(some, piece), self.cut(many, here), send.at[piece])
            if k:
                far.start() if start else far.wait_send()
            elif start:
                self.split(self.active, own.start, far.start)
            else:
                self.split(self.active, own.wait, far.wait_send)
        if not start:
            def receive():
                for k in range(1, self.planes):
                    block = self.cut(many, (here + k) % self.planes)
                    pltpu.make_async_copy(block, block, recv.at[k]).wait()

            self.when(self.active, receive)

    def join(self, many, some, send, recv, across, start, ready=None):
        if across:
            here = self.plane
            index = self.plane // self.per
            address = lambda who: {"blk": who}
        else:
            here = self.chip
            index = self.chip % self.count
            address = lambda who: {"wide": who * self.slots + self.slot}

        def give():
            for k in list(range(1, self.planes)) + [0]:
                who = (here + k) % self.planes
                if ready is not None:
                    ready(who)
                if k:
                    copy = self.remote(
                        self.cut(many, who), self.cut(some, index), send.at[k], recv.at[index], address(who)
                    )
                    copy.start() if start else copy.wait_send()
                else:
                    own = pltpu.make_async_copy(self.cut(many, here), self.cut(some, index), send.at[0])
                    own.start() if start else own.wait()

        self.when(self.active, give)
        if not start:
            for k in range(self.count):
                piece = (index + k) % self.count
                block = self.cut(some, piece)
                arrival = pltpu.make_async_copy(block, block, recv.at[piece])
                if k:
                    arrival.wait()
                elif self.per > 1:
                    pl.when(jnp.logical_not(self.active))(arrival.wait)

    def arrival(self, some, many, send, recv, across):
        here = self.plane if across else self.chip
        own_piece = self.plane // self.per if across else self.chip % self.count

        def ready(who):
            block = self.cut(many, who)

            @pl.when(who == here)
            def _():
                pltpu.make_async_copy(self.cut(some, own_piece), block, send.at[own_piece]).wait()

            @pl.when(who != here)
            def _():
                pltpu.make_async_copy(block, block, recv.at[(who - here + self.planes) % self.planes]).wait()

        return ready

    def sent(self, some, many, send, across):
        pieces = self.plane // self.per if across else self.chip
        for k in range(self.count):
            piece = (pieces + k) % self.count
            block = self.cut(some, piece)
            out = pltpu.make_async_copy(block, block, send.at[piece])
            if k:
                out.wait()
            elif self.per > 1:
                pl.when(jnp.logical_not(self.active))(out.wait)


def hello(peers):
    barrier = pltpu.get_barrier_semaphore()
    for peer in peers:
        pl.semaphore_signal(barrier, inc=1, device_id=peer, device_id_type=MESH)
    pl.semaphore_wait(barrier, len(peers))


def beyond(plane, planes, step, action):
    pl.when((plane + step >= 0) & (plane + step < planes))(action)


def turn_in_body(planes, slots, x_ref, c_ref, w_ref, near_x, near_c, out_ref, lower_ref, upper_ref, *sems):
    hops = Hops(planes, slots, x_ref.shape[0])
    hello(hops.peers())
    w_send, w_recv = sems[6:]

    def lend(step):
        way = 0 if step > 0 else 1
        return hops.remote(
            w_ref, (lower_ref, upper_ref)[way], w_send.at[way], w_recv.at[way], {"blk": hops.plane + step}
        )

    for step in (1, -1):
        beyond(hops.plane, planes, step, lambda step=step: lend(step).start())
    hops.spread(x_ref, near_x, sems[0], sems[1], False, True)
    ready = hops.arrival(x_ref, near_x, sems[0], sems[1], False)
    hops.join(near_x, out_ref, sems[2], sems[3], True, True, ready)
    hops.sent(x_ref, near_x, sems[0], False)
    hops.spread(c_ref, near_c, sems[4], sems[5], False, True)
    hops.spread(c_ref, near_c, sems[4], sems[5], False, False)
    for way, step in ((0, 1), (1, -1)):
        block = (lower_ref, upper_ref)[way]
        beyond(hops.plane, planes, step, lambda step=step: lend(step).wait_send())
        beyond(
            hops.plane, planes, -step,
            lambda block=block, way=way: pltpu.make_async_copy(block, block, w_recv.at[way]).wait(),
        )
    hops.join(near_x, out_ref, sems[2], sems[3], True, False)


def turn_out_body(planes, slots, x_ref, far_c, v_ref, far_x, out_c, out_ref, v_out, *sems):
    hops = Hops(planes, slots, x_ref.shape[0])
    hello(hops.peers())
    parts, send, recv = sems[6:]
    moves = []
    for k in range(1, planes):
        copy = hops.remote(
            v_ref, parts.at[planes - k - 1], send.at[k - 1], recv.at[planes - k - 1],
            {"blk": (hops.plane + k) % planes},
        )
        copy.start()
        moves.append(copy)
    hops.spread(x_ref, far_x, sems[0], sems[1], True, True)
    hops.join(far_c, out_c, sems[2], sems[3], False, True)
    ready = hops.arrival(x_ref, far_x, sems[0], sems[1], True)
    hops.join(far_x, out_ref, sems[4], sems[5], False, True, ready)
    hops.sent(x_ref, far_x, sems[0], True)
    amount = v_ref[...]
    for k in range(1, planes):
        block = parts.at[k - 1]
        pltpu.make_async_copy(block, block, recv.at[k - 1]).wait()
        amount = amount + parts[k - 1]
    v_out[...] = amount
    for copy in moves:
        copy.wait_send()
    hops.join(far_c, out_c, sems[2], sems[3], False, False)
    hops.join(far_x, out_ref, sems[4], sems[5], False, False)


def many_rows(planes, rows):
    count = max(n for n in range(1, planes + 1) if planes % n == 0 and rows % (16 * n) == 0)
    return planes * (rows // count)


def turn_in(x, side, weight, planes, slots, ident, name):
    rows, cols = x.shape
    low, dma = x.dtype, pltpu.SemaphoreType.DMA
    anywhere = pl.BlockSpec(memory_space=pl.ANY)
    many, one = (jax.ShapeDtypeStruct((extent, cols), low) for extent in (many_rows(planes, rows), rows))
    piece = jax.ShapeDtypeStruct(weight.shape, low)
    return pl.pallas_call(
        functools.partial(turn_in_body, planes, slots),
        out_shape=[many, many, one, piece, piece],
        in_specs=[anywhere] * 3,
        out_specs=[anywhere] * 5,
        scratch_shapes=[dma((planes,))] * 6 + [dma((2,)), dma((2,))],
        cost_estimate=busy(10),
        compiler_params=pltpu.CompilerParams(collective_id=ident, has_side_effects=True, vmem_limit_bytes=VMEM_LIMIT),
        name=name,
    )(x, side, weight)


def turn_out(x, side, extra, planes, slots, ident, name):
    rows, cols = x.shape
    low, dma = x.dtype, pltpu.SemaphoreType.DMA
    anywhere, vmem = pl.BlockSpec(memory_space=pl.ANY), pl.BlockSpec(memory_space=pltpu.VMEM)
    many, one = (jax.ShapeDtypeStruct((extent, cols), low) for extent in (many_rows(planes, rows), rows))
    return pl.pallas_call(
        functools.partial(turn_out_body, planes, slots),
        out_shape=[many, one, one, jax.ShapeDtypeStruct(extra.shape, extra.dtype)],
        in_specs=[anywhere] * 2 + [vmem],
        out_specs=[anywhere] * 3 + [vmem],
        scratch_shapes=[dma((planes,))] * 6
        + [pltpu.VMEM((planes - 1,) + extra.shape, extra.dtype), dma((planes - 1,)), dma((planes - 1,))],
        cost_estimate=busy(10),
        compiler_params=pltpu.CompilerParams(collective_id=ident, has_side_effects=True, vmem_limit_bytes=VMEM_LIMIT),
        name=name,
    )(x, side, extra)


def mask_scores(scores, first, begin, size):
    span = scores.shape[0]
    index = lax.broadcasted_iota(jnp.int32, scores.shape, 0)
    query = lax.broadcasted_iota(jnp.int32, scores.shape, 1) + first
    return jnp.where((index <= query) & (index >= begin), scores, NEG_FILL)


def nt(left, right):
    return lax.dot_general(left, right, (((1,), (1,)), ((), ())), preferred_element_type=jnp.float32)


def nn(left, right):
    return jnp.dot(left, right, preferred_element_type=jnp.float32)


def piece_map(span, size):
    planes = span // size
    count = max(n for n in range(1, planes + 1) if planes % n == 0 and size % (16 * n) == 0)
    per, piece = planes // count, size // count
    pairs = []
    for t in range(count):
        for high in range(per):
            for low in range(count):
                natural = ((t * per + high) * count + low) * piece
                pairs.append((natural, ((high * count + low) * count + t) * piece))
    return pairs, piece


def attend_body(size, q_ref, k_ref, v_ref, inv_ref, gain_ref, cos_ref, sin_ref, begin_ref,
                qo_ref, ko_ref, vo_ref, mix_ref, log_ref):
    low = jnp.bfloat16
    span = q_ref.shape[0]

    def prepare(ref, col):
        value = ref[...] * inv_ref[:, col : col + 1] * gain_ref[col : col + 1, :]
        return (value * cos_ref[...] + pltpu.roll(value, HD // 2, 1) * sin_ref[...]).astype(low)

    pairs, piece = piece_map(span, size)

    def arrange(ref, value):
        for natural, block in pairs:
            ref[natural : natural + piece, :] = value[block : block + piece, :]

    arrange(qo_ref, prepare(q_ref, 0))
    arrange(ko_ref, prepare(k_ref, 1))
    arrange(vo_ref, v_ref[...].astype(low))
    flipped = vo_ref[...].astype(jnp.float32).T.astype(low)
    for i in range(span // size):
        last = (i + 1) * size
        cols = slice(i * size, last)
        scores = nt(ko_ref[:last, :], qo_ref[cols, :]) * SCALE
        scores = mask_scores(scores, i * size, begin_ref[:, cols], size)
        top = jnp.max(scores, axis=0, keepdims=True)
        raw = jnp.exp(scores - top)
        weight = jnp.sum(raw, axis=0, keepdims=True)
        mixed = nn(flipped[:, :last], raw.astype(low)) * (1.0 / weight)
        mixed = mixed.T.astype(low)
        for natural, block in pairs:
            if i * size <= natural < last:
                at = natural - i * size
                mix_ref[block : block + piece, :] = mixed[at : at + piece, :]
        log_ref[:, cols] = top + jnp.log(weight)


def attend(pre, inverse, gains, cosine, sine, begin, heads, size):
    slots, span, _ = pre.shape
    low, f32 = jnp.bfloat16, jnp.float32
    head = lambda offset: pl.BlockSpec((None, span, HD), lambda g, h: (g, 0, offset + h))
    every = lambda cols: pl.BlockSpec((None, span, cols), lambda g, h: (g, 0, 0))
    line = pl.BlockSpec((None, 1, span), lambda g, h: (g, 0, 0))
    out = jax.ShapeDtypeStruct((slots, span, heads * HD), low)
    return pl.pallas_call(
        functools.partial(attend_body, size),
        grid=(slots, heads),
        out_shape=[out, out, out, out, jax.ShapeDtypeStruct((slots, heads, 1, span), f32)],
        in_specs=[
            head(0), head(heads), head(2 * heads), every(2),
            pl.BlockSpec((2, HD), lambda g, h: (0, h)), every(HD), every(HD), line,
        ],
        out_specs=[head(0)] * 4 + [pl.BlockSpec((None, None, 1, span), lambda g, h: (g, h, 0, 0))],
        compiler_params=pltpu.CompilerParams(vmem_limit_bytes=VMEM_LIMIT),
        cost_estimate=busy(5),
        name="attend",
    )(pre, pre, pre, inverse, gains, cosine, sine, begin)


def attend_back_body(size, q_ref, k_ref, v_ref, g_ref, log_ref, qp_ref, kp_ref, inv_ref, gain_ref,
                     cos_ref, sin_ref, begin_ref, sq_ref, sk_ref, gv_ref, sums_ref, part_ref,
                     keys_sum, values_sum, queries_sum, held, g_held):
    low = jnp.bfloat16
    span = q_ref.shape[0]
    pairs, piece = piece_map(span, size)
    for natural, block in pairs:
        g_held[natural : natural + piece, :] = g_ref[block : block + piece, :]
    flipped = k_ref[...].astype(jnp.float32).T.astype(low)
    keys_sum[...] = jnp.zeros_like(keys_sum)
    values_sum[...] = jnp.zeros_like(values_sum)
    for i in range(span // size):
        last = (i + 1) * size
        cols = slice(i * size, last)
        scores = nt(k_ref[:last, :], q_ref[cols, :]) * SCALE
        scores = mask_scores(scores, i * size, begin_ref[:, cols], size)
        probs = jnp.exp(scores - log_ref[:, cols])
        grad_probs = nt(v_ref[:last, :], g_held[cols, :])
        delta = jnp.sum(probs * grad_probs, axis=0, keepdims=True)
        grad_scores = (probs * (grad_probs - delta)).astype(low)
        values_sum[:last, :] += nn(probs.astype(low), g_held[cols, :])
        keys_sum[:last, :] += nn(grad_scores, q_ref[cols, :])
        queries_sum[cols, :] = nn(flipped[:, :last], grad_scores).T

    def finish(total_ref, pre_ref, out_ref, col):
        for natural, block in pairs:
            held[block : block + piece, :] = total_ref[natural : natural + piece, :]
        grad = held[...] * SCALE
        back = grad * cos_ref[...] - pltpu.roll(grad, HD // 2, 1) * sin_ref[...]
        normed = pre_ref[...] * inv_ref[:, col : col + 1]
        part_ref[col : col + 1, :] = jnp.sum(back * normed, axis=0, keepdims=True)
        scaled = back * gain_ref[col : col + 1, :]
        out_ref[...] = scaled
        sums_ref[:, col : col + 1] = jnp.sum(scaled * normed, axis=1, keepdims=True)

    finish(queries_sum, qp_ref, sq_ref, 0)
    finish(keys_sum, kp_ref, sk_ref, 1)
    for natural, block in pairs:
        gv_ref[block : block + piece, :] = values_sum[natural : natural + piece, :].astype(low)


def attend_back(queries, keys, values, grads, logs, pre, inverse, gains, cosine, sine, begin, heads, size):
    slots, span, _ = pre.shape
    low, f32 = jnp.bfloat16, jnp.float32
    head = lambda offset: pl.BlockSpec((None, span, HD), lambda g, h: (g, 0, offset + h))
    every = lambda cols: pl.BlockSpec((None, span, cols), lambda g, h: (g, 0, 0))
    line = pl.BlockSpec((None, 1, span), lambda g, h: (g, 0, 0))
    wide = jax.ShapeDtypeStruct((slots, span, heads * HD), f32)
    return pl.pallas_call(
        functools.partial(attend_back_body, size),
        grid=(slots, heads),
        out_shape=[
            wide, wide, jax.ShapeDtypeStruct((slots, span, heads * HD), low),
            jax.ShapeDtypeStruct((heads, slots, span, 2), f32),
            jax.ShapeDtypeStruct((slots, 2, heads * HD), f32),
        ],
        in_specs=[
            head(0), head(0), head(0), head(0),
            pl.BlockSpec((None, None, 1, span), lambda g, h: (g, h, 0, 0)),
            head(0), head(heads), every(2),
            pl.BlockSpec((2, HD), lambda g, h: (0, h)), every(HD), every(HD), line,
        ],
        out_specs=[
            head(0), head(0), head(0),
            pl.BlockSpec((None, None, span, 2), lambda g, h: (h, g, 0, 0)),
            pl.BlockSpec((None, 2, HD), lambda g, h: (g, 0, h)),
        ],
        scratch_shapes=[pltpu.VMEM((span, HD), f32)] * 4 + [pltpu.VMEM((span, HD), low)],
        compiler_params=pltpu.CompilerParams(vmem_limit_bytes=VMEM_LIMIT),
        cost_estimate=busy(5),
        name="attend_back",
    )(queries, keys, values, grads, logs, pre, pre, inverse, gains, cosine, sine, begin)


def row_sums(value):
    return jnp.sum(value.reshape(-1, 8, value.shape[-1]), axis=0)


def feed_body(width, slots, step, h_ref, c_ref, wg_hbm, wu_hbm, wd_hbm, hidden_ref, gain_ref, block_ref,
              first_ref, second_ref, gain_out, all_ref, act_ref, one_ref, two_ref, c_out, buf, wg, wu, wd, stage, out_ref,
              c_held, here, load, send, recv, side_send, side_recv, store, keep, *sum_refs):
    me = lax.axis_index("wide")
    planes = width // slots
    rows, cols = h_ref.shape
    hidden = wg.shape[1]
    half = rows // 2
    low = jnp.bfloat16
    loads = local_copies([(wg_hbm, wg), (wu_hbm, wu), (wd_hbm, wd)], load)
    mine = pltpu.make_async_copy(h_ref, buf.at[me], here)
    mine.start()
    for copy in loads:
        copy.start()
    hops = Hops(planes, slots, rows)
    hello(wide_peers(width, me) + [{"blk": (hops.plane + k) % planes} for k in range(1, planes)])
    flow = Flow(me, h_ref, lambda who, part: buf.at[who, pl.ds(part * half, half)], half, send, recv)
    sums = Sums(width, me, out_ref, sum_refs)
    outs = (act_ref, one_ref, two_ref)
    pending = [[], []]
    turn_count = [0]
    kept = []

    def where(k):
        who = flip(me, k)
        return pl.multiple_of(((who % slots) * planes + who // slots) * rows, rows)

    def keep_block(k):
        copy = pltpu.make_async_copy(buf.at[flip(me, k)], all_ref.at[pl.ds(where(k), rows)], keep.at[k])
        copy.start()
        kept.append(copy)

    def work(k, part, put, adds=()):
        first, count = (0, rows) if part is None else (part * half, half)
        slot = turn_count[0] % 2
        turn_count[0] += 1
        for copy in pending[slot]:
            copy.wait()
        block = buf.at[flip(me, k), pl.ds(first, count)]
        act, one, two = (stage.at[slot, i, pl.ds(0, count)] for i in range(3))

        def inner(n, carry):
            at = pl.ds(pl.multiple_of(n * step, step), step)
            gate = jnp.dot(block[...], wg[:, at], preferred_element_type=jnp.float32)
            upward = jnp.dot(block[...], wu[:, at], preferred_element_type=jnp.float32)
            sigmoid = jax.nn.sigmoid(gate)
            silu = gate * sigmoid
            act[:, at] = (silu * upward).astype(low)
            one[:, at] = silu.astype(low)
            two[:, at] = (upward * (sigmoid + silu * (1.0 - sigmoid))).astype(low)
            return carry

        lax.fori_loop(0, hidden // step, inner, 0)
        target = pl.ds(pl.multiple_of(where(k) + first, half), count)
        pending[slot] = []
        for i, ref in enumerate(outs):
            copy = pltpu.make_async_copy(stage.at[slot, i, pl.ds(0, count)], ref.at[target], store.at[slot, i])
            copy.start()
            pending[slot].append(copy)
        broad = 2 * step

        def outer(n, carry):
            at = pl.ds(pl.multiple_of(n * broad, broad), broad)
            total = jnp.dot(act[...], wd[:, at], preferred_element_type=jnp.float32)
            for ref in adds:
                total = total + ref[:, at].astype(jnp.float32)
            put[:, at] = total.astype(put.dtype)
            return carry

        lax.fori_loop(0, cols // broad, outer, 0)

    def odd_work(k, part):
        if part is None:
            work(k + 1, None, sums.odd.at[k // 2])
            sums.give(k)
        else:
            work(k + 1, part, sums.odd.at[k // 2, sums.rows(part)])
            sums.twin(k, part).start()

    def even_work(k, part):
        i = k // 2
        if part is None:
            sums.got(k)
            work(k, None, sums.even.at[i - 1], (sums.from_twin.at[i],))
        else:
            sums.twin(k, part).wait_recv()
            at = sums.rows(part)
            work(k, part, sums.even.at[i - 1, at], (sums.from_twin.at[i, at],))

    if width == 8:
        flow.go(None, 2, 2, 0)
        flow.go(None, 4, 4, 1)
        flow.go(None, 1, 1, 0)
        flow.go(None, 1, 1, 1)
        hops.join(c_ref, c_out, side_send, side_recv, True, True)
        mine.wait()
        for copy in loads:
            copy.wait()
        work(0, None, out_ref)
        keep_block(0)
        flow.arrived(1, 0)
        flow.arrived(1, 1)
        keep_block(1)
        odd_work(0, None)
        flow.arrived(2, 0)
        flow.go(2, 4, 6, 0)
        flow.arrived(4, 1)
        flow.go(4, 2, 6, 1)
        flow.go(2, 1, 3, 0)
        flow.go(4, 1, 5, 1)
        flow.go(None, 2, 2, 1)
        flow.go(None, 4, 4, 0)
        flow.arrived(3, 0)
        odd_work(2, 0)
        flow.arrived(5, 1)
        odd_work(4, 1)
        even_work(2, 0)
        even_work(4, 1)
        for part in (0, 1):
            flow.arrived(6, part)
            flow.go(6, 1, 7, part)
        for part in (0, 1):
            flow.arrived(7, part)
        keep_block(6)
        keep_block(7)
        odd_work(6, None)
        even_work(6, None)
        sums.relay(0).start()
        sums.relay(1).start()
        flow.arrived(2, 1)
        flow.go(2, 1, 3, 1)
        flow.arrived(4, 0)
        flow.go(4, 1, 5, 0)
        sums.far(2, 0).start()
        sums.far(4, 1).start()
        flow.arrived(3, 1)
        odd_work(2, 1)
        flow.arrived(5, 0)
        odd_work(4, 0)
        for k in (2, 3, 4, 5):
            keep_block(k)
        even_work(2, 1)
        sums.pass_on(2, 1)
        even_work(4, 0)
        sums.pass_on(4, 0)
    else:
        hops.join(c_ref, c_out, side_send, side_recv, True, True)
        for k in range(2, width, 2):
            flow.go(None, k, k, 0)
            flow.go(None, k, k, 1)
        flow.go(None, 1, 1, 0)
        flow.go(None, 1, 1, 1)
        mine.wait()
        for copy in loads:
            copy.wait()
        work(0, None, out_ref)
        keep_block(0)
        flow.arrived(1, 0)
        flow.arrived(1, 1)
        keep_block(1)
        odd_work(0, None)
        for k in range(2, width, 2):
            for part in (0, 1):
                flow.arrived(k, part)
                flow.go(k, 1, k + 1, part)
            for part in (0, 1):
                flow.arrived(k + 1, part)
            keep_block(k)
            keep_block(k + 1)
            odd_work(k, None)
            even_work(k, None)
            sums.far(k, 0).start()
            sums.far(k, 1).start()
    sums.got(0)
    out_ref[...] = out_ref[...] + sums.from_twin[0].astype(jnp.float32)
    sums.finish()
    flow.finish()
    hops.join(c_ref, c_out, side_send, side_recv, True, False)
    held = pltpu.make_async_copy(c_out, c_held, here)
    held.start()
    held.wait()
    gain_out[...] = jnp.zeros_like(gain_out)
    few = 32
    own = cols // planes
    half_own = own // 2

    def norm(n, carry):
        at = pl.ds(pl.multiple_of(n * few, few), few)
        value = out_ref[at, :]
        inverse = lax.rsqrt(jnp.sum(value * value, axis=-1, keepdims=True) * (1.0 / cols) + EPS)
        normed = value * inverse
        block_ref[at, :] = (hidden_ref[at, :] + normed * gain_ref[...]).astype(low)
        grad = c_held[at, :].astype(jnp.float32)
        gain_out[...] = gain_out[...] + row_sums(grad * normed)
        grad = grad * gain_ref[...]
        mean = jnp.sum(grad * normed, axis=-1, keepdims=True) * (1.0 / cols)
        grad = (inverse * (grad - normed * mean)).astype(low)
        for b in range(planes):
            for side in (0, 1):
                first = b * own + side * half_own
                (first_ref, second_ref)[side][at, b * half_own : (b + 1) * half_own] = grad[:, first : first + half_own]
        return carry

    lax.fori_loop(0, rows // few, norm, 0)
    for copy in kept + pending[0] + pending[1]:
        copy.wait()


def feed(h, side_x, gate_weight, up_weight, down_weight, hidden, gain, width, slots, ident, name):
    rows, cols = h.shape
    inner = gate_weight.shape[1]
    low, f32, dma = h.dtype, jnp.float32, pltpu.SemaphoreType.DMA
    step = min(512, inner)
    anywhere, vmem = pl.BlockSpec(memory_space=pl.ANY), pl.BlockSpec(memory_space=pltpu.VMEM)
    saved = jax.ShapeDtypeStruct((rows * width, inner), low)
    return pl.pallas_call(
        functools.partial(feed_body, width, slots, step),
        out_shape=[
            jax.ShapeDtypeStruct((rows, cols), low), jax.ShapeDtypeStruct((rows, cols // 2), low),
            jax.ShapeDtypeStruct((rows, cols // 2), low),
            jax.ShapeDtypeStruct((8, cols), f32), jax.ShapeDtypeStruct((rows * width, cols), low),
            saved, saved, saved, jax.ShapeDtypeStruct((rows, cols), low),
        ],
        in_specs=[anywhere] * 5 + [vmem] * 2,
        out_specs=[vmem] * 4 + [anywhere] * 5,
        scratch_shapes=[
            pltpu.VMEM((width, rows, cols), low), pltpu.VMEM((cols, inner), low), pltpu.VMEM((cols, inner), low),
            pltpu.VMEM((inner, cols), low), pltpu.VMEM((2, 3, rows, inner), low),
            pltpu.VMEM((rows, cols), f32), pltpu.VMEM((rows, cols), low),
            dma, dma((3,)), dma((width, 2)), dma((width, 2)), dma((width // slots,)), dma((width // slots,)),
            dma((2, 3)), dma((width,)),
        ] + sum_scratch(width, rows, cols),
        cost_estimate=busy(90),
        compiler_params=pltpu.CompilerParams(collective_id=ident, has_side_effects=True, vmem_limit_bytes=VMEM_LIMIT),
        name=name,
    )(h, side_x, gate_weight, up_weight, down_weight, hidden, gain)


def push_body(second, width, slots, *refs):
    if second:
        (g_ref, act_hbm, wd_hbm, one_hbm, two_hbm, first_hbm, down_ref, gg_ref, gu_ref,
         buf, held, acts, here, send, recv, fetch, wd, before, ins, outs, load, take, store) = refs
    else:
        (g_ref, act_hbm, c_ref, down_ref, all_ref, c_out,
         buf, held, acts, here, send, recv, fetch, keep, side_send, side_recv) = refs
    me = lax.axis_index("wide")
    planes = width // slots
    pairs = width // 2
    rows, cols = g_ref.shape
    inner = down_ref.shape[0]
    half = rows // 2
    low = jnp.bfloat16
    mine = pltpu.make_async_copy(g_ref, buf.at[me // 2, me % 2], here)
    mine.start()

    def where(pair, side):
        who = flip(me // 2, pair) * 2 + side
        return pl.ds(pl.multiple_of(((who % slots) * planes + who // slots) * rows, rows), rows)

    def fetches(pair):
        copies = [
            pltpu.make_async_copy(act_hbm.at[where(pair, side)], acts.at[pair % 2, side], fetch.at[pair % 2, side])
            for side in (0, 1)
        ]
        if second:
            copies += [
                pltpu.make_async_copy(ref.at[where(pair, side)], ins.at[pair % 2, i, side], take.at[pair % 2, i, side])
                for i, ref in enumerate((one_hbm, two_hbm))
                for side in (0, 1)
            ]
        return copies

    def stores(pair):
        return [
            pltpu.make_async_copy(outs.at[pair % 2, i, side], ref.at[where(pair, side)], store.at[pair % 2, i, side])
            for i, ref in enumerate((gg_ref, gu_ref))
            for side in (0, 1)
        ]

    def keeps(pair):
        chip = flip(me // 2, pair)
        return pltpu.make_async_copy(buf.at[chip], all_ref.at[chip], keep.at[pair])

    for copy in fetches(0):
        copy.start()
    peers = wide_peers(width, me)
    if second:
        own = cols // planes
        loads = [
            pltpu.make_async_copy(
                wd_hbm.at[:, pl.ds((2 * b + side) * own, own)], wd.at[:, pl.ds(side * cols + b * own, own)],
                load.at[b, side],
            )
            for b in range(planes)
            for side in (0, 1)
        ]
        loads.append(pltpu.make_async_copy(first_hbm, before, load.at[planes, 0]))
        for copy in loads:
            copy.start()
    else:
        hops = Hops(planes, slots, rows)
        peers = peers + [{"blk": (hops.plane + k) % planes} for k in range(1, planes)]
    hello(peers)
    flow = Flow(me, g_ref, lambda who, part: buf.at[who // 2, who % 2, pl.ds(part * half, half)], half, send, recv)

    def work(pair):
        for copy in fetches(pair):
            copy.wait()
        if pair + 1 < pairs:
            for copy in fetches(pair + 1):
                copy.start()
        chip = flip(me // 2, pair)
        slot = pair % 2
        grads = buf[chip].reshape(2 * rows, cols)
        if second:
            if pair >= 2:
                for copy in stores(pair - 2):
                    copy.wait()
            old = before[chip].reshape(2 * rows, cols)
            step = min(512, inner)

            def units(n, carry):
                at = pl.ds(pl.multiple_of(n * step, step), step)
                grad = (nt(old, wd[at, :cols]) + nt(grads, wd[at, cols:])).reshape(2, rows, step)
                outs[slot, 0, :, :, at] = (grad * ins[slot, 1, :, :, at].astype(jnp.float32)).astype(low)
                outs[slot, 1, :, :, at] = (grad * ins[slot, 0, :, :, at].astype(jnp.float32)).astype(low)
                return carry

            lax.fori_loop(0, inner // step, units, 0)
            for copy in stores(pair):
                copy.start()
        else:
            keeps(pair).start()
        tall = min(512, inner)

        def outer(n, carry):
            at = pl.ds(pl.multiple_of(n * tall, tall), tall)
            act = acts[slot, :, :, at].reshape(2 * rows, tall)
            term = lax.dot_general(act, grads, (((0,), (0,)), ((), ())), preferred_element_type=jnp.float32)
            if pair:
                term = term + held[at, :]
            if pair + 1 < pairs:
                held[at, :] = term
            else:
                down_ref[at, :] = term.astype(low)
            return carry

        lax.fori_loop(0, inner // tall, outer, 0)

    def pair_ready(k):
        for part in (0, 1):
            flow.arrived(k + 1, part)

    if width == 8:
        flow.go(None, 2, 2, 0)
        flow.go(None, 4, 4, 1)
        flow.go(None, 2, 2, 1)
        flow.go(None, 4, 4, 0)
    else:
        for k in range(2, width, 2):
            flow.go(None, k, k, 0)
            flow.go(None, k, k, 1)
    flow.go(None, 1, 1, 0)
    flow.go(None, 1, 1, 1)
    if second:
        for copy in loads:
            copy.wait()
    else:
        hops.spread(c_ref, c_out, side_send, side_recv, True, True)
    mine.wait()
    pair_ready(0)
    work(0)
    if width == 8:
        flow.arrived(2, 0)
        flow.go(2, 4, 6, 0)
        flow.go(2, 1, 3, 0)
        flow.arrived(4, 1)
        flow.go(4, 2, 6, 1)
        flow.go(4, 1, 5, 1)
        flow.arrived(2, 1)
        flow.go(2, 1, 3, 1)
        flow.arrived(4, 0)
        flow.go(4, 1, 5, 0)
        pair_ready(2)
        work(1)
        pair_ready(4)
        work(2)
        for part in (0, 1):
            flow.arrived(6, part)
            flow.go(6, 1, 7, part)
        pair_ready(6)
        work(3)
    else:
        for k in range(2, width, 2):
            for part in (0, 1):
                flow.arrived(k, part)
                flow.go(k, 1, k + 1, part)
            pair_ready(k)
            work(k // 2)
    flow.finish()
    if second:
        for pair in (pairs - 2, pairs - 1):
            for copy in stores(pair):
                copy.wait()
    else:
        for pair in range(pairs):
            keeps(pair).wait()
        hops.spread(c_ref, c_out, side_send, side_recv, True, False)


def push(second, g, act, width, slots, ident, name, others):
    rows, cols = g.shape
    inner = act.shape[1]
    low, dma = g.dtype, pltpu.SemaphoreType.DMA
    planes, pairs = width // slots, width // 2
    anywhere, vmem = pl.BlockSpec(memory_space=pl.ANY), pl.BlockSpec(memory_space=pltpu.VMEM)
    blocks = (pairs, 2, rows, cols)
    scratch = [
        pltpu.VMEM(blocks, low), pltpu.VMEM((inner, cols), jnp.float32), pltpu.VMEM((2, 2, rows, inner), low),
        dma, dma((width, 2)), dma((width, 2)), dma((2, 2)),
    ]
    shapes = [jax.ShapeDtypeStruct((inner, cols), low)]
    if second:
        saved = jax.ShapeDtypeStruct((rows * width, inner), low)
        shapes += [saved, saved]
        scratch += [
            pltpu.VMEM((inner, 2 * cols), low), pltpu.VMEM(blocks, low), pltpu.VMEM((2, 2, 2, rows, inner), low),
            pltpu.VMEM((2, 2, 2, rows, inner), low), dma((planes + 1, 2)), dma((2, 2, 2)), dma((2, 2, 2)),
        ]
    else:
        shapes += [
            jax.ShapeDtypeStruct(blocks, low),
            jax.ShapeDtypeStruct((many_rows(planes, rows), others[0].shape[1]), low),
        ]
        scratch += [dma((pairs,)), dma((planes,)), dma((planes,))]
    inputs = [g, act] + others
    return pl.pallas_call(
        functools.partial(push_body, second, width, slots),
        out_shape=shapes,
        in_specs=[anywhere] * len(inputs),
        out_specs=[vmem] + [anywhere] * (len(shapes) - 1),
        scratch_shapes=scratch,
        cost_estimate=busy(10),
        compiler_params=pltpu.CompilerParams(collective_id=ident, has_side_effects=True, vmem_limit_bytes=VMEM_LIMIT),
        name=name,
    )(*inputs)


def pull_body(width, slots, step, chunk, gg_hbm, gu_hbm, wg_hbm, wu_hbm, h_hbm, c_ref, normed_ref, inv_ref, gain_ref,
              out_ref, proj_ref, gain_out, du_hbm, gg, gu, wg, wu, columns, tiles, load, take, fetch, store, *sum_refs):
    me = lax.axis_index("wide")
    planes = width // slots
    rows, cols = out_ref.shape
    half = rows // 2
    chunks = cols // chunk
    loads = local_copies([(wg_hbm, wg), (wu_hbm, wu)], load)
    for copy in loads:
        copy.start()

    def where(k, first, count):
        who = flip(me, k)
        start = ((who % slots) * planes + who // slots) * rows + first
        return pl.ds(pl.multiple_of(start, half), count)

    def takes(k):
        at = where(k, 0, rows)
        return [
            pltpu.make_async_copy(src.at[at], dst.at[at], take.at[k, i])
            for i, (src, dst) in enumerate(((gg_hbm, gg), (gu_hbm, gu)))
        ]

    order = [7, 6, 3, 5, 2, 4, 1, 0] if width == 8 else [k ^ 1 for k in range(width)]
    for k in order:
        for copy in takes(k):
            copy.start()
    taken = []

    def need(k):
        if k not in taken:
            taken.append(k)
            for copy in takes(k):
                copy.wait()

    def fetched(n):
        at = pl.ds(pl.multiple_of(n * chunk, chunk), chunk)
        return pltpu.make_async_copy(h_hbm.at[:, at], columns.at[n % 2], fetch.at[n % 2])

    def stored(n):
        at = pl.ds(pl.multiple_of(n * chunk, chunk), chunk)
        return [
            pltpu.make_async_copy(tiles.at[n % 2, i], ref.at[at], store.at[n % 2, i])
            for i, ref in enumerate((du_hbm,))
        ]

    fetched(0).start()
    hello(wide_peers(width, me))
    sums = Sums(width, me, out_ref, sum_refs)

    def produce(k, first, count, put, adds=()):
        need(k)
        at_rows = where(k, first, count)

        def tile(n, carry):
            at = pl.ds(pl.multiple_of(n * step, step), step)
            total = nt(gg[at_rows, :], wg[at, :]) + nt(gu[at_rows, :], wu[at, :])
            for ref in adds:
                total = total + ref[:, at].astype(jnp.float32)
            put[:, at] = total.astype(put.dtype)
            return carry

        lax.fori_loop(0, cols // step, tile, 0)

    def grads(first, last):
        for k in order:
            need(k)

        def one_chunk(n, carry):
            fetched(n).wait()

            @pl.when(n + 1 < chunks)
            def _():
                fetched(n + 1).start()

            @pl.when(n >= 2)
            def _():
                for copy in stored(n - 2):
                    copy.wait()

            for i, ref in enumerate((gu,)):
                tiles[n % 2, i] = lax.dot_general(
                    columns[n % 2], ref[...], (((0,), (0,)), ((), ())), preferred_element_type=jnp.float32
                ).astype(jnp.bfloat16)
            for copy in stored(n):
                copy.start()
            return carry

        lax.fori_loop(first, last, one_chunk, 0)

    for copy in loads:
        copy.wait()
    run_sums(width, sums, produce, grads, chunks)
    gain_out[...] = jnp.zeros_like(gain_out)
    few = 32

    def norm(n, carry):
        at = pl.ds(pl.multiple_of(n * few, few), few)
        grad = out_ref[at, :] + c_ref[at, :].astype(jnp.float32)
        out_ref[at, :] = grad
        normed = normed_ref[at, :]
        gain_out[...] = gain_out[...] + row_sums(grad * normed)
        grad = grad * gain_ref[...]
        mean = jnp.sum(grad * normed, axis=-1, keepdims=True) * (1.0 / cols)
        proj_ref[at, :] = (inv_ref[at, :] * (grad - normed * mean)).astype(jnp.bfloat16)
        return carry

    lax.fori_loop(0, rows // few, norm, 0)
    for copy in stored(chunks - 2) + stored(chunks - 1):
        copy.wait()


def pull(grad_gate, grad_up, gate_weight, up_weight, gathered, grad_out, normed, inverse, gain, width, slots, ident, name):
    count, cols = gathered.shape
    inner = gate_weight.shape[1]
    rows = count // width
    low, f32, dma = gathered.dtype, jnp.float32, pltpu.SemaphoreType.DMA
    chunk = 256
    anywhere, vmem = pl.BlockSpec(memory_space=pl.ANY), pl.BlockSpec(memory_space=pltpu.VMEM)
    return pl.pallas_call(
        functools.partial(pull_body, width, slots, 1024, chunk),
        out_shape=[
            jax.ShapeDtypeStruct((rows, cols), f32), jax.ShapeDtypeStruct((rows, cols), low),
            jax.ShapeDtypeStruct((8, cols), f32), jax.ShapeDtypeStruct((cols, inner), low),
        ],
        in_specs=[anywhere] * 5 + [vmem] * 4,
        out_specs=[vmem] * 3 + [anywhere],
        scratch_shapes=[
            pltpu.VMEM((count, inner), low), pltpu.VMEM((count, inner), low),
            pltpu.VMEM((cols, inner), low), pltpu.VMEM((cols, inner), low),
            pltpu.VMEM((2, count, chunk), low), pltpu.VMEM((2, 1, chunk, inner), low),
            dma((2,)), dma((width, 2)), dma((2,)), dma((2, 1)),
        ] + sum_scratch(width, rows, cols),
        cost_estimate=busy(10),
        compiler_params=pltpu.CompilerParams(collective_id=ident, has_side_effects=True, vmem_limit_bytes=VMEM_LIMIT),
        name=name,
    )(grad_gate, grad_up, gate_weight, up_weight, gathered, grad_out, normed, inverse, gain)


def side_body(x_ref, p_ref, g_ref, m_ref, out_ref):
    dims = (((0,), (0,)), ((), ()))
    split = g_ref.shape[1]
    out_ref[:, :split] = lax.dot_general(
        x_ref[...], g_ref[...], dims, preferred_element_type=jnp.float32
    ).astype(out_ref.dtype)
    out_ref[:, split:] = lax.dot_general(
        p_ref[...], m_ref[...], dims, preferred_element_type=jnp.float32
    ).astype(out_ref.dtype)


def side_grads(inputs, grad_proj, grads, mixed):
    count, cols = inputs.shape
    extent = grads.shape[1] + mixed.shape[1]
    chunk = 256
    return pl.pallas_call(
        side_body,
        grid=(cols // chunk,),
        out_shape=jax.ShapeDtypeStruct((cols, extent), inputs.dtype),
        in_specs=[
            pl.BlockSpec((count, chunk), lambda n: (0, n)), pl.BlockSpec((count, chunk), lambda n: (0, n)),
            pl.BlockSpec(grads.shape, lambda n: (0, 0)), pl.BlockSpec(mixed.shape, lambda n: (0, 0)),
        ],
        out_specs=pl.BlockSpec((chunk, extent), lambda n: (n, 0)),
        compiler_params=pltpu.CompilerParams(vmem_limit_bytes=VMEM_LIMIT),
        cost_estimate=busy(10),
        name="side_grads",
    )(inputs, grad_proj, grads, mixed)


def local(
    tokens,
    lengths,
    query_weight,
    key_weight,
    value_weight,
    output_weight,
    query_gain,
    key_gain,
    attention_gain,
    gate_weight,
    up_weight,
    down_weight,
    feedforward_gain,
    cotangent,
):
    low, f32 = jnp.bfloat16, jnp.float32
    planes, width = lax.axis_size("blk"), lax.axis_size("wide")
    slots = width // planes
    rows = tokens.shape[1]
    span = rows * planes
    count = slots * span
    share = query_weight.shape[1]
    heads = share // HD
    plane, place = lax.axis_index("blk"), lax.axis_index("wide")
    after = lambda value, *others: lax.optimization_barrier((value,) + others)[0]

    def sum_blk(value, axis):
        return lax.psum_scatter(value, "blk", scatter_dimension=axis, tiled=True)

    w_rows = jnp.concatenate([query_weight, key_weight, value_weight], 1)
    _, near_cotangent, mine, lower, upper = turn_in(
        tokens[0], cotangent[0], w_rows, planes, slots, 1, "turn_in"
    )
    gains = jnp.stack([query_gain, key_gain]).astype(f32)
    plane_lengths = lax.dynamic_slice_in_dim(lengths, plane * slots, slots, 0)
    segment, position = jax.vmap(lambda one: layout(one, span))(plane_lengths)
    begin = (jnp.arange(span, dtype=jnp.int32)[None] - position)[:, None, :]
    pairs, piece = piece_map(span, rows)
    order = sorted(pairs, key=lambda pair: pair[1])
    index = np.concatenate([np.arange(at, at + piece) for at, _ in order])
    starts = jnp.stack([plane_lengths[:, 0] * 0, plane_lengths[:, 0], plane_lengths[:, 0] + plane_lengths[:, 1]], 1)
    cos_a, sin_a, cos_b, sin_b, sign = rope_tables(index, starts)
    group = jnp.concatenate([segment[:, at : at + piece] for at, _ in order], 1)[..., None]
    pick = lambda table: jnp.where(
        group == 0, table[:, 0:1], jnp.where(group == 1, table[:, 1:2], table[:, 2:3])
    )
    cos_b, sin_b = pick(cos_b), pick(sin_b)
    cosine = cos_a * cos_b + sin_a * sin_b
    sine = (sin_a * cos_b - cos_a * sin_b) * sign

    inputs, w_qkv = gather(mine, width, slots, 2, "gather_tokens", (w_rows, lower, upper))
    pre = dot(inputs, w_qkv)
    squares = jnp.stack([jnp.sum(pre[:, a * share : (a + 1) * share] ** 2, -1) for a in (0, 1)])
    both = lax.dynamic_update_slice(
        jnp.zeros((2, D), f32), jnp.stack([attention_gain, feedforward_gain]).astype(f32), (0, place * share)
    )
    squares = jnp.concatenate([squares.reshape(-1, 128), both.reshape(-1, 128)])
    squares = total(squares, "wide", width, 3, "total_squares")
    both = squares[2 * count // 128 :].reshape(2, D)
    gain_mix, gain_feed = both[0], both[1]
    inverse = lax.rsqrt(squares[: 2 * count // 128].reshape(2, count) / D + EPS)
    inv_cols = inverse.T.reshape(slots, span, 2)
    w_o = lax.all_gather(after(output_weight, inputs), "blk", axis=1, tiled=True)
    pre_groups = pre.reshape(slots, span, 3 * share)
    queries, keys, values, mixed, logs = attend(
        pre_groups, inv_cols, gains, cosine, sine, begin, heads, rows
    )
    mixed = mixed.reshape(count, share)
    hidden, hidden_low, proj_normed, proj_inv = scatter(
        [mixed], [w_o], width, slots, False, 4, "scatter_mixed", "norm", (mine, gain_mix[None])
    )
    block_output, first_half, second_half, feed_gain_part, gathered, activated, up_factor, gate_factor, grad_out = feed(
        hidden_low, near_cotangent, gate_weight, up_weight, down_weight, hidden, gain_feed[None], width, slots, 5,
        "feed",
    )
    down_first, first_rows, far_output = push(
        False, first_half, activated, width, slots, 6, "push_first", [block_output]
    )
    down_first = sum_blk(down_first, 1)
    down_second, grad_gate, grad_up = push(
        True, second_half, activated, width, slots, 7, "push_second",
        [down_weight, up_factor, gate_factor, first_rows],
    )
    down_second = sum_blk(down_second, 1)
    gate_part = contract_rows(gathered, grad_gate).astype(low)
    gate_grad = sum_blk(gate_part, 0)
    grad_hidden, grad_proj, mix_gain_part, up_part = pull(
        after(grad_gate, gate_part, down_first), grad_up, gate_weight, up_weight, gathered, grad_out, proj_normed,
        proj_inv, gain_mix[None], width, slots, 8, "pull",
    )
    up_grad = sum_blk(up_part, 0)
    grad_proj = gather(grad_proj, width, slots, 9, "gather_proj")
    grad_mixed = contract_cols(after(grad_proj, down_first, down_second), w_o).astype(low).reshape(slots, span, share)
    scaled_q, scaled_k, grad_v, sums, parts = attend_back(
        queries, keys, values, grad_mixed, logs, pre_groups, inv_cols, gains, cosine, sine, begin,
        heads, rows,
    )
    means = jnp.sum(sums, axis=0).reshape(count, 2).T.reshape(-1, 128)
    local_gains = lax.dynamic_update_slice(
        jnp.zeros((2, D), f32), jnp.sum(parts, axis=0), (0, place * share)
    )
    gain_parts = jnp.concatenate([local_gains, jnp.stack([mix_gain_part.sum(0), feed_gain_part.sum(0)])])
    means = jnp.concatenate([means, gain_parts.reshape(-1, 128)])
    means = total(after(means, gate_grad), "wide", width, 10, "total_means")
    gain_parts = means[2 * count // 128 :]
    means = means[: 2 * count // 128].reshape(2, count) / D

    def finish(scaled, index):
        normed = pre[:, index * share : (index + 1) * share] * inverse[index][:, None]
        scaled = scaled.reshape(count, share)
        return (inverse[index][:, None] * (scaled - normed * means[index][:, None])).astype(low)

    grads = jnp.concatenate([finish(scaled_q, 0), finish(scaled_k, 1), grad_v.reshape(count, share)], 1)
    side_part = side_grads(inputs, grad_proj, grads, mixed)
    tokens_low = scatter(
        [grads], [w_qkv], width, slots, True, 11, "scatter_tokens", "add", (grad_hidden,)
    )
    down_grad = jnp.concatenate([down_first, down_second], 1).astype(f32)
    gate_grad, up_grad = gate_grad.astype(f32), up_grad.astype(f32)
    tokens_low, down_grad, gate_grad, up_grad = lax.optimization_barrier((tokens_low, down_grad, gate_grad, up_grad))
    _, block_output, tokens_grad, gain_sums = turn_out(
        tokens_low, far_output, gain_parts, planes, slots, 14, "turn_out"
    )
    side_grad = sum_blk(side_part, 0).astype(f32)

    sums = gain_sums.reshape(4, D)
    portion = D // (planes * width)
    sums = lax.dynamic_slice_in_dim(sums, (plane * width + place) * portion, portion, 1)
    return (
        block_output[None],
        tokens_grad[None].astype(f32),
        side_grad[:, :share],
        side_grad[:, share : 2 * share],
        side_grad[:, 2 * share : 3 * share],
        side_grad[:, 3 * share :].T,
        sums[0],
        sums[1],
        sums[2],
        gate_grad,
        up_grad,
        down_grad,
        sums[3],
    )


def solution(mesh):
    placed = (
        P("wide", "blk", None),
        P(),
        P("blk", "wide"),
        P("blk", "wide"),
        P("blk", "wide"),
        P("wide", "blk"),
        P("wide"),
        P("wide"),
        P("wide"),
        P(None, "wide"),
        P(None, "wide"),
        P("wide", None),
        P("wide"),
        P("wide", "blk", None),
    )
    return jax.shard_map(
        local,
        mesh=mesh,
        in_specs=placed,
        out_specs=(
            P("wide", "blk", None),
            P("wide", "blk", None),
            P("blk", "wide"),
            P("blk", "wide"),
            P("blk", "wide"),
            P("wide", "blk"),
            P(("blk", "wide")),
            P(("blk", "wide")),
            P(("blk", "wide")),
            P("blk", "wide"),
            P("blk", "wide"),
            P("wide", "blk"),
            P(("blk", "wide")),
        ),
        check_vma=False,
    )
```

```python
import functools

import jax
import jax.numpy as jnp
import numpy as np
from jax import lax
from jax.experimental import pallas as pl
from jax.experimental.pallas import tpu as pltpu
from jax.sharding import PartitionSpec as P

MESH = pl.DeviceIdType.MESH

D = 2048
HD = 128
EPS = 1e-06
ROPE_BASE = 500000.0
NEG_FILL = -1e30
VMEM_LIMIT = 60 * 1024 * 1024
SCALE = HD ** (-0.5)


def busy(micros):
    return pl.CostEstimate(flops=0, bytes_accessed=int(micros * 3.5e6), transcendentals=0)


def layout(seq_lengths, row_count):
    indices = jnp.arange(row_count, dtype=jnp.int32)
    first_end = seq_lengths[0]
    second_end = seq_lengths[0] + seq_lengths[1]
    segment = (indices >= first_end).astype(jnp.int32) + (indices >= second_end).astype(jnp.int32)
    offsets = jnp.where(segment == 0, 0, jnp.where(segment == 1, first_end, second_end))
    return (segment, indices - offsets)


def rope_tables(index, begin):
    frequency = ROPE_BASE ** (-np.arange(0, HD, 2, dtype=np.float64) / HD)
    angles = np.asarray(index, np.float64)[:, None] * frequency
    sign = np.concatenate([-np.ones(HD // 2), np.ones(HD // 2)])
    twice = lambda value: np.concatenate([value, value], -1).astype(np.float32)
    cosine, sine = jnp.asarray(twice(np.cos(angles))), jnp.asarray(twice(np.sin(angles)))
    shift = begin.astype(jnp.float32)[..., None] * jnp.asarray(twice(frequency))
    return cosine, sine, jnp.cos(shift), jnp.sin(shift), jnp.asarray(sign.astype(np.float32))


def rms_pair(values):
    inverse = lax.rsqrt(jnp.mean(values * values, axis=-1, keepdims=True) + EPS)
    return (values * inverse, inverse)


def norm_back(normed, inverse, grad_normed):
    return inverse * (grad_normed - normed * jnp.mean(grad_normed * normed, axis=-1, keepdims=True))


def dot(left, right):
    return jnp.dot(left, right, preferred_element_type=jnp.float32)


def contract_rows(left, right):
    return lax.dot_general(
        left, right, (((0,), (0,)), ((), ())), preferred_element_type=jnp.float32
    )


def contract_cols(left, right):
    return lax.dot_general(
        left, right, (((1,), (1,)), ((), ())), preferred_element_type=jnp.float32
    )


def flip(me, k):
    out, bit = me, 1
    while bit <= k:
        if k & bit:
            out = out + bit * (1 - 2 * ((me // bit) % 2))
        bit *= 2
    return out


def greet(axis, me, others):
    barrier = pltpu.get_barrier_semaphore()
    for k in others:
        pl.semaphore_signal(barrier, inc=1, device_id={axis: flip(me, k)}, device_id_type=MESH)
    pl.semaphore_wait(barrier, len(others))


class Flow:
    def __init__(self, me, source, spot, half, send, recv):
        self.me, self.source, self.spot, self.half = me, source, spot, half
        self.send, self.recv, self.moves = send, recv, []

    def go(self, origin, target, k, part):
        if origin is None:
            source = self.source.at[pl.ds(part * self.half, self.half)]
        else:
            source = self.spot(flip(self.me, origin), part)
        copy = pltpu.make_async_remote_copy(
            src_ref=source,
            dst_ref=self.spot(flip(flip(self.me, target), k), part),
            send_sem=self.send.at[k, part],
            recv_sem=self.recv.at[k, part],
            device_id={"wide": flip(self.me, target)},
            device_id_type=MESH,
        )
        copy.start()
        self.moves.append(copy)

    def arrived(self, k, part):
        block = self.spot(flip(self.me, k), part)
        pltpu.make_async_copy(block, block, self.recv.at[k, part]).wait()

    def finish(self):
        for copy in self.moves:
            copy.wait_send()


class Sums:
    def __init__(self, width, me, out_ref, refs):
        self.width, self.me, self.out = width, me, out_ref
        (self.odd, self.even, self.from_twin, self.from_far, self.passing, self.sends, self.recvs,
         self.pass_send, self.pass_recv, self.twin_send, self.twin_recv) = refs
        self.half = out_ref.shape[0] // 2

    def rows(self, part):
        return pl.ds(part * self.half, self.half)

    def copy(self, src, dst, send, recv, k):
        return pltpu.make_async_remote_copy(
            src_ref=src, dst_ref=dst, send_sem=send, recv_sem=recv,
            device_id={"wide": flip(self.me, k)}, device_id_type=MESH,
        )

    def twin(self, k, part):
        i, at = k // 2, self.rows(part)
        return self.copy(
            self.odd.at[i, at], self.from_twin.at[i, at], self.twin_send.at[i, part],
            self.twin_recv.at[i, part], 1,
        )

    def far(self, k, part):
        i, at = k // 2 - 1, self.rows(part)
        return self.copy(
            self.even.at[i, at], self.from_far.at[i, at], self.sends.at[i, part], self.recvs.at[i, part], k
        )

    def relay(self, part):
        return self.copy(
            self.even.at[2, self.rows(part)], self.passing.at[part], self.pass_send.at[part],
            self.pass_recv.at[part], 2 if part == 0 else 4,
        )

    def give(self, k):
        self.twin(k, 0).start()
        self.twin(k, 1).start()

    def got(self, k):
        self.twin(k, 0).wait_recv()
        self.twin(k, 1).wait_recv()

    def pass_on(self, k, part):
        self.relay(part).wait_recv()
        at = self.rows(part)
        self.even[k // 2 - 1, at, :] = (
            self.even[k // 2 - 1, at, :].astype(jnp.float32) + self.passing[part].astype(jnp.float32)
        ).astype(jnp.bfloat16)
        self.far(k, part).start()

    def finish(self):
        sources = [2, 4] if self.width == 8 else list(range(2, self.width, 2))
        for k in sources:
            for part in (0, 1):
                self.far(k, part).wait_recv()
        extra = self.from_far[sources[0] // 2 - 1].astype(jnp.float32)
        for k in sources[1:]:
            extra = extra + self.from_far[k // 2 - 1].astype(jnp.float32)
        self.out[...] = self.out[...] + extra
        for part in (0, 1):
            for k in sources:
                self.far(k, part).wait_send()
            for k in range(0, self.width, 2):
                self.twin(k, part).wait_send()
            if self.width == 8:
                self.relay(part).wait_send()


def run_sums(width, sums, produce, beside=None, steps=0):
    half = sums.half
    rows = 2 * half

    def give(k, part=None):
        if part is None:
            produce(k + 1, 0, rows, sums.odd.at[k // 2])
            sums.give(k)
        else:
            produce(k + 1, part * half, half, sums.odd.at[k // 2, sums.rows(part)])
            sums.twin(k, part).start()

    def merge(k, part=None):
        if part is None:
            sums.got(k)
            produce(k, 0, rows, sums.even.at[k // 2 - 1], (sums.from_twin.at[k // 2],))
        else:
            sums.twin(k, part).wait_recv()
            at = sums.rows(part)
            produce(k, part * half, half, sums.even.at[k // 2 - 1, at], (sums.from_twin.at[k // 2, at],))

    if width == 8:
        give(6, 0)
        give(6, 1)
        merge(6, 0)
        sums.relay(0).start()
        merge(6, 1)
        sums.relay(1).start()
        give(2)
        give(4)
        merge(2)
        sums.far(2, 0).start()
        merge(4)
        sums.far(4, 1).start()
        sums.pass_on(2, 1)
        sums.pass_on(4, 0)
        give(0)
    else:
        for k in range(0, width, 2):
            give(k)
        for k in range(2, width, 2):
            merge(k)
            sums.far(k, 0).start()
            sums.far(k, 1).start()
    if beside is not None:
        beside(0, steps)
    sums.got(0)
    produce(0, 0, rows, sums.out, (sums.from_twin.at[0],))
    sums.finish()


def sum_scratch(width, rows, cols):
    chips, dma = width // 2, pltpu.SemaphoreType.DMA
    block = lambda n: pltpu.VMEM((n, rows, cols), jnp.bfloat16)
    return [
        block(chips), block(chips - 1), block(chips), block(2 if width == 8 else chips - 1),
        pltpu.VMEM((2, rows // 2, cols), jnp.bfloat16),
        dma((chips - 1, 2)), dma((chips - 1, 2)), dma((2,)), dma((2,)), dma((chips, 2)), dma((chips, 2)),
    ]


def wide_peers(width, me):
    return [{"wide": flip(me, k)} for k in [1] + list(range(2, width, 2))]


def local_copies(pairs, sem):
    return [pltpu.make_async_copy(src, dst, sem.at[i]) for i, (src, dst) in enumerate(pairs)]


def gather_body(width, slots, side, *refs):
    if side is None:
        x_ref, out_ref, here, send, recv = refs
    else:
        x_ref, side_ref, out_ref, side_out, here, send, recv, side_send, side_recv = refs
    me = lax.axis_index("wide")
    rows = x_ref.shape[0]
    half = rows // 2
    evens = list(range(2, width, 2))
    peers = [{"wide": flip(me, k)} for k in [1] + evens]
    if side is not None:
        hops = Hops(width // slots, slots, rows)
        peers = peers + [{"blk": (hops.plane + k) % hops.planes} for k in range(1, hops.planes)]
    hello(peers)
    if side is not None:
        job = hops.join if side == "join" else hops.spread
        job(side_ref, side_out, side_send, side_recv, True, True)

    def spot(who, first, count):
        base = ((who % slots) * (width // slots) + who // slots) * rows
        return out_ref.at[pl.ds(pl.multiple_of(base + first, half), count)]

    def move(origin, target, k, part):
        if origin is None:
            source = x_ref.at[pl.ds(part * half, half)]
        else:
            source = spot(flip(me, origin), part * half, half)
        return pltpu.make_async_remote_copy(
            src_ref=source,
            dst_ref=spot(flip(flip(me, target), k), part * half, half),
            send_sem=send.at[k, part],
            recv_sem=recv.at[k, part],
            device_id={"wide": flip(me, target)},
            device_id_type=MESH,
        )

    def arrived(k, part):
        block = spot(flip(me, k), part * half, half)
        pltpu.make_async_copy(block, block, recv.at[k, part]).wait()

    moves = []

    def go(origin, target, k, part):
        copy = move(origin, target, k, part)
        copy.start()
        moves.append(copy)

    mine = pltpu.make_async_copy(x_ref, spot(me, 0, rows), here)
    mine.start()
    if width == 8:
        go(None, 2, 2, 0)
        go(None, 4, 4, 1)
        go(None, 2, 2, 1)
        go(None, 4, 4, 0)
        go(None, 1, 1, 0)
        go(None, 1, 1, 1)
        arrived(2, 0)
        go(2, 4, 6, 0)
        go(2, 1, 3, 0)
        arrived(4, 1)
        go(4, 2, 6, 1)
        go(4, 1, 5, 1)
        order = [(2, 1), (4, 0), (6, 0), (6, 1)]
    else:
        for k in evens:
            go(None, k, k, 0)
            go(None, k, k, 1)
        go(None, 1, 1, 0)
        go(None, 1, 1, 1)
        order = [(k, part) for k in evens for part in (0, 1)]
    for k, part in order:
        arrived(k, part)
        go(k, 1, k + 1, part)
    for k in range(1, width, 2):
        for part in (0, 1):
            arrived(k, part)
    for copy in moves:
        copy.wait_send()
    mine.wait()
    if side is not None:
        job(side_ref, side_out, side_send, side_recv, True, False)


def gather(x, width, slots, ident, name, side=None, side_x=None):
    rows, cols = x.shape
    planes = width // slots
    dma = pltpu.SemaphoreType.DMA
    shapes = [jax.ShapeDtypeStruct((rows * width, cols), x.dtype)]
    scratch = [dma, dma((width, 2)), dma((width, 2))]
    inputs = [x]
    if side is not None:
        inputs.append(side_x)
        extent = rows if side == "join" else many_rows(planes, rows)
        shapes.append(jax.ShapeDtypeStruct((extent, cols), side_x.dtype))
        scratch += [dma((planes,)), dma((planes,))]
    outs = pl.pallas_call(
        functools.partial(gather_body, width, slots, side),
        out_shape=shapes,
        in_specs=[pl.BlockSpec(memory_space=pl.ANY)] * len(inputs),
        out_specs=[pl.BlockSpec(memory_space=pl.ANY)] * len(shapes),
        scratch_shapes=scratch,
        cost_estimate=busy(10),
        compiler_params=pltpu.CompilerParams(collective_id=ident, has_side_effects=True, vmem_limit_bytes=VMEM_LIMIT),
        name=name,
    )(*inputs)
    return outs[0] if side is None else outs


def scatter_body(width, slots, flat, count, step, finish, *refs):
    lefts, rights = refs[:count], refs[count : 2 * count]
    if finish == "norm":
        x_ref, gain_ref, hidden_ref, low_ref, out_ref, inv_ref = refs[2 * count : 2 * count + 6]
        rest = refs[2 * count + 6 :]
    else:
        more_ref, low_ref, out_ref = refs[2 * count : 2 * count + 3]
        rest = refs[2 * count + 3 :]
    me = lax.axis_index("wide")
    rows, cols = out_ref.shape
    hello(wide_peers(width, me))
    sums = Sums(width, me, out_ref, rest)
    dims = (((1,), (1 if flat else 0,)), ((), ()))

    def produce(k, first, some, put, adds=()):
        who = flip(me, k)
        start = ((who % slots) * (width // slots) + who // slots) * rows + first
        start = pl.multiple_of(start, rows // 2)

        def tile(n, carry):
            at = pl.ds(pl.multiple_of(n * step, step), step)
            total = None
            for left, right in zip(lefts, rights):
                other = right[at, :] if flat else right[:, at]
                term = lax.dot_general(
                    left[pl.ds(start, some), :], other, dims, preferred_element_type=jnp.float32
                )
                total = term if total is None else total + term
            for ref in adds:
                total = total + ref[:, at].astype(jnp.float32)
            put[:, at] = total.astype(put.dtype)
            return carry

        lax.fori_loop(0, cols // step, tile, 0)

    run_sums(width, sums, produce)
    if finish == "add":
        def close(n, carry):
            at = pl.ds(pl.multiple_of(n * 32, 32), 32)
            low_ref[at, :] = (out_ref[at, :] + more_ref[at, :]).astype(low_ref.dtype)
            return carry

        lax.fori_loop(0, rows // 32, close, 0)
    if finish != "norm":
        return
    few = 32

    def norm(n, carry):
        at = pl.ds(pl.multiple_of(n * few, few), few)
        value = out_ref[at, :]
        inverse = lax.rsqrt(jnp.sum(value * value, axis=-1, keepdims=True) * (1.0 / cols) + EPS)
        value = value * inverse
        out_ref[at, :] = value
        inv_ref[at, :] = inverse
        hidden = x_ref[at, :].astype(jnp.float32) + value * gain_ref[...]
        hidden_ref[at, :] = hidden
        low_ref[at, :] = hidden.astype(low_ref.dtype)
        return carry

    lax.fori_loop(0, rows // few, norm, 0)


def scatter(lefts, rights, width, slots, flat, ident, name, finish, more, step=1024):
    rows = lefts[0].shape[0] // width
    cols = rights[0].shape[0 if flat else 1]
    f32, vmem = jnp.float32, pl.BlockSpec(memory_space=pltpu.VMEM)
    whole, low = jax.ShapeDtypeStruct((rows, cols), f32), jax.ShapeDtypeStruct((rows, cols), lefts[0].dtype)
    shapes = [whole, low, whole, jax.ShapeDtypeStruct((rows, 1), f32)] if finish == "norm" else [low]
    scratch = sum_scratch(width, rows, cols)
    if finish == "add":
        scratch = [pltpu.VMEM((rows, cols), f32)] + scratch
    outs = pl.pallas_call(
        functools.partial(scatter_body, width, slots, flat, len(lefts), step, finish),
        out_shape=shapes,
        in_specs=[vmem] * (2 * len(lefts) + len(more)),
        out_specs=[vmem] * len(shapes),
        scratch_shapes=scratch,
        cost_estimate=busy(10),
        compiler_params=pltpu.CompilerParams(collective_id=ident, has_side_effects=True, vmem_limit_bytes=VMEM_LIMIT),
        name=name,
    )(*lefts, *rights, *more)
    return outs if finish == "norm" else outs[0]


def total_body(axis, width, x_ref, out_ref, slots, send, recv):
    me = lax.axis_index(axis)
    others = list(range(1, width))
    greet(axis, me, others)
    moves = []
    for k in others:
        copy = pltpu.make_async_remote_copy(
            src_ref=x_ref,
            dst_ref=slots.at[k - 1],
            send_sem=send.at[k - 1],
            recv_sem=recv.at[k - 1],
            device_id={axis: flip(me, k)},
            device_id_type=MESH,
        )
        copy.start()
        moves.append(copy)
    out_ref[...] = x_ref[...]
    for copy, k in zip(moves, others):
        copy.wait_recv()
        out_ref[...] = out_ref[...] + slots[k - 1]
    for copy in moves:
        copy.wait_send()


def total(x, axis, width, ident, name):
    return pl.pallas_call(
        functools.partial(total_body, axis, width),
        out_shape=jax.ShapeDtypeStruct(x.shape, x.dtype),
        in_specs=[pl.BlockSpec(memory_space=pltpu.VMEM)],
        out_specs=pl.BlockSpec(memory_space=pltpu.VMEM),
        scratch_shapes=[
            pltpu.VMEM((width - 1,) + x.shape, x.dtype),
            pltpu.SemaphoreType.DMA((width - 1,)),
            pltpu.SemaphoreType.DMA((width - 1,)),
        ],
        cost_estimate=busy(7),
        compiler_params=pltpu.CompilerParams(collective_id=ident, has_side_effects=True, vmem_limit_bytes=VMEM_LIMIT),
        name=name,
    )(x)


class Hops:
    def __init__(self, planes, slots, rows):
        self.planes, self.slots = planes, slots
        self.count = max(n for n in range(1, planes + 1) if planes % n == 0 and rows % (16 * n) == 0)
        self.per = planes // self.count
        self.piece = rows // self.count
        self.plane, self.place = lax.axis_index("blk"), lax.axis_index("wide")
        self.chip, self.slot = self.place // slots, self.place % slots
        self.active = self.chip // self.count == self.plane % self.per

    def peers(self):
        near = [{"wide": (self.chip + k) % self.planes * self.slots + self.slot} for k in range(1, self.planes)]
        return near + [{"blk": (self.plane + k) % self.planes} for k in range(1, self.planes)]

    def when(self, condition, action):
        if self.per == 1:
            action()
        else:
            pl.when(condition)(action)

    def split(self, condition, yes, no):
        if self.per == 1:
            yes()
        else:
            pl.when(condition)(yes)
            pl.when(jnp.logical_not(condition))(no)

    def cut(self, ref, index):
        return ref.at[pl.ds(pl.multiple_of(index * self.piece, self.piece), self.piece)]

    def remote(self, src, dst, send, recv, device):
        return pltpu.make_async_remote_copy(
            src_ref=src, dst_ref=dst, send_sem=send, recv_sem=recv, device_id=device, device_id_type=MESH
        )

    def spread(self, some, many, send, recv, across, start):
        if across:
            axis, here = "blk", self.plane
            targets = [
                ((self.plane // self.per + k) % self.count) for k in range(self.count)
            ]
            device = lambda piece: piece * self.per + self.chip // self.count
        else:
            axis, here = "wide", self.chip
            targets = [((self.chip + k) % self.count) for k in range(self.count)]
            device = lambda piece: (self.plane % self.per) * self.count + piece
        address = (lambda who: {"blk": who}) if across else (
            lambda who: {"wide": who * self.slots + self.slot}
        )
        for k, piece in enumerate(targets):
            who = device(piece)
            far = self.remote(
                self.cut(some, piece), self.cut(many, here), send.at[piece],
                recv.at[(here - who + self.planes) % self.planes], address(who),
            )
            own = pltpu.make_async_copy(self.cut(some, piece), self.cut(many, here), send.at[piece])
            if k:
                far.start() if start else far.wait_send()
            elif start:
                self.split(self.active, own.start, far.start)
            else:
                self.split(self.active, own.wait, far.wait_send)
        if not start:
            def receive():
                for k in range(1, self.planes):
                    block = self.cut(many, (here + k) % self.planes)
                    pltpu.make_async_copy(block, block, recv.at[k]).wait()

            self.when(self.active, receive)

    def join(self, many, some, send, recv, across, start, ready=None):
        if across:
            here = self.plane
            index = self.plane // self.per
            address = lambda who: {"blk": who}
        else:
            here = self.chip
            index = self.chip % self.count
            address = lambda who: {"wide": who * self.slots + self.slot}

        def give():
            for k in list(range(1, self.planes)) + [0]:
                who = (here + k) % self.planes
                if ready is not None:
                    ready(who)
                if k:
                    copy = self.remote(
                        self.cut(many, who), self.cut(some, index), send.at[k], recv.at[index], address(who)
                    )
                    copy.start() if start else copy.wait_send()
                else:
                    own = pltpu.make_async_copy(self.cut(many, here), self.cut(some, index), send.at[0])
                    own.start() if start else own.wait()

        self.when(self.active, give)
        if not start:
            for k in range(self.count):
                piece = (index + k) % self.count
                block = self.cut(some, piece)
                arrival = pltpu.make_async_copy(block, block, recv.at[piece])
                if k:
                    arrival.wait()
                elif self.per > 1:
                    pl.when(jnp.logical_not(self.active))(arrival.wait)

    def arrival(self, some, many, send, recv, across):
        here = self.plane if across else self.chip
        own_piece = self.plane // self.per if across else self.chip % self.count

        def ready(who):
            block = self.cut(many, who)

            @pl.when(who == here)
            def _():
                pltpu.make_async_copy(self.cut(some, own_piece), block, send.at[own_piece]).wait()

            @pl.when(who != here)
            def _():
                pltpu.make_async_copy(block, block, recv.at[(who - here + self.planes) % self.planes]).wait()

        return ready

    def sent(self, some, many, send, across):
        pieces = self.plane // self.per if across else self.chip
        for k in range(self.count):
            piece = (pieces + k) % self.count
            block = self.cut(some, piece)
            out = pltpu.make_async_copy(block, block, send.at[piece])
            if k:
                out.wait()
            elif self.per > 1:
                pl.when(jnp.logical_not(self.active))(out.wait)


def hello(peers):
    barrier = pltpu.get_barrier_semaphore()
    for peer in peers:
        pl.semaphore_signal(barrier, inc=1, device_id=peer, device_id_type=MESH)
    pl.semaphore_wait(barrier, len(peers))


def turn_in_body(planes, slots, x_ref, c_ref, near_x, near_c, out_ref, *sems):
    hops = Hops(planes, slots, x_ref.shape[0])
    hello(hops.peers())
    hops.spread(x_ref, near_x, sems[0], sems[1], False, True)
    ready = hops.arrival(x_ref, near_x, sems[0], sems[1], False)
    hops.join(near_x, out_ref, sems[2], sems[3], True, True, ready)
    hops.sent(x_ref, near_x, sems[0], False)
    hops.spread(c_ref, near_c, sems[4], sems[5], False, True)
    hops.spread(c_ref, near_c, sems[4], sems[5], False, False)
    hops.join(near_x, out_ref, sems[2], sems[3], True, False)


def turn_out_body(planes, slots, x_ref, far_c, v_ref, far_x, out_c, out_ref, v_out, *sems):
    hops = Hops(planes, slots, x_ref.shape[0])
    hello(hops.peers())
    parts, send, recv = sems[6:]
    moves = []
    for k in range(1, planes):
        copy = hops.remote(
            v_ref, parts.at[planes - k - 1], send.at[k - 1], recv.at[planes - k - 1],
            {"blk": (hops.plane + k) % planes},
        )
        copy.start()
        moves.append(copy)
    hops.spread(x_ref, far_x, sems[0], sems[1], True, True)
    hops.join(far_c, out_c, sems[2], sems[3], False, True)
    ready = hops.arrival(x_ref, far_x, sems[0], sems[1], True)
    hops.join(far_x, out_ref, sems[4], sems[5], False, True, ready)
    hops.sent(x_ref, far_x, sems[0], True)
    amount = v_ref[...]
    for k in range(1, planes):
        block = parts.at[k - 1]
        pltpu.make_async_copy(block, block, recv.at[k - 1]).wait()
        amount = amount + parts[k - 1]
    v_out[...] = amount
    for copy in moves:
        copy.wait_send()
    hops.join(far_c, out_c, sems[2], sems[3], False, False)
    hops.join(far_x, out_ref, sems[4], sems[5], False, False)


def many_rows(planes, rows):
    count = max(n for n in range(1, planes + 1) if planes % n == 0 and rows % (16 * n) == 0)
    return planes * (rows // count)


def turn(body, inputs, outputs, planes, slots, ident, name, extra=None):
    rows, cols = inputs[0].shape
    low = inputs[0].dtype
    dma = pltpu.SemaphoreType.DMA
    shape = lambda many: jax.ShapeDtypeStruct((many_rows(planes, rows) if many else rows, cols), low)
    anywhere, vmem = pl.BlockSpec(memory_space=pl.ANY), pl.BlockSpec(memory_space=pltpu.VMEM)
    more = [] if extra is None else [extra]
    scratch = [dma((planes,))] * 6
    for value in more:
        scratch += [pltpu.VMEM((planes - 1,) + value.shape, value.dtype), dma((planes - 1,)), dma((planes - 1,))]
    return pl.pallas_call(
        functools.partial(body, planes, slots),
        out_shape=[shape(many) for many in outputs] + [jax.ShapeDtypeStruct(v.shape, v.dtype) for v in more],
        in_specs=[anywhere] * len(inputs) + [vmem] * len(more),
        out_specs=[anywhere] * len(outputs) + [vmem] * len(more),
        scratch_shapes=scratch,
        cost_estimate=busy(10),
        compiler_params=pltpu.CompilerParams(collective_id=ident, has_side_effects=True, vmem_limit_bytes=VMEM_LIMIT),
        name=name,
    )(*inputs, *more)


def mask_scores(scores, first, begin, size):
    span = scores.shape[0]
    index = lax.broadcasted_iota(jnp.int32, scores.shape, 0)
    query = lax.broadcasted_iota(jnp.int32, scores.shape, 1) + first
    return jnp.where((index <= query) & (index >= begin), scores, NEG_FILL)


def nt(left, right):
    return lax.dot_general(left, right, (((1,), (1,)), ((), ())), preferred_element_type=jnp.float32)


def nn(left, right):
    return jnp.dot(left, right, preferred_element_type=jnp.float32)


def piece_map(span, size):
    planes = span // size
    count = max(n for n in range(1, planes + 1) if planes % n == 0 and size % (16 * n) == 0)
    per, piece = planes // count, size // count
    pairs = []
    for t in range(count):
        for high in range(per):
            for low in range(count):
                natural = ((t * per + high) * count + low) * piece
                pairs.append((natural, ((high * count + low) * count + t) * piece))
    return pairs, piece


def attend_body(size, q_ref, k_ref, v_ref, inv_ref, gain_ref, cos_ref, sin_ref, begin_ref,
                qo_ref, ko_ref, vo_ref, mix_ref, log_ref):
    low = jnp.bfloat16
    span = q_ref.shape[0]

    def prepare(ref, col):
        value = ref[...] * inv_ref[:, col : col + 1] * gain_ref[col : col + 1, :]
        return (value * cos_ref[...] + pltpu.roll(value, HD // 2, 1) * sin_ref[...]).astype(low)

    pairs, piece = piece_map(span, size)

    def arrange(ref, value):
        for natural, block in pairs:
            ref[natural : natural + piece, :] = value[block : block + piece, :]

    arrange(qo_ref, prepare(q_ref, 0))
    arrange(ko_ref, prepare(k_ref, 1))
    arrange(vo_ref, v_ref[...].astype(low))
    flipped = vo_ref[...].astype(jnp.float32).T.astype(low)
    for i in range(span // size):
        last = (i + 1) * size
        cols = slice(i * size, last)
        scores = nt(ko_ref[:last, :], qo_ref[cols, :]) * SCALE
        scores = mask_scores(scores, i * size, begin_ref[:, cols], size)
        top = jnp.max(scores, axis=0, keepdims=True)
        raw = jnp.exp(scores - top)
        weight = jnp.sum(raw, axis=0, keepdims=True)
        mixed = nn(flipped[:, :last], raw.astype(low)) * (1.0 / weight)
        mixed = mixed.T.astype(low)
        for natural, block in pairs:
            if i * size <= natural < last:
                at = natural - i * size
                mix_ref[block : block + piece, :] = mixed[at : at + piece, :]
        log_ref[:, cols] = top + jnp.log(weight)


def attend(pre, rows, inverse, gains, cosine, sine, begin, heads, size):
    slots, span, _ = pre.shape
    low, f32 = jnp.bfloat16, jnp.float32
    head = lambda offset: pl.BlockSpec((None, span, HD), lambda g, h: (g, 0, offset + h))
    every = lambda cols: pl.BlockSpec((None, span, cols), lambda g, h: (g, 0, 0))
    line = pl.BlockSpec((None, 1, span), lambda g, h: (g, 0, 0))
    out = jax.ShapeDtypeStruct((slots, span, heads * HD), low)
    return pl.pallas_call(
        functools.partial(attend_body, size),
        grid=(slots, heads),
        out_shape=[out, out, out, out, jax.ShapeDtypeStruct((slots, heads, 1, span), f32)],
        in_specs=[
            head(0), head(heads), head(0), every(2),
            pl.BlockSpec((2, HD), lambda g, h: (0, h)), every(HD), every(HD), line,
        ],
        out_specs=[head(0)] * 4 + [pl.BlockSpec((None, None, 1, span), lambda g, h: (g, h, 0, 0))],
        compiler_params=pltpu.CompilerParams(vmem_limit_bytes=VMEM_LIMIT),
        cost_estimate=busy(5),
        name="attend",
    )(pre, pre, rows, inverse, gains, cosine, sine, begin)


def attend_back_body(size, q_ref, k_ref, v_ref, g_ref, log_ref, qp_ref, kp_ref, inv_ref, gain_ref,
                     cos_ref, sin_ref, begin_ref, sq_ref, sk_ref, gv_ref, sums_ref, part_ref,
                     keys_sum, values_sum, queries_sum, held, g_held):
    low = jnp.bfloat16
    span = q_ref.shape[0]
    pairs, piece = piece_map(span, size)
    for natural, block in pairs:
        g_held[natural : natural + piece, :] = g_ref[block : block + piece, :]
    flipped = k_ref[...].astype(jnp.float32).T.astype(low)
    keys_sum[...] = jnp.zeros_like(keys_sum)
    values_sum[...] = jnp.zeros_like(values_sum)
    for i in range(span // size):
        last = (i + 1) * size
        cols = slice(i * size, last)
        scores = nt(k_ref[:last, :], q_ref[cols, :]) * SCALE
        scores = mask_scores(scores, i * size, begin_ref[:, cols], size)
        probs = jnp.exp(scores - log_ref[:, cols])
        grad_probs = nt(v_ref[:last, :], g_held[cols, :])
        delta = jnp.sum(probs * grad_probs, axis=0, keepdims=True)
        grad_scores = (probs * (grad_probs - delta)).astype(low)
        values_sum[:last, :] += nn(probs.astype(low), g_held[cols, :])
        keys_sum[:last, :] += nn(grad_scores, q_ref[cols, :])
        queries_sum[cols, :] = nn(flipped[:, :last], grad_scores).T

    def finish(total_ref, pre_ref, out_ref, col):
        for natural, block in pairs:
            held[block : block + piece, :] = total_ref[natural : natural + piece, :]
        grad = held[...] * SCALE
        back = grad * cos_ref[...] - pltpu.roll(grad, HD // 2, 1) * sin_ref[...]
        normed = pre_ref[...] * inv_ref[:, col : col + 1]
        part_ref[col : col + 1, :] = jnp.sum(back * normed, axis=0, keepdims=True)
        scaled = back * gain_ref[col : col + 1, :]
        out_ref[...] = scaled
        sums_ref[:, col : col + 1] = jnp.sum(scaled * normed, axis=1, keepdims=True)

    finish(queries_sum, qp_ref, sq_ref, 0)
    finish(keys_sum, kp_ref, sk_ref, 1)
    for natural, block in pairs:
        gv_ref[block : block + piece, :] = values_sum[natural : natural + piece, :].astype(low)


def attend_back(queries, keys, values, grads, logs, pre, inverse, gains, cosine, sine, begin, heads, size):
    slots, span, _ = pre.shape
    low, f32 = jnp.bfloat16, jnp.float32
    head = lambda offset: pl.BlockSpec((None, span, HD), lambda g, h: (g, 0, offset + h))
    every = lambda cols: pl.BlockSpec((None, span, cols), lambda g, h: (g, 0, 0))
    line = pl.BlockSpec((None, 1, span), lambda g, h: (g, 0, 0))
    wide = jax.ShapeDtypeStruct((slots, span, heads * HD), f32)
    return pl.pallas_call(
        functools.partial(attend_back_body, size),
        grid=(slots, heads),
        out_shape=[
            wide, wide, jax.ShapeDtypeStruct((slots, span, heads * HD), low),
            jax.ShapeDtypeStruct((heads, slots, span, 2), f32),
            jax.ShapeDtypeStruct((slots, 2, heads * HD), f32),
        ],
        in_specs=[
            head(0), head(0), head(0), head(0),
            pl.BlockSpec((None, None, 1, span), lambda g, h: (g, h, 0, 0)),
            head(0), head(heads), every(2),
            pl.BlockSpec((2, HD), lambda g, h: (0, h)), every(HD), every(HD), line,
        ],
        out_specs=[
            head(0), head(0), head(0),
            pl.BlockSpec((None, None, span, 2), lambda g, h: (h, g, 0, 0)),
            pl.BlockSpec((None, 2, HD), lambda g, h: (g, 0, h)),
        ],
        scratch_shapes=[pltpu.VMEM((span, HD), f32)] * 4 + [pltpu.VMEM((span, HD), low)],
        compiler_params=pltpu.CompilerParams(vmem_limit_bytes=VMEM_LIMIT),
        cost_estimate=busy(5),
        name="attend_back",
    )(queries, keys, values, grads, logs, pre, pre, inverse, gains, cosine, sine, begin)


def row_sums(value):
    return jnp.sum(value.reshape(-1, 8, value.shape[-1]), axis=0)


def feed_body(width, slots, step, h_ref, c_ref, wg_hbm, wu_hbm, wd_hbm, hidden_ref, gain_ref, block_ref,
              first_ref, second_ref, gain_out, all_ref, act_ref, one_ref, two_ref, c_out, buf, wg, wu, wd, stage, out_ref,
              c_held, here, load, send, recv, side_send, side_recv, store, keep, *sum_refs):
    me = lax.axis_index("wide")
    planes = width // slots
    rows, cols = h_ref.shape
    hidden = wg.shape[1]
    half = rows // 2
    low = jnp.bfloat16
    loads = local_copies([(wg_hbm, wg), (wu_hbm, wu), (wd_hbm, wd)], load)
    mine = pltpu.make_async_copy(h_ref, buf.at[me], here)
    mine.start()
    for copy in loads:
        copy.start()
    hops = Hops(planes, slots, rows)
    hello(wide_peers(width, me) + [{"blk": (hops.plane + k) % planes} for k in range(1, planes)])
    flow = Flow(me, h_ref, lambda who, part: buf.at[who, pl.ds(part * half, half)], half, send, recv)
    sums = Sums(width, me, out_ref, sum_refs)
    outs = (act_ref, one_ref, two_ref)
    pending = [[], []]
    turn_count = [0]
    kept = []

    def where(k):
        who = flip(me, k)
        return pl.multiple_of(((who % slots) * planes + who // slots) * rows, rows)

    def keep_block(k):
        copy = pltpu.make_async_copy(buf.at[flip(me, k)], all_ref.at[pl.ds(where(k), rows)], keep.at[k])
        copy.start()
        kept.append(copy)

    def work(k, part, put, adds=()):
        first, count = (0, rows) if part is None else (part * half, half)
        slot = turn_count[0] % 2
        turn_count[0] += 1
        for copy in pending[slot]:
            copy.wait()
        block = buf.at[flip(me, k), pl.ds(first, count)]
        act, one, two = (stage.at[slot, i, pl.ds(0, count)] for i in range(3))

        def inner(n, carry):
            at = pl.ds(pl.multiple_of(n * step, step), step)
            gate = jnp.dot(block[...], wg[:, at], preferred_element_type=jnp.float32)
            upward = jnp.dot(block[...], wu[:, at], preferred_element_type=jnp.float32)
            sigmoid = jax.nn.sigmoid(gate)
            silu = gate * sigmoid
            act[:, at] = (silu * upward).astype(low)
            one[:, at] = silu.astype(low)
            two[:, at] = (upward * (sigmoid + silu * (1.0 - sigmoid))).astype(low)
            return carry

        lax.fori_loop(0, hidden // step, inner, 0)
        target = pl.ds(pl.multiple_of(where(k) + first, half), count)
        pending[slot] = []
        for i, ref in enumerate(outs):
            copy = pltpu.make_async_copy(stage.at[slot, i, pl.ds(0, count)], ref.at[target], store.at[slot, i])
            copy.start()
            pending[slot].append(copy)
        broad = 2 * step

        def outer(n, carry):
            at = pl.ds(pl.multiple_of(n * broad, broad), broad)
            total = jnp.dot(act[...], wd[:, at], preferred_element_type=jnp.float32)
            for ref in adds:
                total = total + ref[:, at].astype(jnp.float32)
            put[:, at] = total.astype(put.dtype)
            return carry

        lax.fori_loop(0, cols // broad, outer, 0)

    def odd_work(k, part):
        if part is None:
            work(k + 1, None, sums.odd.at[k // 2])
            sums.give(k)
        else:
            work(k + 1, part, sums.odd.at[k // 2, sums.rows(part)])
            sums.twin(k, part).start()

    def even_work(k, part):
        i = k // 2
        if part is None:
            sums.got(k)
            work(k, None, sums.even.at[i - 1], (sums.from_twin.at[i],))
        else:
            sums.twin(k, part).wait_recv()
            at = sums.rows(part)
            work(k, part, sums.even.at[i - 1, at], (sums.from_twin.at[i, at],))

    if width == 8:
        flow.go(None, 2, 2, 0)
        flow.go(None, 4, 4, 1)
        flow.go(None, 1, 1, 0)
        flow.go(None, 1, 1, 1)
        hops.join(c_ref, c_out, side_send, side_recv, True, True)
        mine.wait()
        for copy in loads:
            copy.wait()
        work(0, None, out_ref)
        keep_block(0)
        flow.arrived(1, 0)
        flow.arrived(1, 1)
        keep_block(1)
        odd_work(0, None)
        flow.arrived(2, 0)
        flow.go(2, 4, 6, 0)
        flow.arrived(4, 1)
        flow.go(4, 2, 6, 1)
        flow.go(2, 1, 3, 0)
        flow.go(4, 1, 5, 1)
        flow.go(None, 2, 2, 1)
        flow.go(None, 4, 4, 0)
        flow.arrived(3, 0)
        odd_work(2, 0)
        flow.arrived(5, 1)
        odd_work(4, 1)
        even_work(2, 0)
        even_work(4, 1)
        for part in (0, 1):
            flow.arrived(6, part)
            flow.go(6, 1, 7, part)
        for part in (0, 1):
            flow.arrived(7, part)
        keep_block(6)
        keep_block(7)
        odd_work(6, None)
        even_work(6, None)
        sums.relay(0).start()
        sums.relay(1).start()
        flow.arrived(2, 1)
        flow.go(2, 1, 3, 1)
        flow.arrived(4, 0)
        flow.go(4, 1, 5, 0)
        sums.far(2, 0).start()
        sums.far(4, 1).start()
        flow.arrived(3, 1)
        odd_work(2, 1)
        flow.arrived(5, 0)
        odd_work(4, 0)
        for k in (2, 3, 4, 5):
            keep_block(k)
        even_work(2, 1)
        sums.pass_on(2, 1)
        even_work(4, 0)
        sums.pass_on(4, 0)
    else:
        hops.join(c_ref, c_out, side_send, side_recv, True, True)
        for k in range(2, width, 2):
            flow.go(None, k, k, 0)
            flow.go(None, k, k, 1)
        flow.go(None, 1, 1, 0)
        flow.go(None, 1, 1, 1)
        mine.wait()
        for copy in loads:
            copy.wait()
        work(0, None, out_ref)
        keep_block(0)
        flow.arrived(1, 0)
        flow.arrived(1, 1)
        keep_block(1)
        odd_work(0, None)
        for k in range(2, width, 2):
            for part in (0, 1):
                flow.arrived(k, part)
                flow.go(k, 1, k + 1, part)
            for part in (0, 1):
                flow.arrived(k + 1, part)
            keep_block(k)
            keep_block(k + 1)
            odd_work(k, None)
            even_work(k, None)
            sums.far(k, 0).start()
            sums.far(k, 1).start()
    sums.got(0)
    out_ref[...] = out_ref[...] + sums.from_twin[0].astype(jnp.float32)
    sums.finish()
    flow.finish()
    hops.join(c_ref, c_out, side_send, side_recv, True, False)
    held = pltpu.make_async_copy(c_out, c_held, here)
    held.start()
    held.wait()
    gain_out[...] = jnp.zeros_like(gain_out)
    few = 32
    own = cols // planes
    half_own = own // 2

    def norm(n, carry):
        at = pl.ds(pl.multiple_of(n * few, few), few)
        value = out_ref[at, :]
        inverse = lax.rsqrt(jnp.sum(value * value, axis=-1, keepdims=True) * (1.0 / cols) + EPS)
        normed = value * inverse
        block_ref[at, :] = (hidden_ref[at, :] + normed * gain_ref[...]).astype(low)
        grad = c_held[at, :].astype(jnp.float32)
        gain_out[...] = gain_out[...] + row_sums(grad * normed)
        grad = grad * gain_ref[...]
        mean = jnp.sum(grad * normed, axis=-1, keepdims=True) * (1.0 / cols)
        grad = (inverse * (grad - normed * mean)).astype(low)
        for b in range(planes):
            for side in (0, 1):
                first = b * own + side * half_own
                (first_ref, second_ref)[side][at, b * half_own : (b + 1) * half_own] = grad[:, first : first + half_own]
        return carry

    lax.fori_loop(0, rows // few, norm, 0)
    for copy in kept + pending[0] + pending[1]:
        copy.wait()


def feed(h, side_x, gate_weight, up_weight, down_weight, hidden, gain, width, slots, ident, name):
    rows, cols = h.shape
    inner = gate_weight.shape[1]
    low, f32, dma = h.dtype, jnp.float32, pltpu.SemaphoreType.DMA
    step = min(512, inner)
    anywhere, vmem = pl.BlockSpec(memory_space=pl.ANY), pl.BlockSpec(memory_space=pltpu.VMEM)
    saved = jax.ShapeDtypeStruct((rows * width, inner), low)
    return pl.pallas_call(
        functools.partial(feed_body, width, slots, step),
        out_shape=[
            jax.ShapeDtypeStruct((rows, cols), low), jax.ShapeDtypeStruct((rows, cols // 2), low),
            jax.ShapeDtypeStruct((rows, cols // 2), low),
            jax.ShapeDtypeStruct((8, cols), f32), jax.ShapeDtypeStruct((rows * width, cols), low),
            saved, saved, saved, jax.ShapeDtypeStruct((rows, cols), low),
        ],
        in_specs=[anywhere] * 5 + [vmem] * 2,
        out_specs=[vmem] * 4 + [anywhere] * 5,
        scratch_shapes=[
            pltpu.VMEM((width, rows, cols), low), pltpu.VMEM((cols, inner), low), pltpu.VMEM((cols, inner), low),
            pltpu.VMEM((inner, cols), low), pltpu.VMEM((2, 3, rows, inner), low),
            pltpu.VMEM((rows, cols), f32), pltpu.VMEM((rows, cols), low),
            dma, dma((3,)), dma((width, 2)), dma((width, 2)), dma((width // slots,)), dma((width // slots,)),
            dma((2, 3)), dma((width,)),
        ] + sum_scratch(width, rows, cols),
        cost_estimate=busy(90),
        compiler_params=pltpu.CompilerParams(collective_id=ident, has_side_effects=True, vmem_limit_bytes=VMEM_LIMIT),
        name=name,
    )(h, side_x, gate_weight, up_weight, down_weight, hidden, gain)


def push_body(second, width, slots, *refs):
    if second:
        (g_ref, act_hbm, wd_hbm, one_hbm, two_hbm, first_hbm, down_ref, gg_ref, gu_ref,
         buf, held, acts, here, send, recv, fetch, wd, before, ins, outs, load, take, store) = refs
    else:
        (g_ref, act_hbm, c_ref, down_ref, all_ref, c_out,
         buf, held, acts, here, send, recv, fetch, keep, side_send, side_recv) = refs
    me = lax.axis_index("wide")
    planes = width // slots
    pairs = width // 2
    rows, cols = g_ref.shape
    inner = down_ref.shape[0]
    half = rows // 2
    low = jnp.bfloat16
    mine = pltpu.make_async_copy(g_ref, buf.at[me // 2, me % 2], here)
    mine.start()

    def where(pair, side):
        who = flip(me // 2, pair) * 2 + side
        return pl.ds(pl.multiple_of(((who % slots) * planes + who // slots) * rows, rows), rows)

    def fetches(pair):
        copies = [
            pltpu.make_async_copy(act_hbm.at[where(pair, side)], acts.at[pair % 2, side], fetch.at[pair % 2, side])
            for side in (0, 1)
        ]
        if second:
            copies += [
                pltpu.make_async_copy(ref.at[where(pair, side)], ins.at[pair % 2, i, side], take.at[pair % 2, i, side])
                for i, ref in enumerate((one_hbm, two_hbm))
                for side in (0, 1)
            ]
        return copies

    def stores(pair):
        return [
            pltpu.make_async_copy(outs.at[pair % 2, i, side], ref.at[where(pair, side)], store.at[pair % 2, i, side])
            for i, ref in enumerate((gg_ref, gu_ref))
            for side in (0, 1)
        ]

    def keeps(pair):
        chip = flip(me // 2, pair)
        return pltpu.make_async_copy(buf.at[chip], all_ref.at[chip], keep.at[pair])

    for copy in fetches(0):
        copy.start()
    peers = wide_peers(width, me)
    if second:
        own = cols // planes
        loads = [
            pltpu.make_async_copy(
                wd_hbm.at[:, pl.ds((2 * b + side) * own, own)], wd.at[:, pl.ds(side * cols + b * own, own)],
                load.at[b, side],
            )
            for b in range(planes)
            for side in (0, 1)
        ]
        loads.append(pltpu.make_async_copy(first_hbm, before, load.at[planes, 0]))
        for copy in loads:
            copy.start()
    else:
        hops = Hops(planes, slots, rows)
        peers = peers + [{"blk": (hops.plane + k) % planes} for k in range(1, planes)]
    hello(peers)
    flow = Flow(me, g_ref, lambda who, part: buf.at[who // 2, who % 2, pl.ds(part * half, half)], half, send, recv)

    def work(pair):
        for copy in fetches(pair):
            copy.wait()
        if pair + 1 < pairs:
            for copy in fetches(pair + 1):
                copy.start()
        chip = flip(me // 2, pair)
        slot = pair % 2
        grads = buf[chip].reshape(2 * rows, cols)
        if second:
            if pair >= 2:
                for copy in stores(pair - 2):
                    copy.wait()
            old = before[chip].reshape(2 * rows, cols)
            step = min(512, inner)

            def units(n, carry):
                at = pl.ds(pl.multiple_of(n * step, step), step)
                grad = (nt(old, wd[at, :cols]) + nt(grads, wd[at, cols:])).reshape(2, rows, step)
                outs[slot, 0, :, :, at] = (grad * ins[slot, 1, :, :, at].astype(jnp.float32)).astype(low)
                outs[slot, 1, :, :, at] = (grad * ins[slot, 0, :, :, at].astype(jnp.float32)).astype(low)
                return carry

            lax.fori_loop(0, inner // step, units, 0)
            for copy in stores(pair):
                copy.start()
        else:
            keeps(pair).start()
        tall = min(512, inner)

        def outer(n, carry):
            at = pl.ds(pl.multiple_of(n * tall, tall), tall)
            act = acts[slot, :, :, at].reshape(2 * rows, tall)
            term = lax.dot_general(act, grads, (((0,), (0,)), ((), ())), preferred_element_type=jnp.float32)
            if pair:
                term = term + held[at, :]
            if pair + 1 < pairs:
                held[at, :] = term
            else:
                down_ref[at, :] = term.astype(low)
            return carry

        lax.fori_loop(0, inner // tall, outer, 0)

    def pair_ready(k):
        for part in (0, 1):
            flow.arrived(k + 1, part)

    if width == 8:
        flow.go(None, 2, 2, 0)
        flow.go(None, 4, 4, 1)
        flow.go(None, 2, 2, 1)
        flow.go(None, 4, 4, 0)
    else:
        for k in range(2, width, 2):
            flow.go(None, k, k, 0)
            flow.go(None, k, k, 1)
    flow.go(None, 1, 1, 0)
    flow.go(None, 1, 1, 1)
    if second:
        for copy in loads:
            copy.wait()
    else:
        hops.spread(c_ref, c_out, side_send, side_recv, True, True)
    mine.wait()
    pair_ready(0)
    work(0)
    if width == 8:
        flow.arrived(2, 0)
        flow.go(2, 4, 6, 0)
        flow.go(2, 1, 3, 0)
        flow.arrived(4, 1)
        flow.go(4, 2, 6, 1)
        flow.go(4, 1, 5, 1)
        flow.arrived(2, 1)
        flow.go(2, 1, 3, 1)
        flow.arrived(4, 0)
        flow.go(4, 1, 5, 0)
        pair_ready(2)
        work(1)
        pair_ready(4)
        work(2)
        for part in (0, 1):
            flow.arrived(6, part)
            flow.go(6, 1, 7, part)
        pair_ready(6)
        work(3)
    else:
        for k in range(2, width, 2):
            for part in (0, 1):
                flow.arrived(k, part)
                flow.go(k, 1, k + 1, part)
            pair_ready(k)
            work(k // 2)
    flow.finish()
    if second:
        for pair in (pairs - 2, pairs - 1):
            for copy in stores(pair):
                copy.wait()
    else:
        for pair in range(pairs):
            keeps(pair).wait()
        hops.spread(c_ref, c_out, side_send, side_recv, True, False)


def push(second, g, act, width, slots, ident, name, others):
    rows, cols = g.shape
    inner = act.shape[1]
    low, dma = g.dtype, pltpu.SemaphoreType.DMA
    planes, pairs = width // slots, width // 2
    anywhere, vmem = pl.BlockSpec(memory_space=pl.ANY), pl.BlockSpec(memory_space=pltpu.VMEM)
    blocks = (pairs, 2, rows, cols)
    scratch = [
        pltpu.VMEM(blocks, low), pltpu.VMEM((inner, cols), jnp.float32), pltpu.VMEM((2, 2, rows, inner), low),
        dma, dma((width, 2)), dma((width, 2)), dma((2, 2)),
    ]
    shapes = [jax.ShapeDtypeStruct((inner, cols), low)]
    if second:
        saved = jax.ShapeDtypeStruct((rows * width, inner), low)
        shapes += [saved, saved]
        scratch += [
            pltpu.VMEM((inner, 2 * cols), low), pltpu.VMEM(blocks, low), pltpu.VMEM((2, 2, 2, rows, inner), low),
            pltpu.VMEM((2, 2, 2, rows, inner), low), dma((planes + 1, 2)), dma((2, 2, 2)), dma((2, 2, 2)),
        ]
    else:
        shapes += [
            jax.ShapeDtypeStruct(blocks, low),
            jax.ShapeDtypeStruct((many_rows(planes, rows), others[0].shape[1]), low),
        ]
        scratch += [dma((pairs,)), dma((planes,)), dma((planes,))]
    inputs = [g, act] + others
    return pl.pallas_call(
        functools.partial(push_body, second, width, slots),
        out_shape=shapes,
        in_specs=[anywhere] * len(inputs),
        out_specs=[vmem] + [anywhere] * (len(shapes) - 1),
        scratch_shapes=scratch,
        cost_estimate=busy(10),
        compiler_params=pltpu.CompilerParams(collective_id=ident, has_side_effects=True, vmem_limit_bytes=VMEM_LIMIT),
        name=name,
    )(*inputs)


def pull_body(width, slots, step, chunk, gg_hbm, gu_hbm, wg_hbm, wu_hbm, h_hbm, c_ref, normed_ref, inv_ref, gain_ref,
              out_ref, proj_ref, gain_out, du_hbm, gg, gu, wg, wu, columns, tiles, load, take, fetch, store, *sum_refs):
    me = lax.axis_index("wide")
    planes = width // slots
    rows, cols = out_ref.shape
    half = rows // 2
    chunks = cols // chunk
    loads = local_copies([(wg_hbm, wg), (wu_hbm, wu)], load)
    for copy in loads:
        copy.start()

    def where(k, first, count):
        who = flip(me, k)
        start = ((who % slots) * planes + who // slots) * rows + first
        return pl.ds(pl.multiple_of(start, half), count)

    def takes(k):
        at = where(k, 0, rows)
        return [
            pltpu.make_async_copy(src.at[at], dst.at[at], take.at[k, i])
            for i, (src, dst) in enumerate(((gg_hbm, gg), (gu_hbm, gu)))
        ]

    order = [7, 6, 3, 5, 2, 4, 1, 0] if width == 8 else [k ^ 1 for k in range(width)]
    for k in order:
        for copy in takes(k):
            copy.start()
    taken = []

    def need(k):
        if k not in taken:
            taken.append(k)
            for copy in takes(k):
                copy.wait()

    def fetched(n):
        at = pl.ds(pl.multiple_of(n * chunk, chunk), chunk)
        return pltpu.make_async_copy(h_hbm.at[:, at], columns.at[n % 2], fetch.at[n % 2])

    def stored(n):
        at = pl.ds(pl.multiple_of(n * chunk, chunk), chunk)
        return [
            pltpu.make_async_copy(tiles.at[n % 2, i], ref.at[at], store.at[n % 2, i])
            for i, ref in enumerate((du_hbm,))
        ]

    fetched(0).start()
    hello(wide_peers(width, me))
    sums = Sums(width, me, out_ref, sum_refs)

    def produce(k, first, count, put, adds=()):
        need(k)
        at_rows = where(k, first, count)

        def tile(n, carry):
            at = pl.ds(pl.multiple_of(n * step, step), step)
            total = nt(gg[at_rows, :], wg[at, :]) + nt(gu[at_rows, :], wu[at, :])
            for ref in adds:
                total = total + ref[:, at].astype(jnp.float32)
            put[:, at] = total.astype(put.dtype)
            return carry

        lax.fori_loop(0, cols // step, tile, 0)

    def grads(first, last):
        for k in order:
            need(k)

        def one_chunk(n, carry):
            fetched(n).wait()

            @pl.when(n + 1 < chunks)
            def _():
                fetched(n + 1).start()

            @pl.when(n >= 2)
            def _():
                for copy in stored(n - 2):
                    copy.wait()

            for i, ref in enumerate((gu,)):
                tiles[n % 2, i] = lax.dot_general(
                    columns[n % 2], ref[...], (((0,), (0,)), ((), ())), preferred_element_type=jnp.float32
                ).astype(jnp.bfloat16)
            for copy in stored(n):
                copy.start()
            return carry

        lax.fori_loop(first, last, one_chunk, 0)

    for copy in loads:
        copy.wait()
    run_sums(width, sums, produce, grads, chunks)
    gain_out[...] = jnp.zeros_like(gain_out)
    few = 32

    def norm(n, carry):
        at = pl.ds(pl.multiple_of(n * few, few), few)
        grad = out_ref[at, :] + c_ref[at, :].astype(jnp.float32)
        out_ref[at, :] = grad
        normed = normed_ref[at, :]
        gain_out[...] = gain_out[...] + row_sums(grad * normed)
        grad = grad * gain_ref[...]
        mean = jnp.sum(grad * normed, axis=-1, keepdims=True) * (1.0 / cols)
        proj_ref[at, :] = (inv_ref[at, :] * (grad - normed * mean)).astype(jnp.bfloat16)
        return carry

    lax.fori_loop(0, rows // few, norm, 0)
    for copy in stored(chunks - 2) + stored(chunks - 1):
        copy.wait()


def pull(grad_gate, grad_up, gate_weight, up_weight, gathered, grad_out, normed, inverse, gain, width, slots, ident, name):
    count, cols = gathered.shape
    inner = gate_weight.shape[1]
    rows = count // width
    low, f32, dma = gathered.dtype, jnp.float32, pltpu.SemaphoreType.DMA
    chunk = 256
    anywhere, vmem = pl.BlockSpec(memory_space=pl.ANY), pl.BlockSpec(memory_space=pltpu.VMEM)
    return pl.pallas_call(
        functools.partial(pull_body, width, slots, 1024, chunk),
        out_shape=[
            jax.ShapeDtypeStruct((rows, cols), f32), jax.ShapeDtypeStruct((rows, cols), low),
            jax.ShapeDtypeStruct((8, cols), f32), jax.ShapeDtypeStruct((cols, inner), low),
        ],
        in_specs=[anywhere] * 5 + [vmem] * 4,
        out_specs=[vmem] * 3 + [anywhere],
        scratch_shapes=[
            pltpu.VMEM((count, inner), low), pltpu.VMEM((count, inner), low),
            pltpu.VMEM((cols, inner), low), pltpu.VMEM((cols, inner), low),
            pltpu.VMEM((2, count, chunk), low), pltpu.VMEM((2, 1, chunk, inner), low),
            dma((2,)), dma((width, 2)), dma((2,)), dma((2, 1)),
        ] + sum_scratch(width, rows, cols),
        cost_estimate=busy(10),
        compiler_params=pltpu.CompilerParams(collective_id=ident, has_side_effects=True, vmem_limit_bytes=VMEM_LIMIT),
        name=name,
    )(grad_gate, grad_up, gate_weight, up_weight, gathered, grad_out, normed, inverse, gain)


def side_body(x_ref, p_ref, qk_ref, v_ref, m_ref, out_ref):
    first = 0
    for left, right in ((x_ref, qk_ref), (x_ref, v_ref), (p_ref, m_ref)):
        last = first + right.shape[1]
        out_ref[:, first:last] = lax.dot_general(
            left[...], right[...], (((0,), (0,)), ((), ())), preferred_element_type=jnp.float32
        ).astype(out_ref.dtype)
        first = last


def side_grads(inputs, grad_proj, grad_qk, grad_v, mixed):
    count, cols = inputs.shape
    extent = grad_qk.shape[1] + grad_v.shape[1] + mixed.shape[1]
    chunk = 256
    return pl.pallas_call(
        side_body,
        grid=(cols // chunk,),
        out_shape=jax.ShapeDtypeStruct((cols, extent), inputs.dtype),
        in_specs=[
            pl.BlockSpec((count, chunk), lambda n: (0, n)), pl.BlockSpec((count, chunk), lambda n: (0, n)),
            pl.BlockSpec(grad_qk.shape, lambda n: (0, 0)), pl.BlockSpec(grad_v.shape, lambda n: (0, 0)),
            pl.BlockSpec(mixed.shape, lambda n: (0, 0)),
        ],
        out_specs=pl.BlockSpec((chunk, extent), lambda n: (n, 0)),
        compiler_params=pltpu.CompilerParams(vmem_limit_bytes=VMEM_LIMIT),
        cost_estimate=busy(10),
        name="side_grads",
    )(inputs, grad_proj, grad_qk, grad_v, mixed)


def local(
    tokens,
    lengths,
    query_weight,
    key_weight,
    value_weight,
    output_weight,
    query_gain,
    key_gain,
    attention_gain,
    gate_weight,
    up_weight,
    down_weight,
    feedforward_gain,
    cotangent,
):
    low, f32 = jnp.bfloat16, jnp.float32
    planes, width = lax.axis_size("blk"), lax.axis_size("wide")
    slots = width // planes
    rows = tokens.shape[1]
    span = rows * planes
    count = slots * span
    share = query_weight.shape[1]
    heads = share // HD
    plane, place = lax.axis_index("blk"), lax.axis_index("wide")
    after = lambda value, *others: lax.optimization_barrier((value,) + others)[0]

    def sum_blk(value, axis):
        return lax.psum_scatter(value, "blk", scatter_dimension=axis, tiled=True)

    _, near_cotangent, mine = turn(
        turn_in_body, [tokens[0], cotangent[0]], [True, True, False], planes, slots, 1, "turn_in"
    )
    w_qk = after(jnp.concatenate([query_weight, key_weight], 1), mine)
    w_qk = lax.all_gather(w_qk, "blk", axis=0, tiled=True)
    gains = jnp.stack([query_gain, key_gain]).astype(f32)
    plane_lengths = lax.dynamic_slice_in_dim(lengths, plane * slots, slots, 0)
    segment, position = jax.vmap(lambda one: layout(one, span))(plane_lengths)
    begin = (jnp.arange(span, dtype=jnp.int32)[None] - position)[:, None, :]
    pairs, piece = piece_map(span, rows)
    order = sorted(pairs, key=lambda pair: pair[1])
    index = np.concatenate([np.arange(at, at + piece) for at, _ in order])
    starts = jnp.stack([plane_lengths[:, 0] * 0, plane_lengths[:, 0], plane_lengths[:, 0] + plane_lengths[:, 1]], 1)
    cos_a, sin_a, cos_b, sin_b, sign = rope_tables(index, starts)
    group = jnp.concatenate([segment[:, at : at + piece] for at, _ in order], 1)[..., None]
    pick = lambda table: jnp.where(
        group == 0, table[:, 0:1], jnp.where(group == 1, table[:, 1:2], table[:, 2:3])
    )
    cos_b, sin_b = pick(cos_b), pick(sin_b)
    cosine = cos_a * cos_b + sin_a * sin_b
    sine = (sin_a * cos_b - cos_a * sin_b) * sign

    inputs = gather(mine, width, slots, 2, "gather_tokens")
    w_v = lax.all_gather(after(value_weight, inputs), "blk", axis=0, tiled=True)
    pre = dot(inputs, w_qk)
    w_o = lax.all_gather(after(output_weight, pre), "blk", axis=1, tiled=True)
    squares = jnp.stack([jnp.sum(pre[:, a * share : (a + 1) * share] ** 2, -1) for a in (0, 1)])
    both = lax.dynamic_update_slice(
        jnp.zeros((2, D), f32), jnp.stack([attention_gain, feedforward_gain]).astype(f32), (0, place * share)
    )
    squares = jnp.concatenate([squares.reshape(-1, 128), both.reshape(-1, 128)])
    squares = total(squares, "wide", width, 3, "total_squares")
    both = squares[2 * count // 128 :].reshape(2, D)
    gain_mix, gain_feed = both[0], both[1]
    inverse = lax.rsqrt(squares[: 2 * count // 128].reshape(2, count) / D + EPS)
    inv_cols = inverse.T.reshape(slots, span, 2)
    pre_groups = pre.reshape(slots, span, 2 * share)
    value_rows = dot(inputs, after(w_v, squares)).astype(low).reshape(slots, span, share)
    queries, keys, values, mixed, logs = attend(
        pre_groups, value_rows, inv_cols, gains, cosine, sine, begin, heads, rows
    )
    mixed = mixed.reshape(count, share)
    hidden, hidden_low, proj_normed, proj_inv = scatter(
        [mixed], [w_o], width, slots, False, 4, "scatter_mixed", "norm", (mine, gain_mix[None])
    )
    block_output, first_half, second_half, feed_gain_part, gathered, activated, up_factor, gate_factor, grad_out = feed(
        hidden_low, near_cotangent, gate_weight, up_weight, down_weight, hidden, gain_feed[None], width, slots, 5,
        "feed",
    )
    down_first, first_rows, far_output = push(
        False, first_half, activated, width, slots, 6, "push_first", [block_output]
    )
    down_first = sum_blk(down_first, 1)
    down_second, grad_gate, grad_up = push(
        True, second_half, activated, width, slots, 7, "push_second",
        [down_weight, up_factor, gate_factor, first_rows],
    )
    down_second = sum_blk(down_second, 1)
    gate_part = contract_rows(gathered, grad_gate).astype(low)
    gate_grad = sum_blk(gate_part, 0)
    grad_hidden, grad_proj, mix_gain_part, up_part = pull(
        after(grad_gate, gate_part, down_first), grad_up, gate_weight, up_weight, gathered, grad_out, proj_normed,
        proj_inv, gain_mix[None], width, slots, 8, "pull",
    )
    up_grad = sum_blk(up_part, 0)
    grad_proj = gather(grad_proj, width, slots, 9, "gather_proj")
    grad_mixed = contract_cols(after(grad_proj, down_first, down_second), w_o).astype(low).reshape(slots, span, share)
    scaled_q, scaled_k, grad_v, sums, parts = attend_back(
        queries, keys, values, grad_mixed, logs, pre_groups, inv_cols, gains, cosine, sine, begin,
        heads, rows,
    )
    means = jnp.sum(sums, axis=0).reshape(count, 2).T.reshape(-1, 128)
    local_gains = lax.dynamic_update_slice(
        jnp.zeros((2, D), f32), jnp.sum(parts, axis=0), (0, place * share)
    )
    gain_parts = jnp.concatenate([local_gains, jnp.stack([mix_gain_part.sum(0), feed_gain_part.sum(0)])])
    means = jnp.concatenate([means, gain_parts.reshape(-1, 128)])
    means = total(after(means, gate_grad), "wide", width, 10, "total_means")
    gain_parts = means[2 * count // 128 :]
    means = means[: 2 * count // 128].reshape(2, count) / D

    def finish(scaled, index):
        normed = pre[:, index * share : (index + 1) * share] * inverse[index][:, None]
        scaled = scaled.reshape(count, share)
        return (inverse[index][:, None] * (scaled - normed * means[index][:, None])).astype(low)

    grad_qk = jnp.concatenate([finish(scaled_q, 0), finish(scaled_k, 1)], 1)
    grad_v = grad_v.reshape(count, share)
    side_part = side_grads(inputs, grad_proj, grad_qk, grad_v, mixed)
    tokens_low = scatter(
        [grad_qk, grad_v], [w_qk, w_v], width, slots, True, 11, "scatter_tokens", "add", (grad_hidden,)
    )
    down_grad = jnp.concatenate([down_first, down_second], 1).astype(f32)
    gate_grad, up_grad = gate_grad.astype(f32), up_grad.astype(f32)
    tokens_low, down_grad, gate_grad, up_grad = lax.optimization_barrier((tokens_low, down_grad, gate_grad, up_grad))
    _, block_output, tokens_grad, gain_sums = turn(
        turn_out_body, [tokens_low, far_output], [True, False, False],
        planes, slots, 14, "turn_out", gain_parts,
    )
    side_grad = sum_blk(side_part, 0).astype(f32)

    sums = gain_sums.reshape(4, D)
    portion = D // (planes * width)
    sums = lax.dynamic_slice_in_dim(sums, (plane * width + place) * portion, portion, 1)
    return (
        block_output[None],
        tokens_grad[None].astype(f32),
        side_grad[:, :share],
        side_grad[:, share : 2 * share],
        side_grad[:, 2 * share : 3 * share],
        side_grad[:, 3 * share :].T,
        sums[0],
        sums[1],
        sums[2],
        gate_grad,
        up_grad,
        down_grad,
        sums[3],
    )


def solution(mesh):
    placed = (
        P("wide", "blk", None),
        P(),
        P("blk", "wide"),
        P("blk", "wide"),
        P("blk", "wide"),
        P("wide", "blk"),
        P("wide"),
        P("wide"),
        P("wide"),
        P(None, "wide"),
        P(None, "wide"),
        P("wide", None),
        P("wide"),
        P("wide", "blk", None),
    )
    return jax.shard_map(
        local,
        mesh=mesh,
        in_specs=placed,
        out_specs=(
            P("wide", "blk", None),
            P("wide", "blk", None),
            P("blk", "wide"),
            P("blk", "wide"),
            P("blk", "wide"),
            P("wide", "blk"),
            P(("blk", "wide")),
            P(("blk", "wide")),
            P(("blk", "wide")),
            P("blk", "wide"),
            P("blk", "wide"),
            P("wide", "blk"),
            P(("blk", "wide")),
        ),
        check_vma=False,
    )
```

```python
import functools

import jax
import jax.numpy as jnp
import numpy as np
from jax import lax
from jax.experimental import pallas as pl
from jax.experimental.pallas import tpu as pltpu
from jax.sharding import PartitionSpec as P

MESH = pl.DeviceIdType.MESH

D = 2048
HD = 128
EPS = 1e-06
ROPE_BASE = 500000.0
NEG_FILL = -1e30
VMEM_LIMIT = 60 * 1024 * 1024
SCALE = HD ** (-0.5)
FOLD = SCALE * 1.4426950408889634


def busy(micros):
    return pl.CostEstimate(flops=0, bytes_accessed=int(micros * 3.5e6), transcendentals=0)


def layout(seq_lengths, row_count):
    indices = jnp.arange(row_count, dtype=jnp.int32)
    first_end = seq_lengths[0]
    second_end = seq_lengths[0] + seq_lengths[1]
    segment = (indices >= first_end).astype(jnp.int32) + (indices >= second_end).astype(jnp.int32)
    offsets = jnp.where(segment == 0, 0, jnp.where(segment == 1, first_end, second_end))
    return (segment, indices - offsets)


def rope_tables(index, begin):
    frequency = ROPE_BASE ** (-np.arange(0, HD, 2, dtype=np.float64) / HD)
    angles = np.asarray(index, np.float64)[:, None] * frequency
    sign = np.concatenate([-np.ones(HD // 2), np.ones(HD // 2)])
    twice = lambda value: np.concatenate([value, value], -1).astype(np.float32)
    cosine, sine = jnp.asarray(twice(np.cos(angles))), jnp.asarray(twice(np.sin(angles)))
    shift = begin.astype(jnp.float32)[..., None] * jnp.asarray(twice(frequency))
    return cosine, sine, jnp.cos(shift), jnp.sin(shift), jnp.asarray(sign.astype(np.float32))


def rms_pair(values):
    inverse = lax.rsqrt(jnp.mean(values * values, axis=-1, keepdims=True) + EPS)
    return (values * inverse, inverse)


def norm_back(normed, inverse, grad_normed):
    return inverse * (grad_normed - normed * jnp.mean(grad_normed * normed, axis=-1, keepdims=True))


def dot(left, right):
    return jnp.dot(left, right, preferred_element_type=jnp.float32)


def contract_rows(left, right):
    return lax.dot_general(
        left, right, (((0,), (0,)), ((), ())), preferred_element_type=jnp.float32
    )


def contract_cols(left, right):
    return lax.dot_general(
        left, right, (((1,), (1,)), ((), ())), preferred_element_type=jnp.float32
    )


def flip(me, k):
    out, bit = me, 1
    while bit <= k:
        if k & bit:
            out = out + bit * (1 - 2 * ((me // bit) % 2))
        bit *= 2
    return out


def greet(axis, me, others):
    barrier = pltpu.get_barrier_semaphore()
    for k in others:
        pl.semaphore_signal(barrier, inc=1, device_id={axis: flip(me, k)}, device_id_type=MESH)
    pl.semaphore_wait(barrier, len(others))


class Flow:
    def __init__(self, me, source, spot, half, send, recv):
        self.me, self.source, self.spot, self.half = me, source, spot, half
        self.send, self.recv, self.moves = send, recv, []

    def go(self, origin, target, k, part):
        if origin is None:
            source = self.source.at[pl.ds(part * self.half, self.half)]
        else:
            source = self.spot(flip(self.me, origin), part)
        copy = pltpu.make_async_remote_copy(
            src_ref=source,
            dst_ref=self.spot(flip(flip(self.me, target), k), part),
            send_sem=self.send.at[k, part],
            recv_sem=self.recv.at[k, part],
            device_id={"wide": flip(self.me, target)},
            device_id_type=MESH,
        )
        copy.start()
        self.moves.append(copy)

    def arrived(self, k, part):
        block = self.spot(flip(self.me, k), part)
        pltpu.make_async_copy(block, block, self.recv.at[k, part]).wait()

    def finish(self):
        for copy in self.moves:
            copy.wait_send()


class Sums:
    def __init__(self, width, me, out_ref, refs):
        self.width, self.me, self.out = width, me, out_ref
        (self.odd, self.even, self.from_twin, self.from_far, self.passing, self.sends, self.recvs,
         self.pass_send, self.pass_recv, self.twin_send, self.twin_recv) = refs
        self.half = out_ref.shape[0] // 2

    def rows(self, part):
        return pl.ds(part * self.half, self.half)

    def copy(self, src, dst, send, recv, k):
        return pltpu.make_async_remote_copy(
            src_ref=src, dst_ref=dst, send_sem=send, recv_sem=recv,
            device_id={"wide": flip(self.me, k)}, device_id_type=MESH,
        )

    def twin(self, k, part):
        i, at = k // 2, self.rows(part)
        return self.copy(
            self.odd.at[i, at], self.from_twin.at[i, at], self.twin_send.at[i, part],
            self.twin_recv.at[i, part], 1,
        )

    def far(self, k, part):
        i, at = k // 2 - 1, self.rows(part)
        return self.copy(
            self.even.at[i, at], self.from_far.at[i, at], self.sends.at[i, part], self.recvs.at[i, part], k
        )

    def relay(self, part):
        return self.copy(
            self.even.at[2, self.rows(part)], self.passing.at[part], self.pass_send.at[part],
            self.pass_recv.at[part], 2 if part == 0 else 4,
        )

    def give(self, k):
        self.twin(k, 0).start()
        self.twin(k, 1).start()

    def got(self, k):
        self.twin(k, 0).wait_recv()
        self.twin(k, 1).wait_recv()

    def pass_on(self, k, part):
        self.relay(part).wait_recv()
        at = self.rows(part)
        self.even[k // 2 - 1, at, :] = (
            self.even[k // 2 - 1, at, :].astype(jnp.float32) + self.passing[part].astype(jnp.float32)
        ).astype(jnp.bfloat16)
        self.far(k, part).start()

    def finish(self):
        sources = [2, 4] if self.width == 8 else list(range(2, self.width, 2))
        for k in sources:
            for part in (0, 1):
                self.far(k, part).wait_recv()
        extra = self.from_far[sources[0] // 2 - 1].astype(jnp.float32)
        for k in sources[1:]:
            extra = extra + self.from_far[k // 2 - 1].astype(jnp.float32)
        self.out[...] = self.out[...] + extra
        for part in (0, 1):
            for k in sources:
                self.far(k, part).wait_send()
            for k in range(0, self.width, 2):
                self.twin(k, part).wait_send()
            if self.width == 8:
                self.relay(part).wait_send()


def run_sums(width, sums, produce, beside=None, steps=0):
    half = sums.half
    rows = 2 * half

    def give(k, part=None):
        if part is None:
            produce(k + 1, 0, rows, sums.odd.at[k // 2])
            sums.give(k)
        else:
            produce(k + 1, part * half, half, sums.odd.at[k // 2, sums.rows(part)])
            sums.twin(k, part).start()

    def merge(k, part=None):
        if part is None:
            sums.got(k)
            produce(k, 0, rows, sums.even.at[k // 2 - 1], (sums.from_twin.at[k // 2],))
        else:
            sums.twin(k, part).wait_recv()
            at = sums.rows(part)
            produce(k, part * half, half, sums.even.at[k // 2 - 1, at], (sums.from_twin.at[k // 2, at],))

    if width == 8:
        give(6, 0)
        give(6, 1)
        merge(6, 0)
        sums.relay(0).start()
        merge(6, 1)
        sums.relay(1).start()
        give(2)
        give(4)
        merge(2)
        sums.far(2, 0).start()
        merge(4)
        sums.far(4, 1).start()
        sums.pass_on(2, 1)
        sums.pass_on(4, 0)
        give(0)
    else:
        for k in range(0, width, 2):
            give(k)
        for k in range(2, width, 2):
            merge(k)
            sums.far(k, 0).start()
            sums.far(k, 1).start()
    if beside is not None:
        beside(0, steps)
    sums.got(0)
    produce(0, 0, rows, sums.out, (sums.from_twin.at[0],))
    sums.finish()


def sum_scratch(width, rows, cols):
    chips, dma = width // 2, pltpu.SemaphoreType.DMA
    block = lambda n: pltpu.VMEM((n, rows, cols), jnp.bfloat16)
    return [
        block(chips), block(chips - 1), block(chips), block(2 if width == 8 else chips - 1),
        pltpu.VMEM((2, rows // 2, cols), jnp.bfloat16),
        dma((chips - 1, 2)), dma((chips - 1, 2)), dma((2,)), dma((2,)), dma((chips, 2)), dma((chips, 2)),
    ]


def wide_peers(width, me):
    return [{"wide": flip(me, k)} for k in [1] + list(range(2, width, 2))]


def local_copies(pairs, sem):
    return [pltpu.make_async_copy(src, dst, sem.at[i]) for i, (src, dst) in enumerate(pairs)]


def gather_body(width, slots, side, *refs):
    if side is None:
        x_ref, out_ref, here, send, recv = refs
    else:
        x_ref, side_ref, out_ref, side_out, here, send, recv, side_send, side_recv = refs
    me = lax.axis_index("wide")
    rows = x_ref.shape[0]
    half = rows // 2
    evens = list(range(2, width, 2))
    peers = [{"wide": flip(me, k)} for k in [1] + evens]
    if side is not None:
        hops = Hops(width // slots, slots, rows)
        peers = peers + [{"blk": (hops.plane + k) % hops.planes} for k in range(1, hops.planes)]
    hello(peers)
    if side is not None:
        job = hops.join if side == "join" else hops.spread
        job(side_ref, side_out, side_send, side_recv, True, True)

    def spot(who, first, count):
        base = ((who % slots) * (width // slots) + who // slots) * rows
        return out_ref.at[pl.ds(pl.multiple_of(base + first, half), count)]

    def move(origin, target, k, part):
        if origin is None:
            source = x_ref.at[pl.ds(part * half, half)]
        else:
            source = spot(flip(me, origin), part * half, half)
        return pltpu.make_async_remote_copy(
            src_ref=source,
            dst_ref=spot(flip(flip(me, target), k), part * half, half),
            send_sem=send.at[k, part],
            recv_sem=recv.at[k, part],
            device_id={"wide": flip(me, target)},
            device_id_type=MESH,
        )

    def arrived(k, part):
        block = spot(flip(me, k), part * half, half)
        pltpu.make_async_copy(block, block, recv.at[k, part]).wait()

    moves = []

    def go(origin, target, k, part):
        copy = move(origin, target, k, part)
        copy.start()
        moves.append(copy)

    mine = pltpu.make_async_copy(x_ref, spot(me, 0, rows), here)
    mine.start()
    if width == 8:
        go(None, 2, 2, 0)
        go(None, 4, 4, 1)
        go(None, 2, 2, 1)
        go(None, 4, 4, 0)
        go(None, 1, 1, 0)
        go(None, 1, 1, 1)
        arrived(2, 0)
        go(2, 4, 6, 0)
        go(2, 1, 3, 0)
        arrived(4, 1)
        go(4, 2, 6, 1)
        go(4, 1, 5, 1)
        order = [(2, 1), (4, 0), (6, 0), (6, 1)]
    else:
        for k in evens:
            go(None, k, k, 0)
            go(None, k, k, 1)
        go(None, 1, 1, 0)
        go(None, 1, 1, 1)
        order = [(k, part) for k in evens for part in (0, 1)]
    for k, part in order:
        arrived(k, part)
        go(k, 1, k + 1, part)
    for k in range(1, width, 2):
        for part in (0, 1):
            arrived(k, part)
    for copy in moves:
        copy.wait_send()
    mine.wait()
    if side is not None:
        job(side_ref, side_out, side_send, side_recv, True, False)


def gather(x, width, slots, ident, name, side=None, side_x=None):
    rows, cols = x.shape
    planes = width // slots
    dma = pltpu.SemaphoreType.DMA
    shapes = [jax.ShapeDtypeStruct((rows * width, cols), x.dtype)]
    scratch = [dma, dma((width, 2)), dma((width, 2))]
    inputs = [x]
    if side is not None:
        inputs.append(side_x)
        extent = rows if side == "join" else many_rows(planes, rows)
        shapes.append(jax.ShapeDtypeStruct((extent, cols), side_x.dtype))
        scratch += [dma((planes,)), dma((planes,))]
    outs = pl.pallas_call(
        functools.partial(gather_body, width, slots, side),
        out_shape=shapes,
        in_specs=[pl.BlockSpec(memory_space=pl.ANY)] * len(inputs),
        out_specs=[pl.BlockSpec(memory_space=pl.ANY)] * len(shapes),
        scratch_shapes=scratch,
        cost_estimate=busy(10),
        compiler_params=pltpu.CompilerParams(collective_id=ident, has_side_effects=True, vmem_limit_bytes=VMEM_LIMIT),
        name=name,
    )(*inputs)
    return outs[0] if side is None else outs


def scatter_body(width, slots, flat, count, step, finish, *refs):
    lefts, rights = refs[:count], refs[count : 2 * count]
    if finish == "norm":
        x_ref, gain_ref, hidden_ref, low_ref, out_ref, inv_ref = refs[2 * count : 2 * count + 6]
        rest = refs[2 * count + 6 :]
    else:
        more_ref, low_ref, out_ref = refs[2 * count : 2 * count + 3]
        rest = refs[2 * count + 3 :]
    me = lax.axis_index("wide")
    rows, cols = out_ref.shape
    hello(wide_peers(width, me))
    sums = Sums(width, me, out_ref, rest)
    dims = (((1,), (1 if flat else 0,)), ((), ()))

    def produce(k, first, some, put, adds=()):
        who = flip(me, k)
        start = ((who % slots) * (width // slots) + who // slots) * rows + first
        start = pl.multiple_of(start, rows // 2)

        def tile(n, carry):
            at = pl.ds(pl.multiple_of(n * step, step), step)
            total = None
            for left, right in zip(lefts, rights):
                other = right[at, :] if flat else right[:, at]
                term = lax.dot_general(
                    left[pl.ds(start, some), :], other, dims, preferred_element_type=jnp.float32
                )
                total = term if total is None else total + term
            for ref in adds:
                total = total + ref[:, at].astype(jnp.float32)
            put[:, at] = total.astype(put.dtype)
            return carry

        lax.fori_loop(0, cols // step, tile, 0)

    run_sums(width, sums, produce)
    if finish == "add":
        def close(n, carry):
            at = pl.ds(pl.multiple_of(n * 32, 32), 32)
            low_ref[at, :] = (out_ref[at, :] + more_ref[at, :]).astype(low_ref.dtype)
            return carry

        lax.fori_loop(0, rows // 32, close, 0)
    if finish != "norm":
        return
    few = 32

    def norm(n, carry):
        at = pl.ds(pl.multiple_of(n * few, few), few)
        value = out_ref[at, :]
        inverse = lax.rsqrt(jnp.sum(value * value, axis=-1, keepdims=True) * (1.0 / cols) + EPS)
        value = value * inverse
        out_ref[at, :] = value
        inv_ref[at, :] = inverse
        hidden = x_ref[at, :].astype(jnp.float32) + value * gain_ref[...]
        hidden_ref[at, :] = hidden
        low_ref[at, :] = hidden.astype(low_ref.dtype)
        return carry

    lax.fori_loop(0, rows // few, norm, 0)


def scatter(lefts, rights, width, slots, flat, ident, name, finish, more, step=1024):
    rows = lefts[0].shape[0] // width
    cols = rights[0].shape[0 if flat else 1]
    f32, vmem = jnp.float32, pl.BlockSpec(memory_space=pltpu.VMEM)
    whole, low = jax.ShapeDtypeStruct((rows, cols), f32), jax.ShapeDtypeStruct((rows, cols), lefts[0].dtype)
    shapes = [whole, low, whole, jax.ShapeDtypeStruct((rows, 1), f32)] if finish == "norm" else [low]
    scratch = sum_scratch(width, rows, cols)
    if finish == "add":
        scratch = [pltpu.VMEM((rows, cols), f32)] + scratch
    outs = pl.pallas_call(
        functools.partial(scatter_body, width, slots, flat, len(lefts), step, finish),
        out_shape=shapes,
        in_specs=[vmem] * (2 * len(lefts) + len(more)),
        out_specs=[vmem] * len(shapes),
        scratch_shapes=scratch,
        cost_estimate=busy(10),
        compiler_params=pltpu.CompilerParams(collective_id=ident, has_side_effects=True, vmem_limit_bytes=VMEM_LIMIT),
        name=name,
    )(*lefts, *rights, *more)
    return outs if finish == "norm" else outs[0]


def total_body(axis, width, x_ref, out_ref, slots, send, recv):
    me = lax.axis_index(axis)
    others = list(range(1, width))
    greet(axis, me, others)
    moves = []
    for k in others:
        copy = pltpu.make_async_remote_copy(
            src_ref=x_ref,
            dst_ref=slots.at[k - 1],
            send_sem=send.at[k - 1],
            recv_sem=recv.at[k - 1],
            device_id={axis: flip(me, k)},
            device_id_type=MESH,
        )
        copy.start()
        moves.append(copy)
    out_ref[...] = x_ref[...]
    for copy, k in zip(moves, others):
        copy.wait_recv()
        out_ref[...] = out_ref[...] + slots[k - 1]
    for copy in moves:
        copy.wait_send()


def total(x, axis, width, ident, name):
    return pl.pallas_call(
        functools.partial(total_body, axis, width),
        out_shape=jax.ShapeDtypeStruct(x.shape, x.dtype),
        in_specs=[pl.BlockSpec(memory_space=pltpu.VMEM)],
        out_specs=pl.BlockSpec(memory_space=pltpu.VMEM),
        scratch_shapes=[
            pltpu.VMEM((width - 1,) + x.shape, x.dtype),
            pltpu.SemaphoreType.DMA((width - 1,)),
            pltpu.SemaphoreType.DMA((width - 1,)),
        ],
        cost_estimate=busy(7),
        compiler_params=pltpu.CompilerParams(collective_id=ident, has_side_effects=True, vmem_limit_bytes=VMEM_LIMIT),
        name=name,
    )(x)


class Hops:
    def __init__(self, planes, slots, rows):
        self.planes, self.slots = planes, slots
        self.count = max(n for n in range(1, planes + 1) if planes % n == 0 and rows % (16 * n) == 0)
        self.per = planes // self.count
        self.piece = rows // self.count
        self.plane, self.place = lax.axis_index("blk"), lax.axis_index("wide")
        self.chip, self.slot = self.place // slots, self.place % slots
        self.active = self.chip // self.count == self.plane % self.per

    def peers(self):
        near = [{"wide": (self.chip + k) % self.planes * self.slots + self.slot} for k in range(1, self.planes)]
        return near + [{"blk": (self.plane + k) % self.planes} for k in range(1, self.planes)]

    def when(self, condition, action):
        if self.per == 1:
            action()
        else:
            pl.when(condition)(action)

    def split(self, condition, yes, no):
        if self.per == 1:
            yes()
        else:
            pl.when(condition)(yes)
            pl.when(jnp.logical_not(condition))(no)

    def cut(self, ref, index):
        return ref.at[pl.ds(pl.multiple_of(index * self.piece, self.piece), self.piece)]

    def remote(self, src, dst, send, recv, device):
        return pltpu.make_async_remote_copy(
            src_ref=src, dst_ref=dst, send_sem=send, recv_sem=recv, device_id=device, device_id_type=MESH
        )

    def spread(self, some, many, send, recv, across, start):
        if across:
            axis, here = "blk", self.plane
            targets = [
                ((self.plane // self.per + k) % self.count) for k in range(self.count)
            ]
            device = lambda piece: piece * self.per + self.chip // self.count
        else:
            axis, here = "wide", self.chip
            targets = [((self.chip + k) % self.count) for k in range(self.count)]
            device = lambda piece: (self.plane % self.per) * self.count + piece
        address = (lambda who: {"blk": who}) if across else (
            lambda who: {"wide": who * self.slots + self.slot}
        )
        for k, piece in enumerate(targets):
            who = device(piece)
            far = self.remote(
                self.cut(some, piece), self.cut(many, here), send.at[piece],
                recv.at[(here - who + self.planes) % self.planes], address(who),
            )
            own = pltpu.make_async_copy(self.cut(some, piece), self.cut(many, here), send.at[piece])
            if k:
                far.start() if start else far.wait_send()
            elif start:
                self.split(self.active, own.start, far.start)
            else:
                self.split(self.active, own.wait, far.wait_send)
        if not start:
            def receive():
                for k in range(1, self.planes):
                    block = self.cut(many, (here + k) % self.planes)
                    pltpu.make_async_copy(block, block, recv.at[k]).wait()

            self.when(self.active, receive)

    def join(self, many, some, send, recv, across, start, ready=None):
        if across:
            here = self.plane
            index = self.plane // self.per
            address = lambda who: {"blk": who}
        else:
            here = self.chip
            index = self.chip % self.count
            address = lambda who: {"wide": who * self.slots + self.slot}

        def give():
            for k in list(range(1, self.planes)) + [0]:
                who = (here + k) % self.planes
                if ready is not None:
                    ready(who)
                if k:
                    copy = self.remote(
                        self.cut(many, who), self.cut(some, index), send.at[k], recv.at[index], address(who)
                    )
                    copy.start() if start else copy.wait_send()
                else:
                    own = pltpu.make_async_copy(self.cut(many, here), self.cut(some, index), send.at[0])
                    own.start() if start else own.wait()

        self.when(self.active, give)
        if not start:
            for k in range(self.count):
                piece = (index + k) % self.count
                block = self.cut(some, piece)
                arrival = pltpu.make_async_copy(block, block, recv.at[piece])
                if k:
                    arrival.wait()
                elif self.per > 1:
                    pl.when(jnp.logical_not(self.active))(arrival.wait)

    def arrival(self, some, many, send, recv, across):
        here = self.plane if across else self.chip
        own_piece = self.plane // self.per if across else self.chip % self.count

        def ready(who):
            block = self.cut(many, who)

            @pl.when(who == here)
            def _():
                pltpu.make_async_copy(self.cut(some, own_piece), block, send.at[own_piece]).wait()

            @pl.when(who != here)
            def _():
                pltpu.make_async_copy(block, block, recv.at[(who - here + self.planes) % self.planes]).wait()

        return ready

    def sent(self, some, many, send, across):
        pieces = self.plane // self.per if across else self.chip
        for k in range(self.count):
            piece = (pieces + k) % self.count
            block = self.cut(some, piece)
            out = pltpu.make_async_copy(block, block, send.at[piece])
            if k:
                out.wait()
            elif self.per > 1:
                pl.when(jnp.logical_not(self.active))(out.wait)


def hello(peers):
    barrier = pltpu.get_barrier_semaphore()
    for peer in peers:
        pl.semaphore_signal(barrier, inc=1, device_id=peer, device_id_type=MESH)
    pl.semaphore_wait(barrier, len(peers))


def turn_in_body(planes, slots, x_ref, c_ref, near_x, near_c, out_ref, *sems):
    hops = Hops(planes, slots, x_ref.shape[0])
    hello(hops.peers())
    hops.spread(x_ref, near_x, sems[0], sems[1], False, True)
    ready = hops.arrival(x_ref, near_x, sems[0], sems[1], False)
    hops.join(near_x, out_ref, sems[2], sems[3], True, True, ready)
    hops.sent(x_ref, near_x, sems[0], False)
    hops.spread(c_ref, near_c, sems[4], sems[5], False, True)
    hops.spread(c_ref, near_c, sems[4], sems[5], False, False)
    hops.join(near_x, out_ref, sems[2], sems[3], True, False)


def turn_out_body(planes, slots, x_ref, far_c, v_ref, far_x, out_c, out_ref, v_out, *sems):
    hops = Hops(planes, slots, x_ref.shape[0])
    hello(hops.peers())
    parts, send, recv = sems[6:]
    moves = []
    for k in range(1, planes):
        copy = hops.remote(
            v_ref, parts.at[planes - k - 1], send.at[k - 1], recv.at[planes - k - 1],
            {"blk": (hops.plane + k) % planes},
        )
        copy.start()
        moves.append(copy)
    hops.spread(x_ref, far_x, sems[0], sems[1], True, True)
    hops.join(far_c, out_c, sems[2], sems[3], False, True)
    ready = hops.arrival(x_ref, far_x, sems[0], sems[1], True)
    hops.join(far_x, out_ref, sems[4], sems[5], False, True, ready)
    hops.sent(x_ref, far_x, sems[0], True)
    amount = v_ref[...]
    for k in range(1, planes):
        block = parts.at[k - 1]
        pltpu.make_async_copy(block, block, recv.at[k - 1]).wait()
        amount = amount + parts[k - 1]
    v_out[...] = amount
    for copy in moves:
        copy.wait_send()
    hops.join(far_c, out_c, sems[2], sems[3], False, False)
    hops.join(far_x, out_ref, sems[4], sems[5], False, False)


def many_rows(planes, rows):
    count = max(n for n in range(1, planes + 1) if planes % n == 0 and rows % (16 * n) == 0)
    return planes * (rows // count)


def turn(body, inputs, outputs, planes, slots, ident, name, extra=None):
    rows, cols = inputs[0].shape
    low = inputs[0].dtype
    dma = pltpu.SemaphoreType.DMA
    shape = lambda many: jax.ShapeDtypeStruct((many_rows(planes, rows) if many else rows, cols), low)
    anywhere, vmem = pl.BlockSpec(memory_space=pl.ANY), pl.BlockSpec(memory_space=pltpu.VMEM)
    more = [] if extra is None else [extra]
    scratch = [dma((planes,))] * 6
    for value in more:
        scratch += [pltpu.VMEM((planes - 1,) + value.shape, value.dtype), dma((planes - 1,)), dma((planes - 1,))]
    return pl.pallas_call(
        functools.partial(body, planes, slots),
        out_shape=[shape(many) for many in outputs] + [jax.ShapeDtypeStruct(v.shape, v.dtype) for v in more],
        in_specs=[anywhere] * len(inputs) + [vmem] * len(more),
        out_specs=[anywhere] * len(outputs) + [vmem] * len(more),
        scratch_shapes=scratch,
        cost_estimate=busy(10),
        compiler_params=pltpu.CompilerParams(collective_id=ident, has_side_effects=True, vmem_limit_bytes=VMEM_LIMIT),
        name=name,
    )(*inputs, *more)


def mask_scores(scores, first, begin, size):
    span = scores.shape[0]
    index = lax.broadcasted_iota(jnp.int32, scores.shape, 0)
    query = lax.broadcasted_iota(jnp.int32, scores.shape, 1) + first
    return jnp.where((index <= query) & (index >= begin), scores, NEG_FILL)


def nt(left, right):
    return lax.dot_general(left, right, (((1,), (1,)), ((), ())), preferred_element_type=jnp.float32)


def nn(left, right):
    return jnp.dot(left, right, preferred_element_type=jnp.float32)


def piece_map(span, size):
    planes = span // size
    count = max(n for n in range(1, planes + 1) if planes % n == 0 and size % (16 * n) == 0)
    per, piece = planes // count, size // count
    pairs = []
    for t in range(count):
        for high in range(per):
            for low in range(count):
                natural = ((t * per + high) * count + low) * piece
                pairs.append((natural, ((high * count + low) * count + t) * piece))
    return pairs, piece


def attend_body(size, q_ref, k_ref, v_ref, inv_ref, gain_ref, cos_ref, sin_ref, begin_ref,
                qo_ref, ko_ref, vo_ref, mix_ref, log_ref, raw_ref):
    low = jnp.bfloat16
    span = q_ref.shape[0]

    def prepare(ref, col):
        value = ref[...] * inv_ref[:, col : col + 1] * gain_ref[col : col + 1, :]
        return (value * cos_ref[...] + pltpu.roll(value, HD // 2, 1) * sin_ref[...]).astype(low)

    pairs, piece = piece_map(span, size)

    def arrange(ref, value):
        for natural, block in pairs:
            ref[natural : natural + piece, :] = value[block : block + piece, :]

    arrange(qo_ref, prepare(q_ref, 0))
    arrange(ko_ref, prepare(k_ref, 1))
    arrange(vo_ref, v_ref[...].astype(low))
    flipped = vo_ref[...].astype(jnp.float32).T.astype(low)
    for i in range(span // size):
        last = (i + 1) * size
        cols = slice(i * size, last)
        first = i * size
        begin = begin_ref[:, cols]
        near = nt(ko_ref[first:last, :], qo_ref[cols, :])
        index = lax.broadcasted_iota(jnp.int32, near.shape, 0)
        query = lax.broadcasted_iota(jnp.int32, near.shape, 1)
        near = jnp.where((index <= query) & (index >= begin - first), near, NEG_FILL)
        top = jnp.max(near, axis=0, keepdims=True)
        if first:
            past = nt(ko_ref[:first, :], qo_ref[cols, :])
            past = jnp.where(lax.broadcasted_iota(jnp.int32, past.shape, 0) >= begin, past, NEG_FILL)
            top = jnp.maximum(top, jnp.max(past, axis=0, keepdims=True))
        raw = jnp.exp2((near - top) * FOLD)
        weight = jnp.sum(raw, axis=0, keepdims=True)
        raw_ref[first:last, :] = raw.astype(low)
        if first:
            raw = jnp.exp2((past - top) * FOLD)
            weight = weight + jnp.sum(raw, axis=0, keepdims=True)
            raw_ref[:first, :] = raw.astype(low)
        mixed = nn(flipped[:, :last], raw_ref[:last, :]) * (1.0 / weight)
        mixed = mixed.T.astype(low)
        for natural, block in pairs:
            if i * size <= natural < last:
                at = natural - i * size
                mix_ref[block : block + piece, :] = mixed[at : at + piece, :]
        log_ref[:, cols] = top * FOLD + jnp.log2(weight)


def attend(pre, rows, inverse, gains, cosine, sine, begin, heads, size):
    slots, span, _ = pre.shape
    low, f32 = jnp.bfloat16, jnp.float32
    head = lambda offset: pl.BlockSpec((None, span, HD), lambda g, h: (g, 0, offset + h))
    every = lambda cols: pl.BlockSpec((None, span, cols), lambda g, h: (g, 0, 0))
    line = pl.BlockSpec((None, 1, span), lambda g, h: (g, 0, 0))
    out = jax.ShapeDtypeStruct((slots, span, heads * HD), low)
    return pl.pallas_call(
        functools.partial(attend_body, size),
        grid=(slots, heads),
        out_shape=[out, out, out, out, jax.ShapeDtypeStruct((slots, heads, 1, span), f32)],
        in_specs=[
            head(0), head(heads), head(0), every(2),
            pl.BlockSpec((2, HD), lambda g, h: (0, h)), every(HD), every(HD), line,
        ],
        out_specs=[head(0)] * 4 + [pl.BlockSpec((None, None, 1, span), lambda g, h: (g, h, 0, 0))],
        scratch_shapes=[pltpu.VMEM((span, size), low)],
        compiler_params=pltpu.CompilerParams(vmem_limit_bytes=VMEM_LIMIT),
        cost_estimate=busy(5),
        name="attend",
    )(pre, pre, rows, inverse, gains, cosine, sine, begin)


def attend_back_body(size, q_ref, k_ref, v_ref, g_ref, log_ref, qp_ref, kp_ref, inv_ref, gain_ref,
                     cos_ref, sin_ref, begin_ref, sq_ref, sk_ref, gv_ref, sums_ref, part_ref,
                     keys_sum, values_sum, queries_sum, held, g_held):
    low = jnp.bfloat16
    span = q_ref.shape[0]
    pairs, piece = piece_map(span, size)
    for natural, block in pairs:
        g_held[natural : natural + piece, :] = g_ref[block : block + piece, :]
    flipped = k_ref[...].astype(jnp.float32).T.astype(low)
    keys_sum[...] = jnp.zeros_like(keys_sum)
    values_sum[...] = jnp.zeros_like(values_sum)
    for i in range(span // size):
        last = (i + 1) * size
        cols = slice(i * size, last)
        scores = nt(k_ref[:last, :], q_ref[cols, :])
        scores = mask_scores(scores, i * size, begin_ref[:, cols], size)
        probs = jnp.exp2(scores * FOLD - log_ref[:, cols])
        grad_probs = nt(v_ref[:last, :], g_held[cols, :])
        delta = jnp.sum(probs * grad_probs, axis=0, keepdims=True)
        grad_scores = (probs * (grad_probs - delta)).astype(low)
        values_sum[:last, :] += nn(probs.astype(low), g_held[cols, :])
        keys_sum[:last, :] += nn(grad_scores, q_ref[cols, :])
        queries_sum[cols, :] = nn(flipped[:, :last], grad_scores).T

    def finish(total_ref, pre_ref, out_ref, col):
        for natural, block in pairs:
            held[block : block + piece, :] = total_ref[natural : natural + piece, :]
        grad = held[...] * SCALE
        back = grad * cos_ref[...] - pltpu.roll(grad, HD // 2, 1) * sin_ref[...]
        normed = pre_ref[...] * inv_ref[:, col : col + 1]
        part_ref[col : col + 1, :] = jnp.sum(back * normed, axis=0, keepdims=True)
        scaled = back * gain_ref[col : col + 1, :]
        out_ref[...] = scaled
        sums_ref[:, col : col + 1] = jnp.sum(scaled * normed, axis=1, keepdims=True)

    finish(queries_sum, qp_ref, sq_ref, 0)
    finish(keys_sum, kp_ref, sk_ref, 1)
    for natural, block in pairs:
        gv_ref[block : block + piece, :] = values_sum[natural : natural + piece, :].astype(low)


def attend_back(queries, keys, values, grads, logs, pre, inverse, gains, cosine, sine, begin, heads, size):
    slots, span, _ = pre.shape
    low, f32 = jnp.bfloat16, jnp.float32
    head = lambda offset: pl.BlockSpec((None, span, HD), lambda g, h: (g, 0, offset + h))
    every = lambda cols: pl.BlockSpec((None, span, cols), lambda g, h: (g, 0, 0))
    line = pl.BlockSpec((None, 1, span), lambda g, h: (g, 0, 0))
    wide = jax.ShapeDtypeStruct((slots, span, heads * HD), f32)
    return pl.pallas_call(
        functools.partial(attend_back_body, size),
        grid=(slots, heads),
        out_shape=[
            wide, wide, jax.ShapeDtypeStruct((slots, span, heads * HD), low),
            jax.ShapeDtypeStruct((heads, slots, span, 2), f32),
            jax.ShapeDtypeStruct((slots, 2, heads * HD), f32),
        ],
        in_specs=[
            head(0), head(0), head(0), head(0),
            pl.BlockSpec((None, None, 1, span), lambda g, h: (g, h, 0, 0)),
            head(0), head(heads), every(2),
            pl.BlockSpec((2, HD), lambda g, h: (0, h)), every(HD), every(HD), line,
        ],
        out_specs=[
            head(0), head(0), head(0),
            pl.BlockSpec((None, None, span, 2), lambda g, h: (h, g, 0, 0)),
            pl.BlockSpec((None, 2, HD), lambda g, h: (g, 0, h)),
        ],
        scratch_shapes=[pltpu.VMEM((span, HD), f32)] * 4 + [pltpu.VMEM((span, HD), low)],
        compiler_params=pltpu.CompilerParams(vmem_limit_bytes=VMEM_LIMIT),
        cost_estimate=busy(5),
        name="attend_back",
    )(queries, keys, values, grads, logs, pre, pre, inverse, gains, cosine, sine, begin)


def row_sums(value):
    return jnp.sum(value.reshape(-1, 8, value.shape[-1]), axis=0)


def feed_body(width, slots, step, h_ref, c_ref, wg_hbm, wu_hbm, wd_hbm, hidden_ref, gain_ref, block_ref,
              first_ref, second_ref, gain_out, all_ref, act_ref, one_ref, two_ref, c_out, buf, wg, wu, wd, stage, out_ref,
              c_held, here, load, send, recv, side_send, side_recv, store, keep, *sum_refs):
    me = lax.axis_index("wide")
    planes = width // slots
    rows, cols = h_ref.shape
    hidden = wg.shape[1]
    half = rows // 2
    low = jnp.bfloat16
    loads = local_copies([(wg_hbm, wg), (wu_hbm, wu), (wd_hbm, wd)], load)
    mine = pltpu.make_async_copy(h_ref, buf.at[me], here)
    mine.start()
    for copy in loads:
        copy.start()
    hops = Hops(planes, slots, rows)
    hello(wide_peers(width, me) + [{"blk": (hops.plane + k) % planes} for k in range(1, planes)])
    flow = Flow(me, h_ref, lambda who, part: buf.at[who, pl.ds(part * half, half)], half, send, recv)
    sums = Sums(width, me, out_ref, sum_refs)
    outs = (act_ref, one_ref, two_ref)
    pending = [[], []]
    turn_count = [0]
    kept = []

    def where(k):
        who = flip(me, k)
        return pl.multiple_of(((who % slots) * planes + who // slots) * rows, rows)

    def keep_block(k):
        copy = pltpu.make_async_copy(buf.at[flip(me, k)], all_ref.at[pl.ds(where(k), rows)], keep.at[k])
        copy.start()
        kept.append(copy)

    def work(k, part, put, adds=()):
        first, count = (0, rows) if part is None else (part * half, half)
        slot = turn_count[0] % 2
        turn_count[0] += 1
        for copy in pending[slot]:
            copy.wait()
        block = buf.at[flip(me, k), pl.ds(first, count)]
        act, one, two = (stage.at[slot, i, pl.ds(0, count)] for i in range(3))

        def inner(n, carry):
            at = pl.ds(pl.multiple_of(n * step, step), step)
            gate = jnp.dot(block[...], wg[:, at], preferred_element_type=jnp.float32)
            upward = jnp.dot(block[...], wu[:, at], preferred_element_type=jnp.float32)
            sigmoid = jax.nn.sigmoid(gate)
            silu = gate * sigmoid
            act[:, at] = (silu * upward).astype(low)
            one[:, at] = silu.astype(low)
            two[:, at] = (upward * (sigmoid + silu * (1.0 - sigmoid))).astype(low)
            return carry

        lax.fori_loop(0, hidden // step, inner, 0)
        target = pl.ds(pl.multiple_of(where(k) + first, half), count)
        pending[slot] = []
        for i, ref in enumerate(outs):
            copy = pltpu.make_async_copy(stage.at[slot, i, pl.ds(0, count)], ref.at[target], store.at[slot, i])
            copy.start()
            pending[slot].append(copy)
        broad = 2 * step

        def outer(n, carry):
            at = pl.ds(pl.multiple_of(n * broad, broad), broad)
            total = jnp.dot(act[...], wd[:, at], preferred_element_type=jnp.float32)
            for ref in adds:
                total = total + ref[:, at].astype(jnp.float32)
            put[:, at] = total.astype(put.dtype)
            return carry

        lax.fori_loop(0, cols // broad, outer, 0)

    def odd_work(k, part):
        if part is None:
            work(k + 1, None, sums.odd.at[k // 2])
            sums.give(k)
        else:
            work(k + 1, part, sums.odd.at[k // 2, sums.rows(part)])
            sums.twin(k, part).start()

    def even_work(k, part):
        i = k // 2
        if part is None:
            sums.got(k)
            work(k, None, sums.even.at[i - 1], (sums.from_twin.at[i],))
        else:
            sums.twin(k, part).wait_recv()
            at = sums.rows(part)
            work(k, part, sums.even.at[i - 1, at], (sums.from_twin.at[i, at],))

    if width == 8:
        flow.go(None, 2, 2, 0)
        flow.go(None, 4, 4, 1)
        flow.go(None, 1, 1, 0)
        flow.go(None, 1, 1, 1)
        hops.join(c_ref, c_out, side_send, side_recv, True, True)
        mine.wait()
        for copy in loads:
            copy.wait()
        work(0, None, out_ref)
        keep_block(0)
        flow.arrived(1, 0)
        flow.arrived(1, 1)
        keep_block(1)
        odd_work(0, None)
        flow.arrived(2, 0)
        flow.go(2, 4, 6, 0)
        flow.arrived(4, 1)
        flow.go(4, 2, 6, 1)
        flow.go(2, 1, 3, 0)
        flow.go(4, 1, 5, 1)
        flow.go(None, 2, 2, 1)
        flow.go(None, 4, 4, 0)
        flow.arrived(3, 0)
        odd_work(2, 0)
        flow.arrived(5, 1)
        odd_work(4, 1)
        even_work(2, 0)
        even_work(4, 1)
        for part in (0, 1):
            flow.arrived(6, part)
            flow.go(6, 1, 7, part)
        for part in (0, 1):
            flow.arrived(7, part)
        keep_block(6)
        keep_block(7)
        odd_work(6, None)
        even_work(6, None)
        sums.relay(0).start()
        sums.relay(1).start()
        flow.arrived(2, 1)
        flow.go(2, 1, 3, 1)
        flow.arrived(4, 0)
        flow.go(4, 1, 5, 0)
        sums.far(2, 0).start()
        sums.far(4, 1).start()
        flow.arrived(3, 1)
        odd_work(2, 1)
        flow.arrived(5, 0)
        odd_work(4, 0)
        for k in (2, 3, 4, 5):
            keep_block(k)
        even_work(2, 1)
        sums.pass_on(2, 1)
        even_work(4, 0)
        sums.pass_on(4, 0)
    else:
        hops.join(c_ref, c_out, side_send, side_recv, True, True)
        for k in range(2, width, 2):
            flow.go(None, k, k, 0)
            flow.go(None, k, k, 1)
        flow.go(None, 1, 1, 0)
        flow.go(None, 1, 1, 1)
        mine.wait()
        for copy in loads:
            copy.wait()
        work(0, None, out_ref)
        keep_block(0)
        flow.arrived(1, 0)
        flow.arrived(1, 1)
        keep_block(1)
        odd_work(0, None)
        for k in range(2, width, 2):
            for part in (0, 1):
                flow.arrived(k, part)
                flow.go(k, 1, k + 1, part)
            for part in (0, 1):
                flow.arrived(k + 1, part)
            keep_block(k)
            keep_block(k + 1)
            odd_work(k, None)
            even_work(k, None)
            sums.far(k, 0).start()
            sums.far(k, 1).start()
    sums.got(0)
    out_ref[...] = out_ref[...] + sums.from_twin[0].astype(jnp.float32)
    sums.finish()
    flow.finish()
    hops.join(c_ref, c_out, side_send, side_recv, True, False)
    held = pltpu.make_async_copy(c_out, c_held, here)
    held.start()
    held.wait()
    gain_out[...] = jnp.zeros_like(gain_out)
    few = 32
    own = cols // planes
    half_own = own // 2

    def norm(n, carry):
        at = pl.ds(pl.multiple_of(n * few, few), few)
        value = out_ref[at, :]
        inverse = lax.rsqrt(jnp.sum(value * value, axis=-1, keepdims=True) * (1.0 / cols) + EPS)
        normed = value * inverse
        block_ref[at, :] = (hidden_ref[at, :] + normed * gain_ref[...]).astype(low)
        grad = c_held[at, :].astype(jnp.float32)
        gain_out[...] = gain_out[...] + row_sums(grad * normed)
        grad = grad * gain_ref[...]
        mean = jnp.sum(grad * normed, axis=-1, keepdims=True) * (1.0 / cols)
        grad = (inverse * (grad - normed * mean)).astype(low)
        for b in range(planes):
            for side in (0, 1):
                first = b * own + side * half_own
                (first_ref, second_ref)[side][at, b * half_own : (b + 1) * half_own] = grad[:, first : first + half_own]
        return carry

    lax.fori_loop(0, rows // few, norm, 0)
    for copy in kept + pending[0] + pending[1]:
        copy.wait()


def feed(h, side_x, gate_weight, up_weight, down_weight, hidden, gain, width, slots, ident, name):
    rows, cols = h.shape
    inner = gate_weight.shape[1]
    low, f32, dma = h.dtype, jnp.float32, pltpu.SemaphoreType.DMA
    step = min(512, inner)
    anywhere, vmem = pl.BlockSpec(memory_space=pl.ANY), pl.BlockSpec(memory_space=pltpu.VMEM)
    saved = jax.ShapeDtypeStruct((rows * width, inner), low)
    return pl.pallas_call(
        functools.partial(feed_body, width, slots, step),
        out_shape=[
            jax.ShapeDtypeStruct((rows, cols), low), jax.ShapeDtypeStruct((rows, cols // 2), low),
            jax.ShapeDtypeStruct((rows, cols // 2), low),
            jax.ShapeDtypeStruct((8, cols), f32), jax.ShapeDtypeStruct((rows * width, cols), low),
            saved, saved, saved, jax.ShapeDtypeStruct((rows, cols), low),
        ],
        in_specs=[anywhere] * 5 + [vmem] * 2,
        out_specs=[vmem] * 4 + [anywhere] * 5,
        scratch_shapes=[
            pltpu.VMEM((width, rows, cols), low), pltpu.VMEM((cols, inner), low), pltpu.VMEM((cols, inner), low),
            pltpu.VMEM((inner, cols), low), pltpu.VMEM((2, 3, rows, inner), low),
            pltpu.VMEM((rows, cols), f32), pltpu.VMEM((rows, cols), low),
            dma, dma((3,)), dma((width, 2)), dma((width, 2)), dma((width // slots,)), dma((width // slots,)),
            dma((2, 3)), dma((width,)),
        ] + sum_scratch(width, rows, cols),
        cost_estimate=busy(90),
        compiler_params=pltpu.CompilerParams(collective_id=ident, has_side_effects=True, vmem_limit_bytes=VMEM_LIMIT),
        name=name,
    )(h, side_x, gate_weight, up_weight, down_weight, hidden, gain)


def push_body(second, width, slots, *refs):
    if second:
        (g_ref, act_hbm, wd_hbm, one_hbm, two_hbm, first_hbm, down_ref, gg_ref, gu_ref,
         buf, held, acts, here, send, recv, fetch, wd, before, ins, outs, load, take, store) = refs
    else:
        (g_ref, act_hbm, c_ref, down_ref, all_ref, c_out,
         buf, held, acts, here, send, recv, fetch, keep, side_send, side_recv) = refs
    me = lax.axis_index("wide")
    planes = width // slots
    pairs = width // 2
    rows, cols = g_ref.shape
    inner = down_ref.shape[0]
    half = rows // 2
    low = jnp.bfloat16
    mine = pltpu.make_async_copy(g_ref, buf.at[me // 2, me % 2], here)
    mine.start()

    def where(pair, side):
        who = flip(me // 2, pair) * 2 + side
        return pl.ds(pl.multiple_of(((who % slots) * planes + who // slots) * rows, rows), rows)

    def fetches(pair):
        copies = [
            pltpu.make_async_copy(act_hbm.at[where(pair, side)], acts.at[pair % 2, side], fetch.at[pair % 2, side])
            for side in (0, 1)
        ]
        if second:
            copies += [
                pltpu.make_async_copy(ref.at[where(pair, side)], ins.at[pair % 2, i, side], take.at[pair % 2, i, side])
                for i, ref in enumerate((one_hbm, two_hbm))
                for side in (0, 1)
            ]
        return copies

    def stores(pair):
        return [
            pltpu.make_async_copy(outs.at[pair % 2, i, side], ref.at[where(pair, side)], store.at[pair % 2, i, side])
            for i, ref in enumerate((gg_ref, gu_ref))
            for side in (0, 1)
        ]

    def keeps(pair):
        chip = flip(me // 2, pair)
        return pltpu.make_async_copy(buf.at[chip], all_ref.at[chip], keep.at[pair])

    for copy in fetches(0):
        copy.start()
    peers = wide_peers(width, me)
    if second:
        own = cols // planes
        loads = [
            pltpu.make_async_copy(
                wd_hbm.at[:, pl.ds((2 * b + side) * own, own)], wd.at[:, pl.ds(side * cols + b * own, own)],
                load.at[b, side],
            )
            for b in range(planes)
            for side in (0, 1)
        ]
        loads.append(pltpu.make_async_copy(first_hbm, before, load.at[planes, 0]))
        for copy in loads:
            copy.start()
    else:
        hops = Hops(planes, slots, rows)
        peers = peers + [{"blk": (hops.plane + k) % planes} for k in range(1, planes)]
    hello(peers)
    flow = Flow(me, g_ref, lambda who, part: buf.at[who // 2, who % 2, pl.ds(part * half, half)], half, send, recv)

    def work(pair):
        for copy in fetches(pair):
            copy.wait()
        if pair + 1 < pairs:
            for copy in fetches(pair + 1):
                copy.start()
        chip = flip(me // 2, pair)
        slot = pair % 2
        grads = buf[chip].reshape(2 * rows, cols)
        if second:
            if pair >= 2:
                for copy in stores(pair - 2):
                    copy.wait()
            old = before[chip].reshape(2 * rows, cols)
            step = min(512, inner)

            def units(n, carry):
                at = pl.ds(pl.multiple_of(n * step, step), step)
                grad = (nt(old, wd[at, :cols]) + nt(grads, wd[at, cols:])).reshape(2, rows, step)
                outs[slot, 0, :, :, at] = (grad * ins[slot, 1, :, :, at].astype(jnp.float32)).astype(low)
                outs[slot, 1, :, :, at] = (grad * ins[slot, 0, :, :, at].astype(jnp.float32)).astype(low)
                return carry

            lax.fori_loop(0, inner // step, units, 0)
            for copy in stores(pair):
                copy.start()
        else:
            keeps(pair).start()
        tall = min(512, inner)

        def outer(n, carry):
            at = pl.ds(pl.multiple_of(n * tall, tall), tall)
            act = acts[slot, :, :, at].reshape(2 * rows, tall)
            term = lax.dot_general(act, grads, (((0,), (0,)), ((), ())), preferred_element_type=jnp.float32)
            if pair:
                term = term + held[at, :]
            if pair + 1 < pairs:
                held[at, :] = term
            else:
                down_ref[at, :] = term.astype(low)
            return carry

        lax.fori_loop(0, inner // tall, outer, 0)

    def pair_ready(k):
        for part in (0, 1):
            flow.arrived(k + 1, part)

    if width == 8:
        flow.go(None, 2, 2, 0)
        flow.go(None, 4, 4, 1)
        flow.go(None, 2, 2, 1)
        flow.go(None, 4, 4, 0)
    else:
        for k in range(2, width, 2):
            flow.go(None, k, k, 0)
            flow.go(None, k, k, 1)
    flow.go(None, 1, 1, 0)
    flow.go(None, 1, 1, 1)
    if second:
        for copy in loads:
            copy.wait()
    else:
        hops.spread(c_ref, c_out, side_send, side_recv, True, True)
    mine.wait()
    pair_ready(0)
    work(0)
    if width == 8:
        flow.arrived(2, 0)
        flow.go(2, 4, 6, 0)
        flow.go(2, 1, 3, 0)
        flow.arrived(4, 1)
        flow.go(4, 2, 6, 1)
        flow.go(4, 1, 5, 1)
        flow.arrived(2, 1)
        flow.go(2, 1, 3, 1)
        flow.arrived(4, 0)
        flow.go(4, 1, 5, 0)
        pair_ready(2)
        work(1)
        pair_ready(4)
        work(2)
        for part in (0, 1):
            flow.arrived(6, part)
            flow.go(6, 1, 7, part)
        pair_ready(6)
        work(3)
    else:
        for k in range(2, width, 2):
            for part in (0, 1):
                flow.arrived(k, part)
                flow.go(k, 1, k + 1, part)
            pair_ready(k)
            work(k // 2)
    flow.finish()
    if second:
        for pair in (pairs - 2, pairs - 1):
            for copy in stores(pair):
                copy.wait()
    else:
        for pair in range(pairs):
            keeps(pair).wait()
        hops.spread(c_ref, c_out, side_send, side_recv, True, False)


def push(second, g, act, width, slots, ident, name, others):
    rows, cols = g.shape
    inner = act.shape[1]
    low, dma = g.dtype, pltpu.SemaphoreType.DMA
    planes, pairs = width // slots, width // 2
    anywhere, vmem = pl.BlockSpec(memory_space=pl.ANY), pl.BlockSpec(memory_space=pltpu.VMEM)
    blocks = (pairs, 2, rows, cols)
    scratch = [
        pltpu.VMEM(blocks, low), pltpu.VMEM((inner, cols), jnp.float32), pltpu.VMEM((2, 2, rows, inner), low),
        dma, dma((width, 2)), dma((width, 2)), dma((2, 2)),
    ]
    shapes = [jax.ShapeDtypeStruct((inner, cols), low)]
    if second:
        saved = jax.ShapeDtypeStruct((rows * width, inner), low)
        shapes += [saved, saved]
        scratch += [
            pltpu.VMEM((inner, 2 * cols), low), pltpu.VMEM(blocks, low), pltpu.VMEM((2, 2, 2, rows, inner), low),
            pltpu.VMEM((2, 2, 2, rows, inner), low), dma((planes + 1, 2)), dma((2, 2, 2)), dma((2, 2, 2)),
        ]
    else:
        shapes += [
            jax.ShapeDtypeStruct(blocks, low),
            jax.ShapeDtypeStruct((many_rows(planes, rows), others[0].shape[1]), low),
        ]
        scratch += [dma((pairs,)), dma((planes,)), dma((planes,))]
    inputs = [g, act] + others
    return pl.pallas_call(
        functools.partial(push_body, second, width, slots),
        out_shape=shapes,
        in_specs=[anywhere] * len(inputs),
        out_specs=[vmem] + [anywhere] * (len(shapes) - 1),
        scratch_shapes=scratch,
        cost_estimate=busy(10),
        compiler_params=pltpu.CompilerParams(collective_id=ident, has_side_effects=True, vmem_limit_bytes=VMEM_LIMIT),
        name=name,
    )(*inputs)


def pull_body(width, slots, step, chunk, gg_hbm, gu_hbm, wg_hbm, wu_hbm, h_hbm, c_ref, normed_ref, inv_ref, gain_ref,
              out_ref, proj_ref, gain_out, du_hbm, gg, gu, wg, wu, columns, tiles, load, take, fetch, store, *sum_refs):
    me = lax.axis_index("wide")
    planes = width // slots
    rows, cols = out_ref.shape
    half = rows // 2
    chunks = cols // chunk
    loads = local_copies([(wg_hbm, wg), (wu_hbm, wu)], load)
    for copy in loads:
        copy.start()

    def where(k, first, count):
        who = flip(me, k)
        start = ((who % slots) * planes + who // slots) * rows + first
        return pl.ds(pl.multiple_of(start, half), count)

    def takes(k):
        at = where(k, 0, rows)
        return [
            pltpu.make_async_copy(src.at[at], dst.at[at], take.at[k, i])
            for i, (src, dst) in enumerate(((gg_hbm, gg), (gu_hbm, gu)))
        ]

    order = [7, 6, 3, 5, 2, 4, 1, 0] if width == 8 else [k ^ 1 for k in range(width)]
    for k in order:
        for copy in takes(k):
            copy.start()
    taken = []

    def need(k):
        if k not in taken:
            taken.append(k)
            for copy in takes(k):
                copy.wait()

    def fetched(n):
        at = pl.ds(pl.multiple_of(n * chunk, chunk), chunk)
        return pltpu.make_async_copy(h_hbm.at[:, at], columns.at[n % 2], fetch.at[n % 2])

    def stored(n):
        at = pl.ds(pl.multiple_of(n * chunk, chunk), chunk)
        return [
            pltpu.make_async_copy(tiles.at[n % 2, i], ref.at[at], store.at[n % 2, i])
            for i, ref in enumerate((du_hbm,))
        ]

    fetched(0).start()
    hello(wide_peers(width, me))
    sums = Sums(width, me, out_ref, sum_refs)

    def produce(k, first, count, put, adds=()):
        need(k)
        at_rows = where(k, first, count)

        def tile(n, carry):
            at = pl.ds(pl.multiple_of(n * step, step), step)
            total = nt(gg[at_rows, :], wg[at, :]) + nt(gu[at_rows, :], wu[at, :])
            for ref in adds:
                total = total + ref[:, at].astype(jnp.float32)
            put[:, at] = total.astype(put.dtype)
            return carry

        lax.fori_loop(0, cols // step, tile, 0)

    def grads(first, last):
        for k in order:
            need(k)

        def one_chunk(n, carry):
            fetched(n).wait()

            @pl.when(n + 1 < chunks)
            def _():
                fetched(n + 1).start()

            @pl.when(n >= 2)
            def _():
                for copy in stored(n - 2):
                    copy.wait()

            for i, ref in enumerate((gu,)):
                tiles[n % 2, i] = lax.dot_general(
                    columns[n % 2], ref[...], (((0,), (0,)), ((), ())), preferred_element_type=jnp.float32
                ).astype(jnp.bfloat16)
            for copy in stored(n):
                copy.start()
            return carry

        lax.fori_loop(first, last, one_chunk, 0)

    for copy in loads:
        copy.wait()
    run_sums(width, sums, produce, grads, chunks)
    gain_out[...] = jnp.zeros_like(gain_out)
    few = 32

    def norm(n, carry):
        at = pl.ds(pl.multiple_of(n * few, few), few)
        grad = out_ref[at, :] + c_ref[at, :].astype(jnp.float32)
        out_ref[at, :] = grad
        normed = normed_ref[at, :]
        gain_out[...] = gain_out[...] + row_sums(grad * normed)
        grad = grad * gain_ref[...]
        mean = jnp.sum(grad * normed, axis=-1, keepdims=True) * (1.0 / cols)
        proj_ref[at, :] = (inv_ref[at, :] * (grad - normed * mean)).astype(jnp.bfloat16)
        return carry

    lax.fori_loop(0, rows // few, norm, 0)
    for copy in stored(chunks - 2) + stored(chunks - 1):
        copy.wait()


def pull(grad_gate, grad_up, gate_weight, up_weight, gathered, grad_out, normed, inverse, gain, width, slots, ident, name):
    count, cols = gathered.shape
    inner = gate_weight.shape[1]
    rows = count // width
    low, f32, dma = gathered.dtype, jnp.float32, pltpu.SemaphoreType.DMA
    chunk = 256
    anywhere, vmem = pl.BlockSpec(memory_space=pl.ANY), pl.BlockSpec(memory_space=pltpu.VMEM)
    return pl.pallas_call(
        functools.partial(pull_body, width, slots, 1024, chunk),
        out_shape=[
            jax.ShapeDtypeStruct((rows, cols), f32), jax.ShapeDtypeStruct((rows, cols), low),
            jax.ShapeDtypeStruct((8, cols), f32), jax.ShapeDtypeStruct((cols, inner), low),
        ],
        in_specs=[anywhere] * 5 + [vmem] * 4,
        out_specs=[vmem] * 3 + [anywhere],
        scratch_shapes=[
            pltpu.VMEM((count, inner), low), pltpu.VMEM((count, inner), low),
            pltpu.VMEM((cols, inner), low), pltpu.VMEM((cols, inner), low),
            pltpu.VMEM((2, count, chunk), low), pltpu.VMEM((2, 1, chunk, inner), low),
            dma((2,)), dma((width, 2)), dma((2,)), dma((2, 1)),
        ] + sum_scratch(width, rows, cols),
        cost_estimate=busy(10),
        compiler_params=pltpu.CompilerParams(collective_id=ident, has_side_effects=True, vmem_limit_bytes=VMEM_LIMIT),
        name=name,
    )(grad_gate, grad_up, gate_weight, up_weight, gathered, grad_out, normed, inverse, gain)


def close_body(t_ref, s_ref, b_ref, tokens_ref, q_ref, k_ref, v_ref, o_ref, block_ref):
    share = q_ref.shape[1]
    tokens_ref[...] = t_ref[...].astype(jnp.float32)
    block_ref[...] = b_ref[...]
    for i, ref in enumerate((q_ref, k_ref, v_ref)):
        ref[...] = s_ref[:, i * share : (i + 1) * share].astype(jnp.float32)
    o_ref[...] = s_ref[:, 3 * share :].astype(jnp.float32).T


def closing(tokens_low, side_grad, block_output):
    rows, cols = tokens_low.shape
    depth, extent = side_grad.shape
    share, f32, steps = extent // 4, jnp.float32, 2
    down = lambda a, b: pl.BlockSpec((a // steps, b), lambda n: (n, 0))
    weight = jax.ShapeDtypeStruct((depth, share), f32)
    return pl.pallas_call(
        close_body,
        grid=(steps,),
        out_shape=[
            jax.ShapeDtypeStruct((rows, cols), f32), weight, weight, weight,
            jax.ShapeDtypeStruct((share, depth), f32), jax.ShapeDtypeStruct((rows, cols), block_output.dtype),
        ],
        in_specs=[down(rows, cols), down(depth, extent), down(rows, cols)],
        out_specs=[down(rows, cols)] + [down(depth, share)] * 3
        + [pl.BlockSpec((share, depth // steps), lambda n: (0, n)), down(rows, cols)],
        compiler_params=pltpu.CompilerParams(vmem_limit_bytes=VMEM_LIMIT),
        cost_estimate=busy(5),
        name="closing",
    )(tokens_low, side_grad, block_output)


def side_body(x_ref, p_ref, qk_ref, v_ref, m_ref, out_ref):
    first = 0
    for left, right in ((x_ref, qk_ref), (x_ref, v_ref), (p_ref, m_ref)):
        last = first + right.shape[1]
        out_ref[:, first:last] = lax.dot_general(
            left[...], right[...], (((0,), (0,)), ((), ())), preferred_element_type=jnp.float32
        ).astype(out_ref.dtype)
        first = last


def side_grads(inputs, grad_proj, grad_qk, grad_v, mixed):
    count, cols = inputs.shape
    extent = grad_qk.shape[1] + grad_v.shape[1] + mixed.shape[1]
    chunk = 256
    return pl.pallas_call(
        side_body,
        grid=(cols // chunk,),
        out_shape=jax.ShapeDtypeStruct((cols, extent), inputs.dtype),
        in_specs=[
            pl.BlockSpec((count, chunk), lambda n: (0, n)), pl.BlockSpec((count, chunk), lambda n: (0, n)),
            pl.BlockSpec(grad_qk.shape, lambda n: (0, 0)), pl.BlockSpec(grad_v.shape, lambda n: (0, 0)),
            pl.BlockSpec(mixed.shape, lambda n: (0, 0)),
        ],
        out_specs=pl.BlockSpec((chunk, extent), lambda n: (n, 0)),
        compiler_params=pltpu.CompilerParams(vmem_limit_bytes=VMEM_LIMIT),
        cost_estimate=busy(10),
        name="side_grads",
    )(inputs, grad_proj, grad_qk, grad_v, mixed)


def local(
    tokens,
    lengths,
    query_weight,
    key_weight,
    value_weight,
    output_weight,
    query_gain,
    key_gain,
    attention_gain,
    gate_weight,
    up_weight,
    down_weight,
    feedforward_gain,
    cotangent,
):
    low, f32 = jnp.bfloat16, jnp.float32
    planes, width = lax.axis_size("blk"), lax.axis_size("wide")
    slots = width // planes
    rows = tokens.shape[1]
    span = rows * planes
    count = slots * span
    share = query_weight.shape[1]
    heads = share // HD
    plane, place = lax.axis_index("blk"), lax.axis_index("wide")
    after = lambda value, *others: lax.optimization_barrier((value,) + others)[0]

    def sum_blk(value, axis):
        return lax.psum_scatter(value, "blk", scatter_dimension=axis, tiled=True)

    _, near_cotangent, mine = turn(
        turn_in_body, [tokens[0], cotangent[0]], [True, True, False], planes, slots, 1, "turn_in"
    )
    w_qk = after(jnp.concatenate([query_weight, key_weight], 1), mine)
    w_qk = lax.all_gather(w_qk, "blk", axis=0, tiled=True)
    gains = jnp.stack([query_gain, key_gain]).astype(f32)
    plane_lengths = lax.dynamic_slice_in_dim(lengths, plane * slots, slots, 0)
    segment, position = jax.vmap(lambda one: layout(one, span))(plane_lengths)
    begin = (jnp.arange(span, dtype=jnp.int32)[None] - position)[:, None, :]
    pairs, piece = piece_map(span, rows)
    order = sorted(pairs, key=lambda pair: pair[1])
    index = np.concatenate([np.arange(at, at + piece) for at, _ in order])
    starts = jnp.stack([plane_lengths[:, 0] * 0, plane_lengths[:, 0], plane_lengths[:, 0] + plane_lengths[:, 1]], 1)
    cos_a, sin_a, cos_b, sin_b, sign = rope_tables(index, starts)
    group = jnp.concatenate([segment[:, at : at + piece] for at, _ in order], 1)[..., None]
    pick = lambda table: jnp.where(
        group == 0, table[:, 0:1], jnp.where(group == 1, table[:, 1:2], table[:, 2:3])
    )
    cos_b, sin_b = pick(cos_b), pick(sin_b)
    cosine = cos_a * cos_b + sin_a * sin_b
    sine = (sin_a * cos_b - cos_a * sin_b) * sign

    inputs = gather(mine, width, slots, 2, "gather_tokens")
    w_v = lax.all_gather(after(value_weight, inputs), "blk", axis=0, tiled=True)
    pre = dot(inputs, w_qk)
    w_o = lax.all_gather(after(output_weight, pre), "blk", axis=1, tiled=True)
    squares = jnp.stack([jnp.sum(pre[:, a * share : (a + 1) * share] ** 2, -1) for a in (0, 1)])
    both = lax.dynamic_update_slice(
        jnp.zeros((2, D), f32), jnp.stack([attention_gain, feedforward_gain]).astype(f32), (0, place * share)
    )
    squares = jnp.concatenate([squares.reshape(-1, 128), both.reshape(-1, 128)])
    squares = total(squares, "wide", width, 3, "total_squares")
    both = squares[2 * count // 128 :].reshape(2, D)
    gain_mix, gain_feed = both[0], both[1]
    inverse = lax.rsqrt(squares[: 2 * count // 128].reshape(2, count) / D + EPS)
    inv_cols = inverse.T.reshape(slots, span, 2)
    pre_groups = pre.reshape(slots, span, 2 * share)
    value_rows = dot(inputs, after(w_v, squares)).astype(low).reshape(slots, span, share)
    queries, keys, values, mixed, logs = attend(
        pre_groups, value_rows, inv_cols, gains, cosine, sine, begin, heads, rows
    )
    mixed = mixed.reshape(count, share)
    hidden, hidden_low, proj_normed, proj_inv = scatter(
        [mixed], [w_o], width, slots, False, 4, "scatter_mixed", "norm", (mine, gain_mix[None])
    )
    block_output, first_half, second_half, feed_gain_part, gathered, activated, up_factor, gate_factor, grad_out = feed(
        hidden_low, near_cotangent, gate_weight, up_weight, down_weight, hidden, gain_feed[None], width, slots, 5,
        "feed",
    )
    down_first, first_rows, far_output = push(
        False, first_half, activated, width, slots, 6, "push_first", [block_output]
    )
    down_first = sum_blk(down_first, 1)
    down_second, grad_gate, grad_up = push(
        True, second_half, activated, width, slots, 7, "push_second",
        [down_weight, up_factor, gate_factor, first_rows],
    )
    down_second = sum_blk(down_second, 1)
    gate_part = contract_rows(gathered, grad_gate).astype(low)
    gate_grad = sum_blk(gate_part, 0)
    grad_hidden, grad_proj, mix_gain_part, up_part = pull(
        after(grad_gate, gate_part, down_first), grad_up, gate_weight, up_weight, gathered, grad_out, proj_normed,
        proj_inv, gain_mix[None], width, slots, 8, "pull",
    )
    up_grad = sum_blk(up_part, 0)
    grad_proj = gather(grad_proj, width, slots, 9, "gather_proj")
    grad_mixed = contract_cols(after(grad_proj, down_first, down_second), w_o).astype(low).reshape(slots, span, share)
    scaled_q, scaled_k, grad_v, sums, parts = attend_back(
        queries, keys, values, grad_mixed, logs, pre_groups, inv_cols, gains, cosine, sine, begin,
        heads, rows,
    )
    means = jnp.sum(sums, axis=0).reshape(count, 2).T.reshape(-1, 128)
    local_gains = lax.dynamic_update_slice(
        jnp.zeros((2, D), f32), jnp.sum(parts, axis=0), (0, place * share)
    )
    gain_parts = jnp.concatenate([local_gains, jnp.stack([mix_gain_part.sum(0), feed_gain_part.sum(0)])])
    means = jnp.concatenate([means, gain_parts.reshape(-1, 128)])
    means = total(after(means, gate_grad), "wide", width, 10, "total_means")
    gain_parts = means[2 * count // 128 :]
    means = means[: 2 * count // 128].reshape(2, count) / D

    def finish(scaled, index):
        normed = pre[:, index * share : (index + 1) * share] * inverse[index][:, None]
        scaled = scaled.reshape(count, share)
        return (inverse[index][:, None] * (scaled - normed * means[index][:, None])).astype(low)

    grad_qk = jnp.concatenate([finish(scaled_q, 0), finish(scaled_k, 1)], 1)
    grad_v = grad_v.reshape(count, share)
    side_part = side_grads(inputs, grad_proj, grad_qk, grad_v, mixed)
    tokens_low = scatter(
        [grad_qk, grad_v], [w_qk, w_v], width, slots, True, 11, "scatter_tokens", "add", (grad_hidden,)
    )
    down_grad = jnp.concatenate([down_first, down_second], 1).astype(f32)
    gate_grad, up_grad = gate_grad.astype(f32), up_grad.astype(f32)
    tokens_low, down_grad, gate_grad, up_grad = lax.optimization_barrier((tokens_low, down_grad, gate_grad, up_grad))
    _, block_output, tokens_grad, gain_sums = turn(
        turn_out_body, [tokens_low, far_output], [True, False, False],
        planes, slots, 14, "turn_out", gain_parts,
    )
    tokens_grad, query_grad, key_grad, value_grad, output_grad, block_output = closing(
        tokens_grad, sum_blk(side_part, 0), block_output
    )

    sums = gain_sums.reshape(4, D)
    portion = D // (planes * width)
    sums = lax.dynamic_slice_in_dim(sums, (plane * width + place) * portion, portion, 1)
    return (
        block_output[None],
        tokens_grad[None],
        query_grad,
        key_grad,
        value_grad,
        output_grad,
        sums[0],
        sums[1],
        sums[2],
        gate_grad,
        up_grad,
        down_grad,
        sums[3],
    )


def solution(mesh):
    placed = (
        P("wide", "blk", None),
        P(),
        P("blk", "wide"),
        P("blk", "wide"),
        P("blk", "wide"),
        P("wide", "blk"),
        P("wide"),
        P("wide"),
        P("wide"),
        P(None, "wide"),
        P(None, "wide"),
        P("wide", None),
        P("wide"),
        P("wide", "blk", None),
    )
    return jax.shard_map(
        local,
        mesh=mesh,
        in_specs=placed,
        out_specs=(
            P("wide", "blk", None),
            P("wide", "blk", None),
            P("blk", "wide"),
            P("blk", "wide"),
            P("blk", "wide"),
            P("wide", "blk"),
            P(("blk", "wide")),
            P(("blk", "wide")),
            P(("blk", "wide")),
            P("blk", "wide"),
            P("blk", "wide"),
            P("wide", "blk"),
            P(("blk", "wide")),
        ),
        check_vma=False,
    )
```

```python
import functools

import jax
import jax.numpy as jnp
import numpy as np
from jax import lax
from jax.experimental import pallas as pl
from jax.experimental.pallas import tpu as pltpu
from jax.sharding import PartitionSpec as P

MESH = pl.DeviceIdType.MESH

D = 2048
HD = 128
EPS = 1e-06
ROPE_BASE = 500000.0
NEG_FILL = -1e30
VMEM_LIMIT = 60 * 1024 * 1024
SCALE = HD ** (-0.5)
FOLD = SCALE * 1.4426950408889634


def busy(micros):
    return pl.CostEstimate(flops=0, bytes_accessed=int(micros * 3.5e6), transcendentals=0)


def layout(seq_lengths, row_count):
    indices = jnp.arange(row_count, dtype=jnp.int32)
    first_end = seq_lengths[0]
    second_end = seq_lengths[0] + seq_lengths[1]
    segment = (indices >= first_end).astype(jnp.int32) + (indices >= second_end).astype(jnp.int32)
    offsets = jnp.where(segment == 0, 0, jnp.where(segment == 1, first_end, second_end))
    return (segment, indices - offsets)


def rope_tables(index, begin):
    frequency = ROPE_BASE ** (-np.arange(0, HD, 2, dtype=np.float64) / HD)
    angles = np.asarray(index, np.float64)[:, None] * frequency
    sign = np.concatenate([-np.ones(HD // 2), np.ones(HD // 2)])
    twice = lambda value: np.concatenate([value, value], -1).astype(np.float32)
    cosine, sine = jnp.asarray(twice(np.cos(angles))), jnp.asarray(twice(np.sin(angles)))
    shift = begin.astype(jnp.float32)[..., None] * jnp.asarray(twice(frequency))
    return cosine, sine, jnp.cos(shift), jnp.sin(shift), jnp.asarray(sign.astype(np.float32))


def rms_pair(values):
    inverse = lax.rsqrt(jnp.mean(values * values, axis=-1, keepdims=True) + EPS)
    return (values * inverse, inverse)


def norm_back(normed, inverse, grad_normed):
    return inverse * (grad_normed - normed * jnp.mean(grad_normed * normed, axis=-1, keepdims=True))


def dot(left, right):
    return jnp.dot(left, right, preferred_element_type=jnp.float32)


def contract_rows(left, right):
    return lax.dot_general(
        left, right, (((0,), (0,)), ((), ())), preferred_element_type=jnp.float32
    )


def contract_cols(left, right):
    return lax.dot_general(
        left, right, (((1,), (1,)), ((), ())), preferred_element_type=jnp.float32
    )


def flip(me, k):
    out, bit = me, 1
    while bit <= k:
        if k & bit:
            out = out + bit * (1 - 2 * ((me // bit) % 2))
        bit *= 2
    return out


def greet(axis, me, others):
    barrier = pltpu.get_barrier_semaphore()
    for k in others:
        pl.semaphore_signal(barrier, inc=1, device_id={axis: flip(me, k)}, device_id_type=MESH)
    pl.semaphore_wait(barrier, len(others))


class Flow:
    def __init__(self, me, source, spot, half, send, recv):
        self.me, self.source, self.spot, self.half = me, source, spot, half
        self.send, self.recv, self.moves = send, recv, []

    def go(self, origin, target, k, part):
        if origin is None:
            source = self.source.at[pl.ds(part * self.half, self.half)]
        else:
            source = self.spot(flip(self.me, origin), part)
        copy = pltpu.make_async_remote_copy(
            src_ref=source,
            dst_ref=self.spot(flip(flip(self.me, target), k), part),
            send_sem=self.send.at[k, part],
            recv_sem=self.recv.at[k, part],
            device_id={"wide": flip(self.me, target)},
            device_id_type=MESH,
        )
        copy.start()
        self.moves.append(copy)

    def arrived(self, k, part):
        block = self.spot(flip(self.me, k), part)
        pltpu.make_async_copy(block, block, self.recv.at[k, part]).wait()

    def finish(self):
        for copy in self.moves:
            copy.wait_send()


class Sums:
    def __init__(self, width, me, out_ref, refs):
        self.width, self.me, self.out = width, me, out_ref
        (self.odd, self.even, self.from_twin, self.from_far, self.passing, self.sends, self.recvs,
         self.pass_send, self.pass_recv, self.twin_send, self.twin_recv) = refs
        self.half = out_ref.shape[0] // 2

    def rows(self, part):
        return pl.ds(part * self.half, self.half)

    def copy(self, src, dst, send, recv, k):
        return pltpu.make_async_remote_copy(
            src_ref=src, dst_ref=dst, send_sem=send, recv_sem=recv,
            device_id={"wide": flip(self.me, k)}, device_id_type=MESH,
        )

    def twin(self, k, part):
        i, at = k // 2, self.rows(part)
        return self.copy(
            self.odd.at[i, at], self.from_twin.at[i, at], self.twin_send.at[i, part],
            self.twin_recv.at[i, part], 1,
        )

    def far(self, k, part):
        i, at = k // 2 - 1, self.rows(part)
        return self.copy(
            self.even.at[i, at], self.from_far.at[i, at], self.sends.at[i, part], self.recvs.at[i, part], k
        )

    def relay(self, part):
        return self.copy(
            self.even.at[2, self.rows(part)], self.passing.at[part], self.pass_send.at[part],
            self.pass_recv.at[part], 2 if part == 0 else 4,
        )

    def give(self, k):
        self.twin(k, 0).start()
        self.twin(k, 1).start()

    def got(self, k):
        self.twin(k, 0).wait_recv()
        self.twin(k, 1).wait_recv()

    def pass_on(self, k, part):
        self.relay(part).wait_recv()
        at = self.rows(part)
        self.even[k // 2 - 1, at, :] = (
            self.even[k // 2 - 1, at, :].astype(jnp.float32) + self.passing[part].astype(jnp.float32)
        ).astype(jnp.bfloat16)
        self.far(k, part).start()

    def finish(self):
        sources = [2, 4] if self.width == 8 else list(range(2, self.width, 2))
        for k in sources:
            for part in (0, 1):
                self.far(k, part).wait_recv()
        extra = self.from_far[sources[0] // 2 - 1].astype(jnp.float32)
        for k in sources[1:]:
            extra = extra + self.from_far[k // 2 - 1].astype(jnp.float32)
        self.out[...] = self.out[...] + extra
        for part in (0, 1):
            for k in sources:
                self.far(k, part).wait_send()
            for k in range(0, self.width, 2):
                self.twin(k, part).wait_send()
            if self.width == 8:
                self.relay(part).wait_send()


def run_sums(width, sums, produce, beside=None, steps=0):
    half = sums.half
    rows = 2 * half

    def give(k, part=None):
        if part is None:
            produce(k + 1, 0, rows, sums.odd.at[k // 2])
            sums.give(k)
        else:
            produce(k + 1, part * half, half, sums.odd.at[k // 2, sums.rows(part)])
            sums.twin(k, part).start()

    def merge(k, part=None):
        if part is None:
            sums.got(k)
            produce(k, 0, rows, sums.even.at[k // 2 - 1], (sums.from_twin.at[k // 2],))
        else:
            sums.twin(k, part).wait_recv()
            at = sums.rows(part)
            produce(k, part * half, half, sums.even.at[k // 2 - 1, at], (sums.from_twin.at[k // 2, at],))

    if width == 8:
        give(6, 0)
        give(6, 1)
        merge(6, 0)
        sums.relay(0).start()
        merge(6, 1)
        sums.relay(1).start()
        give(2)
        give(4)
        merge(2)
        sums.far(2, 0).start()
        merge(4)
        sums.far(4, 1).start()
        sums.pass_on(2, 1)
        sums.pass_on(4, 0)
        give(0)
    else:
        for k in range(0, width, 2):
            give(k)
        for k in range(2, width, 2):
            merge(k)
            sums.far(k, 0).start()
            sums.far(k, 1).start()
    if beside is not None:
        beside(0, steps)
    sums.got(0)
    produce(0, 0, rows, sums.out, (sums.from_twin.at[0],))
    sums.finish()


def sum_scratch(width, rows, cols):
    chips, dma = width // 2, pltpu.SemaphoreType.DMA
    block = lambda n: pltpu.VMEM((n, rows, cols), jnp.bfloat16)
    return [
        block(chips), block(chips - 1), block(chips), block(2 if width == 8 else chips - 1),
        pltpu.VMEM((2, rows // 2, cols), jnp.bfloat16),
        dma((chips - 1, 2)), dma((chips - 1, 2)), dma((2,)), dma((2,)), dma((chips, 2)), dma((chips, 2)),
    ]


def wide_peers(width, me):
    return [{"wide": flip(me, k)} for k in [1] + list(range(2, width, 2))]


def local_copies(pairs, sem):
    return [pltpu.make_async_copy(src, dst, sem.at[i]) for i, (src, dst) in enumerate(pairs)]


def gather_body(width, slots, side, *refs):
    if side is None:
        x_ref, out_ref, here, send, recv = refs
    else:
        x_ref, side_ref, out_ref, side_out, here, send, recv, side_send, side_recv = refs
    me = lax.axis_index("wide")
    rows = x_ref.shape[0]
    half = rows // 2
    evens = list(range(2, width, 2))
    peers = [{"wide": flip(me, k)} for k in [1] + evens]
    if side is not None:
        hops = Hops(width // slots, slots, rows)
        peers = peers + [{"blk": (hops.plane + k) % hops.planes} for k in range(1, hops.planes)]
    hello(peers)
    if side is not None:
        job = hops.join if side == "join" else hops.spread
        job(side_ref, side_out, side_send, side_recv, True, True)

    def spot(who, first, count):
        base = ((who % slots) * (width // slots) + who // slots) * rows
        return out_ref.at[pl.ds(pl.multiple_of(base + first, half), count)]

    def move(origin, target, k, part):
        if origin is None:
            source = x_ref.at[pl.ds(part * half, half)]
        else:
            source = spot(flip(me, origin), part * half, half)
        return pltpu.make_async_remote_copy(
            src_ref=source,
            dst_ref=spot(flip(flip(me, target), k), part * half, half),
            send_sem=send.at[k, part],
            recv_sem=recv.at[k, part],
            device_id={"wide": flip(me, target)},
            device_id_type=MESH,
        )

    def arrived(k, part):
        block = spot(flip(me, k), part * half, half)
        pltpu.make_async_copy(block, block, recv.at[k, part]).wait()

    moves = []

    def go(origin, target, k, part):
        copy = move(origin, target, k, part)
        copy.start()
        moves.append(copy)

    mine = pltpu.make_async_copy(x_ref, spot(me, 0, rows), here)
    mine.start()
    if width == 8:
        go(None, 2, 2, 0)
        go(None, 4, 4, 1)
        go(None, 2, 2, 1)
        go(None, 4, 4, 0)
        go(None, 1, 1, 0)
        go(None, 1, 1, 1)
        arrived(2, 0)
        go(2, 4, 6, 0)
        go(2, 1, 3, 0)
        arrived(4, 1)
        go(4, 2, 6, 1)
        go(4, 1, 5, 1)
        order = [(2, 1), (4, 0), (6, 0), (6, 1)]
    else:
        for k in evens:
            go(None, k, k, 0)
            go(None, k, k, 1)
        go(None, 1, 1, 0)
        go(None, 1, 1, 1)
        order = [(k, part) for k in evens for part in (0, 1)]
    for k, part in order:
        arrived(k, part)
        go(k, 1, k + 1, part)
    for k in range(1, width, 2):
        for part in (0, 1):
            arrived(k, part)
    for copy in moves:
        copy.wait_send()
    mine.wait()
    if side is not None:
        job(side_ref, side_out, side_send, side_recv, True, False)


def gather(x, width, slots, ident, name, side=None, side_x=None):
    rows, cols = x.shape
    planes = width // slots
    dma = pltpu.SemaphoreType.DMA
    shapes = [jax.ShapeDtypeStruct((rows * width, cols), x.dtype)]
    scratch = [dma, dma((width, 2)), dma((width, 2))]
    inputs = [x]
    if side is not None:
        inputs.append(side_x)
        extent = rows if side == "join" else many_rows(planes, rows)
        shapes.append(jax.ShapeDtypeStruct((extent, cols), side_x.dtype))
        scratch += [dma((planes,)), dma((planes,))]
    outs = pl.pallas_call(
        functools.partial(gather_body, width, slots, side),
        out_shape=shapes,
        in_specs=[pl.BlockSpec(memory_space=pl.ANY)] * len(inputs),
        out_specs=[pl.BlockSpec(memory_space=pl.ANY)] * len(shapes),
        scratch_shapes=scratch,
        cost_estimate=busy(10),
        compiler_params=pltpu.CompilerParams(collective_id=ident, has_side_effects=True, vmem_limit_bytes=VMEM_LIMIT),
        name=name,
    )(*inputs)
    return outs[0] if side is None else outs


def scatter_body(width, slots, flat, count, step, finish, *refs):
    lefts, rights = refs[:count], refs[count : 2 * count]
    if finish == "norm":
        x_ref, gain_ref, hidden_ref, low_ref, out_ref, inv_ref = refs[2 * count : 2 * count + 6]
        rest = refs[2 * count + 6 :]
    else:
        more_ref, low_ref, out_ref = refs[2 * count : 2 * count + 3]
        rest = refs[2 * count + 3 :]
    me = lax.axis_index("wide")
    rows, cols = out_ref.shape
    hello(wide_peers(width, me))
    sums = Sums(width, me, out_ref, rest)
    dims = (((1,), (1 if flat else 0,)), ((), ()))

    def produce(k, first, some, put, adds=()):
        who = flip(me, k)
        start = ((who % slots) * (width // slots) + who // slots) * rows + first
        start = pl.multiple_of(start, rows // 2)

        def tile(n, carry):
            at = pl.ds(pl.multiple_of(n * step, step), step)
            total = None
            for left, right in zip(lefts, rights):
                other = right[at, :] if flat else right[:, at]
                term = lax.dot_general(
                    left[pl.ds(start, some), :], other, dims, preferred_element_type=jnp.float32
                )
                total = term if total is None else total + term
            for ref in adds:
                total = total + ref[:, at].astype(jnp.float32)
            put[:, at] = total.astype(put.dtype)
            return carry

        lax.fori_loop(0, cols // step, tile, 0)

    run_sums(width, sums, produce)
    if finish == "add":
        def close(n, carry):
            at = pl.ds(pl.multiple_of(n * 32, 32), 32)
            low_ref[at, :] = (out_ref[at, :] + more_ref[at, :]).astype(low_ref.dtype)
            return carry

        lax.fori_loop(0, rows // 32, close, 0)
    if finish != "norm":
        return
    few = 32

    def norm(n, carry):
        at = pl.ds(pl.multiple_of(n * few, few), few)
        value = out_ref[at, :]
        inverse = lax.rsqrt(jnp.sum(value * value, axis=-1, keepdims=True) * (1.0 / cols) + EPS)
        value = value * inverse
        out_ref[at, :] = value
        inv_ref[at, :] = inverse
        hidden = x_ref[at, :].astype(jnp.float32) + value * gain_ref[...]
        hidden_ref[at, :] = hidden
        low_ref[at, :] = hidden.astype(low_ref.dtype)
        return carry

    lax.fori_loop(0, rows // few, norm, 0)


def scatter(lefts, rights, width, slots, flat, ident, name, finish, more, step=1024):
    rows = lefts[0].shape[0] // width
    cols = rights[0].shape[0 if flat else 1]
    f32, vmem = jnp.float32, pl.BlockSpec(memory_space=pltpu.VMEM)
    whole, low = jax.ShapeDtypeStruct((rows, cols), f32), jax.ShapeDtypeStruct((rows, cols), lefts[0].dtype)
    shapes = [whole, low, whole, jax.ShapeDtypeStruct((rows, 1), f32)] if finish == "norm" else [low]
    scratch = sum_scratch(width, rows, cols)
    if finish == "add":
        scratch = [pltpu.VMEM((rows, cols), f32)] + scratch
    outs = pl.pallas_call(
        functools.partial(scatter_body, width, slots, flat, len(lefts), step, finish),
        out_shape=shapes,
        in_specs=[vmem] * (2 * len(lefts) + len(more)),
        out_specs=[vmem] * len(shapes),
        scratch_shapes=scratch,
        cost_estimate=busy(10),
        compiler_params=pltpu.CompilerParams(collective_id=ident, has_side_effects=True, vmem_limit_bytes=VMEM_LIMIT),
        name=name,
    )(*lefts, *rights, *more)
    return outs if finish == "norm" else outs[0]


def total_body(axis, width, x_ref, out_ref, slots, send, recv):
    me = lax.axis_index(axis)
    others = list(range(1, width))
    greet(axis, me, others)
    moves = []
    for k in others:
        copy = pltpu.make_async_remote_copy(
            src_ref=x_ref,
            dst_ref=slots.at[k - 1],
            send_sem=send.at[k - 1],
            recv_sem=recv.at[k - 1],
            device_id={axis: flip(me, k)},
            device_id_type=MESH,
        )
        copy.start()
        moves.append(copy)
    out_ref[...] = x_ref[...]
    for copy, k in zip(moves, others):
        copy.wait_recv()
        out_ref[...] = out_ref[...] + slots[k - 1]
    for copy in moves:
        copy.wait_send()


def total(x, axis, width, ident, name):
    return pl.pallas_call(
        functools.partial(total_body, axis, width),
        out_shape=jax.ShapeDtypeStruct(x.shape, x.dtype),
        in_specs=[pl.BlockSpec(memory_space=pltpu.VMEM)],
        out_specs=pl.BlockSpec(memory_space=pltpu.VMEM),
        scratch_shapes=[
            pltpu.VMEM((width - 1,) + x.shape, x.dtype),
            pltpu.SemaphoreType.DMA((width - 1,)),
            pltpu.SemaphoreType.DMA((width - 1,)),
        ],
        cost_estimate=busy(7),
        compiler_params=pltpu.CompilerParams(collective_id=ident, has_side_effects=True, vmem_limit_bytes=VMEM_LIMIT),
        name=name,
    )(x)


class Hops:
    def __init__(self, planes, slots, rows):
        self.planes, self.slots = planes, slots
        self.count = max(n for n in range(1, planes + 1) if planes % n == 0 and rows % (16 * n) == 0)
        self.per = planes // self.count
        self.piece = rows // self.count
        self.plane, self.place = lax.axis_index("blk"), lax.axis_index("wide")
        self.chip, self.slot = self.place // slots, self.place % slots
        self.active = self.chip // self.count == self.plane % self.per

    def peers(self):
        near = [{"wide": (self.chip + k) % self.planes * self.slots + self.slot} for k in range(1, self.planes)]
        return near + [{"blk": (self.plane + k) % self.planes} for k in range(1, self.planes)]

    def when(self, condition, action):
        if self.per == 1:
            action()
        else:
            pl.when(condition)(action)

    def split(self, condition, yes, no):
        if self.per == 1:
            yes()
        else:
            pl.when(condition)(yes)
            pl.when(jnp.logical_not(condition))(no)

    def cut(self, ref, index):
        return ref.at[pl.ds(pl.multiple_of(index * self.piece, self.piece), self.piece)]

    def remote(self, src, dst, send, recv, device):
        return pltpu.make_async_remote_copy(
            src_ref=src, dst_ref=dst, send_sem=send, recv_sem=recv, device_id=device, device_id_type=MESH
        )

    def spread(self, some, many, send, recv, across, start):
        if across:
            axis, here = "blk", self.plane
            targets = [
                ((self.plane // self.per + k) % self.count) for k in range(self.count)
            ]
            device = lambda piece: piece * self.per + self.chip // self.count
        else:
            axis, here = "wide", self.chip
            targets = [((self.chip + k) % self.count) for k in range(self.count)]
            device = lambda piece: (self.plane % self.per) * self.count + piece
        address = (lambda who: {"blk": who}) if across else (
            lambda who: {"wide": who * self.slots + self.slot}
        )
        for k, piece in enumerate(targets):
            who = device(piece)
            far = self.remote(
                self.cut(some, piece), self.cut(many, here), send.at[piece],
                recv.at[(here - who + self.planes) % self.planes], address(who),
            )
            own = pltpu.make_async_copy(self.cut(some, piece), self.cut(many, here), send.at[piece])
            if k:
                far.start() if start else far.wait_send()
            elif start:
                self.split(self.active, own.start, far.start)
            else:
                self.split(self.active, own.wait, far.wait_send)
        if not start:
            def receive():
                for k in range(1, self.planes):
                    block = self.cut(many, (here + k) % self.planes)
                    pltpu.make_async_copy(block, block, recv.at[k]).wait()

            self.when(self.active, receive)

    def join(self, many, some, send, recv, across, start, ready=None):
        if across:
            here = self.plane
            index = self.plane // self.per
            address = lambda who: {"blk": who}
        else:
            here = self.chip
            index = self.chip % self.count
            address = lambda who: {"wide": who * self.slots + self.slot}

        def give():
            for k in list(range(1, self.planes)) + [0]:
                who = (here + k) % self.planes
                if ready is not None:
                    ready(who)
                if k:
                    copy = self.remote(
                        self.cut(many, who), self.cut(some, index), send.at[k], recv.at[index], address(who)
                    )
                    copy.start() if start else copy.wait_send()
                else:
                    own = pltpu.make_async_copy(self.cut(many, here), self.cut(some, index), send.at[0])
                    own.start() if start else own.wait()

        self.when(self.active, give)
        if not start:
            for k in range(self.count):
                piece = (index + k) % self.count
                block = self.cut(some, piece)
                arrival = pltpu.make_async_copy(block, block, recv.at[piece])
                if k:
                    arrival.wait()
                elif self.per > 1:
                    pl.when(jnp.logical_not(self.active))(arrival.wait)

    def arrival(self, some, many, send, recv, across):
        here = self.plane if across else self.chip
        own_piece = self.plane // self.per if across else self.chip % self.count

        def ready(who):
            block = self.cut(many, who)

            @pl.when(who == here)
            def _():
                pltpu.make_async_copy(self.cut(some, own_piece), block, send.at[own_piece]).wait()

            @pl.when(who != here)
            def _():
                pltpu.make_async_copy(block, block, recv.at[(who - here + self.planes) % self.planes]).wait()

        return ready

    def sent(self, some, many, send, across):
        pieces = self.plane // self.per if across else self.chip
        for k in range(self.count):
            piece = (pieces + k) % self.count
            block = self.cut(some, piece)
            out = pltpu.make_async_copy(block, block, send.at[piece])
            if k:
                out.wait()
            elif self.per > 1:
                pl.when(jnp.logical_not(self.active))(out.wait)


def hello(peers):
    barrier = pltpu.get_barrier_semaphore()
    for peer in peers:
        pl.semaphore_signal(barrier, inc=1, device_id=peer, device_id_type=MESH)
    pl.semaphore_wait(barrier, len(peers))


def turn_in_body(planes, slots, x_ref, c_ref, near_x, near_c, out_ref, *sems):
    hops = Hops(planes, slots, x_ref.shape[0])
    hello(hops.peers())
    hops.spread(x_ref, near_x, sems[0], sems[1], False, True)
    ready = hops.arrival(x_ref, near_x, sems[0], sems[1], False)
    hops.join(near_x, out_ref, sems[2], sems[3], True, True, ready)
    hops.sent(x_ref, near_x, sems[0], False)
    hops.spread(c_ref, near_c, sems[4], sems[5], False, True)
    hops.spread(c_ref, near_c, sems[4], sems[5], False, False)
    hops.join(near_x, out_ref, sems[2], sems[3], True, False)


def turn_out_body(planes, slots, x_ref, far_c, v_ref, far_x, out_c, out_ref, v_out, *sems):
    hops = Hops(planes, slots, x_ref.shape[0])
    hello(hops.peers())
    parts, send, recv = sems[6:]
    moves = []
    for k in range(1, planes):
        copy = hops.remote(
            v_ref, parts.at[planes - k - 1], send.at[k - 1], recv.at[planes - k - 1],
            {"blk": (hops.plane + k) % planes},
        )
        copy.start()
        moves.append(copy)
    hops.spread(x_ref, far_x, sems[0], sems[1], True, True)
    hops.join(far_c, out_c, sems[2], sems[3], False, True)
    ready = hops.arrival(x_ref, far_x, sems[0], sems[1], True)
    hops.join(far_x, out_ref, sems[4], sems[5], False, True, ready)
    hops.sent(x_ref, far_x, sems[0], True)
    amount = v_ref[...]
    for k in range(1, planes):
        block = parts.at[k - 1]
        pltpu.make_async_copy(block, block, recv.at[k - 1]).wait()
        amount = amount + parts[k - 1]
    v_out[...] = amount
    for copy in moves:
        copy.wait_send()
    hops.join(far_c, out_c, sems[2], sems[3], False, False)
    hops.join(far_x, out_ref, sems[4], sems[5], False, False)


def many_rows(planes, rows):
    count = max(n for n in range(1, planes + 1) if planes % n == 0 and rows % (16 * n) == 0)
    return planes * (rows // count)


def turn(body, inputs, outputs, planes, slots, ident, name, extra=None):
    rows, cols = inputs[0].shape
    low = inputs[0].dtype
    dma = pltpu.SemaphoreType.DMA
    shape = lambda many: jax.ShapeDtypeStruct((many_rows(planes, rows) if many else rows, cols), low)
    anywhere, vmem = pl.BlockSpec(memory_space=pl.ANY), pl.BlockSpec(memory_space=pltpu.VMEM)
    more = [] if extra is None else [extra]
    scratch = [dma((planes,))] * 6
    for value in more:
        scratch += [pltpu.VMEM((planes - 1,) + value.shape, value.dtype), dma((planes - 1,)), dma((planes - 1,))]
    return pl.pallas_call(
        functools.partial(body, planes, slots),
        out_shape=[shape(many) for many in outputs] + [jax.ShapeDtypeStruct(v.shape, v.dtype) for v in more],
        in_specs=[anywhere] * len(inputs) + [vmem] * len(more),
        out_specs=[anywhere] * len(outputs) + [vmem] * len(more),
        scratch_shapes=scratch,
        cost_estimate=busy(10),
        compiler_params=pltpu.CompilerParams(collective_id=ident, has_side_effects=True, vmem_limit_bytes=VMEM_LIMIT),
        name=name,
    )(*inputs, *more)


def mask_scores(scores, first, begin, size):
    span = scores.shape[0]
    index = lax.broadcasted_iota(jnp.int32, scores.shape, 0)
    query = lax.broadcasted_iota(jnp.int32, scores.shape, 1) + first
    return jnp.where((index <= query) & (index >= begin), scores, NEG_FILL)


def nt(left, right):
    return lax.dot_general(left, right, (((1,), (1,)), ((), ())), preferred_element_type=jnp.float32)


def nn(left, right):
    return jnp.dot(left, right, preferred_element_type=jnp.float32)


def piece_map(span, size):
    planes = span // size
    count = max(n for n in range(1, planes + 1) if planes % n == 0 and size % (16 * n) == 0)
    per, piece = planes // count, size // count
    pairs = []
    for t in range(count):
        for high in range(per):
            for low in range(count):
                natural = ((t * per + high) * count + low) * piece
                pairs.append((natural, ((high * count + low) * count + t) * piece))
    return pairs, piece


def attend_body(size, q_ref, k_ref, v_ref, inv_ref, gain_ref, cos_ref, sin_ref, begin_ref,
                qo_ref, ko_ref, vo_ref, mix_ref, log_ref):
    low = jnp.bfloat16
    span = q_ref.shape[0]

    def prepare(ref, col):
        value = ref[...] * inv_ref[:, col : col + 1] * gain_ref[col : col + 1, :]
        return (value * cos_ref[...] + pltpu.roll(value, HD // 2, 1) * sin_ref[...]).astype(low)

    pairs, piece = piece_map(span, size)

    def arrange(ref, value):
        for natural, block in pairs:
            ref[natural : natural + piece, :] = value[block : block + piece, :]

    arrange(qo_ref, prepare(q_ref, 0))
    arrange(ko_ref, prepare(k_ref, 1))
    arrange(vo_ref, v_ref[...].astype(low))
    flipped = vo_ref[...].astype(jnp.float32).T.astype(low)
    for i in range(span // size):
        last = (i + 1) * size
        cols = slice(i * size, last)
        scores = nt(ko_ref[:last, :], qo_ref[cols, :])
        scores = mask_scores(scores, i * size, begin_ref[:, cols], size)
        top = jnp.max(scores, axis=0, keepdims=True)
        raw = jnp.exp2((scores - top) * FOLD)
        weight = jnp.sum(raw, axis=0, keepdims=True)
        mixed = nn(flipped[:, :last], raw.astype(low)) * (1.0 / weight)
        mixed = mixed.T.astype(low)
        for natural, block in pairs:
            if i * size <= natural < last:
                at = natural - i * size
                mix_ref[block : block + piece, :] = mixed[at : at + piece, :]
        log_ref[:, cols] = top * FOLD + jnp.log2(weight)


def attend(pre, rows, inverse, gains, cosine, sine, begin, heads, size):
    slots, span, _ = pre.shape
    low, f32 = jnp.bfloat16, jnp.float32
    head = lambda offset: pl.BlockSpec((None, span, HD), lambda g, h: (g, 0, offset + h))
    every = lambda cols: pl.BlockSpec((None, span, cols), lambda g, h: (g, 0, 0))
    line = pl.BlockSpec((None, 1, span), lambda g, h: (g, 0, 0))
    out = jax.ShapeDtypeStruct((slots, span, heads * HD), low)
    return pl.pallas_call(
        functools.partial(attend_body, size),
        grid=(slots, heads),
        out_shape=[out, out, out, out, jax.ShapeDtypeStruct((slots, heads, 1, span), f32)],
        in_specs=[
            head(0), head(heads), head(0), every(2),
            pl.BlockSpec((2, HD), lambda g, h: (0, h)), every(HD), every(HD), line,
        ],
        out_specs=[head(0)] * 4 + [pl.BlockSpec((None, None, 1, span), lambda g, h: (g, h, 0, 0))],
        compiler_params=pltpu.CompilerParams(vmem_limit_bytes=VMEM_LIMIT),
        cost_estimate=busy(5),
        name="attend",
    )(pre, pre, rows, inverse, gains, cosine, sine, begin)


def attend_back_body(size, q_ref, k_ref, v_ref, g_ref, log_ref, qp_ref, kp_ref, inv_ref, gain_ref,
                     cos_ref, sin_ref, begin_ref, sq_ref, sk_ref, gv_ref, sums_ref, part_ref,
                     keys_sum, values_sum, queries_sum, held, g_held):
    low = jnp.bfloat16
    span = q_ref.shape[0]
    pairs, piece = piece_map(span, size)
    for natural, block in pairs:
        g_held[natural : natural + piece, :] = g_ref[block : block + piece, :]
    flipped = k_ref[...].astype(jnp.float32).T.astype(low)
    keys_sum[...] = jnp.zeros_like(keys_sum)
    values_sum[...] = jnp.zeros_like(values_sum)
    for i in range(span // size):
        last = (i + 1) * size
        cols = slice(i * size, last)
        scores = nt(k_ref[:last, :], q_ref[cols, :])
        scores = mask_scores(scores, i * size, begin_ref[:, cols], size)
        probs = jnp.exp2(scores * FOLD - log_ref[:, cols])
        grad_probs = nt(v_ref[:last, :], g_held[cols, :])
        delta = jnp.sum(probs * grad_probs, axis=0, keepdims=True)
        grad_scores = (probs * (grad_probs - delta)).astype(low)
        values_sum[:last, :] += nn(probs.astype(low), g_held[cols, :])
        keys_sum[:last, :] += nn(grad_scores, q_ref[cols, :])
        queries_sum[cols, :] = nn(flipped[:, :last], grad_scores).T

    def finish(total_ref, pre_ref, out_ref, col):
        for natural, block in pairs:
            held[block : block + piece, :] = total_ref[natural : natural + piece, :]
        grad = held[...] * SCALE
        back = grad * cos_ref[...] - pltpu.roll(grad, HD // 2, 1) * sin_ref[...]
        normed = pre_ref[...] * inv_ref[:, col : col + 1]
        part_ref[col : col + 1, :] = jnp.sum(back * normed, axis=0, keepdims=True)
        scaled = back * gain_ref[col : col + 1, :]
        out_ref[...] = scaled
        sums_ref[:, col : col + 1] = jnp.sum(scaled * normed, axis=1, keepdims=True)

    finish(queries_sum, qp_ref, sq_ref, 0)
    finish(keys_sum, kp_ref, sk_ref, 1)
    for natural, block in pairs:
        gv_ref[block : block + piece, :] = values_sum[natural : natural + piece, :].astype(low)


def attend_back(queries, keys, values, grads, logs, pre, inverse, gains, cosine, sine, begin, heads, size):
    slots, span, _ = pre.shape
    low, f32 = jnp.bfloat16, jnp.float32
    head = lambda offset: pl.BlockSpec((None, span, HD), lambda g, h: (g, 0, offset + h))
    every = lambda cols: pl.BlockSpec((None, span, cols), lambda g, h: (g, 0, 0))
    line = pl.BlockSpec((None, 1, span), lambda g, h: (g, 0, 0))
    wide = jax.ShapeDtypeStruct((slots, span, heads * HD), f32)
    return pl.pallas_call(
        functools.partial(attend_back_body, size),
        grid=(slots, heads),
        out_shape=[
            wide, wide, jax.ShapeDtypeStruct((slots, span, heads * HD), low),
            jax.ShapeDtypeStruct((heads, slots, span, 2), f32),
            jax.ShapeDtypeStruct((slots, 2, heads * HD), f32),
        ],
        in_specs=[
            head(0), head(0), head(0), head(0),
            pl.BlockSpec((None, None, 1, span), lambda g, h: (g, h, 0, 0)),
            head(0), head(heads), every(2),
            pl.BlockSpec((2, HD), lambda g, h: (0, h)), every(HD), every(HD), line,
        ],
        out_specs=[
            head(0), head(0), head(0),
            pl.BlockSpec((None, None, span, 2), lambda g, h: (h, g, 0, 0)),
            pl.BlockSpec((None, 2, HD), lambda g, h: (g, 0, h)),
        ],
        scratch_shapes=[pltpu.VMEM((span, HD), f32)] * 4 + [pltpu.VMEM((span, HD), low)],
        compiler_params=pltpu.CompilerParams(vmem_limit_bytes=VMEM_LIMIT),
        cost_estimate=busy(5),
        name="attend_back",
    )(queries, keys, values, grads, logs, pre, pre, inverse, gains, cosine, sine, begin)


def row_sums(value):
    return jnp.sum(value.reshape(-1, 8, value.shape[-1]), axis=0)


def feed_body(width, slots, step, h_ref, c_ref, wg_hbm, wu_hbm, wd_hbm, hidden_ref, gain_ref, block_ref,
              first_ref, second_ref, gain_out, all_ref, act_ref, one_ref, two_ref, c_out, buf, wg, wu, wd, stage, out_ref,
              c_held, here, load, send, recv, side_send, side_recv, store, keep, *sum_refs):
    me = lax.axis_index("wide")
    planes = width // slots
    rows, cols = h_ref.shape
    hidden = wg.shape[1]
    half = rows // 2
    low = jnp.bfloat16
    loads = local_copies([(wg_hbm, wg), (wu_hbm, wu), (wd_hbm, wd)], load)
    mine = pltpu.make_async_copy(h_ref, buf.at[me], here)
    mine.start()
    for copy in loads:
        copy.start()
    hops = Hops(planes, slots, rows)
    hello(wide_peers(width, me) + [{"blk": (hops.plane + k) % planes} for k in range(1, planes)])
    flow = Flow(me, h_ref, lambda who, part: buf.at[who, pl.ds(part * half, half)], half, send, recv)
    sums = Sums(width, me, out_ref, sum_refs)
    outs = (act_ref, one_ref, two_ref)
    pending = [[], []]
    turn_count = [0]
    kept = []

    def where(k):
        who = flip(me, k)
        return pl.multiple_of(((who % slots) * planes + who // slots) * rows, rows)

    def keep_block(k):
        copy = pltpu.make_async_copy(buf.at[flip(me, k)], all_ref.at[pl.ds(where(k), rows)], keep.at[k])
        copy.start()
        kept.append(copy)

    def work(k, part, put, adds=()):
        first, count = (0, rows) if part is None else (part * half, half)
        slot = turn_count[0] % 2
        turn_count[0] += 1
        for copy in pending[slot]:
            copy.wait()
        block = buf.at[flip(me, k), pl.ds(first, count)]
        act, one, two = (stage.at[slot, i, pl.ds(0, count)] for i in range(3))

        def inner(n, carry):
            at = pl.ds(pl.multiple_of(n * step, step), step)
            gate = jnp.dot(block[...], wg[:, at], preferred_element_type=jnp.float32)
            upward = jnp.dot(block[...], wu[:, at], preferred_element_type=jnp.float32)
            sigmoid = jax.nn.sigmoid(gate)
            silu = gate * sigmoid
            act[:, at] = (silu * upward).astype(low)
            one[:, at] = silu.astype(low)
            two[:, at] = (upward * (sigmoid + silu * (1.0 - sigmoid))).astype(low)
            return carry

        lax.fori_loop(0, hidden // step, inner, 0)
        target = pl.ds(pl.multiple_of(where(k) + first, half), count)
        pending[slot] = []
        for i, ref in enumerate(outs):
            copy = pltpu.make_async_copy(stage.at[slot, i, pl.ds(0, count)], ref.at[target], store.at[slot, i])
            copy.start()
            pending[slot].append(copy)
        broad = 2 * step

        def outer(n, carry):
            at = pl.ds(pl.multiple_of(n * broad, broad), broad)
            total = jnp.dot(act[...], wd[:, at], preferred_element_type=jnp.float32)
            for ref in adds:
                total = total + ref[:, at].astype(jnp.float32)
            put[:, at] = total.astype(put.dtype)
            return carry

        lax.fori_loop(0, cols // broad, outer, 0)

    def odd_work(k, part):
        if part is None:
            work(k + 1, None, sums.odd.at[k // 2])
            sums.give(k)
        else:
            work(k + 1, part, sums.odd.at[k // 2, sums.rows(part)])
            sums.twin(k, part).start()

    def even_work(k, part):
        i = k // 2
        if part is None:
            sums.got(k)
            work(k, None, sums.even.at[i - 1], (sums.from_twin.at[i],))
        else:
            sums.twin(k, part).wait_recv()
            at = sums.rows(part)
            work(k, part, sums.even.at[i - 1, at], (sums.from_twin.at[i, at],))

    if width == 8:
        flow.go(None, 2, 2, 0)
        flow.go(None, 4, 4, 1)
        flow.go(None, 1, 1, 0)
        flow.go(None, 1, 1, 1)
        hops.join(c_ref, c_out, side_send, side_recv, True, True)
        mine.wait()
        for copy in loads:
            copy.wait()
        work(0, None, out_ref)
        keep_block(0)
        flow.arrived(1, 0)
        flow.arrived(1, 1)
        keep_block(1)
        odd_work(0, None)
        flow.arrived(2, 0)
        flow.go(2, 4, 6, 0)
        flow.arrived(4, 1)
        flow.go(4, 2, 6, 1)
        flow.go(2, 1, 3, 0)
        flow.go(4, 1, 5, 1)
        flow.go(None, 2, 2, 1)
        flow.go(None, 4, 4, 0)
        flow.arrived(3, 0)
        odd_work(2, 0)
        flow.arrived(5, 1)
        odd_work(4, 1)
        even_work(2, 0)
        even_work(4, 1)
        for part in (0, 1):
            flow.arrived(6, part)
            flow.go(6, 1, 7, part)
        for part in (0, 1):
            flow.arrived(7, part)
        keep_block(6)
        keep_block(7)
        odd_work(6, None)
        even_work(6, None)
        sums.relay(0).start()
        sums.relay(1).start()
        flow.arrived(2, 1)
        flow.go(2, 1, 3, 1)
        flow.arrived(4, 0)
        flow.go(4, 1, 5, 0)
        sums.far(2, 0).start()
        sums.far(4, 1).start()
        flow.arrived(3, 1)
        odd_work(2, 1)
        flow.arrived(5, 0)
        odd_work(4, 0)
        for k in (2, 3, 4, 5):
            keep_block(k)
        even_work(2, 1)
        sums.pass_on(2, 1)
        even_work(4, 0)
        sums.pass_on(4, 0)
    else:
        hops.join(c_ref, c_out, side_send, side_recv, True, True)
        for k in range(2, width, 2):
            flow.go(None, k, k, 0)
            flow.go(None, k, k, 1)
        flow.go(None, 1, 1, 0)
        flow.go(None, 1, 1, 1)
        mine.wait()
        for copy in loads:
            copy.wait()
        work(0, None, out_ref)
        keep_block(0)
        flow.arrived(1, 0)
        flow.arrived(1, 1)
        keep_block(1)
        odd_work(0, None)
        for k in range(2, width, 2):
            for part in (0, 1):
                flow.arrived(k, part)
                flow.go(k, 1, k + 1, part)
            for part in (0, 1):
                flow.arrived(k + 1, part)
            keep_block(k)
            keep_block(k + 1)
            odd_work(k, None)
            even_work(k, None)
            sums.far(k, 0).start()
            sums.far(k, 1).start()
    sums.got(0)
    out_ref[...] = out_ref[...] + sums.from_twin[0].astype(jnp.float32)
    sums.finish()
    flow.finish()
    hops.join(c_ref, c_out, side_send, side_recv, True, False)
    held = pltpu.make_async_copy(c_out, c_held, here)
    held.start()
    held.wait()
    gain_out[...] = jnp.zeros_like(gain_out)
    few = 32
    own = cols // planes
    half_own = own // 2

    def norm(n, carry):
        at = pl.ds(pl.multiple_of(n * few, few), few)
        value = out_ref[at, :]
        inverse = lax.rsqrt(jnp.sum(value * value, axis=-1, keepdims=True) * (1.0 / cols) + EPS)
        normed = value * inverse
        block_ref[at, :] = (hidden_ref[at, :] + normed * gain_ref[...]).astype(low)
        grad = c_held[at, :].astype(jnp.float32)
        gain_out[...] = gain_out[...] + row_sums(grad * normed)
        grad = grad * gain_ref[...]
        mean = jnp.sum(grad * normed, axis=-1, keepdims=True) * (1.0 / cols)
        grad = (inverse * (grad - normed * mean)).astype(low)
        for b in range(planes):
            for side in (0, 1):
                first = b * own + side * half_own
                (first_ref, second_ref)[side][at, b * half_own : (b + 1) * half_own] = grad[:, first : first + half_own]
        return carry

    lax.fori_loop(0, rows // few, norm, 0)
    for copy in kept + pending[0] + pending[1]:
        copy.wait()


def feed(h, side_x, gate_weight, up_weight, down_weight, hidden, gain, width, slots, ident, name):
    rows, cols = h.shape
    inner = gate_weight.shape[1]
    low, f32, dma = h.dtype, jnp.float32, pltpu.SemaphoreType.DMA
    step = min(512, inner)
    anywhere, vmem = pl.BlockSpec(memory_space=pl.ANY), pl.BlockSpec(memory_space=pltpu.VMEM)
    saved = jax.ShapeDtypeStruct((rows * width, inner), low)
    return pl.pallas_call(
        functools.partial(feed_body, width, slots, step),
        out_shape=[
            jax.ShapeDtypeStruct((rows, cols), low), jax.ShapeDtypeStruct((rows, cols // 2), low),
            jax.ShapeDtypeStruct((rows, cols // 2), low),
            jax.ShapeDtypeStruct((8, cols), f32), jax.ShapeDtypeStruct((rows * width, cols), low),
            saved, saved, saved, jax.ShapeDtypeStruct((rows, cols), low),
        ],
        in_specs=[anywhere] * 5 + [vmem] * 2,
        out_specs=[vmem] * 4 + [anywhere] * 5,
        scratch_shapes=[
            pltpu.VMEM((width, rows, cols), low), pltpu.VMEM((cols, inner), low), pltpu.VMEM((cols, inner), low),
            pltpu.VMEM((inner, cols), low), pltpu.VMEM((2, 3, rows, inner), low),
            pltpu.VMEM((rows, cols), f32), pltpu.VMEM((rows, cols), low),
            dma, dma((3,)), dma((width, 2)), dma((width, 2)), dma((width // slots,)), dma((width // slots,)),
            dma((2, 3)), dma((width,)),
        ] + sum_scratch(width, rows, cols),
        cost_estimate=busy(90),
        compiler_params=pltpu.CompilerParams(collective_id=ident, has_side_effects=True, vmem_limit_bytes=VMEM_LIMIT),
        name=name,
    )(h, side_x, gate_weight, up_weight, down_weight, hidden, gain)


def push_body(second, width, slots, *refs):
    if second:
        (g_ref, act_hbm, wd_hbm, one_hbm, two_hbm, first_hbm, down_ref, gg_ref, gu_ref,
         buf, held, acts, here, send, recv, fetch, wd, before, ins, outs, load, take, store) = refs
    else:
        (g_ref, act_hbm, c_ref, down_ref, all_ref, c_out,
         buf, held, acts, here, send, recv, fetch, keep, side_send, side_recv) = refs
    me = lax.axis_index("wide")
    planes = width // slots
    pairs = width // 2
    rows, cols = g_ref.shape
    inner = down_ref.shape[0]
    half = rows // 2
    low = jnp.bfloat16
    mine = pltpu.make_async_copy(g_ref, buf.at[me // 2, me % 2], here)
    mine.start()

    def where(pair, side):
        who = flip(me // 2, pair) * 2 + side
        return pl.ds(pl.multiple_of(((who % slots) * planes + who // slots) * rows, rows), rows)

    def fetches(pair):
        copies = [
            pltpu.make_async_copy(act_hbm.at[where(pair, side)], acts.at[pair % 2, side], fetch.at[pair % 2, side])
            for side in (0, 1)
        ]
        if second:
            copies += [
                pltpu.make_async_copy(ref.at[where(pair, side)], ins.at[pair % 2, i, side], take.at[pair % 2, i, side])
                for i, ref in enumerate((one_hbm, two_hbm))
                for side in (0, 1)
            ]
        return copies

    def stores(pair):
        return [
            pltpu.make_async_copy(outs.at[pair % 2, i, side], ref.at[where(pair, side)], store.at[pair % 2, i, side])
            for i, ref in enumerate((gg_ref, gu_ref))
            for side in (0, 1)
        ]

    def keeps(pair):
        chip = flip(me // 2, pair)
        return pltpu.make_async_copy(buf.at[chip], all_ref.at[chip], keep.at[pair])

    for copy in fetches(0):
        copy.start()
    peers = wide_peers(width, me)
    if second:
        own = cols // planes
        loads = [
            pltpu.make_async_copy(
                wd_hbm.at[:, pl.ds((2 * b + side) * own, own)], wd.at[:, pl.ds(side * cols + b * own, own)],
                load.at[b, side],
            )
            for b in range(planes)
            for side in (0, 1)
        ]
        loads.append(pltpu.make_async_copy(first_hbm, before, load.at[planes, 0]))
        for copy in loads:
            copy.start()
    else:
        hops = Hops(planes, slots, rows)
        peers = peers + [{"blk": (hops.plane + k) % planes} for k in range(1, planes)]
    hello(peers)
    flow = Flow(me, g_ref, lambda who, part: buf.at[who // 2, who % 2, pl.ds(part * half, half)], half, send, recv)

    def work(pair):
        for copy in fetches(pair):
            copy.wait()
        if pair + 1 < pairs:
            for copy in fetches(pair + 1):
                copy.start()
        chip = flip(me // 2, pair)
        slot = pair % 2
        grads = buf[chip].reshape(2 * rows, cols)
        if second:
            if pair >= 2:
                for copy in stores(pair - 2):
                    copy.wait()
            old = before[chip].reshape(2 * rows, cols)
            step = min(512, inner)

            def units(n, carry):
                at = pl.ds(pl.multiple_of(n * step, step), step)
                grad = (nt(old, wd[at, :cols]) + nt(grads, wd[at, cols:])).reshape(2, rows, step)
                outs[slot, 0, :, :, at] = (grad * ins[slot, 1, :, :, at].astype(jnp.float32)).astype(low)
                outs[slot, 1, :, :, at] = (grad * ins[slot, 0, :, :, at].astype(jnp.float32)).astype(low)
                return carry

            lax.fori_loop(0, inner // step, units, 0)
            for copy in stores(pair):
                copy.start()
        else:
            keeps(pair).start()
        tall = min(512, inner)

        def outer(n, carry):
            at = pl.ds(pl.multiple_of(n * tall, tall), tall)
            act = acts[slot, :, :, at].reshape(2 * rows, tall)
            term = lax.dot_general(act, grads, (((0,), (0,)), ((), ())), preferred_element_type=jnp.float32)
            if pair:
                term = term + held[at, :]
            if pair + 1 < pairs:
                held[at, :] = term
            else:
                down_ref[at, :] = term.astype(low)
            return carry

        lax.fori_loop(0, inner // tall, outer, 0)

    def pair_ready(k):
        for part in (0, 1):
            flow.arrived(k + 1, part)

    if width == 8:
        flow.go(None, 2, 2, 0)
        flow.go(None, 4, 4, 1)
        flow.go(None, 2, 2, 1)
        flow.go(None, 4, 4, 0)
    else:
        for k in range(2, width, 2):
            flow.go(None, k, k, 0)
            flow.go(None, k, k, 1)
    flow.go(None, 1, 1, 0)
    flow.go(None, 1, 1, 1)
    if second:
        for copy in loads:
            copy.wait()
    else:
        hops.spread(c_ref, c_out, side_send, side_recv, True, True)
    mine.wait()
    pair_ready(0)
    work(0)
    if width == 8:
        flow.arrived(2, 0)
        flow.go(2, 4, 6, 0)
        flow.go(2, 1, 3, 0)
        flow.arrived(4, 1)
        flow.go(4, 2, 6, 1)
        flow.go(4, 1, 5, 1)
        flow.arrived(2, 1)
        flow.go(2, 1, 3, 1)
        flow.arrived(4, 0)
        flow.go(4, 1, 5, 0)
        pair_ready(2)
        work(1)
        pair_ready(4)
        work(2)
        for part in (0, 1):
            flow.arrived(6, part)
            flow.go(6, 1, 7, part)
        pair_ready(6)
        work(3)
    else:
        for k in range(2, width, 2):
            for part in (0, 1):
                flow.arrived(k, part)
                flow.go(k, 1, k + 1, part)
            pair_ready(k)
            work(k // 2)
    flow.finish()
    if second:
        for pair in (pairs - 2, pairs - 1):
            for copy in stores(pair):
                copy.wait()
    else:
        for pair in range(pairs):
            keeps(pair).wait()
        hops.spread(c_ref, c_out, side_send, side_recv, True, False)


def push(second, g, act, width, slots, ident, name, others):
    rows, cols = g.shape
    inner = act.shape[1]
    low, dma = g.dtype, pltpu.SemaphoreType.DMA
    planes, pairs = width // slots, width // 2
    anywhere, vmem = pl.BlockSpec(memory_space=pl.ANY), pl.BlockSpec(memory_space=pltpu.VMEM)
    blocks = (pairs, 2, rows, cols)
    scratch = [
        pltpu.VMEM(blocks, low), pltpu.VMEM((inner, cols), jnp.float32), pltpu.VMEM((2, 2, rows, inner), low),
        dma, dma((width, 2)), dma((width, 2)), dma((2, 2)),
    ]
    shapes = [jax.ShapeDtypeStruct((inner, cols), low)]
    if second:
        saved = jax.ShapeDtypeStruct((rows * width, inner), low)
        shapes += [saved, saved]
        scratch += [
            pltpu.VMEM((inner, 2 * cols), low), pltpu.VMEM(blocks, low), pltpu.VMEM((2, 2, 2, rows, inner), low),
            pltpu.VMEM((2, 2, 2, rows, inner), low), dma((planes + 1, 2)), dma((2, 2, 2)), dma((2, 2, 2)),
        ]
    else:
        shapes += [
            jax.ShapeDtypeStruct(blocks, low),
            jax.ShapeDtypeStruct((many_rows(planes, rows), others[0].shape[1]), low),
        ]
        scratch += [dma((pairs,)), dma((planes,)), dma((planes,))]
    inputs = [g, act] + others
    return pl.pallas_call(
        functools.partial(push_body, second, width, slots),
        out_shape=shapes,
        in_specs=[anywhere] * len(inputs),
        out_specs=[vmem] + [anywhere] * (len(shapes) - 1),
        scratch_shapes=scratch,
        cost_estimate=busy(10),
        compiler_params=pltpu.CompilerParams(collective_id=ident, has_side_effects=True, vmem_limit_bytes=VMEM_LIMIT),
        name=name,
    )(*inputs)


def pull_body(width, slots, step, chunk, gg_hbm, gu_hbm, wg_hbm, wu_hbm, h_hbm, c_ref, normed_ref, inv_ref, gain_ref,
              out_ref, proj_ref, gain_out, du_hbm, gg, gu, wg, wu, columns, tiles, load, take, fetch, store, *sum_refs):
    me = lax.axis_index("wide")
    planes = width // slots
    rows, cols = out_ref.shape
    half = rows // 2
    chunks = cols // chunk
    loads = local_copies([(wg_hbm, wg), (wu_hbm, wu)], load)
    for copy in loads:
        copy.start()

    def where(k, first, count):
        who = flip(me, k)
        start = ((who % slots) * planes + who // slots) * rows + first
        return pl.ds(pl.multiple_of(start, half), count)

    def takes(k):
        at = where(k, 0, rows)
        return [
            pltpu.make_async_copy(src.at[at], dst.at[at], take.at[k, i])
            for i, (src, dst) in enumerate(((gg_hbm, gg), (gu_hbm, gu)))
        ]

    order = [7, 6, 3, 5, 2, 4, 1, 0] if width == 8 else [k ^ 1 for k in range(width)]
    for k in order:
        for copy in takes(k):
            copy.start()
    taken = []

    def need(k):
        if k not in taken:
            taken.append(k)
            for copy in takes(k):
                copy.wait()

    def fetched(n):
        at = pl.ds(pl.multiple_of(n * chunk, chunk), chunk)
        return pltpu.make_async_copy(h_hbm.at[:, at], columns.at[n % 2], fetch.at[n % 2])

    def stored(n):
        at = pl.ds(pl.multiple_of(n * chunk, chunk), chunk)
        return [
            pltpu.make_async_copy(tiles.at[n % 2, i], ref.at[at], store.at[n % 2, i])
            for i, ref in enumerate((du_hbm,))
        ]

    fetched(0).start()
    hello(wide_peers(width, me))
    sums = Sums(width, me, out_ref, sum_refs)

    def produce(k, first, count, put, adds=()):
        need(k)
        at_rows = where(k, first, count)

        def tile(n, carry):
            at = pl.ds(pl.multiple_of(n * step, step), step)
            total = nt(gg[at_rows, :], wg[at, :]) + nt(gu[at_rows, :], wu[at, :])
            for ref in adds:
                total = total + ref[:, at].astype(jnp.float32)
            put[:, at] = total.astype(put.dtype)
            return carry

        lax.fori_loop(0, cols // step, tile, 0)

    def grads(first, last):
        for k in order:
            need(k)

        def one_chunk(n, carry):
            fetched(n).wait()

            @pl.when(n + 1 < chunks)
            def _():
                fetched(n + 1).start()

            @pl.when(n >= 2)
            def _():
                for copy in stored(n - 2):
                    copy.wait()

            for i, ref in enumerate((gu,)):
                tiles[n % 2, i] = lax.dot_general(
                    columns[n % 2], ref[...], (((0,), (0,)), ((), ())), preferred_element_type=jnp.float32
                ).astype(jnp.bfloat16)
            for copy in stored(n):
                copy.start()
            return carry

        lax.fori_loop(first, last, one_chunk, 0)

    for copy in loads:
        copy.wait()
    run_sums(width, sums, produce, grads, chunks)
    gain_out[...] = jnp.zeros_like(gain_out)
    few = 32

    def norm(n, carry):
        at = pl.ds(pl.multiple_of(n * few, few), few)
        grad = out_ref[at, :] + c_ref[at, :].astype(jnp.float32)
        out_ref[at, :] = grad
        normed = normed_ref[at, :]
        gain_out[...] = gain_out[...] + row_sums(grad * normed)
        grad = grad * gain_ref[...]
        mean = jnp.sum(grad * normed, axis=-1, keepdims=True) * (1.0 / cols)
        proj_ref[at, :] = (inv_ref[at, :] * (grad - normed * mean)).astype(jnp.bfloat16)
        return carry

    lax.fori_loop(0, rows // few, norm, 0)
    for copy in stored(chunks - 2) + stored(chunks - 1):
        copy.wait()


def pull(grad_gate, grad_up, gate_weight, up_weight, gathered, grad_out, normed, inverse, gain, width, slots, ident, name):
    count, cols = gathered.shape
    inner = gate_weight.shape[1]
    rows = count // width
    low, f32, dma = gathered.dtype, jnp.float32, pltpu.SemaphoreType.DMA
    chunk = 256
    anywhere, vmem = pl.BlockSpec(memory_space=pl.ANY), pl.BlockSpec(memory_space=pltpu.VMEM)
    return pl.pallas_call(
        functools.partial(pull_body, width, slots, 1024, chunk),
        out_shape=[
            jax.ShapeDtypeStruct((rows, cols), f32), jax.ShapeDtypeStruct((rows, cols), low),
            jax.ShapeDtypeStruct((8, cols), f32), jax.ShapeDtypeStruct((cols, inner), low),
        ],
        in_specs=[anywhere] * 5 + [vmem] * 4,
        out_specs=[vmem] * 3 + [anywhere],
        scratch_shapes=[
            pltpu.VMEM((count, inner), low), pltpu.VMEM((count, inner), low),
            pltpu.VMEM((cols, inner), low), pltpu.VMEM((cols, inner), low),
            pltpu.VMEM((2, count, chunk), low), pltpu.VMEM((2, 1, chunk, inner), low),
            dma((2,)), dma((width, 2)), dma((2,)), dma((2, 1)),
        ] + sum_scratch(width, rows, cols),
        cost_estimate=busy(10),
        compiler_params=pltpu.CompilerParams(collective_id=ident, has_side_effects=True, vmem_limit_bytes=VMEM_LIMIT),
        name=name,
    )(grad_gate, grad_up, gate_weight, up_weight, gathered, grad_out, normed, inverse, gain)


def close_body(t_ref, s_ref, b_ref, tokens_ref, q_ref, k_ref, v_ref, o_ref, block_ref):
    share = q_ref.shape[1]
    tokens_ref[...] = t_ref[...].astype(jnp.float32)
    block_ref[...] = b_ref[...]
    for i, ref in enumerate((q_ref, k_ref, v_ref)):
        ref[...] = s_ref[:, i * share : (i + 1) * share].astype(jnp.float32)
    o_ref[...] = s_ref[:, 3 * share :].astype(jnp.float32).T


def closing(tokens_low, side_grad, block_output):
    rows, cols = tokens_low.shape
    depth, extent = side_grad.shape
    share, f32, steps = extent // 4, jnp.float32, 2
    down = lambda a, b: pl.BlockSpec((a // steps, b), lambda n: (n, 0))
    weight = jax.ShapeDtypeStruct((depth, share), f32)
    return pl.pallas_call(
        close_body,
        grid=(steps,),
        out_shape=[
            jax.ShapeDtypeStruct((rows, cols), f32), weight, weight, weight,
            jax.ShapeDtypeStruct((share, depth), f32), jax.ShapeDtypeStruct((rows, cols), block_output.dtype),
        ],
        in_specs=[down(rows, cols), down(depth, extent), down(rows, cols)],
        out_specs=[down(rows, cols)] + [down(depth, share)] * 3
        + [pl.BlockSpec((share, depth // steps), lambda n: (0, n)), down(rows, cols)],
        compiler_params=pltpu.CompilerParams(vmem_limit_bytes=VMEM_LIMIT),
        cost_estimate=busy(5),
        name="closing",
    )(tokens_low, side_grad, block_output)


def side_body(x_ref, p_ref, qk_ref, v_ref, m_ref, out_ref):
    first = 0
    for left, right in ((x_ref, qk_ref), (x_ref, v_ref), (p_ref, m_ref)):
        last = first + right.shape[1]
        out_ref[:, first:last] = lax.dot_general(
            left[...], right[...], (((0,), (0,)), ((), ())), preferred_element_type=jnp.float32
        ).astype(out_ref.dtype)
        first = last


def side_grads(inputs, grad_proj, grad_qk, grad_v, mixed):
    count, cols = inputs.shape
    extent = grad_qk.shape[1] + grad_v.shape[1] + mixed.shape[1]
    chunk = 256
    return pl.pallas_call(
        side_body,
        grid=(cols // chunk,),
        out_shape=jax.ShapeDtypeStruct((cols, extent), inputs.dtype),
        in_specs=[
            pl.BlockSpec((count, chunk), lambda n: (0, n)), pl.BlockSpec((count, chunk), lambda n: (0, n)),
            pl.BlockSpec(grad_qk.shape, lambda n: (0, 0)), pl.BlockSpec(grad_v.shape, lambda n: (0, 0)),
            pl.BlockSpec(mixed.shape, lambda n: (0, 0)),
        ],
        out_specs=pl.BlockSpec((chunk, extent), lambda n: (n, 0)),
        compiler_params=pltpu.CompilerParams(vmem_limit_bytes=VMEM_LIMIT),
        cost_estimate=busy(10),
        name="side_grads",
    )(inputs, grad_proj, grad_qk, grad_v, mixed)


def local(
    tokens,
    lengths,
    query_weight,
    key_weight,
    value_weight,
    output_weight,
    query_gain,
    key_gain,
    attention_gain,
    gate_weight,
    up_weight,
    down_weight,
    feedforward_gain,
    cotangent,
):
    low, f32 = jnp.bfloat16, jnp.float32
    planes, width = lax.axis_size("blk"), lax.axis_size("wide")
    slots = width // planes
    rows = tokens.shape[1]
    span = rows * planes
    count = slots * span
    share = query_weight.shape[1]
    heads = share // HD
    plane, place = lax.axis_index("blk"), lax.axis_index("wide")
    after = lambda value, *others: lax.optimization_barrier((value,) + others)[0]

    def sum_blk(value, axis):
        return lax.psum_scatter(value, "blk", scatter_dimension=axis, tiled=True)

    _, near_cotangent, mine = turn(
        turn_in_body, [tokens[0], cotangent[0]], [True, True, False], planes, slots, 1, "turn_in"
    )
    w_qk = after(jnp.concatenate([query_weight, key_weight], 1), mine)
    w_qk = lax.all_gather(w_qk, "blk", axis=0, tiled=True)
    gains = jnp.stack([query_gain, key_gain]).astype(f32)
    plane_lengths = lax.dynamic_slice_in_dim(lengths, plane * slots, slots, 0)
    segment, position = jax.vmap(lambda one: layout(one, span))(plane_lengths)
    begin = (jnp.arange(span, dtype=jnp.int32)[None] - position)[:, None, :]
    pairs, piece = piece_map(span, rows)
    order = sorted(pairs, key=lambda pair: pair[1])
    index = np.concatenate([np.arange(at, at + piece) for at, _ in order])
    starts = jnp.stack([plane_lengths[:, 0] * 0, plane_lengths[:, 0], plane_lengths[:, 0] + plane_lengths[:, 1]], 1)
    cos_a, sin_a, cos_b, sin_b, sign = rope_tables(index, starts)
    group = jnp.concatenate([segment[:, at : at + piece] for at, _ in order], 1)[..., None]
    pick = lambda table: jnp.where(
        group == 0, table[:, 0:1], jnp.where(group == 1, table[:, 1:2], table[:, 2:3])
    )
    cos_b, sin_b = pick(cos_b), pick(sin_b)
    cosine = cos_a * cos_b + sin_a * sin_b
    sine = (sin_a * cos_b - cos_a * sin_b) * sign

    inputs = gather(mine, width, slots, 2, "gather_tokens")
    w_v = lax.all_gather(after(value_weight, inputs), "blk", axis=0, tiled=True)
    pre = dot(inputs, w_qk)
    w_o = lax.all_gather(after(output_weight, pre), "blk", axis=1, tiled=True)
    squares = jnp.stack([jnp.sum(pre[:, a * share : (a + 1) * share] ** 2, -1) for a in (0, 1)])
    both = lax.dynamic_update_slice(
        jnp.zeros((2, D), f32), jnp.stack([attention_gain, feedforward_gain]).astype(f32), (0, place * share)
    )
    squares = jnp.concatenate([squares.reshape(-1, 128), both.reshape(-1, 128)])
    squares = total(squares, "wide", width, 3, "total_squares")
    both = squares[2 * count // 128 :].reshape(2, D)
    gain_mix, gain_feed = both[0], both[1]
    inverse = lax.rsqrt(squares[: 2 * count // 128].reshape(2, count) / D + EPS)
    inv_cols = inverse.T.reshape(slots, span, 2)
    pre_groups = pre.reshape(slots, span, 2 * share)
    value_rows = dot(inputs, after(w_v, squares)).astype(low).reshape(slots, span, share)
    queries, keys, values, mixed, logs = attend(
        pre_groups, value_rows, inv_cols, gains, cosine, sine, begin, heads, rows
    )
    mixed = mixed.reshape(count, share)
    hidden, hidden_low, proj_normed, proj_inv = scatter(
        [mixed], [w_o], width, slots, False, 4, "scatter_mixed", "norm", (mine, gain_mix[None])
    )
    block_output, first_half, second_half, feed_gain_part, gathered, activated, up_factor, gate_factor, grad_out = feed(
        hidden_low, near_cotangent, gate_weight, up_weight, down_weight, hidden, gain_feed[None], width, slots, 5,
        "feed",
    )
    down_first, first_rows, far_output = push(
        False, first_half, activated, width, slots, 6, "push_first", [block_output]
    )
    down_first = sum_blk(down_first, 1)
    down_second, grad_gate, grad_up = push(
        True, second_half, activated, width, slots, 7, "push_second",
        [down_weight, up_factor, gate_factor, first_rows],
    )
    down_second = sum_blk(down_second, 1)
    gate_part = contract_rows(gathered, grad_gate).astype(low)
    gate_grad = sum_blk(gate_part, 0)
    grad_hidden, grad_proj, mix_gain_part, up_part = pull(
        after(grad_gate, gate_part, down_first), grad_up, gate_weight, up_weight, gathered, grad_out, proj_normed,
        proj_inv, gain_mix[None], width, slots, 8, "pull",
    )
    up_grad = sum_blk(up_part, 0)
    grad_proj = gather(grad_proj, width, slots, 9, "gather_proj")
    grad_mixed = contract_cols(after(grad_proj, down_first, down_second), w_o).astype(low).reshape(slots, span, share)
    scaled_q, scaled_k, grad_v, sums, parts = attend_back(
        queries, keys, values, grad_mixed, logs, pre_groups, inv_cols, gains, cosine, sine, begin,
        heads, rows,
    )
    means = jnp.sum(sums, axis=0).reshape(count, 2).T.reshape(-1, 128)
    local_gains = lax.dynamic_update_slice(
        jnp.zeros((2, D), f32), jnp.sum(parts, axis=0), (0, place * share)
    )
    gain_parts = jnp.concatenate([local_gains, jnp.stack([mix_gain_part.sum(0), feed_gain_part.sum(0)])])
    means = jnp.concatenate([means, gain_parts.reshape(-1, 128)])
    means = total(after(means, gate_grad), "wide", width, 10, "total_means")
    gain_parts = means[2 * count // 128 :]
    means = means[: 2 * count // 128].reshape(2, count) / D

    def finish(scaled, index):
        normed = pre[:, index * share : (index + 1) * share] * inverse[index][:, None]
        scaled = scaled.reshape(count, share)
        return (inverse[index][:, None] * (scaled - normed * means[index][:, None])).astype(low)

    grad_qk = jnp.concatenate([finish(scaled_q, 0), finish(scaled_k, 1)], 1)
    grad_v = grad_v.reshape(count, share)
    side_part = side_grads(inputs, grad_proj, grad_qk, grad_v, mixed)
    tokens_low = scatter(
        [grad_qk, grad_v], [w_qk, w_v], width, slots, True, 11, "scatter_tokens", "add", (grad_hidden,)
    )
    down_grad = jnp.concatenate([down_first, down_second], 1).astype(f32)
    gate_grad, up_grad = gate_grad.astype(f32), up_grad.astype(f32)
    tokens_low, down_grad, gate_grad, up_grad = lax.optimization_barrier((tokens_low, down_grad, gate_grad, up_grad))
    _, block_output, tokens_grad, gain_sums = turn(
        turn_out_body, [tokens_low, far_output], [True, False, False],
        planes, slots, 14, "turn_out", gain_parts,
    )
    tokens_grad, query_grad, key_grad, value_grad, output_grad, block_output = closing(
        tokens_grad, sum_blk(side_part, 0), block_output
    )

    sums = gain_sums.reshape(4, D)
    portion = D // (planes * width)
    sums = lax.dynamic_slice_in_dim(sums, (plane * width + place) * portion, portion, 1)
    return (
        block_output[None],
        tokens_grad[None],
        query_grad,
        key_grad,
        value_grad,
        output_grad,
        sums[0],
        sums[1],
        sums[2],
        gate_grad,
        up_grad,
        down_grad,
        sums[3],
    )


def solution(mesh):
    placed = (
        P("wide", "blk", None),
        P(),
        P("blk", "wide"),
        P("blk", "wide"),
        P("blk", "wide"),
        P("wide", "blk"),
        P("wide"),
        P("wide"),
        P("wide"),
        P(None, "wide"),
        P(None, "wide"),
        P("wide", None),
        P("wide"),
        P("wide", "blk", None),
    )
    return jax.shard_map(
        local,
        mesh=mesh,
        in_specs=placed,
        out_specs=(
            P("wide", "blk", None),
            P("wide", "blk", None),
            P("blk", "wide"),
            P("blk", "wide"),
            P("blk", "wide"),
            P("wide", "blk"),
            P(("blk", "wide")),
            P(("blk", "wide")),
            P(("blk", "wide")),
            P("blk", "wide"),
            P("blk", "wide"),
            P("wide", "blk"),
            P(("blk", "wide")),
        ),
        check_vma=False,
    )
```
